32 devices in a mesh: grp: 2 (over x), chan: 16 (over z, y, core).
Axes of the slice: x: 2, y: 2, z: 4, core: 2. Of those that a mesh axis runs over, the one named last changes fastest.
Arguments:
- voltages: bfloat16 [2048, 104448], P(('grp', 'chan')), parts along dimension 0, may hold values from -8 to 8
- delays: float32 [4, 2048], P(None, ('grp', 'chan')), parts along dimension 1, may hold values from -2 to 2
- band_feeds: int32 [64, 256], replicated, may hold values from 0 to 1023, as said below
Outputs:
- visibilities: float32 [2048, 2, 256, 256], P(('grp', 'chan')), parts along dimension 0
- beams: float32 [2048, 384], P(('grp', 'chan')), parts along dimension 0
The draws below stay inside these ranges and needn't reach their ends.
There are 2 independent parts, one for each index of `grp`. The reference program is written for one: setup_inputs(seed, part) draws one part's arguments, and reference() takes and returns one part's arrays. A program takes and returns all parts, laid end to end along the dimension named above; an argument that names none is the same for every part. Nothing has to cross between parts.
Inputs may be any that keep to these rules, and one draw needn't show every extreme that they name: `band_feeds`: each row lists 256 distinct feeds in increasing order. Of each aligned block of 64 feeds at most 32 are listed in one row, and every row has a block with exactly 32 listed.
All inputs are finite; a program needn't handle non-finite values.
Results may differ from the reference program's by a relative error of at most 0.0056.
Values may be sent and summed in bfloat16 or wider, within the bound.
No kernel may reach another device: no remote copies, remote signals or barrier semaphores. Data moves between devices by JAX's collectives and lax.ppermute only.
A program may use at most 192 MiB of HBM per device.

```python
import jax
import jax.numpy as jnp
from jax import lax

F = 1024
CHANNELS = 1024
TAPS = 4
BAND_CH = 16
BEAMS = 4
FR = 48
NFFT = 2048
SAMPLES = 104448
BANDS = 64
FSUB = 256
FEED_DEV = 64
FEED_CAP = 32


def draw_voltages(key, part):
    key = jax.random.fold_in(key, 5)
    key_noise, key_rough = jax.random.split(key, 2)
    feed_ids = jnp.arange(F, dtype=jnp.float32)
    ramp = 0.5 * (1.0 + 2.0 * feed_ids / (F - 1))
    rough = jnp.exp(jax.random.uniform(key_rough, (F,), jnp.float32, -0.55, 0.55))
    noise = jax.random.normal(key_noise, (F, SAMPLES), jnp.float32)
    values = (ramp * rough)[:, None] * noise
    return jnp.clip(values, -8.0, 8.0).astype(jnp.bfloat16)


def draw_band_feeds(key, part):
    key = jax.random.fold_in(key, 9)
    key_count, key_pick, key_rank, key_other = jax.random.split(key, 4)
    block_total = F // FEED_DEV
    pair_total = block_total // 2
    low_share = jax.random.randint(key_count, (BANDS, pair_total), 0, FEED_CAP + 1)
    high_share = FEED_CAP - low_share
    forced = jax.random.randint(key_pick, (BANDS,), 0, pair_total)
    offset = jax.random.randint(key_other, (BANDS,), 1, pair_total)
    emptied = (forced + offset) % pair_total
    pair_ids = jnp.arange(pair_total)[None, :]
    is_forced = pair_ids == forced[:, None]
    is_emptied = pair_ids == emptied[:, None]
    low_share = jnp.where(is_forced, FEED_CAP, jnp.where(is_emptied, 0, low_share))
    high_share = jnp.where(is_forced, FEED_CAP, jnp.where(is_emptied, 0, high_share))
    per_block = jnp.stack([low_share, high_share], axis=2).reshape(BANDS, block_total)
    base_ids = jnp.broadcast_to(jnp.arange(FEED_DEV, dtype=jnp.int32), (BANDS, block_total, FEED_DEV))
    ranks = jax.random.permutation(key_rank, base_ids, axis=2, independent=True)
    member = (ranks < per_block[:, :, None]).reshape(BANDS, F).astype(jnp.int32)
    ordered = jnp.argsort(1 - member, axis=1, stable=True)
    return ordered[:, :FSUB].astype(jnp.int32)


def level_of(key, extent, pieces, least, largest):
    level = 1.0
    for axis_at, blocks in pieces:
        heights = jax.random.uniform(jax.random.fold_in(jax.random.fold_in(key, 6), axis_at), (blocks,), jnp.float32, least / len(pieces), largest / len(pieces))
        level = level * jnp.repeat(jnp.exp(heights), extent[axis_at] // blocks).reshape((-1,) + (1,) * (len(extent) - 1 - axis_at))
    return level


def setup_inputs(seed: int = 0, part: int = 0) -> dict:
    keys = jax.random.split(jax.random.key(seed), 4)
    own_keys = jax.random.split(jax.random.fold_in(keys[3], part), 4)
    return {
        "voltages": draw_voltages(jax.random.fold_in(jax.random.fold_in(keys[3], part), 71), part),
        "delays": jnp.clip(jax.random.uniform(own_keys[1], (BEAMS, F), jnp.float32, -2.0, 2.0) * level_of(own_keys[1], (BEAMS, F), ((1, 16),), -0.4, 0.0), -2.0, 2.0),
        "band_feeds": draw_band_feeds(jax.random.fold_in(keys[3], 71), part),
    }


def fir_window(taps, nfft):
    sample_ids = jnp.arange(taps * nfft, dtype=jnp.float32)
    centered = (sample_ids - 0.5 * taps * nfft + 0.5) / nfft
    hann_part = 0.5 - 0.5 * jnp.cos(2.0 * jnp.pi * (sample_ids + 0.5) / (taps * nfft))
    return (jnp.sinc(centered) * hann_part).reshape(taps, nfft)

def dft_basis(nfft, bands, band_ch):
    sample_ids = jnp.arange(nfft, dtype=jnp.int32)
    chan_ids = jnp.arange(bands * band_ch, dtype=jnp.int32)
    turns = sample_ids[:, None] * chan_ids[None, :] % nfft
    angles = turns.astype(jnp.float32) * (2.0 * jnp.pi / nfft)
    cosine = jnp.cos(angles).reshape(nfft, bands, 1, band_ch)
    sine = (-jnp.sin(angles)).reshape(nfft, bands, 1, band_ch)
    return jnp.concatenate([cosine, sine], axis=2).reshape(nfft, bands * 2 * band_ch).astype(jnp.bfloat16)

def reference(voltages, delays, band_feeds):
    window = fir_window(TAPS, NFFT)
    frames_in = voltages.reshape(F, FR + TAPS - 1, NFFT)
    filtered = jnp.zeros((F, FR, NFFT), jnp.float32)
    for tap_index in range(TAPS):
        filtered = filtered + window[tap_index][None, None, :] * frames_in[:, tap_index:tap_index + FR, :].astype(jnp.float32)
    filtered = filtered.astype(jnp.bfloat16)
    basis = dft_basis(NFFT, BANDS, BAND_CH)
    spectral_scale = jnp.sqrt(2.0 / jnp.sum(window * window))
    spectra = jnp.dot(filtered.reshape(F * FR, NFFT).astype(jnp.float32), basis.astype(jnp.float32), precision=lax.Precision.HIGHEST) * spectral_scale
    spectra = spectra.reshape(F, FR, BANDS, 2, BAND_CH)
    sent = spectra.astype(jnp.bfloat16)

    def one_band(band_args):
        band_index, feed_list = band_args
        slab = lax.dynamic_index_in_dim(sent, band_index, 2, keepdims=False)
        chosen = jnp.take(slab, feed_list, axis=0).astype(jnp.float32)
        real_vis = jnp.einsum('ptrk,qtrk->kpq', chosen, chosen, precision=lax.Precision.HIGHEST)
        cross_sum = jnp.einsum('ptk,qtk->kpq', chosen[:, :, 1, :], chosen[:, :, 0, :], precision=lax.Precision.HIGHEST)
        imag_vis = cross_sum - jnp.swapaxes(cross_sum, 1, 2)
        return jnp.stack([real_vis, imag_vis], axis=1) / FR
    band_vis = lax.map(one_band, (jnp.arange(BANDS, dtype=jnp.int32), band_feeds))
    visibilities = band_vis.reshape(CHANNELS, 2, FSUB, FSUB)
    real_component = spectra[:, :, :, 0, :].reshape(F, FR, CHANNELS)
    imaginary_component = spectra[:, :, :, 1, :].reshape(F, FR, CHANNELS)
    chan_float = jnp.arange(CHANNELS, dtype=jnp.int32).astype(jnp.float32)
    phase = 2.0 * jnp.pi / NFFT * (delays[:, :, None] * chan_float[None, None, :])
    cosine_weight = jnp.cos(phase)
    sine_weight = jnp.sin(phase)
    highest_precision = lax.Precision.HIGHEST
    phased_beam_real = jnp.einsum('xez,ebz->zxb', cosine_weight, real_component, precision=highest_precision) + jnp.einsum('xez,ebz->zxb', sine_weight, imaginary_component, precision=highest_precision)
    phased_beam_imaginary = jnp.einsum('xez,ebz->zxb', cosine_weight, imaginary_component, precision=highest_precision) - jnp.einsum('xez,ebz->zxb', sine_weight, real_component, precision=highest_precision)
    beams = jnp.stack([phased_beam_real, phased_beam_imaginary], axis=1).reshape(CHANNELS, 2 * BEAMS * FR) / jnp.sqrt(jnp.float32(F))
    return (visibilities, beams)
```

```python
import functools

import jax
import jax.numpy as jnp
import ml_dtypes
import numpy as np
from jax import lax
from jax.experimental import pallas as pl
from jax.experimental.pallas import tpu as pltpu
from jax.sharding import PartitionSpec as P

F = 1024
CHANNELS = 1024
TAPS = 4
BAND_CH = 16
BEAMS = 4
FR = 48
NFFT = 2048
BANDS = 64
FSUB = 256
LANES = 128
CHUNKS = 4
VMEM = 56 * 1024 * 1024

NT = (((1,), (1,)), ((), ()))
TN = (((0,), (0,)), ((), ()))


def fir_window():
    ids = np.arange(TAPS * NFFT, dtype=np.float64)
    centered = (ids - 0.5 * TAPS * NFFT + 0.5) / NFFT
    hann_part = 0.5 - 0.5 * np.cos(2.0 * np.pi * (ids + 0.5) / (TAPS * NFFT))
    return (np.sinc(centered) * hann_part).reshape(TAPS, NFFT)


def dft_rows(chan_ids):
    m = np.arange(NFFT, dtype=np.int64)
    turns = (chan_ids[..., None].astype(np.int64) * m) % NFFT
    table = 2.0 * np.pi * np.arange(NFFT) / NFFT
    cosine = np.cos(table).astype(np.float32).astype(ml_dtypes.bfloat16)
    sine = (-np.sin(table)).astype(np.float32).astype(ml_dtypes.bfloat16)
    return np.stack([cosine[turns], sine[turns]], axis=1)


class Sizes:
    def __init__(self, devices, feed_dev):
        self.devices = devices
        self.feed_dev = feed_dev
        self.cap = feed_dev // 2
        self.lane_frames = LANES // self.cap
        self.quads = FR // self.lane_frames
        self.width = self.lane_frames * feed_dev
        self.steps = 6 if self.quads % 6 == 0 else self.quads
        self.step_frames = FR // self.steps
        self.step_quads = self.quads // self.steps
        self.step_lanes = self.step_frames * feed_dev
        self.chan_dev = CHANNELS // devices
        self.bands_here = BANDS // devices
        self.chunks = min(CHUNKS, self.chan_dev // 8)
        self.chunk_ch = self.chan_dev // self.chunks
        self.rows_dev = 2 * self.chunk_ch
        self.rows = devices * self.rows_dev
        self.groups = devices // self.lane_frames


def pick_rows(z, st_ref, key_ref, send_ref):
    def body(d, carry):
        start = pl.multiple_of(d * z.rows_dev, z.rows_dev)
        parts = []
        for g in range(z.steps):
            for q in range(z.step_quads):
                parts.append(st_ref[g, pl.ds(start, z.rows_dev), q * z.width : (q + 1) * z.width])
        lhs = jnp.concatenate(parts, axis=0)
        key = key_ref[pl.ds(d, 1), :]
        slot = lax.broadcasted_iota(jnp.int32, (LANES, z.width), 0)
        pick = jnp.where(slot == key, 1.0, 0.0).astype(jnp.bfloat16)
        out = lax.dot_general(lhs, pick, NT, preferred_element_type=jnp.float32)
        send_ref[d] = out.astype(jnp.bfloat16).reshape(z.quads, z.rows_dev, LANES)
        return carry

    lax.fori_loop(0, z.devices, body, 0)


def transform(z, scale, filt_ref, basis_ref, key_ref, spec_ref, send_ref, st_ref):
    g = pl.program_id(0)
    spectra = lax.dot_general(
        basis_ref[...], filt_ref[...], NT, preferred_element_type=jnp.float32
    )
    spectra = (spectra * scale).astype(jnp.bfloat16)
    spec_ref[...] = spectra
    st_ref[g] = spectra

    @pl.when(g == z.steps - 1)
    def _():
        pick_rows(z, st_ref, key_ref, send_ref)


def first_kernel(
    z, scale, main_ref, h0_ref, h1_ref, h2_ref, win_ref, basis_ref, key_ref,
    filt_ref, spec_ref, send_ref, st_ref,
):
    halo = (h0_ref, h1_ref, h2_ref)

    def body(i, carry):
        off = pl.multiple_of(i * LANES, LANES)
        taps = [win_ref[k : k + 1, pl.ds(off, LANES)] for k in range(TAPS)]
        for f0 in range(0, z.feed_dev, 16):
            frames = []
            for t in range(z.step_frames + TAPS - 1):
                if t < z.step_frames:
                    x = main_ref[f0 : f0 + 16, pl.ds(t * NFFT + off, LANES)]
                else:
                    x = halo[t - z.step_frames][f0 : f0 + 16, pl.ds(off, LANES)]
                frames.append(x.astype(jnp.float32))
            for t in range(z.step_frames):
                total = taps[0] * frames[t]
                for k in range(1, TAPS):
                    total = total + taps[k] * frames[t + k]
                row = t * z.feed_dev + f0
                filt_ref[row : row + 16, pl.ds(off, LANES)] = total.astype(jnp.bfloat16)
        return carry

    lax.fori_loop(0, NFFT // LANES, body, 0)
    transform(z, scale, filt_ref, basis_ref, key_ref, spec_ref, send_ref, st_ref)


def next_kernel(z, scale, filt_ref, basis_ref, key_ref, spec_ref, send_ref, st_ref):
    transform(z, scale, filt_ref, basis_ref, key_ref, spec_ref, send_ref, st_ref)


def whole_spec(shape):
    return pl.BlockSpec(shape, lambda g: (0,) * len(shape))


def spectra_call(z, scale, basis, key, filt=None, voltages=None, window=None):
    filt_rows = z.step_frames * z.feed_dev
    filt_spec = pl.BlockSpec((filt_rows, NFFT), lambda g: (g, 0))
    spec_shape = jax.ShapeDtypeStruct((z.rows, FR * z.feed_dev), jnp.bfloat16)
    spec_spec = pl.BlockSpec((z.rows, z.step_lanes), lambda g: (0, g))
    send_dims = (z.devices, z.quads, z.rows_dev, LANES)
    send_shape = jax.ShapeDtypeStruct(send_dims, jnp.bfloat16)
    shared = [whole_spec((z.rows, NFFT)), whole_spec((z.devices, z.width))]
    flops = 2 * z.rows * NFFT * FR * z.feed_dev
    common = dict(
        grid=(z.steps,),
        scratch_shapes=[pltpu.VMEM((z.steps, z.rows, z.step_lanes), jnp.bfloat16)],
        compiler_params=pltpu.CompilerParams(vmem_limit_bytes=VMEM),
        cost_estimate=pl.CostEstimate(
            flops=flops, bytes_accessed=20_000_000, transcendentals=0
        ),
    )
    if filt is not None:
        return pl.pallas_call(
            functools.partial(next_kernel, z, scale),
            in_specs=[filt_spec] + shared,
            out_specs=[spec_spec, whole_spec(send_dims)],
            out_shape=[spec_shape, send_shape],
            name="spectra_next",
            **common,
        )(filt, basis, key)

    def halo_spec(h):
        return pl.BlockSpec((z.feed_dev, NFFT), lambda g: (0, z.step_frames * (g + 1) + h))

    return pl.pallas_call(
        functools.partial(first_kernel, z, scale),
        in_specs=[
            pl.BlockSpec((z.feed_dev, z.step_frames * NFFT), lambda g: (0, g)),
            halo_spec(0),
            halo_spec(1),
            halo_spec(2),
            whole_spec((TAPS, NFFT)),
        ]
        + shared,
        out_specs=[filt_spec, spec_spec, whole_spec(send_dims)],
        out_shape=[
            jax.ShapeDtypeStruct((FR * z.feed_dev, NFFT), jnp.bfloat16),
            spec_shape,
            send_shape,
        ],
        name="filter_spectra",
        **common,
    )(voltages, voltages, voltages, voltages, window, basis, key)


def receive_kernel(z, step_ch, arr_ref, key_ref, *refs):
    vis_ref, rows_ref = refs[-2], refs[-1]
    g = pl.program_id(0)
    depth = z.quads * z.rows_dev
    lf = z.lane_frames

    @pl.when(g == 0)
    def _():
        lane_group = lax.broadcasted_iota(jnp.int32, (depth, LANES), 1) // z.cap
        slot = lax.broadcasted_iota(jnp.int32, (z.groups * LANES, FSUB), 0)

        def body(tau, carry):
            tiles = []
            for big in range(z.groups):
                tile = None
                for lane in range(lf):
                    source = big * lf + lax.rem(lane - tau + lf, lf)
                    block = arr_ref[source].reshape(depth, LANES)
                    if tile is None:
                        tile = block
                    else:
                        tile = jnp.where(lane_group == lane, block, tile)
                tiles.append(tile)
            lhs = jnp.concatenate(tiles, axis=1)
            pick = jnp.where(slot == key_ref[pl.ds(tau, 1), :], 1.0, 0.0).astype(jnp.bfloat16)
            start = pl.multiple_of(tau * depth, depth)
            rows = jnp.dot(lhs, pick, preferred_element_type=jnp.float32)
            for half in range(FSUB // LANES):
                rows_ref[half, pl.ds(start, depth), :] = rows[:, half * LANES : (half + 1) * LANES]
            return carry

        lax.fori_loop(0, lf, body, 0)

    for i in range(step_ch):
        ch = g * step_ch + i
        halves = []
        for part in range(2):
            halves.append(
                jnp.concatenate(
                    [
                        rows_ref[half, pl.ds(ch + part * z.chunk_ch, FR, stride=z.rows_dev), :]
                        for half in range(FSUB // LANES)
                    ],
                    axis=1,
                )
            )
        real, imag = halves
        right = jnp.concatenate([real, imag], axis=0)
        swapped = jnp.concatenate([imag, -real], axis=0)
        left = jnp.concatenate([right.T, swapped.T], axis=0).astype(jnp.bfloat16)
        both = jnp.dot(left, right.astype(jnp.bfloat16), preferred_element_type=jnp.float32)
        both = both * (1.0 / FR)
        vis_ref[i, 0] = both[:FSUB]
        vis_ref[i, 1] = both[FSUB:]


def receive_call(z, chunk, arrived, key, vis):
    step_ch = 4
    steps = z.chunk_ch // step_ch
    out_shape = jax.ShapeDtypeStruct((z.chan_dev, 2, FSUB, FSUB), jnp.float32)
    in_specs = [whole_spec(arrived.shape), whole_spec(key.shape)]
    operands = [arrived, key]
    aliases = {}
    if vis is not None:
        in_specs.append(pl.BlockSpec(memory_space=pl.ANY))
        operands.append(vis)
        aliases = {2: 0}
    return pl.pallas_call(
        functools.partial(receive_kernel, z, step_ch),
        grid=(steps,),
        in_specs=in_specs,
        out_specs=pl.BlockSpec(
            (step_ch, 2, FSUB, FSUB), lambda g: (chunk * steps + g, 0, 0, 0)
        ),
        out_shape=out_shape,
        input_output_aliases=aliases,
        scratch_shapes=[
            pltpu.VMEM((FSUB // LANES, FR * z.rows_dev, LANES), jnp.float32)
        ],
        compiler_params=pltpu.CompilerParams(vmem_limit_bytes=VMEM),
        cost_estimate=pl.CostEstimate(
            flops=4_000_000_000, bytes_accessed=10_000_000, transcendentals=0
        ),
        name="correlate",
    )(*operands)


def beam_kernel(z, step_dev, *refs):
    spec_refs = refs[: z.chunks]
    cos_ref, sin_ref, sum_ref, out_ref, prod_ref = refs[z.chunks :]
    count = step_dev * z.chunk_ch
    for k in range(z.chunks):

        def body(q, carry):
            off = pl.multiple_of(q * z.width, z.width)
            x = spec_refs[k][:, pl.ds(off, z.width)].astype(jnp.float32)
            x = x.reshape(step_dev, 2, z.chunk_ch, z.width)
            real = x[:, 0].reshape(count, z.width)
            imag = x[:, 1].reshape(count, z.width)
            for g in range(BEAMS):
                c = cos_ref[k, g].astype(jnp.float32)
                s = sin_ref[k, g].astype(jnp.float32)
                a = (c * real + s * imag).astype(jnp.bfloat16)
                b = (c * imag - s * real).astype(jnp.bfloat16)
                prod_ref[g * count : (g + 1) * count, pl.ds(off, z.width)] = a
                top = (BEAMS + g) * count
                prod_ref[top : top + count, pl.ds(off, z.width)] = b
            return carry

        lax.fori_loop(0, z.quads, body, 0)
        sums = jnp.dot(prod_ref[...], sum_ref[...], preferred_element_type=jnp.float32)
        sums = sums * (1.0 / np.sqrt(F))
        for j in range(2 * BEAMS):
            part = sums[j * count : (j + 1) * count, :FR].reshape(step_dev, z.chunk_ch, FR)
            rows = slice(k * z.chunk_ch, (k + 1) * z.chunk_ch)
            out_ref[:, rows, j * FR : (j + 1) * FR] = part


def beam_call(z, spectra, cos_w, sin_w):
    step_dev = max(1, 64 // z.chunk_ch)
    steps = z.devices // step_dev
    count = step_dev * z.chunk_ch
    lanes = FR * z.feed_dev
    frame = np.arange(lanes) // z.feed_dev
    sums = (frame[:, None] == np.arange(LANES)[None, :]).astype(ml_dtypes.bfloat16)
    weight_spec = pl.BlockSpec((z.chunks, BEAMS, count, z.width), lambda g: (0, 0, g, 0))
    out = pl.pallas_call(
        functools.partial(beam_kernel, z, step_dev),
        grid=(steps,),
        in_specs=[
            pl.BlockSpec((step_dev * z.rows_dev, lanes), lambda g: (g, 0))
            for _ in range(z.chunks)
        ]
        + [weight_spec, weight_spec, whole_spec((lanes, LANES))],
        out_specs=pl.BlockSpec((step_dev, z.chan_dev, 2 * BEAMS * FR), lambda g: (g, 0, 0)),
        out_shape=jax.ShapeDtypeStruct((z.devices, z.chan_dev, 2 * BEAMS * FR), jnp.float32),
        scratch_shapes=[pltpu.VMEM((2 * BEAMS * count, lanes), jnp.bfloat16)],
        compiler_params=pltpu.CompilerParams(vmem_limit_bytes=VMEM),
        cost_estimate=pl.CostEstimate(
            flops=20_000_000_000, bytes_accessed=20_000_000, transcendentals=0
        ),
        name="beam_sums",
    )(*spectra, cos_w, sin_w, jnp.asarray(sums))
    return out.reshape(CHANNELS, 2 * BEAMS * FR)


def on_device(voltages, delays, band_feeds):
    z = Sizes(lax.axis_size("chan"), voltages.shape[0])
    me = lax.axis_index("chan")
    turn = lax.rem(me, z.lane_frames)
    window = fir_window()
    scale = float(np.sqrt(2.0 / np.sum(window * window)))
    window = jnp.asarray(window.astype(np.float32))

    edges = me * z.feed_dev + jnp.arange(z.feed_dev + 1, dtype=jnp.int32)
    below = jnp.sum(
        (band_feeds[:, None, :] < edges[None, :, None]).astype(jnp.int32), axis=2
    )
    rank = below[:, :-1] - below[:, :1]
    listed = below[:, 1:] > below[:, :-1]
    lane = jnp.arange(z.lane_frames, dtype=jnp.int32)
    group = lax.rem(lane + turn, z.lane_frames) * z.cap
    send_key = jnp.where(listed[:, None, :], rank[:, None, :] + group[None, :, None], -1)
    send_key = send_key.reshape(z.devices, z.bands_here, z.width)

    own = lax.dynamic_slice_in_dim(band_feeds, me * z.bands_here, z.bands_here, 0)
    source = own // z.feed_dev
    before = jnp.sum(
        (own[:, None, :] < (source * z.feed_dev)[:, :, None]).astype(jnp.int32), axis=2
    )
    place = jnp.arange(FSUB, dtype=jnp.int32)[None, :] - before
    base = (source // z.lane_frames) * LANES + place
    shift = lax.rem(source, z.lane_frames)
    take_key = base[:, None, :] + z.cap * lax.rem(
        shift[:, None, :] + lane[None, :, None], z.lane_frames
    )

    ids = np.arange(CHANNELS).reshape(z.devices, z.chunks, z.chunk_ch)
    chunk_ids = np.transpose(ids, (1, 0, 2))

    filt = None
    spectra = []
    arrived = []
    for k in range(z.chunks):
        band = k * z.chunk_ch // BAND_CH
        basis = jnp.asarray(dft_rows(chunk_ids[k]).reshape(z.rows, NFFT))
        key = send_key[:, band]
        if k == 0:
            filt, spec, send = spectra_call(
                z, scale, basis, key, voltages=voltages, window=window
            )
        else:
            spec, send = spectra_call(z, scale, basis, key, filt=filt)
        spectra.append(spec)
        arrived.append(lax.all_to_all(send, "chan", split_axis=0, concat_axis=0, tiled=True))

    chan_float = jnp.asarray(chunk_ids.reshape(z.chunks, 1, -1, 1).astype(np.float32))
    phase = 2.0 * jnp.pi / NFFT * (delays[None, :, None, :] * chan_float)
    cos_w = jnp.tile(jnp.cos(phase).astype(jnp.bfloat16), (1, 1, 1, z.lane_frames))
    sin_w = jnp.tile(jnp.sin(phase).astype(jnp.bfloat16), (1, 1, 1, z.lane_frames))
    partial_beams = beam_call(z, spectra, cos_w, sin_w)
    beams = lax.psum_scatter(partial_beams, "chan", scatter_dimension=0, tiled=True)

    vis = None
    for k in range(z.chunks):
        band = k * z.chunk_ch // BAND_CH
        vis = receive_call(z, k, arrived[k], take_key[band], vis)
    return (vis, beams)


def solution(mesh):
    in_specs = (P(("grp", "chan"), None), P(None, ("grp", "chan")), P())
    out_specs = (P(("grp", "chan"), None, None, None), P(("grp", "chan"), None))
    return jax.shard_map(
        on_device, mesh=mesh, in_specs=in_specs, out_specs=out_specs, check_vma=False
    )
```

```python
import functools

import jax
import jax.numpy as jnp
import ml_dtypes
import numpy as np
from jax import lax
from jax.experimental import pallas as pl
from jax.experimental.pallas import tpu as pltpu
from jax.sharding import PartitionSpec as P

F = 1024
CHANNELS = 1024
TAPS = 4
BAND_CH = 16
BEAMS = 4
FR = 48
NFFT = 2048
BANDS = 64
FSUB = 256
LANES = 128
VMEM = 56 * 1024 * 1024

NT = (((1,), (1,)), ((), ()))


def fir_window():
    ids = np.arange(TAPS * NFFT, dtype=np.float64)
    centered = (ids - 0.5 * TAPS * NFFT + 0.5) / NFFT
    hann_part = 0.5 - 0.5 * np.cos(2.0 * np.pi * (ids + 0.5) / (TAPS * NFFT))
    return (np.sinc(centered) * hann_part).reshape(TAPS, NFFT)


def dft_rows(chan_ids):
    m = np.arange(NFFT, dtype=np.int64)
    turns = (chan_ids[..., None].astype(np.int64) * m) % NFFT
    table = 2.0 * np.pi * np.arange(NFFT) / NFFT
    cosine = np.cos(table).astype(np.float32).astype(ml_dtypes.bfloat16)
    sine = (-np.sin(table)).astype(np.float32).astype(ml_dtypes.bfloat16)
    return np.stack([cosine[turns], sine[turns]], axis=1)


class Sizes:
    def __init__(self, devices, feed_dev):
        self.devices = devices
        self.feed_dev = feed_dev
        self.cap = feed_dev // 2
        self.lane_frames = LANES // self.cap
        self.quads = FR // self.lane_frames
        self.width = self.lane_frames * feed_dev
        self.steps = 6 if self.quads % 6 == 0 else self.quads
        self.step_frames = FR // self.steps
        self.step_quads = self.quads // self.steps
        self.step_lanes = self.step_frames * feed_dev
        self.chan_dev = CHANNELS // devices
        self.bands_here = BANDS // devices
        self.chunks = self.chan_dev // BAND_CH
        self.chunk_ch = BAND_CH
        self.rows_dev = 2 * self.chunk_ch
        self.rows = devices * self.rows_dev
        self.groups = devices // self.lane_frames


def transform(z, scale, count, me_ref, filt_ref, basis_ref, loc_ref, out_refs, st_ref):
    spec_refs, send_refs = out_refs[:count], out_refs[count:]
    me = me_ref[0]
    spectra = lax.dot_general(
        basis_ref[...], filt_ref[...], NT, preferred_element_type=jnp.float32
    )
    spectra = spectra * scale
    st_ref[...] = spectra
    for c in range(count):
        spec_refs[c][...] = spectra[c * z.rows : (c + 1) * z.rows].astype(jnp.bfloat16)
    lane_group = lax.broadcasted_iota(jnp.int32, (z.rows_dev, LANES), 1) // z.cap
    half = z.lane_frames // 2
    for c in range(count):
        for k in range(z.devices):
            owner = me ^ k
            start = pl.multiple_of(c * z.rows + owner * z.rows_dev, z.rows_dev)
            frame = lane_group ^ (k % z.lane_frames)
            lower = frame < half
            index = loc_ref[c, pl.ds(owner, 1), :] + (frame % half) * z.feed_dev
            for q in range(z.step_quads):
                parts = []
                for side in range(2):
                    lane = q * z.width + side * LANES
                    x = st_ref[pl.ds(start, z.rows_dev), lane : lane + LANES]
                    parts.append(
                        jnp.take_along_axis(x, index, axis=1, mode="promise_in_bounds")
                    )
                picked = jnp.where(lower, parts[0], parts[1])
                send_refs[c * z.devices + k][q] = picked.astype(jnp.bfloat16)


def first_kernel(
    z, scale, me_ref, main_ref, h0_ref, h1_ref, h2_ref, win_ref, basis_ref, loc_ref, *refs
):
    filt_ref, out_refs, st_ref = refs[0], refs[1:-1], refs[-1]
    halo = (h0_ref, h1_ref, h2_ref)

    def body(i, carry):
        off = pl.multiple_of(i * LANES, LANES)
        taps = [win_ref[k : k + 1, pl.ds(off, LANES)] for k in range(TAPS)]
        for f0 in range(0, z.feed_dev, 16):
            frames = []
            for t in range(z.step_frames + TAPS - 1):
                if t < z.step_frames:
                    x = main_ref[f0 : f0 + 16, pl.ds(t * NFFT + off, LANES)]
                else:
                    x = halo[t - z.step_frames][f0 : f0 + 16, pl.ds(off, LANES)]
                frames.append(x.astype(jnp.float32))
            for t in range(z.step_frames):
                total = taps[0] * frames[t]
                for k in range(1, TAPS):
                    total = total + taps[k] * frames[t + k]
                row = t * z.feed_dev + f0
                filt_ref[row : row + 16, pl.ds(off, LANES)] = total.astype(jnp.bfloat16)
        return carry

    lax.fori_loop(0, NFFT // LANES, body, 0)
    transform(z, scale, 1, me_ref, filt_ref, basis_ref, loc_ref, out_refs, st_ref)


def next_kernel(z, scale, count, me_ref, filt_ref, basis_ref, loc_ref, *refs):
    transform(z, scale, count, me_ref, filt_ref, basis_ref, loc_ref, refs[:-1], refs[-1])


def whole_spec(shape):
    return pl.BlockSpec(shape, lambda *g: (0,) * len(shape))


def spectra_call(z, scale, me, basis, loc, filt=None, voltages=None, window=None):
    count = loc.shape[0]
    filt_rows = z.step_frames * z.feed_dev
    filt_spec = pl.BlockSpec((filt_rows, NFFT), lambda g: (g, 0))
    spec_shape = jax.ShapeDtypeStruct((z.rows, FR * z.feed_dev), jnp.bfloat16)
    spec_spec = pl.BlockSpec((z.rows, z.step_lanes), lambda g: (0, g))
    send_shape = jax.ShapeDtypeStruct((z.quads, z.rows_dev, LANES), jnp.bfloat16)
    send_spec = pl.BlockSpec((z.step_quads, z.rows_dev, LANES), lambda g: (g, 0, 0))
    me_spec = pl.BlockSpec(memory_space=pltpu.SMEM)
    shared = [whole_spec(basis.shape), whole_spec(loc.shape)]
    out_specs = [spec_spec] * count + [send_spec] * (count * z.devices)
    out_shape = [spec_shape] * count + [send_shape] * (count * z.devices)
    flops = 2 * count * z.rows * NFFT * FR * z.feed_dev
    common = dict(
        grid=(z.steps,),
        scratch_shapes=[pltpu.VMEM((count * z.rows, z.step_lanes), jnp.float32)],
        compiler_params=pltpu.CompilerParams(vmem_limit_bytes=VMEM),
        cost_estimate=pl.CostEstimate(
            flops=flops, bytes_accessed=20_000_000, transcendentals=0
        ),
    )
    if filt is not None:
        outs = pl.pallas_call(
            functools.partial(next_kernel, z, scale, count),
            in_specs=[me_spec, filt_spec] + shared,
            out_specs=out_specs,
            out_shape=out_shape,
            name="spectra_next",
            **common,
        )(me, filt, basis, loc)
        return None, outs[:count], outs[count:]

    def halo_spec(h):
        return pl.BlockSpec((z.feed_dev, NFFT), lambda g: (0, z.step_frames * (g + 1) + h))

    outs = pl.pallas_call(
        functools.partial(first_kernel, z, scale),
        in_specs=[
            me_spec,
            pl.BlockSpec((z.feed_dev, z.step_frames * NFFT), lambda g: (0, g)),
            halo_spec(0),
            halo_spec(1),
            halo_spec(2),
            whole_spec((TAPS, NFFT)),
        ]
        + shared,
        out_specs=[filt_spec] + out_specs,
        out_shape=[jax.ShapeDtypeStruct((FR * z.feed_dev, NFFT), jnp.bfloat16)] + out_shape,
        name="filter_spectra",
        **common,
    )(me, voltages, voltages, voltages, voltages, window, basis, loc)
    return outs[0], outs[1 : 1 + count], outs[1 + count :]


def receive_kernel(z, step_ch, *refs):
    arr_refs, key_ref = refs[: z.devices], refs[z.devices]
    vis_ref, rows_ref = refs[-2], refs[-1]
    g = pl.program_id(0)
    depth = z.quads * z.rows_dev
    lf = z.lane_frames

    @pl.when(g == 0)
    def _():
        lane_group = lax.broadcasted_iota(jnp.int32, (depth, LANES), 1) // z.cap
        slot = lax.broadcasted_iota(jnp.int32, (z.groups * LANES, FSUB), 0)
        for tau in range(lf):
            tiles = []
            for big in range(z.groups):
                tile = arr_refs[big * lf + tau][...].reshape(depth, LANES)
                for lane in range(1, lf):
                    block = arr_refs[big * lf + (lane ^ tau)][...].reshape(depth, LANES)
                    tile = jnp.where(lane_group == lane, block, tile)
                tiles.append(tile)
            lhs = jnp.concatenate(tiles, axis=1)
            pick = jnp.where(slot == key_ref[tau : tau + 1, :], 1.0, 0.0).astype(jnp.bfloat16)
            rows = jnp.dot(lhs, pick, preferred_element_type=jnp.float32)
            for half in range(FSUB // LANES):
                rows_ref[half, tau * depth : (tau + 1) * depth, :] = rows[
                    :, half * LANES : (half + 1) * LANES
                ]

    for i in range(step_ch):
        ch = g * step_ch + i
        halves = []
        for part in range(2):
            halves.append(
                jnp.concatenate(
                    [
                        rows_ref[half, pl.ds(ch + part * z.chunk_ch, FR, stride=z.rows_dev), :]
                        for half in range(FSUB // LANES)
                    ],
                    axis=1,
                )
            )
        real, imag = halves
        right = jnp.concatenate([real, imag], axis=0)
        swapped = jnp.concatenate([imag, -real], axis=0)
        left = jnp.concatenate([right.T, swapped.T], axis=0).astype(jnp.bfloat16)
        both = jnp.dot(left, right.astype(jnp.bfloat16), preferred_element_type=jnp.float32)
        both = both * (1.0 / FR)
        vis_ref[i, 0] = both[:FSUB]
        vis_ref[i, 1] = both[FSUB:]


def receive_call(z, chunk, arrived, key, vis):
    step_ch = 4
    steps = z.chunk_ch // step_ch
    out_shape = jax.ShapeDtypeStruct((z.chan_dev, 2, FSUB, FSUB), jnp.float32)
    in_specs = [whole_spec(x.shape) for x in arrived] + [whole_spec(key.shape)]
    operands = list(arrived) + [key]
    aliases = {}
    if vis is not None:
        in_specs.append(pl.BlockSpec(memory_space=pl.ANY))
        aliases = {len(operands): 0}
        operands.append(vis)
    return pl.pallas_call(
        functools.partial(receive_kernel, z, step_ch),
        grid=(steps,),
        in_specs=in_specs,
        out_specs=pl.BlockSpec(
            (step_ch, 2, FSUB, FSUB), lambda g: (chunk * steps + g, 0, 0, 0)
        ),
        out_shape=out_shape,
        input_output_aliases=aliases,
        scratch_shapes=[
            pltpu.VMEM((FSUB // LANES, FR * z.rows_dev, LANES), jnp.float32)
        ],
        compiler_params=pltpu.CompilerParams(vmem_limit_bytes=VMEM),
        cost_estimate=pl.CostEstimate(
            flops=4_000_000_000, bytes_accessed=10_000_000, transcendentals=0
        ),
        name="correlate",
    )(*operands)


def beam_kernel(z, me_ref, *refs):
    spec_refs = refs[: z.chunks]
    cos_ref, sin_ref, sum_ref, out_ref, acc_ref = refs[z.chunks :]
    count = z.chan_dev
    weights = []
    for g in range(BEAMS):
        weights.append(
            [jnp.concatenate([w[g]] * z.lane_frames, axis=1) for w in (cos_ref, sin_ref)]
        )
    acc_ref[...] = jnp.zeros_like(acc_ref)

    def body(q, carry):
        off = pl.multiple_of(q * z.width, z.width)
        x = [spec_refs[k][:, pl.ds(off, z.width)] for k in range(z.chunks)]
        real = jnp.concatenate([v[: z.chunk_ch] for v in x], axis=0)
        imag = jnp.concatenate([v[z.chunk_ch :] for v in x], axis=0)
        ones = sum_ref[pl.ds(off, z.width), :]
        for g in range(BEAMS):
            c, s = weights[g]
            both = jnp.concatenate([c * real + s * imag, c * imag - s * real], axis=0)
            acc_ref[g] += jnp.dot(both, ones, preferred_element_type=jnp.float32)
        return carry

    lax.fori_loop(0, z.quads, body, 0)
    for g in range(BEAMS):
        sums = acc_ref[g] * (1.0 / np.sqrt(F))
        for part in range(2):
            j = part * BEAMS + g
            out_ref[0, :, j * FR : (j + 1) * FR] = sums[part * count : (part + 1) * count, :FR]


def beam_call(z, me, spectra, cos_w, sin_w):
    bits = z.devices.bit_length() - 1
    lanes = FR * z.feed_dev
    frame = np.arange(lanes) // z.feed_dev
    sums = (frame[:, None] == np.arange(LANES)[None, :]).astype(ml_dtypes.bfloat16)

    def owner(j, me_ref):
        k = 0
        for b in range(bits):
            k = k | (((j >> b) & 1) << (bits - 1 - b))
        return me_ref[0] ^ k

    weight_spec = pl.BlockSpec(
        (BEAMS, z.chan_dev, z.feed_dev), lambda j, me_ref: (0, owner(j, me_ref), 0)
    )
    grid_spec = pltpu.PrefetchScalarGridSpec(
        num_scalar_prefetch=1,
        grid=(z.devices,),
        in_specs=[
            pl.BlockSpec((z.rows_dev, lanes), lambda j, me_ref: (owner(j, me_ref), 0))
            for _ in range(z.chunks)
        ]
        + [weight_spec, weight_spec, whole_spec((lanes, LANES))],
        out_specs=pl.BlockSpec(
            (1, z.chan_dev, 2 * BEAMS * FR), lambda j, me_ref: (j, 0, 0)
        ),
        scratch_shapes=[pltpu.VMEM((BEAMS, 2 * z.chan_dev, LANES), jnp.float32)],
    )
    return pl.pallas_call(
        functools.partial(beam_kernel, z),
        grid_spec=grid_spec,
        out_shape=jax.ShapeDtypeStruct((z.devices, z.chan_dev, 2 * BEAMS * FR), jnp.float32),
        compiler_params=pltpu.CompilerParams(vmem_limit_bytes=VMEM),
        cost_estimate=pl.CostEstimate(
            flops=20_000_000_000, bytes_accessed=20_000_000, transcendentals=0
        ),
        name="beam_sums",
    )(me, *spectra, cos_w, sin_w, jnp.asarray(sums))


def swap(z, x, offset):
    return lax.ppermute(x, "chan", [(i, i ^ offset) for i in range(z.devices)])


def on_device(voltages, delays, band_feeds):
    z = Sizes(lax.axis_size("chan"), voltages.shape[0])
    me = lax.axis_index("chan")
    me_array = me.astype(jnp.int32).reshape(1)
    window = fir_window()
    scale = float(np.sqrt(2.0 / np.sum(window * window)))
    window = jnp.asarray(window.astype(np.float32))

    base = me * z.feed_dev
    edges = base + jnp.arange(z.feed_dev + 1, dtype=jnp.int32)
    below = jnp.sum(
        (band_feeds[:, None, :] < edges[None, :, None]).astype(jnp.int32), axis=2
    )
    rank = below[:, :-1] - below[:, :1]
    listed = below[:, 1:] > below[:, :-1]
    rank = jnp.where(listed, rank, -1)
    slots = jnp.arange(LANES, dtype=jnp.int32) % z.cap
    local = jnp.arange(z.feed_dev, dtype=jnp.int32)
    loc = jnp.sum(
        jnp.where(rank[:, None, :] == slots[None, :, None], local[None, None, :], 0), axis=2
    )
    loc = jnp.swapaxes(loc.reshape(z.devices, z.bands_here, LANES), 0, 1)

    own = lax.dynamic_slice_in_dim(band_feeds, me * z.bands_here, z.bands_here, 0)
    source = own // z.feed_dev
    before = jnp.sum(
        (own[:, None, :] < (source * z.feed_dev)[:, :, None]).astype(jnp.int32), axis=2
    )
    place = jnp.arange(FSUB, dtype=jnp.int32)[None, :] - before
    offset = source ^ me
    tau = jnp.arange(z.lane_frames, dtype=jnp.int32)
    big = (offset // z.lane_frames) * LANES + place
    group = (offset % z.lane_frames)[:, None, :] ^ tau[None, :, None]
    take_key = big[:, None, :] + z.cap * group

    ids = np.arange(CHANNELS).reshape(z.devices, z.chunks, z.chunk_ch)
    chunk_ids = np.transpose(ids, (1, 0, 2))
    basis = [dft_rows(chunk_ids[k]).reshape(z.rows, NFFT) for k in range(z.chunks)]

    calls = [c for c in ([0], [1], [2, 3]) if c[-1] < z.chunks]
    filt = None
    spectra = []
    arrived = []
    for call in calls:
        rows = jnp.asarray(np.concatenate([basis[k] for k in call], axis=0))
        places = loc[call[0] : call[-1] + 1]
        if filt is None:
            filt, spec, send = spectra_call(
                z, scale, me_array, rows, places, voltages=voltages, window=window
            )
        else:
            _, spec, send = spectra_call(z, scale, me_array, rows, places, filt=filt)
        spectra.extend(spec)
        for c in range(len(call)):
            mine = send[c * z.devices : (c + 1) * z.devices]
            got = [mine[0]] + [None] * (z.devices - 1)
            far = z.devices // 2
            for i in range(far):
                for k in (far + i, i):
                    if k > 0:
                        got[k] = swap(z, mine[k], k)
            arrived.append(got)

    chan_float = jnp.arange(CHANNELS, dtype=jnp.int32).astype(jnp.float32)
    phase = 2.0 * jnp.pi / NFFT * (delays[:, None, :] * chan_float[None, :, None])
    cos_w = jnp.cos(phase).astype(jnp.bfloat16)
    sin_w = jnp.sin(phase).astype(jnp.bfloat16)
    beams = beam_call(z, me_array, spectra, cos_w, sin_w)
    bit = 1
    while beams.shape[0] > 1:
        half = beams.shape[0] // 2
        beams = beams[:half] + swap(z, beams[half:], bit)
        bit *= 2
    beams = beams.reshape(z.chan_dev, 2 * BEAMS * FR)

    vis = None
    for k in range(z.chunks):
        vis = receive_call(z, k, arrived[k], take_key[k], vis)
    return (vis, beams)


def solution(mesh):
    in_specs = (P(("grp", "chan"), None), P(None, ("grp", "chan")), P())
    out_specs = (P(("grp", "chan"), None, None, None), P(("grp", "chan"), None))
    return jax.shard_map(
        on_device, mesh=mesh, in_specs=in_specs, out_specs=out_specs, check_vma=False
    )
```

```python
import functools

import jax
import jax.numpy as jnp
import ml_dtypes
import numpy as np
from jax import lax
from jax.experimental import pallas as pl
from jax.experimental.pallas import tpu as pltpu
from jax.sharding import PartitionSpec as P

F = 1024
CHANNELS = 1024
TAPS = 4
BAND_CH = 16
BEAMS = 4
FR = 48
NFFT = 2048
BANDS = 64
FSUB = 256
LANES = 128
CALLS = ((0,), (1, 2), (3,))
VMEM = 56 * 1024 * 1024

NT = (((1,), (1,)), ((), ()))


def fir_window():
    ids = np.arange(TAPS * NFFT, dtype=np.float64)
    centered = (ids - 0.5 * TAPS * NFFT + 0.5) / NFFT
    hann_part = 0.5 - 0.5 * np.cos(2.0 * np.pi * (ids + 0.5) / (TAPS * NFFT))
    return (np.sinc(centered) * hann_part).reshape(TAPS, NFFT)


def dft_rows(chan_ids):
    m = np.arange(NFFT, dtype=np.int64)
    turns = (chan_ids[..., None].astype(np.int64) * m) % NFFT
    table = 2.0 * np.pi * np.arange(NFFT) / NFFT
    cosine = np.cos(table).astype(np.float32).astype(ml_dtypes.bfloat16)
    sine = (-np.sin(table)).astype(np.float32).astype(ml_dtypes.bfloat16)
    return np.stack([cosine[turns], sine[turns]], axis=1)


class Sizes:
    def __init__(self, devices, feed_dev):
        self.devices = devices
        self.feed_dev = feed_dev
        self.cap = feed_dev // 2
        self.lane_frames = LANES // self.cap
        self.quads = FR // self.lane_frames
        self.width = self.lane_frames * feed_dev
        self.steps = 6 if self.quads % 6 == 0 else self.quads
        self.step_frames = FR // self.steps
        self.step_quads = self.quads // self.steps
        self.step_lanes = self.step_frames * feed_dev
        self.chan_dev = CHANNELS // devices
        self.bands_here = BANDS // devices
        self.chunks = self.chan_dev // BAND_CH
        self.rows_dev = 2 * BAND_CH
        self.rows = devices * self.rows_dev
        self.groups = devices // self.lane_frames


def emit_spectra(z, scale, count, me_ref, spectra, loc_ref, spec_refs, send_ref):
    spectra = spectra * scale
    for c in range(count):
        spec_refs[c][...] = spectra[c * z.rows : (c + 1) * z.rows].astype(jnp.bfloat16)
    lane = lax.broadcasted_iota(jnp.int32, (z.rows_dev, LANES), 1)
    frame = (lane // z.cap) ^ (me_ref[0] % z.lane_frames)
    start = frame * z.cap
    for c in range(count):
        for owner in range(z.devices):
            loc = loc_ref[c, owner : owner + 1, :]
            index = start + loc % z.cap
            lower = jnp.broadcast_to(loc, index.shape) < z.cap
            row = c * z.rows + owner * z.rows_dev
            for q in range(z.step_quads):
                parts = []
                for side in range(2):
                    left = q * z.width + side * LANES
                    x = spectra[row : row + z.rows_dev, left : left + LANES]
                    parts.append(
                        jnp.take_along_axis(x, index, axis=1, mode="promise_in_bounds")
                    )
                picked = jnp.where(lower, parts[0], parts[1])
                send_ref[owner, c, q] = picked.astype(jnp.bfloat16)


def filter_piece(z, main_ref, halo, win_ref, filt_ref, off):
    lanes = slice(off, off + LANES)
    taps = [win_ref[k : k + 1, lanes] for k in range(TAPS)]
    for f0 in range(0, z.feed_dev, 16):
        frames = []
        for t in range(z.step_frames + TAPS - 1):
            if t < z.step_frames:
                x = main_ref[f0 : f0 + 16, t * NFFT + off : t * NFFT + off + LANES]
            else:
                x = halo[t - z.step_frames][f0 : f0 + 16, lanes]
            frames.append(x.astype(jnp.float32))
        totals = []
        for t in range(z.step_frames):
            total = taps[0] * frames[t]
            for k in range(1, TAPS):
                total = total + taps[k] * frames[t + k]
            totals.append(total)
        if z.cap < 16:
            totals = [
                jnp.concatenate([totals[t][h : h + 8], totals[t + 1][h : h + 8]], axis=0)
                for t in range(0, z.step_frames, 2)
                for h in (0, 8)
            ]
        for i, total in enumerate(totals):
            if z.cap < 16:
                t, half, feed = 2 * (i // 2), i % 2, 0
            else:
                t, half, feed = i, f0 // z.cap, f0 % z.cap
            row = (t // z.lane_frames) * z.width + half * LANES
            row += (t % z.lane_frames) * z.cap + feed
            filt_ref[row : row + 16, lanes] = total.astype(jnp.bfloat16)


def first_kernel(
    z, scale, count, me_ref, main_ref, h0_ref, h1_ref, h2_ref, win_ref, basis_ref, loc_ref,
    filt_ref, *refs,
):
    halo = (h0_ref, h1_ref, h2_ref)
    piece = 512
    spectra = None
    for off in range(0, NFFT, piece):
        for tile in range(off, off + piece, LANES):
            filter_piece(z, main_ref, halo, win_ref, filt_ref, tile)
        part = lax.dot_general(
            basis_ref[:, off : off + piece],
            filt_ref[:, off : off + piece],
            NT,
            preferred_element_type=jnp.float32,
        )
        spectra = part if spectra is None else spectra + part
    emit_spectra(z, scale, count, me_ref, spectra, loc_ref, refs[:-1], refs[-1])


def next_kernel(z, scale, count, me_ref, filt_ref, basis_ref, loc_ref, *refs):
    spectra = lax.dot_general(
        basis_ref[...], filt_ref[...], NT, preferred_element_type=jnp.float32
    )
    emit_spectra(z, scale, count, me_ref, spectra, loc_ref, refs[:-1], refs[-1])


def whole_spec(shape):
    return pl.BlockSpec(shape, lambda *g: (0,) * len(shape))


def spectra_call(z, scale, me, basis, loc, filt=None, voltages=None, window=None):
    count = loc.shape[0]
    filt_rows = z.step_frames * z.feed_dev
    filt_spec = pl.BlockSpec((filt_rows, NFFT), lambda g: (g, 0))
    spec_shape = jax.ShapeDtypeStruct((z.rows, FR * z.feed_dev), jnp.bfloat16)
    spec_spec = pl.BlockSpec((z.rows, z.step_lanes), lambda g: (0, g))
    send_shape = jax.ShapeDtypeStruct(
        (z.devices, count, z.quads, z.rows_dev, LANES), jnp.bfloat16
    )
    send_spec = pl.BlockSpec(
        (z.devices, count, z.step_quads, z.rows_dev, LANES), lambda g: (0, 0, g, 0, 0)
    )
    me_spec = pl.BlockSpec(memory_space=pltpu.SMEM)
    shared = [whole_spec(basis.shape), whole_spec(loc.shape)]
    out_specs = [spec_spec] * count + [send_spec]
    out_shape = [spec_shape] * count + [send_shape]
    flops = 2 * count * z.rows * NFFT * FR * z.feed_dev
    common = dict(
        grid=(z.steps,),
        compiler_params=pltpu.CompilerParams(vmem_limit_bytes=VMEM),
        cost_estimate=pl.CostEstimate(
            flops=flops, bytes_accessed=20_000_000, transcendentals=0
        ),
    )
    if filt is not None:
        outs = pl.pallas_call(
            functools.partial(next_kernel, z, scale, count),
            in_specs=[me_spec, filt_spec] + shared,
            out_specs=out_specs,
            out_shape=out_shape,
            name="spectra_next",
            **common,
        )(me, filt, basis, loc)
        return None, outs[:-1], outs[-1]

    def halo_spec(h):
        return pl.BlockSpec((z.feed_dev, NFFT), lambda g: (0, z.step_frames * (g + 1) + h))

    outs = pl.pallas_call(
        functools.partial(first_kernel, z, scale, count),
        in_specs=[
            me_spec,
            pl.BlockSpec((z.feed_dev, z.step_frames * NFFT), lambda g: (0, g)),
            halo_spec(0),
            halo_spec(1),
            halo_spec(2),
            whole_spec((TAPS, NFFT)),
        ]
        + shared,
        out_specs=[filt_spec] + out_specs,
        out_shape=[jax.ShapeDtypeStruct((FR * z.feed_dev, NFFT), jnp.bfloat16)] + out_shape,
        name="filter_spectra",
        **common,
    )(me, voltages, voltages, voltages, voltages, window, basis, loc)
    return outs[0], outs[1:-1], outs[-1]


def receive_kernel(z, step_ch, arr_ref, key_ref, *refs):
    vis_ref, rows_ref = refs[-2], refs[-1]
    g = pl.program_id(0)
    depth = z.quads * z.rows_dev
    lf = z.lane_frames

    @pl.when(g == 0)
    def _():
        lane_group = lax.broadcasted_iota(jnp.int32, (depth, LANES), 1) // z.cap
        slot = lax.broadcasted_iota(jnp.int32, (z.groups * LANES, FSUB), 0)
        for tau in range(lf):
            tiles = []
            for big in range(z.groups):
                tile = arr_ref[big * lf + tau, 0].reshape(depth, LANES)
                for lane in range(1, lf):
                    block = arr_ref[big * lf + (lane ^ tau), 0].reshape(depth, LANES)
                    tile = jnp.where(lane_group == lane, block, tile)
                tiles.append(tile)
            lhs = jnp.concatenate(tiles, axis=1)
            pick = jnp.where(slot == key_ref[tau : tau + 1, :], 1.0, 0.0).astype(jnp.bfloat16)
            rows = jnp.dot(lhs, pick, preferred_element_type=jnp.float32)
            for half in range(FSUB // LANES):
                rows_ref[half, tau * depth : (tau + 1) * depth, :] = rows[
                    :, half * LANES : (half + 1) * LANES
                ]

    for i in range(step_ch):
        ch = g * step_ch + i
        halves = []
        for part in range(2):
            halves.append(
                jnp.concatenate(
                    [
                        rows_ref[half, pl.ds(ch + part * BAND_CH, FR, stride=z.rows_dev), :]
                        for half in range(FSUB // LANES)
                    ],
                    axis=1,
                )
            )
        real, imag = halves
        right = jnp.concatenate([real, imag], axis=0)
        swapped = jnp.concatenate([imag, -real], axis=0)
        left = jnp.concatenate([right.T, swapped.T], axis=0).astype(jnp.bfloat16)
        both = jnp.dot(left, right.astype(jnp.bfloat16), preferred_element_type=jnp.float32)
        both = both * (1.0 / FR)
        vis_ref[i, 0] = both[:FSUB]
        vis_ref[i, 1] = both[FSUB:]


def receive_call(z, chunk, arrived, at, key, vis):
    step_ch = 4
    steps = BAND_CH // step_ch
    out_shape = jax.ShapeDtypeStruct((z.chan_dev, 2, FSUB, FSUB), jnp.float32)
    block = (z.devices, 1) + arrived.shape[2:]
    in_specs = [pl.BlockSpec(block, lambda g: (0, at, 0, 0, 0)), whole_spec(key.shape)]
    operands = [arrived, key]
    aliases = {}
    if vis is not None:
        in_specs.append(pl.BlockSpec(memory_space=pl.ANY))
        aliases = {len(operands): 0}
        operands.append(vis)
    return pl.pallas_call(
        functools.partial(receive_kernel, z, step_ch),
        grid=(steps,),
        in_specs=in_specs,
        out_specs=pl.BlockSpec(
            (step_ch, 2, FSUB, FSUB), lambda g: (chunk * steps + g, 0, 0, 0)
        ),
        out_shape=out_shape,
        input_output_aliases=aliases,
        scratch_shapes=[
            pltpu.VMEM((FSUB // LANES, FR * z.rows_dev, LANES), jnp.float32)
        ],
        compiler_params=pltpu.CompilerParams(vmem_limit_bytes=VMEM),
        cost_estimate=pl.CostEstimate(
            flops=4_000_000_000, bytes_accessed=10_000_000, transcendentals=0
        ),
        name="correlate",
    )(*operands)


def beam_kernel(z, me_ref, *refs):
    spec_refs = refs[: z.chunks]
    cos_base, sin_base, cos_step, sin_step, sum_ref, out_ref, prod_ref = refs[z.chunks :]
    count = z.chan_dev
    weights = []
    for g in range(BEAMS):
        c0, s0 = cos_base[0, g : g + 1, :], sin_base[0, g : g + 1, :]
        c1, s1 = cos_step[g], sin_step[g]
        weights.append(
            ((c0 * c1 - s0 * s1).astype(jnp.bfloat16), (s0 * c1 + c0 * s1).astype(jnp.bfloat16))
        )
    for q in range(z.quads):
        lanes = slice(q * z.width, (q + 1) * z.width)
        x = [ref[:, lanes] for ref in spec_refs]
        real = jnp.concatenate([v[:BAND_CH] for v in x], axis=0)
        imag = jnp.concatenate([v[BAND_CH:] for v in x], axis=0)
        for g in range(BEAMS):
            c, s = weights[g]
            pair = (c * real + s * imag, c * imag - s * real)
            for part in range(2):
                row = (part * BEAMS + g) * count
                both = pair[part][:, :LANES] + pair[part][:, LANES:]
                prod_ref[row : row + count, q * LANES : (q + 1) * LANES] = both
    sums = jnp.dot(prod_ref[...], sum_ref[...], preferred_element_type=jnp.float32)
    sums = sums * (1.0 / np.sqrt(F))
    for j in range(2 * BEAMS):
        out_ref[0, :, j * FR : (j + 1) * FR] = sums[j * count : (j + 1) * count, :FR]


def beam_call(z, me, spectra, delays):
    bits = z.devices.bit_length() - 1
    lanes = FR * z.feed_dev
    halves = delays.reshape(BEAMS, 2, 1, z.cap)
    spread = jnp.broadcast_to(halves, (BEAMS, 2, z.lane_frames, z.cap)).reshape(BEAMS, z.width)
    unit = 2.0 * jnp.pi / NFFT
    owners = jnp.arange(z.devices, dtype=jnp.int32).astype(jnp.float32) * z.chan_dev
    inner = jnp.arange(z.chan_dev, dtype=jnp.int32).astype(jnp.float32)
    base = unit * (spread[None, :, :] * owners[:, None, None])
    step = unit * (spread[:, None, :] * inner[None, :, None])
    frame = (np.arange(FR * z.cap) // LANES) * z.lane_frames
    frame = frame + (np.arange(FR * z.cap) % LANES) // z.cap
    sums = (frame[:, None] == np.arange(LANES)[None, :]).astype(ml_dtypes.bfloat16)

    def owner(j, me_ref):
        k = 0
        for b in range(bits):
            k = k | (((j >> b) & 1) << (bits - 1 - b))
        return me_ref[0] ^ k

    base_spec = pl.BlockSpec(
        (1, BEAMS, z.width), lambda j, me_ref: (owner(j, me_ref), 0, 0)
    )
    grid_spec = pltpu.PrefetchScalarGridSpec(
        num_scalar_prefetch=1,
        grid=(z.devices,),
        in_specs=[
            pl.BlockSpec((z.rows_dev, lanes), lambda j, me_ref: (owner(j, me_ref), 0))
            for _ in range(z.chunks)
        ]
        + [base_spec, base_spec, whole_spec(step.shape), whole_spec(step.shape)]
        + [whole_spec(sums.shape)],
        out_specs=pl.BlockSpec(
            (1, z.chan_dev, 2 * BEAMS * FR), lambda j, me_ref: (j, 0, 0)
        ),
        scratch_shapes=[pltpu.VMEM((2 * BEAMS * z.chan_dev, FR * z.cap), jnp.bfloat16)],
    )
    return pl.pallas_call(
        functools.partial(beam_kernel, z),
        grid_spec=grid_spec,
        out_shape=jax.ShapeDtypeStruct((z.devices, z.chan_dev, 2 * BEAMS * FR), jnp.float32),
        compiler_params=pltpu.CompilerParams(vmem_limit_bytes=VMEM),
        cost_estimate=pl.CostEstimate(
            flops=20_000_000_000, bytes_accessed=20_000_000, transcendentals=0
        ),
        name="beam_sums",
    )(
        me, *spectra, jnp.cos(base), jnp.sin(base), jnp.cos(step), jnp.sin(step),
        jnp.asarray(sums),
    )


def swap(z, x, offset):
    return lax.ppermute(x, "chan", [(i, i ^ offset) for i in range(z.devices)])


def listed_places(z, me, lists):
    base = me * z.feed_dev
    edges = base + jnp.arange(z.feed_dev + 1, dtype=jnp.int32)
    below = jnp.sum((lists[:, None, :] < edges[None, :, None]).astype(jnp.int32), axis=2)
    rank = below[:, :-1] - below[:, :1]
    rank = jnp.where(below[:, 1:] > below[:, :-1], rank, -1)
    slots = jnp.arange(LANES, dtype=jnp.int32) % z.cap
    local = jnp.arange(z.feed_dev, dtype=jnp.int32)
    return jnp.sum(
        jnp.where(rank[:, None, :] == slots[None, :, None], local[None, None, :], 0), axis=2
    )


def on_device(voltages, delays, band_feeds):
    z = Sizes(lax.axis_size("chan"), voltages.shape[0])
    me = lax.axis_index("chan")
    me_array = me.astype(jnp.int32).reshape(1)
    window = fir_window()
    scale = float(np.sqrt(2.0 / np.sum(window * window)))
    window = jnp.asarray(window.astype(np.float32))
    lists = band_feeds.reshape(z.devices, z.bands_here, FSUB)

    own = lax.dynamic_slice_in_dim(band_feeds, me * z.bands_here, z.bands_here, 0)
    source = own // z.feed_dev
    before = jnp.sum(
        (own[:, None, :] < (source * z.feed_dev)[:, :, None]).astype(jnp.int32), axis=2
    )
    place = jnp.arange(FSUB, dtype=jnp.int32)[None, :] - before
    tau = jnp.arange(z.lane_frames, dtype=jnp.int32)
    big = (source // z.lane_frames) * LANES + place
    group = (source % z.lane_frames)[:, None, :] ^ tau[None, :, None]
    take_key = big[:, None, :] + z.cap * group

    ids = np.arange(CHANNELS).reshape(z.devices, z.chunks, BAND_CH)
    chunk_ids = np.transpose(ids, (1, 0, 2))

    filt = None
    spectra = []
    arrived = []
    for call in CALLS:
        call = [k for k in call if k < z.chunks]
        if not call:
            continue
        basis = np.concatenate([dft_rows(chunk_ids[k]).reshape(z.rows, NFFT) for k in call])
        basis = jnp.asarray(basis)
        places = jnp.stack([listed_places(z, me, lists[:, k]) for k in call])
        if filt is None:
            filt, spec, send = spectra_call(
                z, scale, me_array, basis, places, voltages=voltages, window=window
            )
        else:
            _, spec, send = spectra_call(z, scale, me_array, basis, places, filt=filt)
        spectra.extend(spec)
        got = lax.all_to_all(send, "chan", split_axis=0, concat_axis=0, tiled=True)
        arrived.extend((got, at) for at in range(len(call)))

    beams = beam_call(z, me_array, spectra, delays)
    bit = 1
    while beams.shape[0] > 1:
        half = beams.shape[0] // 2
        beams = beams[:half] + swap(z, beams[half:], bit)
        bit *= 2
    beams = beams.reshape(z.chan_dev, 2 * BEAMS * FR)

    vis = None
    for k in range(z.chunks):
        got, at = arrived[k]
        vis = receive_call(z, k, got, at, take_key[k], vis)
    return (vis, beams)


def solution(mesh):
    in_specs = (P(("grp", "chan"), None), P(None, ("grp", "chan")), P())
    out_specs = (P(("grp", "chan"), None, None, None), P(("grp", "chan"), None))
    return jax.shard_map(
        on_device, mesh=mesh, in_specs=in_specs, out_specs=out_specs, check_vma=False
    )
```

```python
import functools

import jax
import jax.numpy as jnp
import ml_dtypes
import numpy as np
from jax import lax
from jax.experimental import pallas as pl
from jax.experimental.pallas import tpu as pltpu
from jax.sharding import PartitionSpec as P

F = 1024
CHANNELS = 1024
TAPS = 4
BAND_CH = 16
BEAMS = 4
FR = 48
NFFT = 2048
BANDS = 64
FSUB = 256
LANES = 128
VMEM = 56 * 1024 * 1024

NT = (((1,), (1,)), ((), ()))


def fir_window():
    ids = np.arange(TAPS * NFFT, dtype=np.float64)
    centered = (ids - 0.5 * TAPS * NFFT + 0.5) / NFFT
    hann_part = 0.5 - 0.5 * np.cos(2.0 * np.pi * (ids + 0.5) / (TAPS * NFFT))
    return (np.sinc(centered) * hann_part).reshape(TAPS, NFFT)


def dft_rows(chan_ids):
    m = np.arange(NFFT, dtype=np.int64)
    turns = (chan_ids[..., None].astype(np.int64) * m) % NFFT
    table = 2.0 * np.pi * np.arange(NFFT) / NFFT
    cosine = np.cos(table).astype(np.float32).astype(ml_dtypes.bfloat16)
    sine = (-np.sin(table)).astype(np.float32).astype(ml_dtypes.bfloat16)
    return np.stack([cosine[turns], sine[turns]], axis=1)


class Sizes:
    def __init__(self, devices, feed_dev):
        self.devices = devices
        self.feed_dev = feed_dev
        self.cap = feed_dev // 2
        self.lane_frames = LANES // self.cap
        self.quads = FR // self.lane_frames
        self.width = self.lane_frames * feed_dev
        self.steps = 6 if self.quads % 6 == 0 else self.quads
        self.step_frames = FR // self.steps
        self.step_quads = self.quads // self.steps
        self.step_lanes = self.step_frames * feed_dev
        self.chan_dev = CHANNELS // devices
        self.bands_here = BANDS // devices
        self.chunks = self.chan_dev // BAND_CH
        self.rows_dev = 2 * BAND_CH
        self.rows = devices * self.rows_dev
        self.groups = devices // self.lane_frames
        self.halves = 2 if self.chunks > 2 and self.steps % 2 == 0 else 1


def find_places(z, me, lists):
    base = me * z.feed_dev
    first = jnp.sum((lists < base).astype(jnp.int32), axis=1, keepdims=True)
    lane = lax.broadcasted_iota(jnp.int32, (lists.shape[0], LANES), 1)
    at = first + lane % z.cap
    parts = []
    for side in range(FSUB // LANES):
        index = jnp.clip(at - side * LANES, 0, LANES - 1)
        half = lists[:, side * LANES : (side + 1) * LANES]
        parts.append(jnp.take_along_axis(half, index, axis=1, mode="promise_in_bounds"))
    loc = jnp.where(at < LANES, parts[0], parts[1]) - base
    return jnp.clip(loc, 0, z.feed_dev - 1)


def emit_spectra(z, scale, chunks, me_ref, spectra, lists_ref, loc_ref, spec_refs, send_refs):
    loc_ref[...] = find_places(z, me_ref[0], lists_ref[...])
    spectra = spectra * scale
    for c in range(len(chunks)):
        spec_refs[c][...] = spectra[c * z.rows : (c + 1) * z.rows].astype(jnp.bfloat16)
    lane = lax.broadcasted_iota(jnp.int32, (z.rows_dev, LANES), 1)
    frame = (lane // z.cap) ^ (me_ref[0] % z.lane_frames)
    start = frame * z.cap
    for c, chunk in enumerate(chunks):
        send_ref, unit = send_refs[c]
        for owner in range(z.devices):
            band = owner * z.bands_here + chunk
            loc = loc_ref[band : band + 1, :]
            index = start + loc % z.cap
            lower = jnp.broadcast_to(loc, index.shape) < z.cap
            row = c * z.rows + owner * z.rows_dev
            for q in range(z.step_quads):
                parts = []
                for side in range(2):
                    left = q * z.width + side * LANES
                    x = spectra[row : row + z.rows_dev, left : left + LANES]
                    parts.append(
                        jnp.take_along_axis(x, index, axis=1, mode="promise_in_bounds")
                    )
                picked = jnp.where(lower, parts[0], parts[1])
                send_ref[owner, unit, q] = picked.astype(jnp.bfloat16)


def filter_piece(z, main_ref, halo, win_ref, filt_ref, off):
    lanes = slice(off, off + LANES)
    taps = [win_ref[k : k + 1, lanes] for k in range(TAPS)]
    for f0 in range(0, z.feed_dev, 16):
        frames = []
        for t in range(z.step_frames + TAPS - 1):
            if t < z.step_frames:
                x = main_ref[f0 : f0 + 16, t * NFFT + off : t * NFFT + off + LANES]
            else:
                x = halo[t - z.step_frames][f0 : f0 + 16, lanes]
            frames.append(x.astype(jnp.float32))
        totals = []
        for t in range(z.step_frames):
            total = taps[0] * frames[t]
            for k in range(1, TAPS):
                total = total + taps[k] * frames[t + k]
            totals.append(total)
        if z.cap < 16:
            totals = [
                jnp.concatenate([totals[t][h : h + 8], totals[t + 1][h : h + 8]], axis=0)
                for t in range(0, z.step_frames, 2)
                for h in (0, 8)
            ]
        for i, total in enumerate(totals):
            if z.cap < 16:
                t, half, feed = 2 * (i // 2), i % 2, 0
            else:
                t, half, feed = i, f0 // z.cap, f0 % z.cap
            row = (t // z.lane_frames) * z.width + half * LANES
            row += (t % z.lane_frames) * z.cap + feed
            filt_ref[row : row + 16, lanes] = total.astype(jnp.bfloat16)


def first_kernel(
    z, scale, chunks, held, me_ref, main_ref, h0_ref, h1_ref, h2_ref, win_ref, basis_ref,
    lists_ref, *refs,
):
    filt_ref, spec_refs, send_ref, loc_ref = refs[held], refs[held + 1 : -2], refs[-2], refs[-1]
    halo = (h0_ref, h1_ref, h2_ref)
    piece = 512
    spectra = None
    for off in range(0, NFFT, piece):
        for tile in range(off, off + piece, LANES):
            filter_piece(z, main_ref, halo, win_ref, filt_ref, tile)
        part = lax.dot_general(
            basis_ref[:, off : off + piece],
            filt_ref[:, off : off + piece],
            NT,
            preferred_element_type=jnp.float32,
        )
        spectra = part if spectra is None else spectra + part
    sends = [(send_ref, c) for c in range(len(chunks))]
    emit_spectra(z, scale, chunks, me_ref, spectra, lists_ref, loc_ref, spec_refs, sends)


def next_kernel(z, scale, chunks, me_ref, filt_ref, basis_ref, lists_ref, held_ref, *refs):
    spectra = lax.dot_general(
        basis_ref[...], filt_ref[...], NT, preferred_element_type=jnp.float32
    )
    count = len(chunks)
    sends = [(refs[count + c], 0) for c in range(count)]
    emit_spectra(
        z, scale, chunks, me_ref, spectra, lists_ref, refs[-1], refs[:count], sends
    )


def whole_spec(shape):
    return pl.BlockSpec(shape, lambda *g: (0,) * len(shape))


class Spectra:

    def __init__(self, z, me, voltages, band_feeds):
        window = fir_window()
        self.z = z
        self.me = me
        self.scale = float(np.sqrt(2.0 / np.sum(window * window)))
        self.window = jnp.asarray(window.astype(np.float32))
        self.voltages = voltages
        self.lists = band_feeds
        ids = np.arange(CHANNELS).reshape(z.devices, z.chunks, BAND_CH)
        self.ids = np.transpose(ids, (1, 0, 2))
        self.half_quads = z.quads // z.halves
        self.half_steps = z.steps // z.halves
        self.me_spec = pl.BlockSpec(memory_space=pltpu.SMEM)
        self.spec_shape = jax.ShapeDtypeStruct((z.rows, FR * z.feed_dev), jnp.bfloat16)
        self.filt_shape = jax.ShapeDtypeStruct((FR * z.feed_dev, NFFT), jnp.bfloat16)

    def basis(self, chunks):
        rows = [dft_rows(self.ids[k]).reshape(self.z.rows, NFFT) for k in chunks]
        return jnp.asarray(np.concatenate(rows))

    def message(self, units):
        z = self.z
        dims = (z.devices, units, self.half_quads, z.rows_dev, LANES)
        return jax.ShapeDtypeStruct(dims, jnp.bfloat16)

    def common(self, steps, chunks):
        z = self.z
        flops = 2 * len(chunks) * z.rows * NFFT * z.step_lanes * steps
        return dict(
            grid=(steps,),
            scratch_shapes=[pltpu.VMEM((BANDS, LANES), jnp.int32)],
            compiler_params=pltpu.CompilerParams(vmem_limit_bytes=VMEM),
            cost_estimate=pl.CostEstimate(
                flops=flops, bytes_accessed=3_000_000 * steps, transcendentals=0
            ),
        )

    def first(self, half, chunks, basis, units, held):
        z = self.z
        count = len(chunks)
        steps = self.half_steps
        begin = half * steps

        def halo_spec(h):
            return pl.BlockSpec(
                (z.feed_dev, NFFT), lambda g: (0, z.step_frames * (begin + g + 1) + h)
            )

        send_block = (z.devices, count, z.step_quads, z.rows_dev, LANES)
        operands = [self.me] + [self.voltages] * 4 + [self.window, basis, self.lists]
        aliases = {len(operands) + i: i for i in range(len(held))}
        return pl.pallas_call(
            functools.partial(first_kernel, z, self.scale, chunks, len(held)),
            in_specs=[
                self.me_spec,
                pl.BlockSpec((z.feed_dev, z.step_frames * NFFT), lambda g: (0, begin + g)),
                halo_spec(0),
                halo_spec(1),
                halo_spec(2),
                whole_spec((TAPS, NFFT)),
                whole_spec(basis.shape),
                whole_spec(self.lists.shape),
            ]
            + [pl.BlockSpec(memory_space=pl.ANY)] * len(held),
            out_specs=[
                pl.BlockSpec((z.step_lanes, NFFT), lambda g: (begin + g, 0)),
            ]
            + [pl.BlockSpec((z.rows, z.step_lanes), lambda g: (0, begin + g))] * count
            + [pl.BlockSpec(send_block, lambda g: (0, 0, g, 0, 0))],
            out_shape=[self.filt_shape] + [self.spec_shape] * count + [self.message(units)],
            input_output_aliases=aliases,
            name="filter_spectra",
            **self.common(steps, chunks),
        )(*operands, *held)

    def next(self, chunks, filt, held):
        z = self.z
        count = len(chunks)
        per = self.half_steps
        basis = self.basis(chunks)
        block = (z.devices, 1, z.step_quads, z.rows_dev, LANES)
        first_unit = held.shape[1] - z.halves
        operands = [self.me, filt, basis, self.lists, held]
        return pl.pallas_call(
            functools.partial(next_kernel, z, self.scale, chunks),
            in_specs=[
                self.me_spec,
                pl.BlockSpec((z.step_lanes, NFFT), lambda g: (g, 0)),
                whole_spec(basis.shape),
                whole_spec(self.lists.shape),
                pl.BlockSpec(memory_space=pl.ANY),
            ],
            out_specs=[pl.BlockSpec((z.rows, z.step_lanes), lambda g: (0, g))] * count
            + [
                pl.BlockSpec(block, lambda g: (0, first_unit + g // per, g % per, 0, 0)),
                pl.BlockSpec(block, lambda g: (0, g // per, g % per, 0, 0)),
            ],
            out_shape=[self.spec_shape] * count
            + [self.message(held.shape[1]), self.message(z.halves)],
            input_output_aliases={4: count},
            name="spectra_next",
            **self.common(z.steps, chunks),
        )(*operands)


def receive_kernel(z, step_ch, *refs):
    arr_refs, key_ref = refs[: z.halves], refs[z.halves]
    vis_ref, rows_ref = refs[-2], refs[-1]
    g = pl.program_id(0)
    depth = z.quads // z.halves * z.rows_dev
    lf = z.lane_frames

    @pl.when(g == 0)
    def _():
        lane_group = lax.broadcasted_iota(jnp.int32, (depth, LANES), 1) // z.cap
        slot = lax.broadcasted_iota(jnp.int32, (z.groups * LANES, FSUB), 0)
        for tau in range(lf):
            pick = jnp.where(slot == key_ref[tau : tau + 1, :], 1.0, 0.0).astype(jnp.bfloat16)
            for h, arr_ref in enumerate(arr_refs):
                tiles = []
                for big in range(z.groups):
                    tile = arr_ref[big * lf + tau, 0].reshape(depth, LANES)
                    for lane in range(1, lf):
                        block = arr_ref[big * lf + (lane ^ tau), 0].reshape(depth, LANES)
                        tile = jnp.where(lane_group == lane, block, tile)
                    tiles.append(tile)
                lhs = jnp.concatenate(tiles, axis=1)
                rows = jnp.dot(lhs, pick, preferred_element_type=jnp.float32)
                top = (tau * z.halves + h) * depth
                for side in range(FSUB // LANES):
                    rows_ref[side, top : top + depth, :] = rows[
                        :, side * LANES : (side + 1) * LANES
                    ]

    for i in range(step_ch):
        ch = g * step_ch + i
        halves = []
        for part in range(2):
            halves.append(
                jnp.concatenate(
                    [
                        rows_ref[side, pl.ds(ch + part * BAND_CH, FR, stride=z.rows_dev), :]
                        for side in range(FSUB // LANES)
                    ],
                    axis=1,
                )
            )
        real, imag = halves
        both = jnp.concatenate([real, imag], axis=0)
        turned = jnp.concatenate([-imag, real], axis=0)
        right = jnp.concatenate([both, turned], axis=1).astype(jnp.bfloat16)
        left = both.astype(jnp.bfloat16).T
        out = jnp.dot(left, right, preferred_element_type=jnp.float32) * (1.0 / FR)
        vis_ref[i, 0] = out[:, :FSUB]
        vis_ref[i, 1] = out[:, FSUB:]


def receive_call(z, chunk, arrived, key, vis):
    step_ch = 4
    steps = BAND_CH // step_ch
    out_shape = jax.ShapeDtypeStruct((z.chan_dev, 2, FSUB, FSUB), jnp.float32)

    def unit_spec(got, unit):
        return pl.BlockSpec((z.devices, 1) + got.shape[2:], lambda g: (0, unit, 0, 0, 0))

    in_specs = [unit_spec(got, unit) for got, unit in arrived] + [whole_spec(key.shape)]
    operands = [got for got, _ in arrived] + [key]
    aliases = {}
    if vis is not None:
        in_specs.append(pl.BlockSpec(memory_space=pl.ANY))
        aliases = {len(operands): 0}
        operands.append(vis)
    return pl.pallas_call(
        functools.partial(receive_kernel, z, step_ch),
        grid=(steps,),
        in_specs=in_specs,
        out_specs=pl.BlockSpec(
            (step_ch, 2, FSUB, FSUB), lambda g: (chunk * steps + g, 0, 0, 0)
        ),
        out_shape=out_shape,
        input_output_aliases=aliases,
        scratch_shapes=[
            pltpu.VMEM((FSUB // LANES, FR * z.rows_dev, LANES), jnp.float32)
        ],
        compiler_params=pltpu.CompilerParams(vmem_limit_bytes=VMEM),
        cost_estimate=pl.CostEstimate(
            flops=4_000_000_000, bytes_accessed=10_000_000, transcendentals=0
        ),
        name="correlate",
    )(*operands)


def beam_kernel(z, me_ref, *refs):
    spec_refs = refs[: z.chunks]
    cos_base, sin_base, cos_step, sin_step, sum_ref, out_ref, prod_ref = refs[z.chunks :]
    count = z.chan_dev
    weights = []
    for g in range(BEAMS):
        c0, s0 = cos_base[0, g : g + 1, :], sin_base[0, g : g + 1, :]
        c1, s1 = cos_step[g], sin_step[g]
        weights.append(
            ((c0 * c1 - s0 * s1).astype(jnp.bfloat16), (s0 * c1 + c0 * s1).astype(jnp.bfloat16))
        )
    for q in range(z.quads):
        lanes = slice(q * z.width, (q + 1) * z.width)
        x = [ref[:, lanes] for ref in spec_refs]
        real = jnp.concatenate([v[:BAND_CH] for v in x], axis=0)
        imag = jnp.concatenate([v[BAND_CH:] for v in x], axis=0)
        for g in range(BEAMS):
            c, s = weights[g]
            pair = (c * real + s * imag, c * imag - s * real)
            for part in range(2):
                row = (part * BEAMS + g) * count
                both = pair[part][:, :LANES] + pair[part][:, LANES:]
                prod_ref[row : row + count, q * LANES : (q + 1) * LANES] = both
    sums = jnp.dot(prod_ref[...], sum_ref[...], preferred_element_type=jnp.float32)
    sums = sums * (1.0 / np.sqrt(F))
    for j in range(2 * BEAMS):
        out_ref[0, :, j * FR : (j + 1) * FR] = sums[j * count : (j + 1) * count, :FR]


def beam_call(z, me, spectra, delays):
    bits = z.devices.bit_length() - 1
    lanes = FR * z.feed_dev
    halves = delays.reshape(BEAMS, 2, 1, z.cap)
    spread = jnp.broadcast_to(halves, (BEAMS, 2, z.lane_frames, z.cap)).reshape(BEAMS, z.width)
    unit = 2.0 * jnp.pi / NFFT
    owners = jnp.arange(z.devices, dtype=jnp.int32).astype(jnp.float32) * z.chan_dev
    inner = jnp.arange(z.chan_dev, dtype=jnp.int32).astype(jnp.float32)
    base = unit * (spread[None, :, :] * owners[:, None, None])
    step = unit * (spread[:, None, :] * inner[None, :, None])
    frame = (np.arange(FR * z.cap) // LANES) * z.lane_frames
    frame = frame + (np.arange(FR * z.cap) % LANES) // z.cap
    sums = (frame[:, None] == np.arange(LANES)[None, :]).astype(ml_dtypes.bfloat16)

    def owner(j, me_ref):
        k = 0
        for b in range(bits):
            k = k | (((j >> b) & 1) << (bits - 1 - b))
        return me_ref[0] ^ k

    base_spec = pl.BlockSpec(
        (1, BEAMS, z.width), lambda j, me_ref: (owner(j, me_ref), 0, 0)
    )
    grid_spec = pltpu.PrefetchScalarGridSpec(
        num_scalar_prefetch=1,
        grid=(z.devices,),
        in_specs=[
            pl.BlockSpec((z.rows_dev, lanes), lambda j, me_ref: (owner(j, me_ref), 0))
            for _ in range(z.chunks)
        ]
        + [base_spec, base_spec, whole_spec(step.shape), whole_spec(step.shape)]
        + [whole_spec(sums.shape)],
        out_specs=pl.BlockSpec(
            (1, z.chan_dev, 2 * BEAMS * FR), lambda j, me_ref: (j, 0, 0)
        ),
        scratch_shapes=[pltpu.VMEM((2 * BEAMS * z.chan_dev, FR * z.cap), jnp.bfloat16)],
    )
    return pl.pallas_call(
        functools.partial(beam_kernel, z),
        grid_spec=grid_spec,
        out_shape=jax.ShapeDtypeStruct((z.devices, z.chan_dev, 2 * BEAMS * FR), jnp.float32),
        compiler_params=pltpu.CompilerParams(vmem_limit_bytes=VMEM),
        cost_estimate=pl.CostEstimate(
            flops=20_000_000_000, bytes_accessed=20_000_000, transcendentals=0
        ),
        name="beam_sums",
    )(
        me, *spectra, jnp.cos(base), jnp.sin(base), jnp.cos(step), jnp.sin(step),
        jnp.asarray(sums),
    )


def swap(z, x, offset):
    return lax.ppermute(x, "chan", [(i, i ^ offset) for i in range(z.devices)])


def exchange(x):
    return lax.all_to_all(x, "chan", split_axis=0, concat_axis=0, tiled=True)


def on_device(voltages, delays, band_feeds):
    z = Sizes(lax.axis_size("chan"), voltages.shape[0])
    me = lax.axis_index("chan")
    me_array = me.astype(jnp.int32).reshape(1)

    own = lax.dynamic_slice_in_dim(band_feeds, me * z.bands_here, z.bands_here, 0)
    source = own // z.feed_dev
    before = jnp.sum(
        (own[:, None, :] < (source * z.feed_dev)[:, :, None]).astype(jnp.int32), axis=2
    )
    place = jnp.arange(FSUB, dtype=jnp.int32)[None, :] - before
    tau = jnp.arange(z.lane_frames, dtype=jnp.int32)
    big = (source // z.lane_frames) * LANES + place
    group = (source % z.lane_frames)[:, None, :] ^ tau[None, :, None]
    take_key = big[:, None, :] + z.cap * group

    calls = Spectra(z, me_array, voltages, band_feeds)
    early = list(range(max(1, z.chunks - 2)))
    basis = calls.basis(early)
    filt, *spectra, send = calls.first(0, early, basis, len(early), [])
    got = exchange(send)
    arrived = [[(got, c)] for c in early]
    if z.halves > 1:
        units = len(early) + z.halves
        filt, *spectra, send = calls.first(1, early, basis, units, [filt, *spectra])
        late = [z.chunks - 2, z.chunks - 1]
        *more, send, last = calls.next(late, filt, send)
        spectra = spectra + more
        got = exchange(send)
        for c in early:
            arrived[c].append((got, c))
        arrived.append([(got, len(early) + h) for h in range(z.halves)])
        got = exchange(last)
        arrived.append([(got, h) for h in range(z.halves)])

    beams = beam_call(z, me_array, spectra, delays)
    bit = 1
    while beams.shape[0] > 1:
        half = beams.shape[0] // 2
        beams = beams[:half] + swap(z, beams[half:], bit)
        bit *= 2
    beams = beams.reshape(z.chan_dev, 2 * BEAMS * FR)

    vis = None
    for k in range(z.chunks):
        vis = receive_call(z, k, arrived[k], take_key[k], vis)
    return (vis, beams)


def solution(mesh):
    in_specs = (P(("grp", "chan"), None), P(None, ("grp", "chan")), P())
    out_specs = (P(("grp", "chan"), None, None, None), P(("grp", "chan"), None))
    return jax.shard_map(
        on_device, mesh=mesh, in_specs=in_specs, out_specs=out_specs, check_vma=False
    )
```

```python
import functools

import jax
import jax.numpy as jnp
import ml_dtypes
import numpy as np
from jax import lax
from jax.experimental import pallas as pl
from jax.experimental.pallas import tpu as pltpu
from jax.sharding import PartitionSpec as P

F = 1024
CHANNELS = 1024
TAPS = 4
BAND_CH = 16
BEAMS = 4
FR = 48
NFFT = 2048
BANDS = 64
FSUB = 256
LANES = 128
VMEM = 56 * 1024 * 1024

NT = (((1,), (1,)), ((), ()))


def fir_window():
    ids = np.arange(TAPS * NFFT, dtype=np.float64)
    centered = (ids - 0.5 * TAPS * NFFT + 0.5) / NFFT
    hann_part = 0.5 - 0.5 * np.cos(2.0 * np.pi * (ids + 0.5) / (TAPS * NFFT))
    return (np.sinc(centered) * hann_part).reshape(TAPS, NFFT)


def dft_rows(chan_ids):
    m = np.arange(NFFT, dtype=np.int64)
    turns = (chan_ids[..., None].astype(np.int64) * m) % NFFT
    table = 2.0 * np.pi * np.arange(NFFT) / NFFT
    cosine = np.cos(table).astype(np.float32).astype(ml_dtypes.bfloat16)
    sine = (-np.sin(table)).astype(np.float32).astype(ml_dtypes.bfloat16)
    return np.stack([cosine[turns], sine[turns]], axis=1)


class Sizes:
    def __init__(self, devices, feed_dev):
        self.devices = devices
        self.feed_dev = feed_dev
        self.cap = feed_dev // 2
        self.lane_frames = LANES // self.cap
        self.quads = FR // self.lane_frames
        self.width = self.lane_frames * feed_dev
        self.steps = 6 if self.quads % 6 == 0 else self.quads
        self.step_frames = FR // self.steps
        self.step_quads = self.quads // self.steps
        self.step_lanes = self.step_frames * feed_dev
        self.chan_dev = CHANNELS // devices
        self.bands_here = BANDS // devices
        self.chunks = self.chan_dev // BAND_CH
        self.rows_dev = 2 * BAND_CH
        self.rows = devices * self.rows_dev
        self.groups = devices // self.lane_frames
        self.halves = 2 if self.chunks > 2 and self.steps % 2 == 0 else 1


def find_places(z, me, lists):
    base = me * z.feed_dev
    first = jnp.sum((lists < base).astype(jnp.int32), axis=1, keepdims=True)
    lane = lax.broadcasted_iota(jnp.int32, (lists.shape[0], LANES), 1)
    at = first + lane % z.cap
    parts = []
    for side in range(FSUB // LANES):
        index = jnp.clip(at - side * LANES, 0, LANES - 1)
        half = lists[:, side * LANES : (side + 1) * LANES]
        parts.append(jnp.take_along_axis(half, index, axis=1, mode="promise_in_bounds"))
    loc = jnp.where(at < LANES, parts[0], parts[1]) - base
    return jnp.clip(loc, 0, z.feed_dev - 1)


def emit_spectra(z, scale, chunks, me_ref, spectra, lists_ref, loc_ref, spec_refs, send_refs):
    loc_ref[...] = find_places(z, me_ref[0], lists_ref[...])
    spectra = spectra * scale
    for c in range(len(chunks)):
        spec_refs[c][...] = spectra[c * z.rows : (c + 1) * z.rows].astype(jnp.bfloat16)
    lane = lax.broadcasted_iota(jnp.int32, (z.rows_dev, LANES), 1)
    frame = (lane // z.cap) ^ (me_ref[0] % z.lane_frames)
    start = frame * z.cap
    for c, chunk in enumerate(chunks):
        send_ref, unit = send_refs[c]
        for owner in range(z.devices):
            band = owner * z.bands_here + chunk
            loc = loc_ref[band : band + 1, :]
            index = start + loc % z.cap
            lower = jnp.broadcast_to(loc, index.shape) < z.cap
            row = c * z.rows + owner * z.rows_dev
            for q in range(z.step_quads):
                parts = []
                for side in range(2):
                    left = q * z.width + side * LANES
                    x = spectra[row : row + z.rows_dev, left : left + LANES]
                    parts.append(
                        jnp.take_along_axis(x, index, axis=1, mode="promise_in_bounds")
                    )
                picked = jnp.where(lower, parts[0], parts[1])
                send_ref[owner, unit, q] = picked.astype(jnp.bfloat16)


def filter_piece(z, main_ref, halo, win_ref, filt_ref, off):
    lanes = slice(off, off + LANES)
    taps = [win_ref[k : k + 1, lanes] for k in range(TAPS)]
    for f0 in range(0, z.feed_dev, 16):
        frames = []
        for t in range(z.step_frames + TAPS - 1):
            if t < z.step_frames:
                x = main_ref[f0 : f0 + 16, t * NFFT + off : t * NFFT + off + LANES]
            else:
                x = halo[t - z.step_frames][f0 : f0 + 16, lanes]
            frames.append(x.astype(jnp.float32))
        totals = []
        for t in range(z.step_frames):
            total = taps[0] * frames[t]
            for k in range(1, TAPS):
                total = total + taps[k] * frames[t + k]
            totals.append(total)
        if z.cap < 16:
            totals = [
                jnp.concatenate([totals[t][h : h + 8], totals[t + 1][h : h + 8]], axis=0)
                for t in range(0, z.step_frames, 2)
                for h in (0, 8)
            ]
        for i, total in enumerate(totals):
            if z.cap < 16:
                t, half, feed = 2 * (i // 2), i % 2, 0
            else:
                t, half, feed = i, f0 // z.cap, f0 % z.cap
            row = (t // z.lane_frames) * z.width + half * LANES
            row += (t % z.lane_frames) * z.cap + feed
            filt_ref[row : row + 16, lanes] = total.astype(jnp.bfloat16)


def first_kernel(
    z, scale, chunks, held, me_ref, main_ref, h0_ref, h1_ref, h2_ref, win_ref, basis_ref,
    lists_ref, *refs,
):
    filt_ref, spec_refs, send_ref, loc_ref = refs[held], refs[held + 1 : -2], refs[-2], refs[-1]
    halo = (h0_ref, h1_ref, h2_ref)
    piece = 512
    spectra = None
    for off in range(0, NFFT, piece):
        for tile in range(off, off + piece, LANES):
            filter_piece(z, main_ref, halo, win_ref, filt_ref, tile)
        part = lax.dot_general(
            basis_ref[:, off : off + piece],
            filt_ref[:, off : off + piece],
            NT,
            preferred_element_type=jnp.float32,
        )
        spectra = part if spectra is None else spectra + part
    sends = [(send_ref, c) for c in range(len(chunks))]
    emit_spectra(z, scale, chunks, me_ref, spectra, lists_ref, loc_ref, spec_refs, sends)


def next_kernel(z, scale, chunks, me_ref, filt_ref, basis_ref, lists_ref, held_ref, *refs):
    spectra = lax.dot_general(
        basis_ref[...], filt_ref[...], NT, preferred_element_type=jnp.float32
    )
    count = len(chunks)
    sends = [(refs[count + c], 0) for c in range(count)]
    emit_spectra(
        z, scale, chunks, me_ref, spectra, lists_ref, refs[-1], refs[:count], sends
    )


def whole_spec(shape):
    return pl.BlockSpec(shape, lambda *g: (0,) * len(shape))


class Spectra:

    def __init__(self, z, me, voltages, band_feeds):
        window = fir_window()
        self.z = z
        self.me = me
        self.scale = float(np.sqrt(2.0 / np.sum(window * window)))
        self.window = jnp.asarray(window.astype(np.float32))
        self.voltages = voltages
        self.lists = band_feeds
        ids = np.arange(CHANNELS).reshape(z.devices, z.chunks, BAND_CH)
        self.ids = np.transpose(ids, (1, 0, 2))
        self.half_quads = z.quads // z.halves
        self.half_steps = z.steps // z.halves
        self.me_spec = pl.BlockSpec(memory_space=pltpu.SMEM)
        self.spec_shape = jax.ShapeDtypeStruct((z.rows, FR * z.feed_dev), jnp.bfloat16)
        self.filt_shape = jax.ShapeDtypeStruct((FR * z.feed_dev, NFFT), jnp.bfloat16)

    def basis(self, chunks):
        rows = [dft_rows(self.ids[k]).reshape(self.z.rows, NFFT) for k in chunks]
        return jnp.asarray(np.concatenate(rows))

    def message(self, units):
        z = self.z
        dims = (z.devices, units, self.half_quads, z.rows_dev, LANES)
        return jax.ShapeDtypeStruct(dims, jnp.bfloat16)

    def common(self, steps, chunks):
        z = self.z
        flops = 2 * len(chunks) * z.rows * NFFT * z.step_lanes * steps
        return dict(
            grid=(steps,),
            scratch_shapes=[pltpu.VMEM((BANDS, LANES), jnp.int32)],
            compiler_params=pltpu.CompilerParams(vmem_limit_bytes=VMEM),
            cost_estimate=pl.CostEstimate(
                flops=flops, bytes_accessed=3_000_000 * steps, transcendentals=0
            ),
        )

    def first(self, half, chunks, basis, units, held):
        z = self.z
        count = len(chunks)
        steps = self.half_steps
        begin = half * steps

        def halo_spec(h):
            return pl.BlockSpec(
                (z.feed_dev, NFFT), lambda g: (0, z.step_frames * (begin + g + 1) + h)
            )

        send_block = (z.devices, count, z.step_quads, z.rows_dev, LANES)
        operands = [self.me] + [self.voltages] * 4 + [self.window, basis, self.lists]
        aliases = {len(operands) + i: i for i in range(len(held))}
        return pl.pallas_call(
            functools.partial(first_kernel, z, self.scale, chunks, len(held)),
            in_specs=[
                self.me_spec,
                pl.BlockSpec((z.feed_dev, z.step_frames * NFFT), lambda g: (0, begin + g)),
                halo_spec(0),
                halo_spec(1),
                halo_spec(2),
                whole_spec((TAPS, NFFT)),
                whole_spec(basis.shape),
                whole_spec(self.lists.shape),
            ]
            + [pl.BlockSpec(memory_space=pl.ANY)] * len(held),
            out_specs=[
                pl.BlockSpec((z.step_lanes, NFFT), lambda g: (begin + g, 0)),
            ]
            + [pl.BlockSpec((z.rows, z.step_lanes), lambda g: (0, begin + g))] * count
            + [pl.BlockSpec(send_block, lambda g: (0, 0, g, 0, 0))],
            out_shape=[self.filt_shape] + [self.spec_shape] * count + [self.message(units)],
            input_output_aliases=aliases,
            name="filter_spectra",
            **self.common(steps, chunks),
        )(*operands, *held)

    def next(self, chunks, filt, held):
        z = self.z
        count = len(chunks)
        per = self.half_steps
        basis = self.basis(chunks)
        block = (z.devices, 1, z.step_quads, z.rows_dev, LANES)
        first_unit = held.shape[1] - z.halves
        operands = [self.me, filt, basis, self.lists, held]
        return pl.pallas_call(
            functools.partial(next_kernel, z, self.scale, chunks),
            in_specs=[
                self.me_spec,
                pl.BlockSpec((z.step_lanes, NFFT), lambda g: (g, 0)),
                whole_spec(basis.shape),
                whole_spec(self.lists.shape),
                pl.BlockSpec(memory_space=pl.ANY),
            ],
            out_specs=[pl.BlockSpec((z.rows, z.step_lanes), lambda g: (0, g))] * count
            + [
                pl.BlockSpec(block, lambda g: (0, first_unit + g // per, g % per, 0, 0)),
                pl.BlockSpec(block, lambda g: (0, g // per, g % per, 0, 0)),
            ],
            out_shape=[self.spec_shape] * count
            + [self.message(held.shape[1]), self.message(z.halves)],
            input_output_aliases={4: count},
            name="spectra_next",
            **self.common(z.steps, chunks),
        )(*operands)


def receive_kernel(z, step_ch, *refs):
    arr_refs, key_ref = refs[: z.halves], refs[z.halves]
    vis_ref, rows_ref = refs[-2], refs[-1]
    g = pl.program_id(0)
    depth = z.quads // z.halves * z.rows_dev
    lf = z.lane_frames

    @pl.when(g == 0)
    def _():
        lane_group = lax.broadcasted_iota(jnp.int32, (depth, LANES), 1) // z.cap
        slot = lax.broadcasted_iota(jnp.int32, (z.groups * LANES, FSUB), 0)
        for tau in range(lf):
            pick = jnp.where(slot == key_ref[tau : tau + 1, :], 1.0, 0.0).astype(jnp.bfloat16)
            parts = []
            for arr_ref in arr_refs:
                tiles = []
                for big in range(z.groups):
                    tile = arr_ref[big * lf + tau, 0].reshape(depth, LANES)
                    for lane in range(1, lf):
                        block = arr_ref[big * lf + (lane ^ tau), 0].reshape(depth, LANES)
                        tile = jnp.where(lane_group == lane, block, tile)
                    tiles.append(tile)
                parts.append(jnp.concatenate(tiles, axis=1))
            rows = jnp.dot(
                jnp.concatenate(parts, axis=0), pick, preferred_element_type=jnp.float32
            )
            size = z.quads * z.rows_dev
            for side in range(FSUB // LANES):
                rows_ref[side, tau * size : (tau + 1) * size, :] = rows[
                    :, side * LANES : (side + 1) * LANES
                ]

    for i in range(step_ch):
        ch = g * step_ch + i
        halves = []
        for part in range(2):
            halves.append(
                jnp.concatenate(
                    [
                        rows_ref[side, pl.ds(ch + part * BAND_CH, FR, stride=z.rows_dev), :]
                        for side in range(FSUB // LANES)
                    ],
                    axis=1,
                )
            )
        real, imag = halves
        both = jnp.concatenate([real, imag], axis=0)
        turned = jnp.concatenate([-imag, real], axis=0)
        right = jnp.concatenate([both, turned], axis=1).astype(jnp.bfloat16)
        left = both.astype(jnp.bfloat16).T
        out = jnp.dot(left, right, preferred_element_type=jnp.float32) * (1.0 / FR)
        vis_ref[i, 0] = out[:, :FSUB]
        vis_ref[i, 1] = out[:, FSUB:]


def receive_call(z, chunk, arrived, key, vis):
    step_ch = 4
    steps = BAND_CH // step_ch
    out_shape = jax.ShapeDtypeStruct((z.chan_dev, 2, FSUB, FSUB), jnp.float32)

    def unit_spec(got, unit):
        return pl.BlockSpec((z.devices, 1) + got.shape[2:], lambda g: (0, unit, 0, 0, 0))

    in_specs = [unit_spec(got, unit) for got, unit in arrived] + [whole_spec(key.shape)]
    operands = [got for got, _ in arrived] + [key]
    aliases = {}
    if vis is not None:
        in_specs.append(pl.BlockSpec(memory_space=pl.ANY))
        aliases = {len(operands): 0}
        operands.append(vis)
    return pl.pallas_call(
        functools.partial(receive_kernel, z, step_ch),
        grid=(steps,),
        in_specs=in_specs,
        out_specs=pl.BlockSpec(
            (step_ch, 2, FSUB, FSUB), lambda g: (chunk * steps + g, 0, 0, 0)
        ),
        out_shape=out_shape,
        input_output_aliases=aliases,
        scratch_shapes=[
            pltpu.VMEM((FSUB // LANES, FR * z.rows_dev, LANES), jnp.float32)
        ],
        compiler_params=pltpu.CompilerParams(vmem_limit_bytes=VMEM),
        cost_estimate=pl.CostEstimate(
            flops=4_000_000_000, bytes_accessed=10_000_000, transcendentals=0
        ),
        name="correlate",
    )(*operands)


def beam_kernel(z, me_ref, *refs):
    spec_refs = refs[: z.chunks]
    cos_base, sin_base, cos_step, sin_step, sum_ref, out_ref, prod_ref = refs[z.chunks :]
    count = z.chan_dev
    weights = []
    for g in range(BEAMS):
        c0, s0 = cos_base[0, g : g + 1, :], sin_base[0, g : g + 1, :]
        c1, s1 = cos_step[g], sin_step[g]
        weights.append(
            ((c0 * c1 - s0 * s1).astype(jnp.bfloat16), (s0 * c1 + c0 * s1).astype(jnp.bfloat16))
        )
    for q in range(z.quads):
        lanes = slice(q * z.width, (q + 1) * z.width)
        x = [ref[:, lanes] for ref in spec_refs]
        real = jnp.concatenate([v[:BAND_CH] for v in x], axis=0)
        imag = jnp.concatenate([v[BAND_CH:] for v in x], axis=0)
        for g in range(BEAMS):
            c, s = weights[g]
            pair = (c * real + s * imag, c * imag - s * real)
            for part in range(2):
                row = (part * BEAMS + g) * count
                both = pair[part][:, :LANES] + pair[part][:, LANES:]
                prod_ref[row : row + count, q * LANES : (q + 1) * LANES] = both
    sums = jnp.dot(prod_ref[...], sum_ref[...], preferred_element_type=jnp.float32)
    sums = sums * (1.0 / np.sqrt(F))
    for j in range(2 * BEAMS):
        out_ref[0, :, j * FR : (j + 1) * FR] = sums[j * count : (j + 1) * count, :FR]


def beam_call(z, me, spectra, delays):
    bits = z.devices.bit_length() - 1
    lanes = FR * z.feed_dev
    halves = delays.reshape(BEAMS, 2, 1, z.cap)
    spread = jnp.broadcast_to(halves, (BEAMS, 2, z.lane_frames, z.cap)).reshape(BEAMS, z.width)
    unit = 2.0 * jnp.pi / NFFT
    owners = jnp.arange(z.devices, dtype=jnp.int32).astype(jnp.float32) * z.chan_dev
    inner = jnp.arange(z.chan_dev, dtype=jnp.int32).astype(jnp.float32)
    base = unit * (spread[None, :, :] * owners[:, None, None])
    step = unit * (spread[:, None, :] * inner[None, :, None])
    frame = (np.arange(FR * z.cap) // LANES) * z.lane_frames
    frame = frame + (np.arange(FR * z.cap) % LANES) // z.cap
    sums = (frame[:, None] == np.arange(LANES)[None, :]).astype(ml_dtypes.bfloat16)

    def owner(j, me_ref):
        k = 0
        for b in range(bits):
            k = k | (((j >> b) & 1) << (bits - 1 - b))
        return me_ref[0] ^ k

    base_spec = pl.BlockSpec(
        (1, BEAMS, z.width), lambda j, me_ref: (owner(j, me_ref), 0, 0)
    )
    grid_spec = pltpu.PrefetchScalarGridSpec(
        num_scalar_prefetch=1,
        grid=(z.devices,),
        in_specs=[
            pl.BlockSpec((z.rows_dev, lanes), lambda j, me_ref: (owner(j, me_ref), 0))
            for _ in range(z.chunks)
        ]
        + [base_spec, base_spec, whole_spec(step.shape), whole_spec(step.shape)]
        + [whole_spec(sums.shape)],
        out_specs=pl.BlockSpec(
            (1, z.chan_dev, 2 * BEAMS * FR), lambda j, me_ref: (j, 0, 0)
        ),
        scratch_shapes=[pltpu.VMEM((2 * BEAMS * z.chan_dev, FR * z.cap), jnp.bfloat16)],
    )
    return pl.pallas_call(
        functools.partial(beam_kernel, z),
        grid_spec=grid_spec,
        out_shape=jax.ShapeDtypeStruct((z.devices, z.chan_dev, 2 * BEAMS * FR), jnp.float32),
        compiler_params=pltpu.CompilerParams(vmem_limit_bytes=VMEM),
        cost_estimate=pl.CostEstimate(
            flops=20_000_000_000, bytes_accessed=20_000_000, transcendentals=0
        ),
        name="beam_sums",
    )(
        me, *spectra, jnp.cos(base), jnp.sin(base), jnp.cos(step), jnp.sin(step),
        jnp.asarray(sums),
    )


def swap(z, x, offset):
    return lax.ppermute(x, "chan", [(i, i ^ offset) for i in range(z.devices)])


def halve(z, x, bit):
    half = x.shape[0] // 2
    return x[:half] + swap(z, x[half:], bit), 2 * bit


def exchange(x):
    return lax.all_to_all(x, "chan", split_axis=0, concat_axis=0, tiled=True)


def on_device(voltages, delays, band_feeds):
    z = Sizes(lax.axis_size("chan"), voltages.shape[0])
    me = lax.axis_index("chan")
    me_array = me.astype(jnp.int32).reshape(1)

    own = lax.dynamic_slice_in_dim(band_feeds, me * z.bands_here, z.bands_here, 0)
    source = own // z.feed_dev
    before = jnp.sum(
        (own[:, None, :] < (source * z.feed_dev)[:, :, None]).astype(jnp.int32), axis=2
    )
    place = jnp.arange(FSUB, dtype=jnp.int32)[None, :] - before
    tau = jnp.arange(z.lane_frames, dtype=jnp.int32)
    big = (source // z.lane_frames) * LANES + place
    group = (source % z.lane_frames)[:, None, :] ^ tau[None, :, None]
    take_key = big[:, None, :] + z.cap * group

    calls = Spectra(z, me_array, voltages, band_feeds)
    early = list(range(max(1, z.chunks - 2)))
    basis = calls.basis(early)
    filt, *spectra, send = calls.first(0, early, basis, len(early), [])
    got = exchange(send)
    arrived = [[(got, c)] for c in early]
    if z.halves > 1:
        units = len(early) + z.halves
        filt, *spectra, send = calls.first(1, early, basis, units, [filt, *spectra])
        late = [z.chunks - 2, z.chunks - 1]
        *more, send, last = calls.next(late, filt, send)
        spectra = spectra + more
        got = exchange(send)
        for c in early:
            arrived[c].append((got, c))
        arrived.append([(got, len(early) + h) for h in range(z.halves)])

    beams, bit = beam_call(z, me_array, spectra, delays), 1
    beams, bit = halve(z, beams, bit)
    beams, bit = halve(z, beams, bit)
    if z.halves > 1:
        last, beams = lax.optimization_barrier((last, beams))
        got = exchange(last)
        arrived.append([(got, h) for h in range(z.halves)])
    beams, bit = halve(z, beams, bit)

    vis = None
    for k in range(z.chunks):
        vis = receive_call(z, k, arrived[k], take_key[k], vis)
        if k == 0:
            beams, vis = lax.optimization_barrier((beams, vis))
            while beams.shape[0] > 1:
                beams, bit = halve(z, beams, bit)
    return (vis, beams.reshape(z.chan_dev, 2 * BEAMS * FR))


def solution(mesh):
    in_specs = (P(("grp", "chan"), None), P(None, ("grp", "chan")), P())
    out_specs = (P(("grp", "chan"), None, None, None), P(("grp", "chan"), None))
    return jax.shard_map(
        on_device, mesh=mesh, in_specs=in_specs, out_specs=out_specs, check_vma=False
    )
```

```python
import functools
import math

import jax
import jax.numpy as jnp
import ml_dtypes
import numpy as np
from jax import lax
from jax.experimental import pallas as pl
from jax.experimental.pallas import tpu as pltpu
from jax.sharding import PartitionSpec as P

F = 1024
CHANNELS = 1024
TAPS = 4
BAND_CH = 16
BEAMS = 4
FR = 48
NFFT = 2048
BANDS = 64
FSUB = 256
LANES = 128
VMEM = 56 * 1024 * 1024

NT = (((1,), (1,)), ((), ()))


def fir_window():
    ids = np.arange(TAPS * NFFT, dtype=np.float64)
    centered = (ids - 0.5 * TAPS * NFFT + 0.5) / NFFT
    hann_part = 0.5 - 0.5 * np.cos(2.0 * np.pi * (ids + 0.5) / (TAPS * NFFT))
    return (np.sinc(centered) * hann_part).reshape(TAPS, NFFT)


ORDER = np.concatenate([np.arange(0, BAND_CH, 2), np.arange(1, BAND_CH, 2)])


def dft_rows(chan_ids):
    m = np.arange(NFFT // 2, dtype=np.int64)
    turns = (chan_ids[..., None].astype(np.int64) * m) % NFFT
    table = 2.0 * np.pi * np.arange(NFFT) / NFFT
    cosine = np.cos(table).astype(np.float32).astype(ml_dtypes.bfloat16)
    sine = (-np.sin(table)).astype(np.float32).astype(ml_dtypes.bfloat16)
    return np.stack([cosine[turns], sine[turns]], axis=1)


class Sizes:
    def __init__(self, devices, feed_dev):
        self.devices = devices
        self.feed_dev = feed_dev
        self.cap = feed_dev // 2
        self.lane_frames = LANES // self.cap
        self.quads = FR // self.lane_frames
        self.width = self.lane_frames * feed_dev
        self.steps = 6 if self.quads % 6 == 0 else self.quads
        self.step_frames = FR // self.steps
        self.step_quads = self.quads // self.steps
        self.step_lanes = self.step_frames * feed_dev
        self.chan_dev = CHANNELS // devices
        self.bands_here = BANDS // devices
        self.chunks = self.chan_dev // BAND_CH
        self.rows_dev = 2 * BAND_CH
        self.rows = devices * self.rows_dev
        self.groups = devices // self.lane_frames
        self.early = min(2, self.chunks)
        if self.chunks == 4:
            self.parts = (self.steps // 3, self.steps - self.steps // 3)
        else:
            self.early, self.parts = self.chunks, (self.steps,)


def find_places(z, me, lists):
    base = me * z.feed_dev
    first = jnp.sum((lists < base).astype(jnp.int32), axis=1, keepdims=True)
    lane = lax.broadcasted_iota(jnp.int32, (lists.shape[0], LANES), 1)
    at = first + lane % z.cap
    parts = []
    for side in range(FSUB // LANES):
        index = jnp.clip(at - side * LANES, 0, LANES - 1)
        half = lists[:, side * LANES : (side + 1) * LANES]
        parts.append(jnp.take_along_axis(half, index, axis=1, mode="promise_in_bounds"))
    loc = jnp.where(at < LANES, parts[0], parts[1]) - base
    return jnp.clip(loc, 0, z.feed_dev - 1)


def emit_spectra(z, scale, chunks, me_ref, spectra, lists_ref, loc_ref, spec_refs, send_refs):
    loc_ref[...] = find_places(z, me_ref[0], lists_ref[...])
    lane = lax.broadcasted_iota(jnp.int32, (z.rows_dev, LANES), 1)
    frame = (lane // z.cap) ^ (me_ref[0] % z.lane_frames)
    start = frame * z.cap
    few = BAND_CH // 2
    for c, chunk in enumerate(chunks):
        send_ref, unit = send_refs[c]
        for owner in range(z.devices):
            top = (c * z.devices + owner) * BAND_CH
            rows = [x[top + p : top + p + few] for p in (0, few) for x in spectra]
            rows = jnp.concatenate(rows, axis=0) * scale
            spec_refs[c][owner * z.rows_dev : (owner + 1) * z.rows_dev, :] = rows.astype(
                jnp.bfloat16
            )
            band = owner * z.bands_here + chunk
            loc = loc_ref[band : band + 1, :]
            index = start + loc % z.cap
            lower = jnp.broadcast_to(loc, index.shape) < z.cap
            for q in range(z.step_quads):
                parts = []
                for side in range(2):
                    left = q * z.width + side * LANES
                    parts.append(
                        jnp.take_along_axis(
                            rows[:, left : left + LANES], index, axis=1,
                            mode="promise_in_bounds",
                        )
                    )
                picked = jnp.where(lower, parts[0], parts[1])
                send_ref[owner, unit + q] = picked.astype(jnp.bfloat16)


def filter_tile(z, main_ref, halo, win_ref, off, f0):
    lanes = slice(off, off + LANES)
    taps = [win_ref[k : k + 1, lanes] for k in range(TAPS)]
    frames = []
    for t in range(z.step_frames + TAPS - 1):
        if t < z.step_frames:
            x = main_ref[f0 : f0 + 16, t * NFFT + off : t * NFFT + off + LANES]
        else:
            x = halo[t - z.step_frames][f0 : f0 + 16, lanes]
        frames.append(x.astype(jnp.float32))
    totals = []
    for t in range(z.step_frames):
        total = taps[0] * frames[t]
        for k in range(1, TAPS):
            total = total + taps[k] * frames[t + k]
        totals.append(total)
    if z.cap < 16:
        totals = [
            jnp.concatenate([totals[t][h : h + 8], totals[t + 1][h : h + 8]], axis=0)
            for t in range(0, z.step_frames, 2)
            for h in (0, 8)
        ]
    out = []
    for i, total in enumerate(totals):
        if z.cap < 16:
            t, half, feed = 2 * (i // 2), i % 2, 0
        else:
            t, half, feed = i, f0 // z.cap, f0 % z.cap
        row = (t // z.lane_frames) * z.width + half * LANES
        row += (t % z.lane_frames) * z.cap + feed
        out.append((row, total.astype(jnp.bfloat16)))
    return out


def filter_fold(z, main_ref, halo, win_ref, filt_ref, off):
    far = off + NFFT // 2
    for f0 in range(0, z.feed_dev, 16):
        low = filter_tile(z, main_ref, halo, win_ref, off, f0)
        high = filter_tile(z, main_ref, halo, win_ref, far, f0)
        for (row, a), (_, b) in zip(low, high):
            filt_ref[row : row + 16, off : off + LANES] = a + b
            filt_ref[row : row + 16, far : far + LANES] = a - b


def transform(basis_ref, filt_ref, begin, end):
    return [
        lax.dot_general(
            basis_ref[parity, :, begin:end],
            filt_ref[:, parity * (NFFT // 2) + begin : parity * (NFFT // 2) + end],
            NT,
            preferred_element_type=jnp.float32,
        )
        for parity in range(2)
    ]


def first_kernel(
    z, scale, chunks, held, me_ref, main_ref, h0_ref, h1_ref, h2_ref, win_ref, basis_ref,
    lists_ref, *refs,
):
    filt_ref, spec_refs, send_ref, loc_ref = refs[held], refs[held + 1 : -2], refs[-2], refs[-1]
    halo = (h0_ref, h1_ref, h2_ref)
    piece = 512
    spectra = None
    for off in range(0, NFFT // 2, piece):
        for tile in range(off, off + piece, LANES):
            filter_fold(z, main_ref, halo, win_ref, filt_ref, tile)
        part = transform(basis_ref, filt_ref, off, off + piece)
        spectra = part if spectra is None else [x + y for x, y in zip(spectra, part)]
    sends = [(send_ref, c * z.step_quads) for c in range(len(chunks))]
    emit_spectra(z, scale, chunks, me_ref, spectra, lists_ref, loc_ref, spec_refs, sends)


def next_kernel(z, scale, chunks, me_ref, filt_ref, basis_ref, lists_ref, held_ref, *refs):
    spectra = transform(basis_ref, filt_ref, 0, NFFT // 2)
    count = len(chunks)
    sends = [(refs[count + c], 0) for c in range(count)]
    emit_spectra(
        z, scale, chunks, me_ref, spectra, lists_ref, refs[-1], refs[:count], sends
    )


def whole_spec(shape):
    return pl.BlockSpec(shape, lambda *g: (0,) * len(shape))


class Spectra:

    def __init__(self, z, me, voltages, band_feeds):
        window = fir_window()
        self.z = z
        self.me = me
        self.scale = float(np.sqrt(2.0 / np.sum(window * window)))
        self.window = jnp.asarray(window.astype(np.float32))
        self.voltages = voltages
        self.lists = band_feeds
        self.ids = np.arange(CHANNELS).reshape(z.devices, z.chunks, BAND_CH)
        self.me_spec = pl.BlockSpec(memory_space=pltpu.SMEM)
        self.spec_shape = jax.ShapeDtypeStruct((z.rows, FR * z.feed_dev), jnp.bfloat16)
        self.filt_shape = jax.ShapeDtypeStruct((FR * z.feed_dev, NFFT), jnp.bfloat16)

    def basis(self, chunks):
        sides = []
        for parity in range(2):
            rows = [dft_rows(self.ids[:, k, parity::2].reshape(-1)) for k in chunks]
            rows = np.stack(rows).reshape(len(chunks), self.z.devices, BAND_CH // 2, 2, -1)
            rows = np.transpose(rows, (0, 1, 3, 2, 4))
            sides.append(rows.reshape(len(chunks) * self.z.rows // 2, NFFT // 2))
        return jnp.asarray(np.stack(sides))

    def message(self, quads):
        z = self.z
        return jax.ShapeDtypeStruct((z.devices, quads, z.rows_dev, LANES), jnp.bfloat16)

    def common(self, steps, chunks):
        z = self.z
        flops = len(chunks) * z.rows * NFFT * z.step_lanes * steps
        return dict(
            grid=(steps,),
            scratch_shapes=[pltpu.VMEM((BANDS, LANES), jnp.int32)],
            compiler_params=pltpu.CompilerParams(vmem_limit_bytes=VMEM),
            cost_estimate=pl.CostEstimate(
                flops=flops, bytes_accessed=3_000_000 * steps, transcendentals=0
            ),
        )

    def first(self, begin, steps, chunks, basis, quads, held):
        z = self.z
        count = len(chunks)

        def halo_spec(h):
            return pl.BlockSpec(
                (z.feed_dev, NFFT), lambda g: (0, z.step_frames * (begin + g + 1) + h)
            )

        send_block = (z.devices, count * z.step_quads, z.rows_dev, LANES)
        operands = [self.me] + [self.voltages] * 4 + [self.window, basis, self.lists]
        aliases = {len(operands) + i: i for i in range(len(held))}
        return pl.pallas_call(
            functools.partial(first_kernel, z, self.scale, chunks, len(held)),
            in_specs=[
                self.me_spec,
                pl.BlockSpec((z.feed_dev, z.step_frames * NFFT), lambda g: (0, begin + g)),
                halo_spec(0),
                halo_spec(1),
                halo_spec(2),
                whole_spec((TAPS, NFFT)),
                whole_spec(basis.shape),
                whole_spec(self.lists.shape),
            ]
            + [pl.BlockSpec(memory_space=pl.ANY)] * len(held),
            out_specs=[
                pl.BlockSpec((z.step_lanes, NFFT), lambda g: (begin + g, 0)),
            ]
            + [pl.BlockSpec((z.rows, z.step_lanes), lambda g: (0, begin + g))] * count
            + [pl.BlockSpec(send_block, lambda g: (0, g, 0, 0))],
            out_shape=[self.filt_shape] + [self.spec_shape] * count + [self.message(quads)],
            input_output_aliases=aliases,
            name="filter_spectra",
            **self.common(steps, chunks),
        )(*operands, *held)

    def next(self, chunks, filt, held):
        z = self.z
        count = len(chunks)
        basis = self.basis(chunks)
        block = (z.devices, z.step_quads, z.rows_dev, LANES)
        base = (held.shape[1] - z.quads) // z.step_quads
        operands = [self.me, filt, basis, self.lists, held]
        return pl.pallas_call(
            functools.partial(next_kernel, z, self.scale, chunks),
            in_specs=[
                self.me_spec,
                pl.BlockSpec((z.step_lanes, NFFT), lambda g: (g, 0)),
                whole_spec(basis.shape),
                whole_spec(self.lists.shape),
                pl.BlockSpec(memory_space=pl.ANY),
            ],
            out_specs=[pl.BlockSpec((z.rows, z.step_lanes), lambda g: (0, g))] * count
            + [
                pl.BlockSpec(block, lambda g: (0, base + g, 0, 0)),
                pl.BlockSpec(block, lambda g: (0, g, 0, 0)),
            ],
            out_shape=[self.spec_shape] * count
            + [self.message(held.shape[1]), self.message(z.quads)],
            input_output_aliases={4: count},
            name="spectra_next",
            **self.common(z.steps, chunks),
        )(*operands)


def receive_kernel(z, step_ch, runs, *refs):
    arr_refs, key_ref = refs[: len(runs)], refs[len(runs)]
    vis_ref, rows_ref = refs[-2], refs[-1]
    g = pl.program_id(0)
    lf = z.lane_frames

    @pl.when(g == 0)
    def _():
        slot = lax.broadcasted_iota(jnp.int32, (z.groups * LANES, FSUB), 0)
        size = z.quads * z.rows_dev
        for tau in range(lf):
            pick = jnp.where(slot == key_ref[tau : tau + 1, :], 1.0, 0.0).astype(jnp.bfloat16)
            parts = []
            for arr_ref, places in zip(arr_refs, runs):
                for first, count in places:
                    depth = count * z.rows_dev
                    lane_group = lax.broadcasted_iota(jnp.int32, (depth, LANES), 1) // z.cap
                    tiles = []
                    for big in range(z.groups):
                        tile = None
                        for lane in range(lf):
                            block = arr_ref[big * lf + (lane ^ tau), first : first + count]
                            block = block.reshape(depth, LANES)
                            if tile is None:
                                tile = block
                            else:
                                tile = jnp.where(lane_group == lane, block, tile)
                        tiles.append(tile)
                    parts.append(jnp.concatenate(tiles, axis=1))
            rows = jnp.dot(
                jnp.concatenate(parts, axis=0), pick, preferred_element_type=jnp.float32
            )
            for side in range(FSUB // LANES):
                rows_ref[side, tau * size : (tau + 1) * size, :] = rows[
                    :, side * LANES : (side + 1) * LANES
                ]

    for i in range(step_ch):
        ch = (i % 2) * (BAND_CH // 2) + g * (step_ch // 2) + i // 2
        halves = []
        for part in range(2):
            halves.append(
                jnp.concatenate(
                    [
                        rows_ref[side, pl.ds(ch + part * BAND_CH, FR, stride=z.rows_dev), :]
                        for side in range(FSUB // LANES)
                    ],
                    axis=1,
                )
            )
        real, imag = halves
        both = jnp.concatenate([real, imag], axis=0)
        turned = jnp.concatenate([-imag, real], axis=0)
        right = jnp.concatenate([both, turned], axis=1).astype(jnp.bfloat16)
        left = both.astype(jnp.bfloat16).T
        out = jnp.dot(left, right, preferred_element_type=jnp.float32) * (1.0 / FR)
        vis_ref[i, 0] = out[:, :FSUB]
        vis_ref[i, 1] = out[:, FSUB:]


def receive_call(z, chunk, arrived, key, vis):
    step_ch = 4
    steps = BAND_CH // step_ch
    out_shape = jax.ShapeDtypeStruct((z.chan_dev, 2, FSUB, FSUB), jnp.float32)

    def block_spec(got, quads, at, places):
        shape = (z.devices, quads) + got.shape[2:]
        return pl.BlockSpec(shape, lambda g: (0, at, 0, 0))

    in_specs = [block_spec(*x) for x in arrived] + [whole_spec(key.shape)]
    operands = [x[0] for x in arrived] + [key]
    runs = [x[3] for x in arrived]
    aliases = {}
    if vis is not None:
        in_specs.append(pl.BlockSpec(memory_space=pl.ANY))
        aliases = {len(operands): 0}
        operands.append(vis)
    return pl.pallas_call(
        functools.partial(receive_kernel, z, step_ch, runs),
        grid=(steps,),
        in_specs=in_specs,
        out_specs=pl.BlockSpec(
            (step_ch, 2, FSUB, FSUB), lambda g: (chunk * steps + g, 0, 0, 0)
        ),
        out_shape=out_shape,
        input_output_aliases=aliases,
        scratch_shapes=[
            pltpu.VMEM((FSUB // LANES, FR * z.rows_dev, LANES), jnp.float32)
        ],
        compiler_params=pltpu.CompilerParams(vmem_limit_bytes=VMEM),
        cost_estimate=pl.CostEstimate(
            flops=4_000_000_000, bytes_accessed=10_000_000, transcendentals=0
        ),
        name="correlate",
    )(*operands)


def beam_kernel(z, me_ref, *refs):
    spec_refs = refs[: z.chunks]
    cos_base, sin_base, cos_step, sin_step, sum_ref, out_ref, prod_ref = refs[z.chunks :]
    count = z.chan_dev
    weights = []
    for g in range(BEAMS):
        c0, s0 = cos_base[0, g : g + 1, :], sin_base[0, g : g + 1, :]
        c1, s1 = cos_step[g], sin_step[g]
        weights.append(
            ((c0 * c1 - s0 * s1).astype(jnp.bfloat16), (s0 * c1 + c0 * s1).astype(jnp.bfloat16))
        )
    for q in range(z.quads):
        lanes = slice(q * z.width, (q + 1) * z.width)
        x = [ref[:, lanes] for ref in spec_refs]
        real = jnp.concatenate([v[:BAND_CH] for v in x], axis=0)
        imag = jnp.concatenate([v[BAND_CH:] for v in x], axis=0)
        for g in range(BEAMS):
            c, s = weights[g]
            pair = (c * real + s * imag, c * imag - s * real)
            for part in range(2):
                row = (part * BEAMS + g) * count
                both = pair[part][:, :LANES] + pair[part][:, LANES:]
                prod_ref[row : row + count, q * LANES : (q + 1) * LANES] = both
    sums = jnp.dot(prod_ref[...], sum_ref[...], preferred_element_type=jnp.float32)
    sums = sums * (1.0 / np.sqrt(F))
    for j in range(2 * BEAMS):
        out_ref[0, :, j * FR : (j + 1) * FR] = sums[j * count : (j + 1) * count, :FR]


def beam_call(z, me, spectra, delays):
    bits = z.devices.bit_length() - 1
    lanes = FR * z.feed_dev
    halves = delays.reshape(BEAMS, 2, 1, z.cap)
    spread = jnp.broadcast_to(halves, (BEAMS, 2, z.lane_frames, z.cap)).reshape(BEAMS, z.width)
    unit = 2.0 * jnp.pi / NFFT
    owners = jnp.arange(z.devices, dtype=jnp.int32).astype(jnp.float32) * z.chan_dev
    inner = np.arange(z.chunks)[:, None] * BAND_CH + ORDER[None, :]
    inner = jnp.asarray(inner.reshape(-1).astype(np.float32))
    base = unit * (spread[None, :, :] * owners[:, None, None])
    step = unit * (spread[:, None, :] * inner[None, :, None])
    frame = (np.arange(FR * z.cap) // LANES) * z.lane_frames
    frame = frame + (np.arange(FR * z.cap) % LANES) // z.cap
    sums = (frame[:, None] == np.arange(LANES)[None, :]).astype(ml_dtypes.bfloat16)

    def owner(j, me_ref):
        k = 0
        for b in range(bits):
            k = k | (((j >> b) & 1) << (bits - 1 - b))
        return me_ref[0] ^ k

    base_spec = pl.BlockSpec(
        (1, BEAMS, z.width), lambda j, me_ref: (owner(j, me_ref), 0, 0)
    )
    grid_spec = pltpu.PrefetchScalarGridSpec(
        num_scalar_prefetch=1,
        grid=(z.devices,),
        in_specs=[
            pl.BlockSpec((z.rows_dev, lanes), lambda j, me_ref: (owner(j, me_ref), 0))
            for _ in range(z.chunks)
        ]
        + [base_spec, base_spec, whole_spec(step.shape), whole_spec(step.shape)]
        + [whole_spec(sums.shape)],
        out_specs=pl.BlockSpec(
            (1, z.chan_dev, 2 * BEAMS * FR), lambda j, me_ref: (j, 0, 0)
        ),
        scratch_shapes=[pltpu.VMEM((2 * BEAMS * z.chan_dev, FR * z.cap), jnp.bfloat16)],
    )
    return pl.pallas_call(
        functools.partial(beam_kernel, z),
        grid_spec=grid_spec,
        out_shape=jax.ShapeDtypeStruct((z.devices, z.chan_dev, 2 * BEAMS * FR), jnp.float32),
        compiler_params=pltpu.CompilerParams(vmem_limit_bytes=VMEM),
        cost_estimate=pl.CostEstimate(
            flops=20_000_000_000, bytes_accessed=20_000_000, transcendentals=0
        ),
        name="beam_sums",
    )(
        me, *spectra, jnp.cos(base), jnp.sin(base), jnp.cos(step), jnp.sin(step),
        jnp.asarray(sums),
    )


def swap(z, x, offset):
    return lax.ppermute(x, "chan", [(i, i ^ offset) for i in range(z.devices)])


def exchange(x):
    return lax.all_to_all(x, "chan", split_axis=0, concat_axis=0, tiled=True)


def on_device(voltages, delays, band_feeds):
    z = Sizes(lax.axis_size("chan"), voltages.shape[0])
    me = lax.axis_index("chan")
    me_array = me.astype(jnp.int32).reshape(1)

    own = lax.dynamic_slice_in_dim(band_feeds, me * z.bands_here, z.bands_here, 0)
    source = own // z.feed_dev
    before = jnp.sum(
        (own[:, None, :] < (source * z.feed_dev)[:, :, None]).astype(jnp.int32), axis=2
    )
    place = jnp.arange(FSUB, dtype=jnp.int32)[None, :] - before
    tau = jnp.arange(z.lane_frames, dtype=jnp.int32)
    big = (source // z.lane_frames) * LANES + place
    group = (source % z.lane_frames)[:, None, :] ^ tau[None, :, None]
    take_key = big[:, None, :] + z.cap * group

    calls = Spectra(z, me_array, voltages, band_feeds)
    early = list(range(z.early))
    basis = calls.basis(early)
    step = z.early * z.step_quads
    arrived = [[] for _ in range(z.chunks)]

    def early_places(got, steps):
        for c in early:
            places = [(g * step + c * z.step_quads, z.step_quads) for g in range(steps)]
            arrived[c].append((got, steps * step, 0, places))

    steps = z.parts[0]
    filt, *spectra, send = calls.first(0, steps, early, basis, steps * step, [])
    early_places(exchange(send), steps)
    if len(z.parts) > 1:
        begin, steps = steps, z.parts[1]
        base = steps * step
        filt, *spectra, send = calls.first(
            begin, steps, early, basis, base + z.quads, [filt, *spectra]
        )
        *more, send, last = calls.next([z.chunks - 2, z.chunks - 1], filt, send)
        spectra = spectra + more
        got = exchange(send)
        early_places(got, steps)
        block = math.gcd(base, z.quads)
        for i in range(z.quads // block):
            arrived[-2].append((got, block, base // block + i, [(0, block)]))

    beams, bit = beam_call(z, me_array, spectra, delays), 1
    while beams.shape[0] > 1:
        half = beams.shape[0] // 2
        beams, bit = beams[:half] + swap(z, beams[half:], bit), 2 * bit
    beams = beams.reshape(z.chunks, 2, BAND_CH // 2, 2 * BEAMS * FR)
    beams = jnp.swapaxes(beams, 1, 2).reshape(z.chan_dev, 2 * BEAMS * FR)
    if len(z.parts) > 1:
        last, beams = lax.optimization_barrier((last, beams))
        arrived[-1].append((exchange(last), z.quads, 0, [(0, z.quads)]))

    vis = None
    for k in range(z.chunks):
        vis = receive_call(z, k, arrived[k], take_key[k], vis)
    return (vis, beams)


def solution(mesh):
    in_specs = (P(("grp", "chan"), None), P(None, ("grp", "chan")), P())
    out_specs = (P(("grp", "chan"), None, None, None), P(("grp", "chan"), None))
    return jax.shard_map(
        on_device, mesh=mesh, in_specs=in_specs, out_specs=out_specs, check_vma=False
    )
```

```python
import functools

import jax
import jax.numpy as jnp
import ml_dtypes
import numpy as np
from jax import lax
from jax.experimental import pallas as pl
from jax.experimental.pallas import tpu as pltpu
from jax.sharding import PartitionSpec as P

F = 1024
CHANNELS = 1024
TAPS = 4
BAND_CH = 16
BEAMS = 4
FR = 48
NFFT = 2048
BANDS = 64
FSUB = 256
LANES = 128
VMEM = 56 * 1024 * 1024

NT = (((1,), (1,)), ((), ()))


def fir_window():
    ids = np.arange(TAPS * NFFT, dtype=np.float64)
    centered = (ids - 0.5 * TAPS * NFFT + 0.5) / NFFT
    hann_part = 0.5 - 0.5 * np.cos(2.0 * np.pi * (ids + 0.5) / (TAPS * NFFT))
    return (np.sinc(centered) * hann_part).reshape(TAPS, NFFT)


ORDER = np.concatenate([np.arange(0, BAND_CH, 2), np.arange(1, BAND_CH, 2)])


def dft_rows(chan_ids):
    m = np.arange(NFFT // 2, dtype=np.int64)
    turns = (chan_ids[..., None].astype(np.int64) * m) % NFFT
    table = 2.0 * np.pi * np.arange(NFFT) / NFFT
    cosine = np.cos(table).astype(np.float32).astype(ml_dtypes.bfloat16)
    sine = (-np.sin(table)).astype(np.float32).astype(ml_dtypes.bfloat16)
    return np.stack([cosine[turns], sine[turns]], axis=1)


class Sizes:
    def __init__(self, devices, feed_dev):
        self.devices = devices
        self.feed_dev = feed_dev
        self.cap = feed_dev // 2
        self.lane_frames = LANES // self.cap
        self.quads = FR // self.lane_frames
        self.width = self.lane_frames * feed_dev
        self.steps = 6 if self.quads % 6 == 0 else self.quads
        self.step_frames = FR // self.steps
        self.step_quads = self.quads // self.steps
        self.step_lanes = self.step_frames * feed_dev
        self.chan_dev = CHANNELS // devices
        self.bands_here = BANDS // devices
        self.chunks = self.chan_dev // BAND_CH
        self.rows_dev = 2 * BAND_CH
        self.rows = devices * self.rows_dev
        self.groups = devices // self.lane_frames
        self.early = min(2, self.chunks)
        if self.chunks == 4:
            self.parts = (self.steps // 2, self.steps - self.steps // 2)
        else:
            self.early, self.parts = self.chunks, (self.steps,)


def find_places(z, me, lists):
    base = me * z.feed_dev
    first = jnp.sum((lists < base).astype(jnp.int32), axis=1, keepdims=True)
    lane = lax.broadcasted_iota(jnp.int32, (lists.shape[0], LANES), 1)
    at = first + lane % z.cap
    parts = []
    for side in range(FSUB // LANES):
        index = jnp.clip(at - side * LANES, 0, LANES - 1)
        half = lists[:, side * LANES : (side + 1) * LANES]
        parts.append(jnp.take_along_axis(half, index, axis=1, mode="promise_in_bounds"))
    loc = jnp.where(at < LANES, parts[0], parts[1]) - base
    return jnp.clip(loc, 0, z.feed_dev - 1)


def emit_spectra(z, scale, chunks, me_ref, spectra, lists_ref, loc_ref, spec_refs, send_refs):
    loc_ref[...] = find_places(z, me_ref[0], lists_ref[...])
    lane = lax.broadcasted_iota(jnp.int32, (z.rows_dev, LANES), 1)
    frame = (lane // z.cap) ^ (me_ref[0] % z.lane_frames)
    start = frame * z.cap
    few = BAND_CH // 2
    for c, chunk in enumerate(chunks):
        for owner in range(z.devices):
            top = (c * z.devices + owner) * BAND_CH
            rows = [x[top + p : top + p + few] for p in (0, few) for x in spectra]
            rows = jnp.concatenate(rows, axis=0) * scale
            spec_refs[c][owner * z.rows_dev : (owner + 1) * z.rows_dev, :] = rows.astype(
                jnp.bfloat16
            )
            band = owner * z.bands_here + chunk
            loc = loc_ref[band : band + 1, :]
            index = start + loc % z.cap
            lower = jnp.broadcast_to(loc, index.shape) < z.cap
            for q in range(z.step_quads):
                parts = []
                for side in range(2):
                    left = q * z.width + side * LANES
                    parts.append(
                        jnp.take_along_axis(
                            rows[:, left : left + LANES], index, axis=1,
                            mode="promise_in_bounds",
                        )
                    )
                picked = jnp.where(lower, parts[0], parts[1])
                for parity, (send_ref, unit, stride) in enumerate(send_refs[c]):
                    half = [
                        picked[p * BAND_CH + parity * few : p * BAND_CH + parity * few + few]
                        for p in range(2)
                    ]
                    half = jnp.concatenate(half, axis=0).astype(jnp.bfloat16)
                    send_ref[owner, unit + q * stride] = half


def filter_tile(z, main_ref, halo, win_ref, off, f0):
    lanes = slice(off, off + LANES)
    taps = [win_ref[k : k + 1, lanes] for k in range(TAPS)]
    frames = []
    for t in range(z.step_frames + TAPS - 1):
        if t < z.step_frames:
            x = main_ref[f0 : f0 + 16, t * NFFT + off : t * NFFT + off + LANES]
        else:
            x = halo[t - z.step_frames][f0 : f0 + 16, lanes]
        frames.append(x.astype(jnp.float32))
    totals = []
    for t in range(z.step_frames):
        total = taps[0] * frames[t]
        for k in range(1, TAPS):
            total = total + taps[k] * frames[t + k]
        totals.append(total)
    if z.cap < 16:
        totals = [
            jnp.concatenate([totals[t][h : h + 8], totals[t + 1][h : h + 8]], axis=0)
            for t in range(0, z.step_frames, 2)
            for h in (0, 8)
        ]
    out = []
    for i, total in enumerate(totals):
        if z.cap < 16:
            t, half, feed = 2 * (i // 2), i % 2, 0
        else:
            t, half, feed = i, f0 // z.cap, f0 % z.cap
        row = (t // z.lane_frames) * z.width + half * LANES
        row += (t % z.lane_frames) * z.cap + feed
        out.append((row, total.astype(jnp.bfloat16)))
    return out


def filter_fold(z, main_ref, halo, win_ref, filt_ref, off):
    far = off + NFFT // 2
    for f0 in range(0, z.feed_dev, 16):
        low = filter_tile(z, main_ref, halo, win_ref, off, f0)
        high = filter_tile(z, main_ref, halo, win_ref, far, f0)
        for (row, a), (_, b) in zip(low, high):
            filt_ref[row : row + 16, off : off + LANES] = a + b
            filt_ref[row : row + 16, far : far + LANES] = a - b


def transform(basis_ref, filt_ref, begin, end):
    return [
        lax.dot_general(
            basis_ref[parity, :, begin:end],
            filt_ref[:, parity * (NFFT // 2) + begin : parity * (NFFT // 2) + end],
            NT,
            preferred_element_type=jnp.float32,
        )
        for parity in range(2)
    ]


def first_kernel(
    z, scale, chunks, held, me_ref, main_ref, h0_ref, h1_ref, h2_ref, win_ref, basis_ref,
    lists_ref, *refs,
):
    filt_ref, spec_refs, send_ref, loc_ref = refs[held], refs[held + 1 : -2], refs[-2], refs[-1]
    halo = (h0_ref, h1_ref, h2_ref)
    piece = 512
    spectra = None
    for off in range(0, NFFT // 2, piece):
        for tile in range(off, off + piece, LANES):
            filter_fold(z, main_ref, halo, win_ref, filt_ref, tile)
        part = transform(basis_ref, filt_ref, off, off + piece)
        spectra = part if spectra is None else [x + y for x, y in zip(spectra, part)]
    sends = []
    for c in range(len(chunks)):
        unit = c * 2 * z.step_quads
        sends.append([(send_ref, unit, 2), (send_ref, unit + 1, 2)])
    emit_spectra(z, scale, chunks, me_ref, spectra, lists_ref, loc_ref, spec_refs, sends)


def next_kernel(z, scale, chunks, me_ref, filt_ref, basis_ref, lists_ref, held_ref, *refs):
    spectra = transform(basis_ref, filt_ref, 0, NFFT // 2)
    begun_ref, last_ref = refs[2], refs[3]
    sends = [
        [(begun_ref, 0, 2), (begun_ref, 1, 2)],
        [(begun_ref, 2 * z.step_quads, 1), (last_ref, 0, 1)],
    ]
    emit_spectra(z, scale, chunks, me_ref, spectra, lists_ref, refs[-1], refs[:2], sends)


def whole_spec(shape):
    return pl.BlockSpec(shape, lambda *g: (0,) * len(shape))


class Spectra:

    def __init__(self, z, me, voltages, band_feeds):
        window = fir_window()
        self.z = z
        self.me = me
        self.scale = float(np.sqrt(2.0 / np.sum(window * window)))
        self.window = jnp.asarray(window.astype(np.float32))
        self.voltages = voltages
        self.lists = band_feeds
        self.ids = np.arange(CHANNELS).reshape(z.devices, z.chunks, BAND_CH)
        self.me_spec = pl.BlockSpec(memory_space=pltpu.SMEM)
        self.spec_shape = jax.ShapeDtypeStruct((z.rows, FR * z.feed_dev), jnp.bfloat16)
        self.filt_shape = jax.ShapeDtypeStruct((FR * z.feed_dev, NFFT), jnp.bfloat16)

    def basis(self, chunks):
        sides = []
        for parity in range(2):
            rows = [dft_rows(self.ids[:, k, parity::2].reshape(-1)) for k in chunks]
            rows = np.stack(rows).reshape(len(chunks), self.z.devices, BAND_CH // 2, 2, -1)
            rows = np.transpose(rows, (0, 1, 3, 2, 4))
            sides.append(rows.reshape(len(chunks) * self.z.rows // 2, NFFT // 2))
        return jnp.asarray(np.stack(sides))

    def message(self, units):
        return jax.ShapeDtypeStruct((self.z.devices, units, BAND_CH, LANES), jnp.bfloat16)

    def common(self, steps, chunks):
        z = self.z
        flops = len(chunks) * z.rows * NFFT * z.step_lanes * steps
        return dict(
            grid=(steps,),
            scratch_shapes=[pltpu.VMEM((BANDS, LANES), jnp.int32)],
            compiler_params=pltpu.CompilerParams(vmem_limit_bytes=VMEM),
            cost_estimate=pl.CostEstimate(
                flops=flops, bytes_accessed=3_000_000 * steps, transcendentals=0
            ),
        )

    def first(self, begin, steps, chunks, basis, units, held):
        z = self.z
        count = len(chunks)

        def halo_spec(h):
            return pl.BlockSpec(
                (z.feed_dev, NFFT), lambda g: (0, z.step_frames * (begin + g + 1) + h)
            )

        send_block = (z.devices, count * 2 * z.step_quads, BAND_CH, LANES)
        operands = [self.me] + [self.voltages] * 4 + [self.window, basis, self.lists]
        aliases = {len(operands) + i: i for i in range(len(held))}
        return pl.pallas_call(
            functools.partial(first_kernel, z, self.scale, chunks, len(held)),
            in_specs=[
                self.me_spec,
                pl.BlockSpec((z.feed_dev, z.step_frames * NFFT), lambda g: (0, begin + g)),
                halo_spec(0),
                halo_spec(1),
                halo_spec(2),
                whole_spec((TAPS, NFFT)),
                whole_spec(basis.shape),
                whole_spec(self.lists.shape),
            ]
            + [pl.BlockSpec(memory_space=pl.ANY)] * len(held),
            out_specs=[
                pl.BlockSpec((z.step_lanes, NFFT), lambda g: (begin + g, 0)),
            ]
            + [pl.BlockSpec((z.rows, z.step_lanes), lambda g: (0, begin + g))] * count
            + [pl.BlockSpec(send_block, lambda g: (0, g, 0, 0))],
            out_shape=[self.filt_shape] + [self.spec_shape] * count + [self.message(units)],
            input_output_aliases=aliases,
            name="filter_spectra",
            **self.common(steps, chunks),
        )(*operands, *held)

    def next(self, chunks, filt, held):
        z = self.z
        basis = self.basis(chunks)
        begun = 3 * z.step_quads
        base = held.shape[1] // begun - z.steps
        operands = [self.me, filt, basis, self.lists, held]
        return pl.pallas_call(
            functools.partial(next_kernel, z, self.scale, chunks),
            in_specs=[
                self.me_spec,
                pl.BlockSpec((z.step_lanes, NFFT), lambda g: (g, 0)),
                whole_spec(basis.shape),
                whole_spec(self.lists.shape),
                pl.BlockSpec(memory_space=pl.ANY),
            ],
            out_specs=[pl.BlockSpec((z.rows, z.step_lanes), lambda g: (0, g))] * 2
            + [
                pl.BlockSpec((z.devices, begun, BAND_CH, LANES), lambda g: (0, base + g, 0, 0)),
                pl.BlockSpec((z.devices, z.step_quads, BAND_CH, LANES), lambda g: (0, g, 0, 0)),
            ],
            out_shape=[self.spec_shape] * 2
            + [self.message(held.shape[1]), self.message(z.quads)],
            input_output_aliases={4: 2},
            name="spectra_next",
            **self.common(z.steps, chunks),
        )(*operands)


def receive_kernel(z, parities, step_pairs, runs, arrays, *refs):
    arr_refs, key_ref = refs[:arrays], refs[arrays]
    vis_ref, buf_ref, rows_ref, sems = refs[-4:]
    g = pl.program_id(0)
    lf = z.lane_frames
    few = BAND_CH // 2
    depth = buf_ref.shape[1] * BAND_CH

    @pl.when(g == 0)
    def _():
        copies = []
        place = 0
        for i, (array, first, count) in enumerate(runs):
            copy = pltpu.make_async_copy(
                arr_refs[array].at[:, first : first + count],
                buf_ref.at[:, place : place + count],
                sems.at[i],
            )
            copy.start()
            copies.append(copy)
            place += count
        for copy in copies:
            copy.wait()
        slot = lax.broadcasted_iota(jnp.int32, (z.groups * LANES, FSUB), 0)
        lane_group = lax.broadcasted_iota(jnp.int32, (depth, LANES), 1) // z.cap
        for tau in range(lf):
            tiles = []
            for big in range(z.groups):
                tile = buf_ref[big * lf + tau].reshape(depth, LANES)
                for lane in range(1, lf):
                    block = buf_ref[big * lf + (lane ^ tau)].reshape(depth, LANES)
                    tile = jnp.where(lane_group == lane, block, tile)
                tiles.append(tile)
            pick = jnp.where(slot == key_ref[tau : tau + 1, :], 1.0, 0.0).astype(jnp.bfloat16)
            rows = jnp.dot(
                jnp.concatenate(tiles, axis=1), pick, preferred_element_type=jnp.float32
            )
            for side in range(FSUB // LANES):
                rows_ref[side, tau * depth : (tau + 1) * depth, :] = rows[
                    :, side * LANES : (side + 1) * LANES
                ]

    for i in range(step_pairs):
        for p in range(parities):
            halves = []
            for part in range(2):
                first = p * BAND_CH + part * few + g * step_pairs + i
                halves.append(
                    jnp.concatenate(
                        [
                            rows_ref[side, pl.ds(first, FR, stride=parities * BAND_CH), :]
                            for side in range(FSUB // LANES)
                        ],
                        axis=1,
                    )
                )
            real, imag = halves
            both = jnp.concatenate([real, imag], axis=0)
            turned = jnp.concatenate([-imag, real], axis=0)
            right = jnp.concatenate([both, turned], axis=1).astype(jnp.bfloat16)
            left = both.astype(jnp.bfloat16).T
            out = jnp.dot(left, right, preferred_element_type=jnp.float32) * (1.0 / FR)
            vis_ref[i, p, 0] = out[:, :FSUB]
            vis_ref[i, p, 1] = out[:, FSUB:]


def receive_call(z, chunk, parity, arrived, key, vis):
    parities = 2 if parity is None else 1
    step_pairs = 4 // parities
    steps = BAND_CH // 2 // step_pairs
    at = 0 if parity is None else parity
    out_shape = jax.ShapeDtypeStruct((z.chan_dev // 2, 2, 2, FSUB, FSUB), jnp.float32)
    arrays = []
    runs = []
    for got, first, count in arrived:
        if not any(got is x for x in arrays):
            arrays.append(got)
        runs.append(([got is x for x in arrays].index(True), first, count))
    units = sum(count for _, _, count in runs)
    operands = arrays + [key]
    in_specs = [pl.BlockSpec(memory_space=pl.ANY)] * len(arrays) + [whole_spec(key.shape)]
    aliases = {}
    if vis is not None:
        in_specs.append(pl.BlockSpec(memory_space=pl.ANY))
        aliases = {len(operands): 0}
        operands.append(vis)
    return pl.pallas_call(
        functools.partial(receive_kernel, z, parities, step_pairs, runs, len(arrays)),
        grid=(steps,),
        in_specs=in_specs,
        out_specs=pl.BlockSpec(
            (step_pairs, parities, 2, FSUB, FSUB),
            lambda g: (chunk * steps + g, at, 0, 0, 0),
        ),
        out_shape=out_shape,
        input_output_aliases=aliases,
        scratch_shapes=[
            pltpu.VMEM((z.devices, units, BAND_CH, LANES), jnp.bfloat16),
            pltpu.VMEM((FSUB // LANES, z.lane_frames * units * BAND_CH, LANES), jnp.float32),
            pltpu.SemaphoreType.DMA((len(runs),)),
        ],
        compiler_params=pltpu.CompilerParams(vmem_limit_bytes=VMEM // 2),
        cost_estimate=pl.CostEstimate(
            flops=2_000_000_000 * parities, bytes_accessed=5_000_000 * parities,
            transcendentals=0,
        ),
        name="correlate",
    )(*operands)


def beam_kernel(z, me_ref, *refs):
    spec_refs = refs[: z.chunks]
    cos_base, sin_base, cos_step, sin_step, sum_ref, out_ref, prod_ref = refs[z.chunks :]
    count = z.chan_dev
    weights = []
    for g in range(BEAMS):
        c0, s0 = cos_base[0, g : g + 1, :], sin_base[0, g : g + 1, :]
        c1, s1 = cos_step[g], sin_step[g]
        weights.append(
            ((c0 * c1 - s0 * s1).astype(jnp.bfloat16), (s0 * c1 + c0 * s1).astype(jnp.bfloat16))
        )
    for q in range(z.quads):
        lanes = slice(q * z.width, (q + 1) * z.width)
        x = [ref[:, lanes] for ref in spec_refs]
        real = jnp.concatenate([v[:BAND_CH] for v in x], axis=0)
        imag = jnp.concatenate([v[BAND_CH:] for v in x], axis=0)
        for g in range(BEAMS):
            c, s = weights[g]
            pair = (c * real + s * imag, c * imag - s * real)
            for part in range(2):
                row = (part * BEAMS + g) * count
                both = pair[part][:, :LANES] + pair[part][:, LANES:]
                prod_ref[row : row + count, q * LANES : (q + 1) * LANES] = both
    sums = jnp.dot(prod_ref[...], sum_ref[...], preferred_element_type=jnp.float32)
    sums = sums * (1.0 / np.sqrt(F))
    for j in range(2 * BEAMS):
        out_ref[0, :, j * FR : (j + 1) * FR] = sums[j * count : (j + 1) * count, :FR]


def beam_call(z, me, spectra, delays):
    bits = z.devices.bit_length() - 1
    lanes = FR * z.feed_dev
    halves = delays.reshape(BEAMS, 2, 1, z.cap)
    spread = jnp.broadcast_to(halves, (BEAMS, 2, z.lane_frames, z.cap)).reshape(BEAMS, z.width)
    unit = 2.0 * jnp.pi / NFFT
    owners = jnp.arange(z.devices, dtype=jnp.int32).astype(jnp.float32) * z.chan_dev
    inner = np.arange(z.chunks)[:, None] * BAND_CH + ORDER[None, :]
    inner = jnp.asarray(inner.reshape(-1).astype(np.float32))
    base = unit * (spread[None, :, :] * owners[:, None, None])
    step = unit * (spread[:, None, :] * inner[None, :, None])
    frame = (np.arange(FR * z.cap) // LANES) * z.lane_frames
    frame = frame + (np.arange(FR * z.cap) % LANES) // z.cap
    sums = (frame[:, None] == np.arange(LANES)[None, :]).astype(ml_dtypes.bfloat16)

    def owner(j, me_ref):
        k = 0
        for b in range(bits):
            k = k | (((j >> b) & 1) << (bits - 1 - b))
        return me_ref[0] ^ k

    base_spec = pl.BlockSpec(
        (1, BEAMS, z.width), lambda j, me_ref: (owner(j, me_ref), 0, 0)
    )
    grid_spec = pltpu.PrefetchScalarGridSpec(
        num_scalar_prefetch=1,
        grid=(z.devices,),
        in_specs=[
            pl.BlockSpec((z.rows_dev, lanes), lambda j, me_ref: (owner(j, me_ref), 0))
            for _ in range(z.chunks)
        ]
        + [base_spec, base_spec, whole_spec(step.shape), whole_spec(step.shape)]
        + [whole_spec(sums.shape)],
        out_specs=pl.BlockSpec(
            (1, z.chan_dev, 2 * BEAMS * FR), lambda j, me_ref: (j, 0, 0)
        ),
        scratch_shapes=[pltpu.VMEM((2 * BEAMS * z.chan_dev, FR * z.cap), jnp.bfloat16)],
    )
    return pl.pallas_call(
        functools.partial(beam_kernel, z),
        grid_spec=grid_spec,
        out_shape=jax.ShapeDtypeStruct((z.devices, z.chan_dev, 2 * BEAMS * FR), jnp.float32),
        compiler_params=pltpu.CompilerParams(vmem_limit_bytes=VMEM),
        cost_estimate=pl.CostEstimate(
            flops=20_000_000_000, bytes_accessed=20_000_000, transcendentals=0
        ),
        name="beam_sums",
    )(
        me, *spectra, jnp.cos(base), jnp.sin(base), jnp.cos(step), jnp.sin(step),
        jnp.asarray(sums),
    )


def swap(z, x, offset):
    return lax.ppermute(x, "chan", [(i, i ^ offset) for i in range(z.devices)])


def exchange(x):
    return lax.all_to_all(x, "chan", split_axis=0, concat_axis=0, tiled=True)


def on_device(voltages, delays, band_feeds):
    z = Sizes(lax.axis_size("chan"), voltages.shape[0])
    me = lax.axis_index("chan")
    me_array = me.astype(jnp.int32).reshape(1)

    own = lax.dynamic_slice_in_dim(band_feeds, me * z.bands_here, z.bands_here, 0)
    source = own // z.feed_dev
    before = jnp.sum(
        (own[:, None, :] < (source * z.feed_dev)[:, :, None]).astype(jnp.int32), axis=2
    )
    place = jnp.arange(FSUB, dtype=jnp.int32)[None, :] - before
    tau = jnp.arange(z.lane_frames, dtype=jnp.int32)
    big = (source // z.lane_frames) * LANES + place
    group = (source % z.lane_frames)[:, None, :] ^ tau[None, :, None]
    take_key = big[:, None, :] + z.cap * group

    calls = Spectra(z, me_array, voltages, band_feeds)
    early = list(range(z.early))
    basis = calls.basis(early)
    share = 2 * z.step_quads
    step = z.early * share
    arrived = [[] for _ in range(z.chunks)]
    steps = z.parts[0]
    filt, *spectra, send = calls.first(0, steps, early, basis, steps * step, [])
    got = exchange(send)
    for c in early:
        arrived[c] += [(got, g * step + c * share, share) for g in range(steps)]
    if len(z.parts) > 1:
        begin, steps = steps, z.parts[1]
        base = steps * step
        begun = 3 * z.step_quads
        filt, *spectra, send = calls.first(
            begin, steps, early, basis, base + z.steps * begun, [filt, *spectra]
        )
        *more, send, last = calls.next([z.chunks - 2, z.chunks - 1], filt, send)
        spectra = spectra + more
        got = exchange(send)
        for c in early:
            arrived[c] += [(got, g * step + c * share, share) for g in range(steps)]
        arrived[-2] += [(got, base + g * begun, share) for g in range(z.steps)]
        arrived[-1] += [(got, base + g * begun + share, z.step_quads) for g in range(z.steps)]

    beams, bit = beam_call(z, me_array, spectra, delays), 1
    while beams.shape[0] > 1:
        half = beams.shape[0] // 2
        beams, bit = beams[:half] + swap(z, beams[half:], bit), 2 * bit
    beams = beams.reshape(z.chunks, 2, BAND_CH // 2, 2 * BEAMS * FR)
    beams = jnp.swapaxes(beams, 1, 2).reshape(z.chan_dev, 2 * BEAMS * FR)
    wanted = [(k, None, arrived[k]) for k in range(z.chunks)]
    if len(z.parts) > 1:
        last, beams = lax.optimization_barrier((last, beams))
        got = exchange(last)
        k = z.chunks - 1
        wanted = wanted[:-1] + [(k, 0, arrived[k]), (k, 1, [(got, 0, z.quads)])]

    vis = None
    for k, parity, runs in wanted:
        vis = receive_call(z, k, parity, runs, take_key[k], vis)
    return (vis.reshape(z.chan_dev, 2, FSUB, FSUB), beams)


def solution(mesh):
    in_specs = (P(("grp", "chan"), None), P(None, ("grp", "chan")), P())
    out_specs = (P(("grp", "chan"), None, None, None), P(("grp", "chan"), None))
    return jax.shard_map(
        on_device, mesh=mesh, in_specs=in_specs, out_specs=out_specs, check_vma=False
    )
```

```python
import functools

import jax
import jax.numpy as jnp
import ml_dtypes
import numpy as np
from jax import lax
from jax.experimental import pallas as pl
from jax.experimental.pallas import tpu as pltpu
from jax.sharding import PartitionSpec as P

F = 1024
CHANNELS = 1024
TAPS = 4
BAND_CH = 16
BEAMS = 4
FR = 48
NFFT = 2048
BANDS = 64
FSUB = 256
LANES = 128
VMEM = 56 * 1024 * 1024

NT = (((1,), (1,)), ((), ()))


def fir_window():
    ids = np.arange(TAPS * NFFT, dtype=np.float64)
    centered = (ids - 0.5 * TAPS * NFFT + 0.5) / NFFT
    hann_part = 0.5 - 0.5 * np.cos(2.0 * np.pi * (ids + 0.5) / (TAPS * NFFT))
    return (np.sinc(centered) * hann_part).reshape(TAPS, NFFT)


ORDER = np.concatenate([np.arange(0, BAND_CH, 2), np.arange(1, BAND_CH, 2)])


def dft_rows(chan_ids):
    m = np.arange(NFFT // 2, dtype=np.int64)
    turns = (chan_ids[..., None].astype(np.int64) * m) % NFFT
    table = 2.0 * np.pi * np.arange(NFFT) / NFFT
    cosine = np.cos(table).astype(np.float32).astype(ml_dtypes.bfloat16)
    sine = (-np.sin(table)).astype(np.float32).astype(ml_dtypes.bfloat16)
    return np.stack([cosine[turns], sine[turns]], axis=1)


class Sizes:
    def __init__(self, devices, feed_dev):
        self.devices = devices
        self.feed_dev = feed_dev
        self.cap = feed_dev // 2
        self.lane_frames = LANES // self.cap
        self.quads = FR // self.lane_frames
        self.width = self.lane_frames * feed_dev
        self.steps = 6 if self.quads % 6 == 0 else self.quads
        self.step_frames = FR // self.steps
        self.step_quads = self.quads // self.steps
        self.step_lanes = self.step_frames * feed_dev
        self.chan_dev = CHANNELS // devices
        self.bands_here = BANDS // devices
        self.chunks = self.chan_dev // BAND_CH
        self.rows_dev = 2 * BAND_CH
        self.rows = devices * self.rows_dev
        self.groups = devices // self.lane_frames
        self.early = min(2, self.chunks)
        if self.chunks == 4:
            self.parts = (self.steps // 2, self.steps - self.steps // 2)
        else:
            self.early, self.parts = self.chunks, (self.steps,)


def find_places(z, me, lists):
    base = me * z.feed_dev
    first = jnp.sum((lists < base).astype(jnp.int32), axis=1, keepdims=True)
    lane = lax.broadcasted_iota(jnp.int32, (lists.shape[0], LANES), 1)
    at = first + lane % z.cap
    parts = []
    for side in range(FSUB // LANES):
        index = jnp.clip(at - side * LANES, 0, LANES - 1)
        half = lists[:, side * LANES : (side + 1) * LANES]
        parts.append(jnp.take_along_axis(half, index, axis=1, mode="promise_in_bounds"))
    loc = jnp.where(at < LANES, parts[0], parts[1]) - base
    return jnp.clip(loc, 0, z.feed_dev - 1)


def emit_spectra(z, scale, chunks, me_ref, spectra, lists_ref, loc_ref, spec_refs, send_refs):
    loc_ref[...] = find_places(z, me_ref[0], lists_ref[...])
    lane = lax.broadcasted_iota(jnp.int32, (z.rows_dev, LANES), 1)
    frame = (lane // z.cap) ^ (me_ref[0] % z.lane_frames)
    start = frame * z.cap
    few = BAND_CH // 2
    for c, chunk in enumerate(chunks):
        for owner in range(z.devices):
            top = (c * z.devices + owner) * BAND_CH
            rows = [x[top + p : top + p + few] for p in (0, few) for x in spectra]
            rows = jnp.concatenate(rows, axis=0) * scale
            spec_refs[c][owner * z.rows_dev : (owner + 1) * z.rows_dev, :] = rows.astype(
                jnp.bfloat16
            )
            band = owner * z.bands_here + chunk
            loc = loc_ref[band : band + 1, :]
            index = start + loc % z.cap
            lower = jnp.broadcast_to(loc, index.shape) < z.cap
            for q in range(z.step_quads):
                parts = []
                for side in range(2):
                    left = q * z.width + side * LANES
                    parts.append(
                        jnp.take_along_axis(
                            rows[:, left : left + LANES], index, axis=1,
                            mode="promise_in_bounds",
                        )
                    )
                picked = jnp.where(lower, parts[0], parts[1])
                for parity, (send_ref, unit, stride) in enumerate(send_refs[c]):
                    half = [
                        picked[p * BAND_CH + parity * few : p * BAND_CH + parity * few + few]
                        for p in range(2)
                    ]
                    half = jnp.concatenate(half, axis=0).astype(jnp.bfloat16)
                    send_ref[owner, unit + q * stride] = half


def filter_tile(z, main_ref, halo, win_ref, off, f0):
    lanes = slice(off, off + LANES)
    taps = [win_ref[k : k + 1, lanes] for k in range(TAPS)]
    frames = []
    for t in range(z.step_frames + TAPS - 1):
        if t < z.step_frames:
            x = main_ref[f0 : f0 + 16, t * NFFT + off : t * NFFT + off + LANES]
        else:
            x = halo[t - z.step_frames][f0 : f0 + 16, lanes]
        frames.append(x.astype(jnp.float32))
    totals = []
    for t in range(z.step_frames):
        total = taps[0] * frames[t]
        for k in range(1, TAPS):
            total = total + taps[k] * frames[t + k]
        totals.append(total)
    if z.cap < 16:
        totals = [
            jnp.concatenate([totals[t][h : h + 8], totals[t + 1][h : h + 8]], axis=0)
            for t in range(0, z.step_frames, 2)
            for h in (0, 8)
        ]
    out = []
    for i, total in enumerate(totals):
        if z.cap < 16:
            t, half, feed = 2 * (i // 2), i % 2, 0
        else:
            t, half, feed = i, f0 // z.cap, f0 % z.cap
        row = (t // z.lane_frames) * z.width + half * LANES
        row += (t % z.lane_frames) * z.cap + feed
        out.append((row, total.astype(jnp.bfloat16)))
    return out


def filter_fold(z, main_ref, halo, win_ref, filt_ref, off):
    far = off + NFFT // 2
    for f0 in range(0, z.feed_dev, 16):
        low = filter_tile(z, main_ref, halo, win_ref, off, f0)
        high = filter_tile(z, main_ref, halo, win_ref, far, f0)
        for (row, a), (_, b) in zip(low, high):
            filt_ref[row : row + 16, off : off + LANES] = a + b
            filt_ref[row : row + 16, far : far + LANES] = a - b


def transform(basis_ref, filt_ref, begin, end):
    return [
        lax.dot_general(
            basis_ref[parity, :, begin:end],
            filt_ref[:, parity * (NFFT // 2) + begin : parity * (NFFT // 2) + end],
            NT,
            preferred_element_type=jnp.float32,
        )
        for parity in range(2)
    ]


def first_kernel(
    z, scale, chunks, held, me_ref, main_ref, h0_ref, h1_ref, h2_ref, win_ref, basis_ref,
    lists_ref, *refs,
):
    filt_ref, spec_refs, send_ref, loc_ref = refs[held], refs[held + 1 : -2], refs[-2], refs[-1]
    halo = (h0_ref, h1_ref, h2_ref)
    piece = 512
    spectra = None
    for off in range(0, NFFT // 2, piece):
        for tile in range(off, off + piece, LANES):
            filter_fold(z, main_ref, halo, win_ref, filt_ref, tile)
        part = transform(basis_ref, filt_ref, off, off + piece)
        spectra = part if spectra is None else [x + y for x, y in zip(spectra, part)]
    sends = []
    for c in range(len(chunks)):
        unit = c * 2 * z.step_quads
        sends.append([(send_ref, unit, 2), (send_ref, unit + 1, 2)])
    emit_spectra(z, scale, chunks, me_ref, spectra, lists_ref, loc_ref, spec_refs, sends)


def next_kernel(z, scale, chunks, me_ref, filt_ref, basis_ref, lists_ref, held_ref, *refs):
    spectra = transform(basis_ref, filt_ref, 0, NFFT // 2)
    begun_ref, last_ref = refs[2], refs[3]
    sends = [
        [(begun_ref, 0, 2), (begun_ref, 1, 2)],
        [(begun_ref, 2 * z.step_quads, 1), (last_ref, 0, 1)],
    ]
    emit_spectra(z, scale, chunks, me_ref, spectra, lists_ref, refs[-1], refs[:2], sends)


def whole_spec(shape):
    return pl.BlockSpec(shape, lambda *g: (0,) * len(shape))


class Spectra:

    def __init__(self, z, me, voltages, band_feeds):
        window = fir_window()
        self.z = z
        self.me = me
        self.scale = float(np.sqrt(2.0 / np.sum(window * window)))
        self.window = jnp.asarray(window.astype(np.float32))
        self.voltages = voltages
        self.lists = band_feeds
        self.ids = np.arange(CHANNELS).reshape(z.devices, z.chunks, BAND_CH)
        self.me_spec = pl.BlockSpec(memory_space=pltpu.SMEM)
        self.spec_shape = jax.ShapeDtypeStruct((z.rows, FR * z.feed_dev), jnp.bfloat16)
        self.filt_shape = jax.ShapeDtypeStruct((FR * z.feed_dev, NFFT), jnp.bfloat16)

    def basis(self, chunks):
        sides = []
        for parity in range(2):
            rows = [dft_rows(self.ids[:, k, parity::2].reshape(-1)) for k in chunks]
            rows = np.stack(rows).reshape(len(chunks), self.z.devices, BAND_CH // 2, 2, -1)
            rows = np.transpose(rows, (0, 1, 3, 2, 4))
            sides.append(rows.reshape(len(chunks) * self.z.rows // 2, NFFT // 2))
        return jnp.asarray(np.stack(sides))

    def message(self, units):
        return jax.ShapeDtypeStruct((self.z.devices, units, BAND_CH, LANES), jnp.bfloat16)

    def common(self, steps, chunks):
        z = self.z
        flops = len(chunks) * z.rows * NFFT * z.step_lanes * steps
        return dict(
            grid=(steps,),
            scratch_shapes=[pltpu.VMEM((BANDS, LANES), jnp.int32)],
            compiler_params=pltpu.CompilerParams(vmem_limit_bytes=VMEM),
            cost_estimate=pl.CostEstimate(
                flops=flops, bytes_accessed=3_000_000 * steps, transcendentals=0
            ),
        )

    def first(self, begin, steps, chunks, basis, units, held):
        z = self.z
        count = len(chunks)

        def halo_spec(h):
            return pl.BlockSpec(
                (z.feed_dev, NFFT), lambda g: (0, z.step_frames * (begin + g + 1) + h)
            )

        send_block = (z.devices, count * 2 * z.step_quads, BAND_CH, LANES)
        operands = [self.me] + [self.voltages] * 4 + [self.window, basis, self.lists]
        aliases = {len(operands) + i: i for i in range(len(held))}
        return pl.pallas_call(
            functools.partial(first_kernel, z, self.scale, chunks, len(held)),
            in_specs=[
                self.me_spec,
                pl.BlockSpec((z.feed_dev, z.step_frames * NFFT), lambda g: (0, begin + g)),
                halo_spec(0),
                halo_spec(1),
                halo_spec(2),
                whole_spec((TAPS, NFFT)),
                whole_spec(basis.shape),
                whole_spec(self.lists.shape),
            ]
            + [pl.BlockSpec(memory_space=pl.ANY)] * len(held),
            out_specs=[
                pl.BlockSpec((z.step_lanes, NFFT), lambda g: (begin + g, 0)),
            ]
            + [pl.BlockSpec((z.rows, z.step_lanes), lambda g: (0, begin + g))] * count
            + [pl.BlockSpec(send_block, lambda g: (0, g, 0, 0))],
            out_shape=[self.filt_shape] + [self.spec_shape] * count + [self.message(units)],
            input_output_aliases=aliases,
            name="filter_spectra",
            **self.common(steps, chunks),
        )(*operands, *held)

    def next(self, chunks, filt, held):
        z = self.z
        basis = self.basis(chunks)
        begun = 3 * z.step_quads
        base = held.shape[1] // begun - z.steps
        operands = [self.me, filt, basis, self.lists, held]
        return pl.pallas_call(
            functools.partial(next_kernel, z, self.scale, chunks),
            in_specs=[
                self.me_spec,
                pl.BlockSpec((z.step_lanes, NFFT), lambda g: (g, 0)),
                whole_spec(basis.shape),
                whole_spec(self.lists.shape),
                pl.BlockSpec(memory_space=pl.ANY),
            ],
            out_specs=[pl.BlockSpec((z.rows, z.step_lanes), lambda g: (0, g))] * 2
            + [
                pl.BlockSpec((z.devices, begun, BAND_CH, LANES), lambda g: (0, base + g, 0, 0)),
                pl.BlockSpec((z.devices, z.step_quads, BAND_CH, LANES), lambda g: (0, g, 0, 0)),
            ],
            out_shape=[self.spec_shape] * 2
            + [self.message(held.shape[1]), self.message(z.quads)],
            input_output_aliases={4: 2},
            name="spectra_next",
            **self.common(z.steps, chunks),
        )(*operands)


def receive_kernel(z, parities, step_pairs, runs, arrays, *refs):
    arr_refs, key_ref = refs[:arrays], refs[arrays]
    vis_ref, buf_ref, rows_ref, sems = refs[-4:]
    g = pl.program_id(0)
    lf = z.lane_frames
    few = BAND_CH // 2
    steps = few // step_pairs
    depth = buf_ref.shape[2] * BAND_CH
    slots = buf_ref.shape[0]
    at = g % steps

    def copies(c):
        place = 0
        out = []
        for i, (array, first, count) in enumerate(runs[c]):
            out.append(
                pltpu.make_async_copy(
                    arr_refs[array].at[:, first : first + count],
                    buf_ref.at[c % slots, :, place : place + count],
                    sems.at[c % slots, i],
                )
            )
            place += count
        return out

    for c in range(len(runs)):

        @pl.when(g == c * steps)
        def _():
            if c == 0:
                for copy in copies(c):
                    copy.start()
            for copy in copies(c):
                copy.wait()
            if c + 1 < len(runs):
                for copy in copies(c + 1):
                    copy.start()

    @pl.when(at == 0)
    def _():
        c = g // steps
        slot = lax.broadcasted_iota(jnp.int32, (z.groups * LANES, FSUB), 0)
        lane_group = lax.broadcasted_iota(jnp.int32, (depth, LANES), 1) // z.cap
        for tau in range(lf):
            tiles = []
            for big in range(z.groups):
                tile = buf_ref[c % slots, big * lf + tau].reshape(depth, LANES)
                for lane in range(1, lf):
                    block = buf_ref[c % slots, big * lf + (lane ^ tau)].reshape(depth, LANES)
                    tile = jnp.where(lane_group == lane, block, tile)
                tiles.append(tile)
            key = key_ref[c, tau : tau + 1, :]
            pick = jnp.where(slot == key, 1.0, 0.0).astype(jnp.bfloat16)
            rows = jnp.dot(
                jnp.concatenate(tiles, axis=1), pick, preferred_element_type=jnp.float32
            )
            for side in range(FSUB // LANES):
                rows_ref[side, tau * depth : (tau + 1) * depth, :] = rows[
                    :, side * LANES : (side + 1) * LANES
                ]

    todo = [(i, p) for i in range(step_pairs) for p in range(parities)]
    operands = []
    for i, p in todo:
        halves = []
        for part in range(2):
            first = p * BAND_CH + part * few + at * step_pairs + i
            halves.append(
                jnp.concatenate(
                    [
                        rows_ref[side, pl.ds(first, FR, stride=parities * BAND_CH), :]
                        for side in range(FSUB // LANES)
                    ],
                    axis=1,
                )
            )
        real, imag = halves
        both = jnp.concatenate([real, imag], axis=0)
        turned = jnp.concatenate([-imag, real], axis=0)
        right = jnp.concatenate([both, turned], axis=1).astype(jnp.bfloat16)
        operands.append((both.astype(jnp.bfloat16).T, right))
    outs = [
        jnp.dot(left, right, preferred_element_type=jnp.float32) for left, right in operands
    ]
    for (i, p), out in zip(todo, outs):
        out = out * (1.0 / FR)
        vis_ref[i, p, 0] = out[:, :FSUB]
        vis_ref[i, p, 1] = out[:, FSUB:]


def receive_call(z, chunk, parity, arrived, keys, vis):
    parities = 2 if parity is None else 1
    step_pairs = 4 // parities
    steps = BAND_CH // 2 // step_pairs
    at = 0 if parity is None else parity
    out_shape = jax.ShapeDtypeStruct((z.chan_dev // 2, 2, 2, FSUB, FSUB), jnp.float32)
    arrays = []
    runs = []
    for one in arrived:
        runs.append([])
        for got, first, count in one:
            if not any(got is x for x in arrays):
                arrays.append(got)
            runs[-1].append(([got is x for x in arrays].index(True), first, count))
    units = sum(count for _, _, count in runs[0])
    slots = min(2, len(runs))
    operands = arrays + [keys]
    in_specs = [pl.BlockSpec(memory_space=pl.ANY)] * len(arrays) + [whole_spec(keys.shape)]
    aliases = {}
    if vis is not None:
        in_specs.append(pl.BlockSpec(memory_space=pl.ANY))
        aliases = {len(operands): 0}
        operands.append(vis)
    share = parities * len(runs)
    return pl.pallas_call(
        functools.partial(receive_kernel, z, parities, step_pairs, runs, len(arrays)),
        grid=(len(runs) * steps,),
        in_specs=in_specs,
        out_specs=pl.BlockSpec(
            (step_pairs, parities, 2, FSUB, FSUB),
            lambda g: (chunk * steps + g, at, 0, 0, 0),
        ),
        out_shape=out_shape,
        input_output_aliases=aliases,
        scratch_shapes=[
            pltpu.VMEM((slots, z.devices, units, BAND_CH, LANES), jnp.bfloat16),
            pltpu.VMEM((FSUB // LANES, z.lane_frames * units * BAND_CH, LANES), jnp.float32),
            pltpu.SemaphoreType.DMA((slots, max(len(x) for x in runs))),
        ],
        compiler_params=pltpu.CompilerParams(vmem_limit_bytes=VMEM // 2),
        cost_estimate=pl.CostEstimate(
            flops=2_000_000_000 * share, bytes_accessed=5_000_000 * share, transcendentals=0
        ),
        name="correlate",
    )(*operands)


def beam_kernel(z, me_ref, *refs):
    spec_refs = refs[: z.chunks]
    cos_base, sin_base, cos_step, sin_step, sum_ref, out_ref, prod_ref = refs[z.chunks :]
    count = z.chan_dev
    weights = []
    for g in range(BEAMS):
        c0, s0 = cos_base[0, g : g + 1, :], sin_base[0, g : g + 1, :]
        c1, s1 = cos_step[g], sin_step[g]
        weights.append(
            ((c0 * c1 - s0 * s1).astype(jnp.bfloat16), (s0 * c1 + c0 * s1).astype(jnp.bfloat16))
        )
    for q in range(z.quads):
        lanes = slice(q * z.width, (q + 1) * z.width)
        x = [ref[:, lanes] for ref in spec_refs]
        real = jnp.concatenate([v[:BAND_CH] for v in x], axis=0)
        imag = jnp.concatenate([v[BAND_CH:] for v in x], axis=0)
        for g in range(BEAMS):
            c, s = weights[g]
            pair = (c * real + s * imag, c * imag - s * real)
            for part in range(2):
                row = (part * BEAMS + g) * count
                both = pair[part][:, :LANES] + pair[part][:, LANES:]
                prod_ref[row : row + count, q * LANES : (q + 1) * LANES] = both
    sums = jnp.dot(prod_ref[...], sum_ref[...], preferred_element_type=jnp.float32)
    sums = sums * (1.0 / np.sqrt(F))
    for j in range(2 * BEAMS):
        out_ref[0, :, j * FR : (j + 1) * FR] = sums[j * count : (j + 1) * count, :FR]


def beam_call(z, me, spectra, delays):
    bits = z.devices.bit_length() - 1
    lanes = FR * z.feed_dev
    halves = delays.reshape(BEAMS, 2, 1, z.cap)
    spread = jnp.broadcast_to(halves, (BEAMS, 2, z.lane_frames, z.cap)).reshape(BEAMS, z.width)
    unit = 2.0 * jnp.pi / NFFT
    owners = jnp.arange(z.devices, dtype=jnp.int32).astype(jnp.float32) * z.chan_dev
    inner = np.arange(z.chunks)[:, None] * BAND_CH + ORDER[None, :]
    inner = jnp.asarray(inner.reshape(-1).astype(np.float32))
    base = unit * (spread[None, :, :] * owners[:, None, None])
    step = unit * (spread[:, None, :] * inner[None, :, None])
    frame = (np.arange(FR * z.cap) // LANES) * z.lane_frames
    frame = frame + (np.arange(FR * z.cap) % LANES) // z.cap
    sums = (frame[:, None] == np.arange(LANES)[None, :]).astype(ml_dtypes.bfloat16)

    def owner(j, me_ref):
        k = 0
        for b in range(bits):
            k = k | (((j >> b) & 1) << (bits - 1 - b))
        return me_ref[0] ^ k

    base_spec = pl.BlockSpec(
        (1, BEAMS, z.width), lambda j, me_ref: (owner(j, me_ref), 0, 0)
    )
    grid_spec = pltpu.PrefetchScalarGridSpec(
        num_scalar_prefetch=1,
        grid=(z.devices,),
        in_specs=[
            pl.BlockSpec((z.rows_dev, lanes), lambda j, me_ref: (owner(j, me_ref), 0))
            for _ in range(z.chunks)
        ]
        + [base_spec, base_spec, whole_spec(step.shape), whole_spec(step.shape)]
        + [whole_spec(sums.shape)],
        out_specs=pl.BlockSpec(
            (1, z.chan_dev, 2 * BEAMS * FR), lambda j, me_ref: (j, 0, 0)
        ),
        scratch_shapes=[pltpu.VMEM((2 * BEAMS * z.chan_dev, FR * z.cap), jnp.bfloat16)],
    )
    return pl.pallas_call(
        functools.partial(beam_kernel, z),
        grid_spec=grid_spec,
        out_shape=jax.ShapeDtypeStruct((z.devices, z.chan_dev, 2 * BEAMS * FR), jnp.float32),
        compiler_params=pltpu.CompilerParams(vmem_limit_bytes=VMEM),
        cost_estimate=pl.CostEstimate(
            flops=20_000_000_000, bytes_accessed=20_000_000, transcendentals=0
        ),
        name="beam_sums",
    )(
        me, *spectra, jnp.cos(base), jnp.sin(base), jnp.cos(step), jnp.sin(step),
        jnp.asarray(sums),
    )


def swap(z, x, offset):
    return lax.ppermute(x, "chan", [(i, i ^ offset) for i in range(z.devices)])


def exchange(x):
    return lax.all_to_all(x, "chan", split_axis=0, concat_axis=0, tiled=True)


def on_device(voltages, delays, band_feeds):
    z = Sizes(lax.axis_size("chan"), voltages.shape[0])
    me = lax.axis_index("chan")
    me_array = me.astype(jnp.int32).reshape(1)

    own = lax.dynamic_slice_in_dim(band_feeds, me * z.bands_here, z.bands_here, 0)
    source = own // z.feed_dev
    before = jnp.sum(
        (own[:, None, :] < (source * z.feed_dev)[:, :, None]).astype(jnp.int32), axis=2
    )
    place = jnp.arange(FSUB, dtype=jnp.int32)[None, :] - before
    tau = jnp.arange(z.lane_frames, dtype=jnp.int32)
    big = (source // z.lane_frames) * LANES + place
    group = (source % z.lane_frames)[:, None, :] ^ tau[None, :, None]
    take_key = big[:, None, :] + z.cap * group

    calls = Spectra(z, me_array, voltages, band_feeds)
    early = list(range(z.early))
    basis = calls.basis(early)
    share = 2 * z.step_quads
    step = z.early * share
    arrived = [[] for _ in range(z.chunks)]
    steps = z.parts[0]
    filt, *spectra, send = calls.first(0, steps, early, basis, steps * step, [])
    got = exchange(send)
    for c in early:
        arrived[c] += [(got, g * step + c * share, share) for g in range(steps)]
    if len(z.parts) > 1:
        begin, steps = steps, z.parts[1]
        base = steps * step
        begun = 3 * z.step_quads
        filt, *spectra, send = calls.first(
            begin, steps, early, basis, base + z.steps * begun, [filt, *spectra]
        )
        *more, send, last = calls.next([z.chunks - 2, z.chunks - 1], filt, send)
        spectra = spectra + more
        got = exchange(send)
        for c in early:
            arrived[c] += [(got, g * step + c * share, share) for g in range(steps)]
        arrived[-2] += [(got, base + g * begun, share) for g in range(z.steps)]
        arrived[-1] += [(got, base + g * begun + share, z.step_quads) for g in range(z.steps)]

    beams, bit = beam_call(z, me_array, spectra, delays), 1
    while beams.shape[0] > 1:
        half = beams.shape[0] // 2
        beams, bit = beams[:half] + swap(z, beams[half:], bit), 2 * bit
    beams = beams.reshape(z.chunks, 2, BAND_CH // 2, 2 * BEAMS * FR)
    beams = jnp.swapaxes(beams, 1, 2).reshape(z.chan_dev, 2 * BEAMS * FR)
    if len(z.parts) > 1:
        last, beams = lax.optimization_barrier((last, beams))
        got = exchange(last)
        k = z.chunks - 1
        vis = receive_call(z, 0, None, arrived[:k], take_key[:k], None)
        vis = receive_call(z, k, 0, arrived[k:], take_key[k:], vis)
        vis = receive_call(z, k, 1, [[(got, 0, z.quads)]], take_key[k:], vis)
    else:
        vis = receive_call(z, 0, None, arrived, take_key, None)
    return (vis.reshape(z.chan_dev, 2, FSUB, FSUB), beams)


def solution(mesh):
    in_specs = (P(("grp", "chan"), None), P(None, ("grp", "chan")), P())
    out_specs = (P(("grp", "chan"), None, None, None), P(("grp", "chan"), None))
    return jax.shard_map(
        on_device, mesh=mesh, in_specs=in_specs, out_specs=out_specs, check_vma=False
    )
```

```python
import functools

import jax
import jax.numpy as jnp
import ml_dtypes
import numpy as np
from jax import lax
from jax.experimental import pallas as pl
from jax.experimental.pallas import tpu as pltpu
from jax.sharding import PartitionSpec as P

F = 1024
CHANNELS = 1024
TAPS = 4
BAND_CH = 16
BEAMS = 4
FR = 48
NFFT = 2048
BANDS = 64
FSUB = 256
LANES = 128
VMEM = 56 * 1024 * 1024

NT = (((1,), (1,)), ((), ()))


def fir_window():
    ids = np.arange(TAPS * NFFT, dtype=np.float64)
    centered = (ids - 0.5 * TAPS * NFFT + 0.5) / NFFT
    hann_part = 0.5 - 0.5 * np.cos(2.0 * np.pi * (ids + 0.5) / (TAPS * NFFT))
    return (np.sinc(centered) * hann_part).reshape(TAPS, NFFT)


ORDER = np.concatenate([np.arange(0, BAND_CH, 2), np.arange(1, BAND_CH, 2)])


def dft_rows(chan_ids):
    m = np.arange(NFFT // 2, dtype=np.int64)
    turns = (chan_ids[..., None].astype(np.int64) * m) % NFFT
    table = 2.0 * np.pi * np.arange(NFFT) / NFFT
    cosine = np.cos(table).astype(np.float32).astype(ml_dtypes.bfloat16)
    sine = (-np.sin(table)).astype(np.float32).astype(ml_dtypes.bfloat16)
    return np.stack([cosine[turns], sine[turns]], axis=1)


class Sizes:
    def __init__(self, devices, feed_dev):
        self.devices = devices
        self.feed_dev = feed_dev
        self.cap = feed_dev // 2
        self.lane_frames = LANES // self.cap
        self.quads = FR // self.lane_frames
        self.width = self.lane_frames * feed_dev
        self.steps = 6 if self.quads % 6 == 0 else self.quads
        self.step_frames = FR // self.steps
        self.step_quads = self.quads // self.steps
        self.step_lanes = self.step_frames * feed_dev
        self.chan_dev = CHANNELS // devices
        self.bands_here = BANDS // devices
        self.chunks = self.chan_dev // BAND_CH
        self.rows_dev = 2 * BAND_CH
        self.rows = devices * self.rows_dev
        self.groups = devices // self.lane_frames
        self.early = min(2, self.chunks)
        if self.chunks == 4:
            self.parts = (self.steps // 2, self.steps - self.steps // 2)
        else:
            self.early, self.parts = self.chunks, (self.steps,)


def find_places(z, me, lists):
    base = me * z.feed_dev
    first = jnp.sum((lists < base).astype(jnp.int32), axis=1, keepdims=True)
    lane = lax.broadcasted_iota(jnp.int32, (lists.shape[0], LANES), 1)
    at = first + lane % z.cap
    parts = []
    for side in range(FSUB // LANES):
        index = jnp.clip(at - side * LANES, 0, LANES - 1)
        half = lists[:, side * LANES : (side + 1) * LANES]
        parts.append(jnp.take_along_axis(half, index, axis=1, mode="promise_in_bounds"))
    loc = jnp.where(at < LANES, parts[0], parts[1]) - base
    return jnp.clip(loc, 0, z.feed_dev - 1)


def emit_spectra(z, scale, chunks, me_ref, spectra, lists_ref, loc_ref, spec_refs, send_refs):
    loc_ref[...] = find_places(z, me_ref[0], lists_ref[...])
    lane = lax.broadcasted_iota(jnp.int32, (z.rows_dev, LANES), 1)
    frame = (lane // z.cap) ^ (me_ref[0] % z.lane_frames)
    start = frame * z.cap
    few = BAND_CH // 2
    for c, chunk in enumerate(chunks):
        for owner in range(z.devices):
            top = (c * z.devices + owner) * BAND_CH
            rows = [x[top + p : top + p + few] for p in (0, few) for x in spectra]
            rows = jnp.concatenate(rows, axis=0) * scale
            spec_refs[c][owner * z.rows_dev : (owner + 1) * z.rows_dev, :] = rows.astype(
                jnp.bfloat16
            )
            band = owner * z.bands_here + chunk
            loc = loc_ref[band : band + 1, :]
            index = start + loc % z.cap
            lower = jnp.broadcast_to(loc, index.shape) < z.cap
            for q in range(z.step_quads):
                parts = []
                for side in range(2):
                    left = q * z.width + side * LANES
                    parts.append(
                        jnp.take_along_axis(
                            rows[:, left : left + LANES], index, axis=1,
                            mode="promise_in_bounds",
                        )
                    )
                picked = jnp.where(lower, parts[0], parts[1])
                for parity, (send_ref, unit, stride) in enumerate(send_refs[c]):
                    half = [
                        picked[p * BAND_CH + parity * few : p * BAND_CH + parity * few + few]
                        for p in range(2)
                    ]
                    half = jnp.concatenate(half, axis=0).astype(jnp.bfloat16)
                    send_ref[owner, unit + q * stride] = half


def filter_tile(z, main_ref, halo, win_ref, off, f0):
    lanes = slice(off, off + LANES)
    taps = [win_ref[k : k + 1, lanes] for k in range(TAPS)]
    frames = []
    for t in range(z.step_frames + TAPS - 1):
        if t < z.step_frames:
            x = main_ref[f0 : f0 + 16, t * NFFT + off : t * NFFT + off + LANES]
        else:
            x = halo[t - z.step_frames][f0 : f0 + 16, lanes]
        frames.append(x.astype(jnp.float32))
    totals = []
    for t in range(z.step_frames):
        total = taps[0] * frames[t]
        for k in range(1, TAPS):
            total = total + taps[k] * frames[t + k]
        totals.append(total)
    if z.cap < 16:
        totals = [
            jnp.concatenate([totals[t][h : h + 8], totals[t + 1][h : h + 8]], axis=0)
            for t in range(0, z.step_frames, 2)
            for h in (0, 8)
        ]
    out = []
    for i, total in enumerate(totals):
        if z.cap < 16:
            t, half, feed = 2 * (i // 2), i % 2, 0
        else:
            t, half, feed = i, f0 // z.cap, f0 % z.cap
        row = (t // z.lane_frames) * z.width + half * LANES
        row += (t % z.lane_frames) * z.cap + feed
        out.append((row, total.astype(jnp.bfloat16)))
    return out


def filter_fold(z, main_ref, halo, win_ref, filt_ref, off):
    far = off + NFFT // 2
    folded = {}
    for f0 in range(0, z.feed_dev, 16):
        low = filter_tile(z, main_ref, halo, win_ref, off, f0)
        high = filter_tile(z, main_ref, halo, win_ref, far, f0)
        for (row, a), (_, b) in zip(low, high):
            folded[row] = (a + b, a - b)
            filt_ref[row : row + 16, off : off + LANES] = folded[row][0]
            filt_ref[row : row + 16, far : far + LANES] = folded[row][1]
    return [
        jnp.concatenate([folded[row][parity] for row in sorted(folded)], axis=0)
        for parity in range(2)
    ]


def first_kernel(
    z, scale, chunks, held, me_ref, main_ref, h0_ref, h1_ref, h2_ref, win_ref, basis_ref,
    lists_ref, *refs,
):
    filt_ref, spec_refs, send_ref, loc_ref = refs[held], refs[held + 1 : -2], refs[-2], refs[-1]
    halo = (h0_ref, h1_ref, h2_ref)
    piece = 512
    spectra = None
    for off in range(0, NFFT // 2, piece):
        tiles = [
            filter_fold(z, main_ref, halo, win_ref, filt_ref, tile)
            for tile in range(off, off + piece, LANES)
        ]
        part = [
            lax.dot_general(
                basis_ref[parity, :, off : off + piece],
                jnp.concatenate([tile[parity] for tile in tiles], axis=1),
                NT,
                preferred_element_type=jnp.float32,
            )
            for parity in range(2)
        ]
        spectra = part if spectra is None else [x + y for x, y in zip(spectra, part)]
    sends = []
    for c in range(len(chunks)):
        unit = c * 2 * z.step_quads
        sends.append([(send_ref, unit, 2), (send_ref, unit + 1, 2)])
    emit_spectra(z, scale, chunks, me_ref, spectra, lists_ref, loc_ref, spec_refs, sends)


def next_kernel(z, scale, chunks, me_ref, filt_ref, basis_ref, lists_ref, held_ref, *refs):
    half = NFFT // 2
    spectra = [
        lax.dot_general(
            basis_ref[parity],
            filt_ref[:, parity * half : (parity + 1) * half],
            NT,
            preferred_element_type=jnp.float32,
        )
        for parity in range(2)
    ]
    begun_ref, last_ref = refs[2], refs[3]
    sends = [
        [(begun_ref, 0, 2), (begun_ref, 1, 2)],
        [(begun_ref, 2 * z.step_quads, 1), (last_ref, 0, 1)],
    ]
    emit_spectra(z, scale, chunks, me_ref, spectra, lists_ref, refs[-1], refs[:2], sends)


def whole_spec(shape):
    return pl.BlockSpec(shape, lambda *g: (0,) * len(shape))


class Spectra:

    def __init__(self, z, me, voltages, band_feeds):
        window = fir_window()
        self.z = z
        self.me = me
        self.scale = float(np.sqrt(2.0 / np.sum(window * window)))
        self.window = jnp.asarray(window.astype(np.float32))
        self.voltages = voltages
        self.lists = band_feeds
        self.ids = np.arange(CHANNELS).reshape(z.devices, z.chunks, BAND_CH)
        self.me_spec = pl.BlockSpec(memory_space=pltpu.SMEM)
        self.spec_shape = jax.ShapeDtypeStruct((z.rows, FR * z.feed_dev), jnp.bfloat16)
        self.filt_shape = jax.ShapeDtypeStruct((FR * z.feed_dev, NFFT), jnp.bfloat16)

    def basis(self, chunks):
        sides = []
        for parity in range(2):
            rows = [dft_rows(self.ids[:, k, parity::2].reshape(-1)) for k in chunks]
            rows = np.stack(rows).reshape(len(chunks), self.z.devices, BAND_CH // 2, 2, -1)
            rows = np.transpose(rows, (0, 1, 3, 2, 4))
            sides.append(rows.reshape(len(chunks) * self.z.rows // 2, NFFT // 2))
        return jnp.asarray(np.stack(sides))

    def message(self, units):
        return jax.ShapeDtypeStruct((self.z.devices, units, BAND_CH, LANES), jnp.bfloat16)

    def common(self, steps, chunks):
        z = self.z
        flops = len(chunks) * z.rows * NFFT * z.step_lanes * steps
        return dict(
            grid=(steps,),
            scratch_shapes=[pltpu.VMEM((BANDS, LANES), jnp.int32)],
            compiler_params=pltpu.CompilerParams(vmem_limit_bytes=VMEM),
            cost_estimate=pl.CostEstimate(
                flops=flops, bytes_accessed=3_000_000 * steps, transcendentals=0
            ),
        )

    def first(self, begin, steps, chunks, basis, units, held):
        z = self.z
        count = len(chunks)

        def halo_spec(h):
            return pl.BlockSpec(
                (z.feed_dev, NFFT), lambda g: (0, z.step_frames * (begin + g + 1) + h)
            )

        send_block = (z.devices, count * 2 * z.step_quads, BAND_CH, LANES)
        operands = [self.me] + [self.voltages] * 4 + [self.window, basis, self.lists]
        aliases = {len(operands) + i: i for i in range(len(held))}
        return pl.pallas_call(
            functools.partial(first_kernel, z, self.scale, chunks, len(held)),
            in_specs=[
                self.me_spec,
                pl.BlockSpec((z.feed_dev, z.step_frames * NFFT), lambda g: (0, begin + g)),
                halo_spec(0),
                halo_spec(1),
                halo_spec(2),
                whole_spec((TAPS, NFFT)),
                whole_spec(basis.shape),
                whole_spec(self.lists.shape),
            ]
            + [pl.BlockSpec(memory_space=pl.ANY)] * len(held),
            out_specs=[
                pl.BlockSpec((z.step_lanes, NFFT), lambda g: (begin + g, 0)),
            ]
            + [pl.BlockSpec((z.rows, z.step_lanes), lambda g: (0, begin + g))] * count
            + [pl.BlockSpec(send_block, lambda g: (0, g, 0, 0))],
            out_shape=[self.filt_shape] + [self.spec_shape] * count + [self.message(units)],
            input_output_aliases=aliases,
            name="filter_spectra",
            **self.common(steps, chunks),
        )(*operands, *held)

    def next(self, chunks, filt, held):
        z = self.z
        basis = self.basis(chunks)
        begun = 3 * z.step_quads
        base = held.shape[1] // begun - z.steps
        operands = [self.me, filt, basis, self.lists, held]
        return pl.pallas_call(
            functools.partial(next_kernel, z, self.scale, chunks),
            in_specs=[
                self.me_spec,
                pl.BlockSpec((z.step_lanes, NFFT), lambda g: (g, 0)),
                whole_spec(basis.shape),
                whole_spec(self.lists.shape),
                pl.BlockSpec(memory_space=pl.ANY),
            ],
            out_specs=[pl.BlockSpec((z.rows, z.step_lanes), lambda g: (0, g))] * 2
            + [
                pl.BlockSpec((z.devices, begun, BAND_CH, LANES), lambda g: (0, base + g, 0, 0)),
                pl.BlockSpec((z.devices, z.step_quads, BAND_CH, LANES), lambda g: (0, g, 0, 0)),
            ],
            out_shape=[self.spec_shape] * 2
            + [self.message(held.shape[1]), self.message(z.quads)],
            input_output_aliases={4: 2},
            name="spectra_next",
            **self.common(z.steps, chunks),
        )(*operands)


def receive_kernel(z, parities, step_pairs, runs, arrays, *refs):
    arr_refs, key_ref = refs[:arrays], refs[arrays]
    vis_ref, buf_ref, rows_ref, sems = refs[-4:]
    g = pl.program_id(0)
    lf = z.lane_frames
    few = BAND_CH // 2
    steps = few // step_pairs
    depth = buf_ref.shape[2] * BAND_CH
    slots = buf_ref.shape[0]
    at = g % steps

    def copies(c):
        place = 0
        out = []
        for i, (array, first, count) in enumerate(runs[c]):
            out.append(
                pltpu.make_async_copy(
                    arr_refs[array].at[:, first : first + count],
                    buf_ref.at[c % slots, :, place : place + count],
                    sems.at[c % slots, i],
                )
            )
            place += count
        return out

    for c in range(len(runs)):

        @pl.when(g == c * steps)
        def _():
            if c == 0:
                for copy in copies(c):
                    copy.start()
            for copy in copies(c):
                copy.wait()
            if c + 1 < len(runs):
                for copy in copies(c + 1):
                    copy.start()

    @pl.when(at == 0)
    def _():
        c = g // steps
        slot = lax.broadcasted_iota(jnp.int32, (z.groups * LANES, FSUB), 0)
        lane_group = lax.broadcasted_iota(jnp.int32, (depth, LANES), 1) // z.cap
        for tau in range(lf):
            tiles = []
            for big in range(z.groups):
                tile = buf_ref[c % slots, big * lf + tau].reshape(depth, LANES)
                for lane in range(1, lf):
                    block = buf_ref[c % slots, big * lf + (lane ^ tau)].reshape(depth, LANES)
                    tile = jnp.where(lane_group == lane, block, tile)
                tiles.append(tile)
            key = key_ref[c, tau : tau + 1, :]
            pick = jnp.where(slot == key, 1.0, 0.0).astype(jnp.bfloat16)
            rows = jnp.dot(
                jnp.concatenate(tiles, axis=1), pick, preferred_element_type=jnp.float32
            )
            for side in range(FSUB // LANES):
                rows_ref[side, tau * depth : (tau + 1) * depth, :] = rows[
                    :, side * LANES : (side + 1) * LANES
                ]

    todo = [(i, p) for i in range(step_pairs) for p in range(parities)]
    operands = []
    for i, p in todo:
        halves = []
        for part in range(2):
            first = p * BAND_CH + part * few + at * step_pairs + i
            halves.append(
                jnp.concatenate(
                    [
                        rows_ref[side, pl.ds(first, FR, stride=parities * BAND_CH), :]
                        for side in range(FSUB // LANES)
                    ],
                    axis=1,
                )
            )
        real, imag = halves
        both = jnp.concatenate([real, imag], axis=0)
        turned = jnp.concatenate([-imag, real], axis=0)
        right = jnp.concatenate([both, turned], axis=1).astype(jnp.bfloat16)
        operands.append((both.astype(jnp.bfloat16).T, right))
    outs = [
        jnp.dot(left, right, preferred_element_type=jnp.float32) for left, right in operands
    ]
    for (i, p), out in zip(todo, outs):
        out = out * (1.0 / FR)
        vis_ref[i, p, 0] = out[:, :FSUB]
        vis_ref[i, p, 1] = out[:, FSUB:]


def receive_call(z, chunk, parity, arrived, keys, vis):
    parities = 2 if parity is None else 1
    step_pairs = 4 // parities
    steps = BAND_CH // 2 // step_pairs
    at = 0 if parity is None else parity
    out_shape = jax.ShapeDtypeStruct((z.chan_dev // 2, 2, 2, FSUB, FSUB), jnp.float32)
    arrays = []
    runs = []
    for one in arrived:
        runs.append([])
        for got, first, count in one:
            if not any(got is x for x in arrays):
                arrays.append(got)
            runs[-1].append(([got is x for x in arrays].index(True), first, count))
    units = sum(count for _, _, count in runs[0])
    slots = min(2, len(runs))
    operands = arrays + [keys]
    in_specs = [pl.BlockSpec(memory_space=pl.ANY)] * len(arrays) + [whole_spec(keys.shape)]
    aliases = {}
    if vis is not None:
        in_specs.append(pl.BlockSpec(memory_space=pl.ANY))
        aliases = {len(operands): 0}
        operands.append(vis)
    share = parities * len(runs)
    return pl.pallas_call(
        functools.partial(receive_kernel, z, parities, step_pairs, runs, len(arrays)),
        grid=(len(runs) * steps,),
        in_specs=in_specs,
        out_specs=pl.BlockSpec(
            (step_pairs, parities, 2, FSUB, FSUB),
            lambda g: (chunk * steps + g, at, 0, 0, 0),
        ),
        out_shape=out_shape,
        input_output_aliases=aliases,
        scratch_shapes=[
            pltpu.VMEM((slots, z.devices, units, BAND_CH, LANES), jnp.bfloat16),
            pltpu.VMEM((FSUB // LANES, z.lane_frames * units * BAND_CH, LANES), jnp.float32),
            pltpu.SemaphoreType.DMA((slots, max(len(x) for x in runs))),
        ],
        compiler_params=pltpu.CompilerParams(vmem_limit_bytes=VMEM // 2),
        cost_estimate=pl.CostEstimate(
            flops=2_000_000_000 * share, bytes_accessed=5_000_000 * share, transcendentals=0
        ),
        name="correlate",
    )(*operands)


def beam_kernel(z, me_ref, *refs):
    spec_refs = refs[: z.chunks]
    cos_base, sin_base, cos_step, sin_step, sum_ref, out_ref, prod_ref = refs[z.chunks :]
    count = z.chan_dev
    weights = []
    for g in range(BEAMS):
        c0, s0 = cos_base[0, g : g + 1, :], sin_base[0, g : g + 1, :]
        c1, s1 = cos_step[g], sin_step[g]
        weights.append(
            ((c0 * c1 - s0 * s1).astype(jnp.bfloat16), (s0 * c1 + c0 * s1).astype(jnp.bfloat16))
        )
    for q in range(z.quads):
        lanes = slice(q * z.width, (q + 1) * z.width)
        x = [ref[:, lanes] for ref in spec_refs]
        real = jnp.concatenate([v[:BAND_CH] for v in x], axis=0)
        imag = jnp.concatenate([v[BAND_CH:] for v in x], axis=0)
        for g in range(BEAMS):
            c, s = weights[g]
            pair = (c * real + s * imag, c * imag - s * real)
            for part in range(2):
                row = (part * BEAMS + g) * count
                both = pair[part][:, :LANES] + pair[part][:, LANES:]
                prod_ref[row : row + count, q * LANES : (q + 1) * LANES] = both
    sums = jnp.dot(prod_ref[...], sum_ref[...], preferred_element_type=jnp.float32)
    sums = sums * (1.0 / np.sqrt(F))
    for j in range(2 * BEAMS):
        out_ref[0, :, j * FR : (j + 1) * FR] = sums[j * count : (j + 1) * count, :FR]


def beam_call(z, me, spectra, delays):
    bits = z.devices.bit_length() - 1
    lanes = FR * z.feed_dev
    halves = delays.reshape(BEAMS, 2, 1, z.cap)
    spread = jnp.broadcast_to(halves, (BEAMS, 2, z.lane_frames, z.cap)).reshape(BEAMS, z.width)
    unit = 2.0 * jnp.pi / NFFT
    owners = jnp.arange(z.devices, dtype=jnp.int32).astype(jnp.float32) * z.chan_dev
    inner = np.arange(z.chunks)[:, None] * BAND_CH + ORDER[None, :]
    inner = jnp.asarray(inner.reshape(-1).astype(np.float32))
    base = unit * (spread[None, :, :] * owners[:, None, None])
    step = unit * (spread[:, None, :] * inner[None, :, None])
    frame = (np.arange(FR * z.cap) // LANES) * z.lane_frames
    frame = frame + (np.arange(FR * z.cap) % LANES) // z.cap
    sums = (frame[:, None] == np.arange(LANES)[None, :]).astype(ml_dtypes.bfloat16)

    def owner(j, me_ref):
        k = 0
        for b in range(bits):
            k = k | (((j >> b) & 1) << (bits - 1 - b))
        return me_ref[0] ^ k

    base_spec = pl.BlockSpec(
        (1, BEAMS, z.width), lambda j, me_ref: (owner(j, me_ref), 0, 0)
    )
    grid_spec = pltpu.PrefetchScalarGridSpec(
        num_scalar_prefetch=1,
        grid=(z.devices,),
        in_specs=[
            pl.BlockSpec((z.rows_dev, lanes), lambda j, me_ref: (owner(j, me_ref), 0))
            for _ in range(z.chunks)
        ]
        + [base_spec, base_spec, whole_spec(step.shape), whole_spec(step.shape)]
        + [whole_spec(sums.shape)],
        out_specs=pl.BlockSpec(
            (1, z.chan_dev, 2 * BEAMS * FR), lambda j, me_ref: (j, 0, 0)
        ),
        scratch_shapes=[pltpu.VMEM((2 * BEAMS * z.chan_dev, FR * z.cap), jnp.bfloat16)],
    )
    return pl.pallas_call(
        functools.partial(beam_kernel, z),
        grid_spec=grid_spec,
        out_shape=jax.ShapeDtypeStruct((z.devices, z.chan_dev, 2 * BEAMS * FR), jnp.float32),
        compiler_params=pltpu.CompilerParams(vmem_limit_bytes=VMEM),
        cost_estimate=pl.CostEstimate(
            flops=20_000_000_000, bytes_accessed=20_000_000, transcendentals=0
        ),
        name="beam_sums",
    )(
        me, *spectra, jnp.cos(base), jnp.sin(base), jnp.cos(step), jnp.sin(step),
        jnp.asarray(sums),
    )


def swap(z, x, offset):
    return lax.ppermute(x, "chan", [(i, i ^ offset) for i in range(z.devices)])


def exchange(x):
    return lax.all_to_all(x, "chan", split_axis=0, concat_axis=0, tiled=True)


def on_device(voltages, delays, band_feeds):
    z = Sizes(lax.axis_size("chan"), voltages.shape[0])
    me = lax.axis_index("chan")
    me_array = me.astype(jnp.int32).reshape(1)

    own = lax.dynamic_slice_in_dim(band_feeds, me * z.bands_here, z.bands_here, 0)
    source = own // z.feed_dev
    before = jnp.sum(
        (own[:, None, :] < (source * z.feed_dev)[:, :, None]).astype(jnp.int32), axis=2
    )
    place = jnp.arange(FSUB, dtype=jnp.int32)[None, :] - before
    tau = jnp.arange(z.lane_frames, dtype=jnp.int32)
    big = (source // z.lane_frames) * LANES + place
    group = (source % z.lane_frames)[:, None, :] ^ tau[None, :, None]
    take_key = big[:, None, :] + z.cap * group

    calls = Spectra(z, me_array, voltages, band_feeds)
    early = list(range(z.early))
    basis = calls.basis(early)
    share = 2 * z.step_quads
    step = z.early * share
    arrived = [[] for _ in range(z.chunks)]
    steps = z.parts[0]
    filt, *spectra, send = calls.first(0, steps, early, basis, steps * step, [])
    got = exchange(send)
    for c in early:
        arrived[c] += [(got, g * step + c * share, share) for g in range(steps)]
    if len(z.parts) > 1:
        begin, steps = steps, z.parts[1]
        base = steps * step
        begun = 3 * z.step_quads
        filt, *spectra, send = calls.first(
            begin, steps, early, basis, base + z.steps * begun, [filt, *spectra]
        )
        *more, send, last = calls.next([z.chunks - 2, z.chunks - 1], filt, send)
        spectra = spectra + more
        got = exchange(send)
        for c in early:
            arrived[c] += [(got, g * step + c * share, share) for g in range(steps)]
        arrived[-2] += [(got, base + g * begun, share) for g in range(z.steps)]
        arrived[-1] += [(got, base + g * begun + share, z.step_quads) for g in range(z.steps)]

    beams, bit = beam_call(z, me_array, spectra, delays), 1
    while beams.shape[0] > 1:
        half = beams.shape[0] // 2
        away = beams[half:].astype(jnp.bfloat16) if half == 1 else beams[half:]
        beams, bit = beams[:half] + swap(z, away, bit).astype(jnp.float32), 2 * bit
    if len(z.parts) > 1:
        last, beams = lax.optimization_barrier((last, beams))
        got = exchange(last)
        k = z.chunks - 1
        vis = receive_call(z, 0, None, arrived[:k], take_key[:k], None)
        vis = receive_call(z, k, 0, arrived[k:], take_key[k:], vis)
        vis = receive_call(z, k, 1, [[(got, 0, z.quads)]], take_key[k:], vis)
    else:
        vis = receive_call(z, 0, None, arrived, take_key, None)
    beams = beams.reshape(z.chunks, 2, BAND_CH // 2, 2 * BEAMS * FR)
    beams = jnp.swapaxes(beams, 1, 2).reshape(z.chan_dev, 2 * BEAMS * FR)
    return (vis.reshape(z.chan_dev, 2, FSUB, FSUB), beams)


def solution(mesh):
    in_specs = (P(("grp", "chan"), None), P(None, ("grp", "chan")), P())
    out_specs = (P(("grp", "chan"), None, None, None), P(("grp", "chan"), None))
    return jax.shard_map(
        on_device, mesh=mesh, in_specs=in_specs, out_specs=out_specs, check_vma=False
    )
```

```python
import functools

import jax
import jax.numpy as jnp
import ml_dtypes
import numpy as np
from jax import lax
from jax.experimental import pallas as pl
from jax.experimental.pallas import tpu as pltpu
from jax.sharding import PartitionSpec as P

F = 1024
CHANNELS = 1024
TAPS = 4
BAND_CH = 16
BEAMS = 4
FR = 48
NFFT = 2048
BANDS = 64
FSUB = 256
LANES = 128
VMEM = 56 * 1024 * 1024

NT = (((1,), (1,)), ((), ()))


def fir_window():
    ids = np.arange(TAPS * NFFT, dtype=np.float64)
    centered = (ids - 0.5 * TAPS * NFFT + 0.5) / NFFT
    hann_part = 0.5 - 0.5 * np.cos(2.0 * np.pi * (ids + 0.5) / (TAPS * NFFT))
    return (np.sinc(centered) * hann_part).reshape(TAPS, NFFT)


ORDER = np.concatenate([np.arange(0, BAND_CH, 2), np.arange(1, BAND_CH, 2)])


def dft_rows(chan_ids):
    m = np.arange(NFFT // 2, dtype=np.int64)
    turns = (chan_ids[..., None].astype(np.int64) * m) % NFFT
    table = 2.0 * np.pi * np.arange(NFFT) / NFFT
    cosine = np.cos(table).astype(np.float32).astype(ml_dtypes.bfloat16)
    sine = (-np.sin(table)).astype(np.float32).astype(ml_dtypes.bfloat16)
    return np.stack([cosine[turns], sine[turns]], axis=1)


class Sizes:
    def __init__(self, devices, feed_dev):
        self.devices = devices
        self.feed_dev = feed_dev
        self.cap = feed_dev // 2
        self.lane_frames = LANES // self.cap
        self.quads = FR // self.lane_frames
        self.width = self.lane_frames * feed_dev
        self.steps = 6 if self.quads % 6 == 0 else self.quads
        self.step_frames = FR // self.steps
        self.step_quads = self.quads // self.steps
        self.step_lanes = self.step_frames * feed_dev
        self.chan_dev = CHANNELS // devices
        self.bands_here = BANDS // devices
        self.chunks = self.chan_dev // BAND_CH
        self.rows_dev = 2 * BAND_CH
        self.rows = devices * self.rows_dev
        self.groups = devices // self.lane_frames
        self.early = min(2, self.chunks)
        if self.chunks == 4:
            self.parts = (self.steps // 2, self.steps - self.steps // 2)
        else:
            self.early, self.parts = self.chunks, (self.steps,)


def find_places(z, me, lists):
    base = me * z.feed_dev
    first = jnp.sum((lists < base).astype(jnp.int32), axis=1, keepdims=True)
    lane = lax.broadcasted_iota(jnp.int32, (lists.shape[0], LANES), 1)
    at = first + lane % z.cap
    parts = []
    for side in range(FSUB // LANES):
        index = jnp.clip(at - side * LANES, 0, LANES - 1)
        half = lists[:, side * LANES : (side + 1) * LANES]
        parts.append(jnp.take_along_axis(half, index, axis=1, mode="promise_in_bounds"))
    loc = jnp.where(at < LANES, parts[0], parts[1]) - base
    return jnp.clip(loc, 0, z.feed_dev - 1)


def emit_spectra(z, scale, chunk, me_ref, spectra, loc_ref, spec_ref, sends):
    lane = lax.broadcasted_iota(jnp.int32, (z.rows_dev, LANES), 1)
    frame = (lane // z.cap) ^ (me_ref[0] % z.lane_frames)
    start = frame * z.cap
    few = BAND_CH // 2
    for owner in range(z.devices):
        top = owner * BAND_CH
        rows = [x[top + p : top + p + few] for p in (0, few) for x in spectra]
        rows = jnp.concatenate(rows, axis=0) * scale
        spec_ref[owner * z.rows_dev : (owner + 1) * z.rows_dev, :] = rows.astype(jnp.bfloat16)
        band = owner * z.bands_here + chunk
        loc = loc_ref[band : band + 1, :]
        index = start + loc % z.cap
        lower = jnp.broadcast_to(loc, index.shape) < z.cap
        for q in range(z.step_quads):
            parts = []
            for side in range(2):
                left = q * z.width + side * LANES
                parts.append(
                    jnp.take_along_axis(
                        rows[:, left : left + LANES], index, axis=1, mode="promise_in_bounds"
                    )
                )
            picked = jnp.where(lower, parts[0], parts[1])
            for parity, (send_ref, unit, stride) in enumerate(sends):
                half = [
                    picked[p * BAND_CH + parity * few : p * BAND_CH + parity * few + few]
                    for p in range(2)
                ]
                half = jnp.concatenate(half, axis=0).astype(jnp.bfloat16)
                send_ref[owner, unit + q * stride] = half


def product(z, basis_ref, parity, c, begin, end, samples):
    rows = slice(c * z.rows // 2, (c + 1) * z.rows // 2)
    return lax.dot_general(
        basis_ref[parity, rows, begin:end], samples, NT, preferred_element_type=jnp.float32
    )


def filter_tile(z, main_ref, halo, win_ref, off, f0):
    lanes = slice(off, off + LANES)
    taps = [win_ref[k : k + 1, lanes] for k in range(TAPS)]
    frames = []
    for t in range(z.step_frames + TAPS - 1):
        if t < z.step_frames:
            x = main_ref[f0 : f0 + 16, t * NFFT + off : t * NFFT + off + LANES]
        else:
            x = halo[t - z.step_frames][f0 : f0 + 16, lanes]
        frames.append(x.astype(jnp.float32))
    totals = []
    for t in range(z.step_frames):
        total = taps[0] * frames[t]
        for k in range(1, TAPS):
            total = total + taps[k] * frames[t + k]
        totals.append(total)
    if z.cap < 16:
        totals = [
            jnp.concatenate([totals[t][h : h + 8], totals[t + 1][h : h + 8]], axis=0)
            for t in range(0, z.step_frames, 2)
            for h in (0, 8)
        ]
    out = []
    for i, total in enumerate(totals):
        if z.cap < 16:
            t, half, feed = 2 * (i // 2), i % 2, 0
        else:
            t, half, feed = i, f0 // z.cap, f0 % z.cap
        row = (t // z.lane_frames) * z.width + half * LANES
        row += (t % z.lane_frames) * z.cap + feed
        out.append((row, total.astype(jnp.bfloat16)))
    return out


def filter_fold(z, main_ref, halo, win_ref, filt_ref, off):
    far = off + NFFT // 2
    folded = {}
    for f0 in range(0, z.feed_dev, 16):
        low = filter_tile(z, main_ref, halo, win_ref, off, f0)
        high = filter_tile(z, main_ref, halo, win_ref, far, f0)
        for (row, a), (_, b) in zip(low, high):
            folded[row] = (a + b, a - b)
            filt_ref[row : row + 16, off : off + LANES] = folded[row][0]
            filt_ref[row : row + 16, far : far + LANES] = folded[row][1]
    return [
        jnp.concatenate([folded[row][parity] for row in sorted(folded)], axis=0)
        for parity in range(2)
    ]


def first_kernel(
    z, scale, chunks, held, me_ref, main_ref, h0_ref, h1_ref, h2_ref, win_ref, basis_ref,
    lists_ref, *refs,
):
    filt_ref, spec_refs, send_ref, loc_ref = refs[held], refs[held + 1 : -2], refs[-2], refs[-1]
    halo = (h0_ref, h1_ref, h2_ref)
    loc_ref[...] = find_places(z, me_ref[0], lists_ref[...])
    piece = 512
    count = len(chunks)
    spectra = [[None, None] for _ in chunks]
    for off in range(0, NFFT // 2, piece):
        tiles = [
            filter_fold(z, main_ref, halo, win_ref, filt_ref, tile)
            for tile in range(off, off + piece, LANES)
        ]
        for parity in range(2):
            samples = jnp.concatenate([tile[parity] for tile in tiles], axis=1)
            for c in range(count):
                part = product(z, basis_ref, parity, c, off, off + piece, samples)
                old = spectra[c][parity]
                spectra[c][parity] = part if old is None else old + part
    for c, chunk in enumerate(chunks):
        unit = c * 2 * z.step_quads
        sends = [(send_ref, unit, 2), (send_ref, unit + 1, 2)]
        emit_spectra(z, scale, chunk, me_ref, spectra[c], loc_ref, spec_refs[c], sends)


def next_kernel(z, scale, chunks, me_ref, filt_ref, basis_ref, lists_ref, held_ref, *refs):
    begun_ref, last_ref, loc_ref = refs[2], refs[3], refs[-1]
    loc_ref[...] = find_places(z, me_ref[0], lists_ref[...])
    half = NFFT // 2
    spectra = [
        [
            product(z, basis_ref, p, c, 0, half, filt_ref[:, p * half : (p + 1) * half])
            for p in range(2)
        ]
        for c in range(2)
    ]
    sends = [
        [(begun_ref, 0, 2), (begun_ref, 1, 2)],
        [(begun_ref, 2 * z.step_quads, 1), (last_ref, 0, 1)],
    ]
    for c, chunk in enumerate(chunks):
        emit_spectra(z, scale, chunk, me_ref, spectra[c], loc_ref, refs[c], sends[c])


def whole_spec(shape):
    return pl.BlockSpec(shape, lambda *g: (0,) * len(shape))


class Spectra:

    def __init__(self, z, me, voltages, band_feeds):
        window = fir_window()
        self.z = z
        self.me = me
        self.scale = float(np.sqrt(2.0 / np.sum(window * window)))
        self.window = jnp.asarray(window.astype(np.float32))
        self.voltages = voltages
        self.lists = band_feeds
        self.ids = np.arange(CHANNELS).reshape(z.devices, z.chunks, BAND_CH)
        self.me_spec = pl.BlockSpec(memory_space=pltpu.SMEM)
        self.spec_shape = jax.ShapeDtypeStruct((z.rows, FR * z.feed_dev), jnp.bfloat16)
        self.filt_shape = jax.ShapeDtypeStruct((FR * z.feed_dev, NFFT), jnp.bfloat16)

    def basis(self, chunks):
        sides = []
        for parity in range(2):
            rows = [dft_rows(self.ids[:, k, parity::2].reshape(-1)) for k in chunks]
            rows = np.stack(rows).reshape(len(chunks), self.z.devices, BAND_CH // 2, 2, -1)
            rows = np.transpose(rows, (0, 1, 3, 2, 4))
            sides.append(rows.reshape(len(chunks) * self.z.rows // 2, NFFT // 2))
        return jnp.asarray(np.stack(sides))

    def message(self, units):
        return jax.ShapeDtypeStruct((self.z.devices, units, BAND_CH, LANES), jnp.bfloat16)

    def common(self, steps, chunks):
        z = self.z
        flops = len(chunks) * z.rows * NFFT * z.step_lanes * steps
        return dict(
            grid=(steps,),
            scratch_shapes=[pltpu.VMEM((BANDS, LANES), jnp.int32)],
            compiler_params=pltpu.CompilerParams(vmem_limit_bytes=VMEM),
            cost_estimate=pl.CostEstimate(
                flops=flops, bytes_accessed=3_000_000 * steps, transcendentals=0
            ),
        )

    def first(self, begin, steps, chunks, basis, units, held):
        z = self.z
        count = len(chunks)

        def halo_spec(h):
            return pl.BlockSpec(
                (z.feed_dev, NFFT), lambda g: (0, z.step_frames * (begin + g + 1) + h)
            )

        send_block = (z.devices, count * 2 * z.step_quads, BAND_CH, LANES)
        operands = [self.me] + [self.voltages] * 4 + [self.window, basis, self.lists]
        aliases = {len(operands) + i: i for i in range(len(held))}
        return pl.pallas_call(
            functools.partial(first_kernel, z, self.scale, chunks, len(held)),
            in_specs=[
                self.me_spec,
                pl.BlockSpec((z.feed_dev, z.step_frames * NFFT), lambda g: (0, begin + g)),
                halo_spec(0),
                halo_spec(1),
                halo_spec(2),
                whole_spec((TAPS, NFFT)),
                whole_spec(basis.shape),
                whole_spec(self.lists.shape),
            ]
            + [pl.BlockSpec(memory_space=pl.ANY)] * len(held),
            out_specs=[
                pl.BlockSpec((z.step_lanes, NFFT), lambda g: (begin + g, 0)),
            ]
            + [pl.BlockSpec((z.rows, z.step_lanes), lambda g: (0, begin + g))] * count
            + [pl.BlockSpec(send_block, lambda g: (0, g, 0, 0))],
            out_shape=[self.filt_shape] + [self.spec_shape] * count + [self.message(units)],
            input_output_aliases=aliases,
            name="filter_spectra",
            **self.common(steps, chunks),
        )(*operands, *held)

    def next(self, chunks, filt, held):
        z = self.z
        basis = self.basis(chunks)
        begun = 3 * z.step_quads
        base = held.shape[1] // begun - z.steps
        operands = [self.me, filt, basis, self.lists, held]
        return pl.pallas_call(
            functools.partial(next_kernel, z, self.scale, chunks),
            in_specs=[
                self.me_spec,
                pl.BlockSpec((z.step_lanes, NFFT), lambda g: (g, 0)),
                whole_spec(basis.shape),
                whole_spec(self.lists.shape),
                pl.BlockSpec(memory_space=pl.ANY),
            ],
            out_specs=[pl.BlockSpec((z.rows, z.step_lanes), lambda g: (0, g))] * 2
            + [
                pl.BlockSpec((z.devices, begun, BAND_CH, LANES), lambda g: (0, base + g, 0, 0)),
                pl.BlockSpec((z.devices, z.step_quads, BAND_CH, LANES), lambda g: (0, g, 0, 0)),
            ],
            out_shape=[self.spec_shape] * 2
            + [self.message(held.shape[1]), self.message(z.quads)],
            input_output_aliases={4: 2},
            name="spectra_next",
            **self.common(z.steps, chunks),
        )(*operands)


def receive_kernel(z, parities, step_pairs, runs, arrays, even_steps, *refs):
    arr_refs, key_ref = refs[:arrays], refs[arrays]
    vis_ref, buf_ref, rows_ref, sems = refs[-4:]
    g = pl.program_id(0)
    lf = z.lane_frames
    few = BAND_CH // 2
    steps = few // step_pairs
    depth = buf_ref.shape[2] * BAND_CH
    slots = buf_ref.shape[0]
    at = g % steps

    def copies(c):
        return [
            pltpu.make_async_copy(
                arr_refs[array].at[:, first : first + count],
                buf_ref.at[c % slots, :, place : place + count],
                sems.at[c % slots, i],
            )
            for i, (array, first, count, place) in enumerate(runs[c])
        ]

    for c in range(len(runs)):

        @pl.when(g == c * steps)
        def _():
            if c == 0:
                for copy in copies(c):
                    copy.start()
            for copy in copies(c):
                copy.wait()
            if c + 1 < len(runs):
                for copy in copies(c + 1):
                    copy.start()

    @pl.when(at == 0)
    def _():
        c = g // steps
        slot = lax.broadcasted_iota(jnp.int32, (z.groups * LANES, FSUB), 0)
        lane_group = lax.broadcasted_iota(jnp.int32, (depth, LANES), 1) // z.cap
        for tau in range(lf):
            tiles = []
            for big in range(z.groups):
                tile = buf_ref[c % slots, big * lf + tau].reshape(depth, LANES)
                for lane in range(1, lf):
                    block = buf_ref[c % slots, big * lf + (lane ^ tau)].reshape(depth, LANES)
                    tile = jnp.where(lane_group == lane, block, tile)
                tiles.append(tile)
            key = key_ref[c, tau : tau + 1, :]
            pick = jnp.where(slot == key, 1.0, 0.0).astype(jnp.bfloat16)
            rows = jnp.dot(
                jnp.concatenate(tiles, axis=1), pick, preferred_element_type=jnp.float32
            )
            for side in range(FSUB // LANES):
                rows_ref[side, tau * depth : (tau + 1) * depth, :] = rows[
                    :, side * LANES : (side + 1) * LANES
                ]

    def correlate(todo):
        operands = []
        for i, p in todo:
            halves = []
            for part in range(2):
                first = p * BAND_CH + part * few + at * step_pairs + i
                halves.append(
                    jnp.concatenate(
                        [
                            rows_ref[side, pl.ds(first, FR, stride=parities * BAND_CH), :]
                            for side in range(FSUB // LANES)
                        ],
                        axis=1,
                    )
                )
            real, imag = halves
            both = jnp.concatenate([real, imag], axis=0)
            turned = jnp.concatenate([-imag, real], axis=0)
            right = jnp.concatenate([both, turned], axis=1).astype(jnp.bfloat16)
            operands.append((both.astype(jnp.bfloat16).T, right))
        outs = [
            jnp.dot(left, right, preferred_element_type=jnp.float32)
            for left, right in operands
        ]
        for (i, p), out in zip(todo, outs):
            out = out * (1.0 / FR)
            vis_ref[i, p, 0] = out[:, :FSUB]
            vis_ref[i, p, 1] = out[:, FSUB:]

    every = [(i, p) for i in range(step_pairs) for p in range(parities)]
    if even_steps:
        begin = len(runs) * steps - even_steps

        @pl.when(g < begin)
        def _():
            correlate(every)

        @pl.when(g >= begin)
        def _():
            correlate([(i, p) for i, p in every if p == 0])

    else:
        correlate(every)


def receive_call(z, chunk, parity, arrived, keys, vis, even_last=False):
    parities = 2 if parity is None else 1
    step_pairs = 4 // parities
    steps = BAND_CH // 2 // step_pairs
    at = 0 if parity is None else parity
    out_shape = jax.ShapeDtypeStruct((z.chan_dev // 2, 2, 2, FSUB, FSUB), jnp.float32)
    arrays = []
    runs = []
    for one in arrived:
        runs.append([])
        for got, first, count, place in one:
            if not any(got is x for x in arrays):
                arrays.append(got)
            index = [got is x for x in arrays].index(True)
            runs[-1].append((index, first, count, place))
    units = parities * z.quads
    slots = min(2, len(runs))
    operands = arrays + [keys]
    in_specs = [pl.BlockSpec(memory_space=pl.ANY)] * len(arrays) + [whole_spec(keys.shape)]
    aliases = {}
    if vis is not None:
        in_specs.append(pl.BlockSpec(memory_space=pl.ANY))
        aliases = {len(operands): 0}
        operands.append(vis)
    share = parities * len(runs)
    return pl.pallas_call(
        functools.partial(
            receive_kernel, z, parities, step_pairs, runs, len(arrays), steps if even_last else 0
        ),
        grid=(len(runs) * steps,),
        in_specs=in_specs,
        out_specs=pl.BlockSpec(
            (step_pairs, parities, 2, FSUB, FSUB),
            lambda g: (chunk * steps + g, at, 0, 0, 0),
        ),
        out_shape=out_shape,
        input_output_aliases=aliases,
        scratch_shapes=[
            pltpu.VMEM((slots, z.devices, units, BAND_CH, LANES), jnp.bfloat16),
            pltpu.VMEM((FSUB // LANES, z.lane_frames * units * BAND_CH, LANES), jnp.float32),
            pltpu.SemaphoreType.DMA((slots, max(len(x) for x in runs))),
        ],
        compiler_params=pltpu.CompilerParams(vmem_limit_bytes=VMEM // 2),
        cost_estimate=pl.CostEstimate(
            flops=2_000_000_000 * share, bytes_accessed=5_000_000 * share, transcendentals=0
        ),
        name="correlate",
    )(*operands)


def beam_kernel(z, me_ref, *refs):
    spec_refs = refs[: z.chunks]
    cos_base, sin_base, cos_step, sin_step, sum_ref, out_ref, prod_ref, row_ref = refs[z.chunks :]
    count = z.chan_dev
    weights = []
    for g in range(BEAMS):
        c0, s0 = cos_base[0, g : g + 1, :], sin_base[0, g : g + 1, :]
        c1, s1 = cos_step[g], sin_step[g]
        weights.append(
            ((c0 * c1 - s0 * s1).astype(jnp.bfloat16), (s0 * c1 + c0 * s1).astype(jnp.bfloat16))
        )
    for q in range(z.quads):
        lanes = slice(q * z.width, (q + 1) * z.width)
        x = [ref[:, lanes] for ref in spec_refs]
        real = jnp.concatenate([v[:BAND_CH] for v in x], axis=0)
        imag = jnp.concatenate([v[BAND_CH:] for v in x], axis=0)
        for g in range(BEAMS):
            c, s = weights[g]
            pair = (c * real + s * imag, c * imag - s * real)
            for part in range(2):
                row = (part * BEAMS + g) * count
                both = pair[part][:, :LANES] + pair[part][:, LANES:]
                prod_ref[row : row + count, q * LANES : (q + 1) * LANES] = both
    sums = jnp.dot(prod_ref[...], sum_ref[...], preferred_element_type=jnp.float32)
    sums = sums * (1.0 / np.sqrt(F))
    few = BAND_CH // 2
    for j in range(2 * BEAMS):
        for i in range(count // few):
            first = i // 2 * BAND_CH + i % 2
            top = j * count + i * few
            row_ref[j, pl.ds(first, few, stride=2), :] = sums[top : top + few]
        out_ref[0, :, j * FR : (j + 1) * FR] = row_ref[j][:, :FR]


def beam_call(z, me, spectra, delays):
    bits = z.devices.bit_length() - 1
    lanes = FR * z.feed_dev
    halves = delays.reshape(BEAMS, 2, 1, z.cap)
    spread = jnp.broadcast_to(halves, (BEAMS, 2, z.lane_frames, z.cap)).reshape(BEAMS, z.width)
    unit = 2.0 * jnp.pi / NFFT
    owners = jnp.arange(z.devices, dtype=jnp.int32).astype(jnp.float32) * z.chan_dev
    inner = np.arange(z.chunks)[:, None] * BAND_CH + ORDER[None, :]
    inner = jnp.asarray(inner.reshape(-1).astype(np.float32))
    base = unit * (spread[None, :, :] * owners[:, None, None])
    step = unit * (spread[:, None, :] * inner[None, :, None])
    frame = (np.arange(FR * z.cap) // LANES) * z.lane_frames
    frame = frame + (np.arange(FR * z.cap) % LANES) // z.cap
    sums = (frame[:, None] == np.arange(LANES)[None, :]).astype(ml_dtypes.bfloat16)

    def owner(j, me_ref):
        k = 0
        for b in range(bits):
            k = k | (((j >> b) & 1) << (bits - 1 - b))
        return me_ref[0] ^ k

    base_spec = pl.BlockSpec(
        (1, BEAMS, z.width), lambda j, me_ref: (owner(j, me_ref), 0, 0)
    )
    grid_spec = pltpu.PrefetchScalarGridSpec(
        num_scalar_prefetch=1,
        grid=(z.devices,),
        in_specs=[
            pl.BlockSpec((z.rows_dev, lanes), lambda j, me_ref: (owner(j, me_ref), 0))
            for _ in range(z.chunks)
        ]
        + [base_spec, base_spec, whole_spec(step.shape), whole_spec(step.shape)]
        + [whole_spec(sums.shape)],
        out_specs=pl.BlockSpec(
            (1, z.chan_dev, 2 * BEAMS * FR), lambda j, me_ref: (j, 0, 0)
        ),
        scratch_shapes=[
            pltpu.VMEM((2 * BEAMS * z.chan_dev, FR * z.cap), jnp.bfloat16),
            pltpu.VMEM((2 * BEAMS, z.chan_dev, LANES), jnp.float32),
        ],
    )
    return pl.pallas_call(
        functools.partial(beam_kernel, z),
        grid_spec=grid_spec,
        out_shape=jax.ShapeDtypeStruct((z.devices, z.chan_dev, 2 * BEAMS * FR), jnp.float32),
        compiler_params=pltpu.CompilerParams(vmem_limit_bytes=VMEM),
        cost_estimate=pl.CostEstimate(
            flops=20_000_000_000, bytes_accessed=20_000_000, transcendentals=0
        ),
        name="beam_sums",
    )(
        me, *spectra, jnp.cos(base), jnp.sin(base), jnp.cos(step), jnp.sin(step),
        jnp.asarray(sums),
    )


def swap(z, x, offset):
    return lax.ppermute(x, "chan", [(i, i ^ offset) for i in range(z.devices)])


def exchange(x):
    return lax.all_to_all(x, "chan", split_axis=0, concat_axis=0, tiled=True)


def on_device(voltages, delays, band_feeds):
    z = Sizes(lax.axis_size("chan"), voltages.shape[0])
    me = lax.axis_index("chan")
    me_array = me.astype(jnp.int32).reshape(1)

    own = lax.dynamic_slice_in_dim(band_feeds, me * z.bands_here, z.bands_here, 0)
    source = own // z.feed_dev
    before = jnp.sum(
        (own[:, None, :] < (source * z.feed_dev)[:, :, None]).astype(jnp.int32), axis=2
    )
    place = jnp.arange(FSUB, dtype=jnp.int32)[None, :] - before
    tau = jnp.arange(z.lane_frames, dtype=jnp.int32)
    big = (source // z.lane_frames) * LANES + place
    group = (source % z.lane_frames)[:, None, :] ^ tau[None, :, None]
    take_key = big[:, None, :] + z.cap * group

    calls = Spectra(z, me_array, voltages, band_feeds)
    early = list(range(z.early))
    basis = calls.basis(early)
    share = 2 * z.step_quads
    step = z.early * share
    arrived = [[] for _ in range(z.chunks)]
    steps = z.parts[0]
    filt, *spectra, send = calls.first(0, steps, early, basis, steps * step, [])
    got = exchange(send)
    for c in early:
        arrived[c] += [(got, g * step + c * share, share, g * share) for g in range(steps)]
    if len(z.parts) > 1:
        begin, steps = steps, z.parts[1]
        base = steps * step
        begun = 3 * z.step_quads
        filt, *spectra, send = calls.first(
            begin, steps, early, basis, base + z.steps * begun, [filt, *spectra]
        )
        *more, send, last = calls.next([z.chunks - 2, z.chunks - 1], filt, send)
        spectra = spectra + more
        got = exchange(send)
        for c in early:
            arrived[c] += [
                (got, g * step + c * share, share, (begin + g) * share) for g in range(steps)
            ]
        for g in range(z.steps):
            first = base + g * begun
            arrived[-2].append((got, first, share, g * share))
            arrived[-1] += [
                (got, first + share + q, 1, g * share + 2 * q) for q in range(z.step_quads)
            ]

    beams, bit = beam_call(z, me_array, spectra, delays), 1
    while beams.shape[0] > 1:
        half = beams.shape[0] // 2
        away = beams[half:].astype(jnp.bfloat16) if half == 1 else beams[half:]
        beams, bit = beams[:half] + swap(z, away, bit).astype(jnp.float32), 2 * bit
    if len(z.parts) > 1:
        last, beams = lax.optimization_barrier((last, beams))
        got = exchange(last)
        k = z.chunks - 1
        vis = receive_call(z, 0, None, arrived, take_key, None, even_last=True)
        vis = receive_call(z, k, 1, [[(got, 0, z.quads, 0)]], take_key[k:], vis)
    else:
        vis = receive_call(z, 0, None, arrived, take_key, None)
    beams = beams.reshape(z.chan_dev, 2 * BEAMS * FR)
    return (vis.reshape(z.chan_dev, 2, FSUB, FSUB), beams)


def solution(mesh):
    in_specs = (P(("grp", "chan"), None), P(None, ("grp", "chan")), P())
    out_specs = (P(("grp", "chan"), None, None, None), P(("grp", "chan"), None))
    return jax.shard_map(
        on_device, mesh=mesh, in_specs=in_specs, out_specs=out_specs, check_vma=False
    )
```

```python
import functools

import jax
import jax.numpy as jnp
import ml_dtypes
import numpy as np
from jax import lax
from jax.experimental import pallas as pl
from jax.experimental.pallas import tpu as pltpu
from jax.sharding import PartitionSpec as P

F = 1024
CHANNELS = 1024
TAPS = 4
BAND_CH = 16
BEAMS = 4
FR = 48
NFFT = 2048
BANDS = 64
FSUB = 256
LANES = 128
VMEM = 56 * 1024 * 1024

NT = (((1,), (1,)), ((), ()))


def fir_window():
    ids = np.arange(TAPS * NFFT, dtype=np.float64)
    centered = (ids - 0.5 * TAPS * NFFT + 0.5) / NFFT
    hann_part = 0.5 - 0.5 * np.cos(2.0 * np.pi * (ids + 0.5) / (TAPS * NFFT))
    return (np.sinc(centered) * hann_part).reshape(TAPS, NFFT)


ORDER = np.concatenate([np.arange(0, BAND_CH, 2), np.arange(1, BAND_CH, 2)])


def dft_rows(chan_ids):
    m = np.arange(NFFT // 2, dtype=np.int64)
    turns = (chan_ids[..., None].astype(np.int64) * m) % NFFT
    table = 2.0 * np.pi * np.arange(NFFT) / NFFT
    cosine = np.cos(table).astype(np.float32).astype(ml_dtypes.bfloat16)
    sine = (-np.sin(table)).astype(np.float32).astype(ml_dtypes.bfloat16)
    return np.stack([cosine[turns], sine[turns]], axis=1)


class Sizes:
    def __init__(self, devices, feed_dev):
        self.devices = devices
        self.feed_dev = feed_dev
        self.cap = feed_dev // 2
        self.lane_frames = LANES // self.cap
        self.quads = FR // self.lane_frames
        self.width = self.lane_frames * feed_dev
        self.steps = 6 if self.quads % 6 == 0 else self.quads
        self.step_frames = FR // self.steps
        self.step_quads = self.quads // self.steps
        self.step_lanes = self.step_frames * feed_dev
        self.chan_dev = CHANNELS // devices
        self.bands_here = BANDS // devices
        self.chunks = self.chan_dev // BAND_CH
        self.rows_dev = 2 * BAND_CH
        self.rows = devices * self.rows_dev
        self.groups = devices // self.lane_frames
        self.early = min(2, self.chunks)
        if self.chunks == 4:
            self.parts = (self.steps // 2, self.steps - self.steps // 2)
        else:
            self.early, self.parts = self.chunks, (self.steps,)


def find_places(z, me, lists):
    base = me * z.feed_dev
    first = jnp.sum((lists < base).astype(jnp.int32), axis=1, keepdims=True)
    lane = lax.broadcasted_iota(jnp.int32, (lists.shape[0], LANES), 1)
    at = first + lane % z.cap
    parts = []
    for side in range(FSUB // LANES):
        index = jnp.clip(at - side * LANES, 0, LANES - 1)
        half = lists[:, side * LANES : (side + 1) * LANES]
        parts.append(jnp.take_along_axis(half, index, axis=1, mode="promise_in_bounds"))
    loc = jnp.where(at < LANES, parts[0], parts[1]) - base
    return jnp.clip(loc, 0, z.feed_dev - 1)


def emit_spectra(z, scale, chunk, me_ref, spectra, loc_ref, spec_ref, sends):
    lane = lax.broadcasted_iota(jnp.int32, (z.rows_dev, LANES), 1)
    frame = (lane // z.cap) ^ (me_ref[0] % z.lane_frames)
    start = frame * z.cap
    few = BAND_CH // 2
    for owner in range(z.devices):
        top = owner * BAND_CH
        rows = [x[top + p : top + p + few] for p in (0, few) for x in spectra]
        rows = jnp.concatenate(rows, axis=0) * scale
        spec_ref[owner * z.rows_dev : (owner + 1) * z.rows_dev, :] = rows.astype(jnp.bfloat16)
        band = owner * z.bands_here + chunk
        loc = loc_ref[band : band + 1, :]
        index = start + loc % z.cap
        lower = jnp.broadcast_to(loc, index.shape) < z.cap
        for q in range(z.step_quads):
            parts = []
            for side in range(2):
                left = q * z.width + side * LANES
                parts.append(
                    jnp.take_along_axis(
                        rows[:, left : left + LANES], index, axis=1, mode="promise_in_bounds"
                    )
                )
            picked = jnp.where(lower, parts[0], parts[1])
            for parity, (send_ref, unit, stride) in enumerate(sends):
                half = [
                    picked[p * BAND_CH + parity * few : p * BAND_CH + parity * few + few]
                    for p in range(2)
                ]
                half = jnp.concatenate(half, axis=0).astype(jnp.bfloat16)
                send_ref[owner, unit + q * stride] = half


def product(z, basis_ref, parity, c, begin, end, samples):
    rows = slice(c * z.rows // 2, (c + 1) * z.rows // 2)
    return lax.dot_general(
        basis_ref[parity, rows, begin:end], samples, NT, preferred_element_type=jnp.float32
    )


def filter_tile(z, main_ref, halo, win_ref, off, f0):
    lanes = slice(off, off + LANES)
    taps = [win_ref[k : k + 1, lanes] for k in range(TAPS)]
    frames = []
    for t in range(z.step_frames + TAPS - 1):
        if t < z.step_frames:
            x = main_ref[f0 : f0 + 16, t * NFFT + off : t * NFFT + off + LANES]
        else:
            x = halo[t - z.step_frames][f0 : f0 + 16, lanes]
        frames.append(x.astype(jnp.float32))
    totals = []
    for t in range(z.step_frames):
        total = taps[0] * frames[t]
        for k in range(1, TAPS):
            total = total + taps[k] * frames[t + k]
        totals.append(total)
    if z.cap < 16:
        totals = [
            jnp.concatenate([totals[t][h : h + 8], totals[t + 1][h : h + 8]], axis=0)
            for t in range(0, z.step_frames, 2)
            for h in (0, 8)
        ]
    out = []
    for i, total in enumerate(totals):
        if z.cap < 16:
            t, half, feed = 2 * (i // 2), i % 2, 0
        else:
            t, half, feed = i, f0 // z.cap, f0 % z.cap
        row = (t // z.lane_frames) * z.width + half * LANES
        row += (t % z.lane_frames) * z.cap + feed
        out.append((row, total.astype(jnp.bfloat16)))
    return out


def filter_fold(z, main_ref, halo, win_ref, filt_ref, off):
    far = off + NFFT // 2
    folded = {}
    for f0 in range(0, z.feed_dev, 16):
        low = filter_tile(z, main_ref, halo, win_ref, off, f0)
        high = filter_tile(z, main_ref, halo, win_ref, far, f0)
        for (row, a), (_, b) in zip(low, high):
            folded[row] = (a + b, a - b)
            filt_ref[row : row + 16, off : off + LANES] = folded[row][0]
            filt_ref[row : row + 16, far : far + LANES] = folded[row][1]
    return [
        jnp.concatenate([folded[row][parity] for row in sorted(folded)], axis=0)
        for parity in range(2)
    ]


def first_kernel(
    z, scale, chunks, held, me_ref, main_ref, h0_ref, h1_ref, h2_ref, win_ref, basis_ref,
    lists_ref, *refs,
):
    filt_ref, spec_refs, send_ref, loc_ref = refs[held], refs[held + 1 : -2], refs[-2], refs[-1]
    halo = (h0_ref, h1_ref, h2_ref)
    loc_ref[...] = find_places(z, me_ref[0], lists_ref[...])
    piece = 512
    count = len(chunks)
    spectra = [[None, None] for _ in chunks]
    for off in range(0, NFFT // 2, piece):
        tiles = [
            filter_fold(z, main_ref, halo, win_ref, filt_ref, tile)
            for tile in range(off, off + piece, LANES)
        ]
        for parity in range(2):
            samples = jnp.concatenate([tile[parity] for tile in tiles], axis=1)
            for c in range(count):
                part = product(z, basis_ref, parity, c, off, off + piece, samples)
                old = spectra[c][parity]
                spectra[c][parity] = part if old is None else old + part
    for c, chunk in enumerate(chunks):
        unit = c * 2 * z.step_quads
        sends = [(send_ref, unit, 2), (send_ref, unit + 1, 2)]
        emit_spectra(z, scale, chunk, me_ref, spectra[c], loc_ref, spec_refs[c], sends)


def next_kernel(z, scale, chunks, me_ref, filt_ref, basis_ref, lists_ref, held_ref, *refs):
    begun_ref, last_ref, loc_ref = refs[2], refs[3], refs[-1]
    loc_ref[...] = find_places(z, me_ref[0], lists_ref[...])
    half = NFFT // 2
    spectra = [
        [
            product(z, basis_ref, p, c, 0, half, filt_ref[:, p * half : (p + 1) * half])
            for p in range(2)
        ]
        for c in range(2)
    ]
    sends = [
        [(begun_ref, 0, 2), (begun_ref, 1, 2)],
        [(begun_ref, 2 * z.step_quads, 1), (last_ref, 0, 1)],
    ]
    for c, chunk in enumerate(chunks):
        emit_spectra(z, scale, chunk, me_ref, spectra[c], loc_ref, refs[c], sends[c])


def whole_spec(shape):
    return pl.BlockSpec(shape, lambda *g: (0,) * len(shape))


class Spectra:

    def __init__(self, z, me, voltages, band_feeds):
        window = fir_window()
        self.z = z
        self.me = me
        self.scale = float(np.sqrt(2.0 / np.sum(window * window)))
        self.window = jnp.asarray(window.astype(np.float32))
        self.voltages = voltages
        self.lists = band_feeds
        self.ids = np.arange(CHANNELS).reshape(z.devices, z.chunks, BAND_CH)
        self.me_spec = pl.BlockSpec(memory_space=pltpu.SMEM)
        self.spec_shape = jax.ShapeDtypeStruct((z.rows, FR * z.feed_dev), jnp.bfloat16)
        self.filt_shape = jax.ShapeDtypeStruct((FR * z.feed_dev, NFFT), jnp.bfloat16)

    def basis(self, chunks):
        sides = []
        for parity in range(2):
            rows = [dft_rows(self.ids[:, k, parity::2].reshape(-1)) for k in chunks]
            rows = np.stack(rows).reshape(len(chunks), self.z.devices, BAND_CH // 2, 2, -1)
            rows = np.transpose(rows, (0, 1, 3, 2, 4))
            sides.append(rows.reshape(len(chunks) * self.z.rows // 2, NFFT // 2))
        return jnp.asarray(np.stack(sides))

    def message(self, units):
        return jax.ShapeDtypeStruct((self.z.devices, units, BAND_CH, LANES), jnp.bfloat16)

    def common(self, steps, chunks):
        z = self.z
        flops = len(chunks) * z.rows * NFFT * z.step_lanes * steps
        return dict(
            grid=(steps,),
            scratch_shapes=[pltpu.VMEM((BANDS, LANES), jnp.int32)],
            compiler_params=pltpu.CompilerParams(vmem_limit_bytes=VMEM),
            cost_estimate=pl.CostEstimate(
                flops=flops, bytes_accessed=3_000_000 * steps, transcendentals=0
            ),
        )

    def first(self, begin, steps, chunks, basis, units, held):
        z = self.z
        count = len(chunks)

        def halo_spec(h):
            return pl.BlockSpec(
                (z.feed_dev, NFFT), lambda g: (0, z.step_frames * (begin + g + 1) + h)
            )

        send_block = (z.devices, count * 2 * z.step_quads, BAND_CH, LANES)
        operands = [self.me] + [self.voltages] * 4 + [self.window, basis, self.lists]
        aliases = {len(operands) + i: i for i in range(len(held))}
        return pl.pallas_call(
            functools.partial(first_kernel, z, self.scale, chunks, len(held)),
            in_specs=[
                self.me_spec,
                pl.BlockSpec((z.feed_dev, z.step_frames * NFFT), lambda g: (0, begin + g)),
                halo_spec(0),
                halo_spec(1),
                halo_spec(2),
                whole_spec((TAPS, NFFT)),
                whole_spec(basis.shape),
                whole_spec(self.lists.shape),
            ]
            + [pl.BlockSpec(memory_space=pl.ANY)] * len(held),
            out_specs=[
                pl.BlockSpec((z.step_lanes, NFFT), lambda g: (begin + g, 0)),
            ]
            + [pl.BlockSpec((z.rows, z.step_lanes), lambda g: (0, begin + g))] * count
            + [pl.BlockSpec(send_block, lambda g: (0, g, 0, 0))],
            out_shape=[self.filt_shape] + [self.spec_shape] * count + [self.message(units)],
            input_output_aliases=aliases,
            name="filter_spectra",
            **self.common(steps, chunks),
        )(*operands, *held)

    def next(self, chunks, filt, held):
        z = self.z
        basis = self.basis(chunks)
        begun = 3 * z.step_quads
        base = held.shape[1] // begun - z.steps
        operands = [self.me, filt, basis, self.lists, held]
        return pl.pallas_call(
            functools.partial(next_kernel, z, self.scale, chunks),
            in_specs=[
                self.me_spec,
                pl.BlockSpec((z.step_lanes, NFFT), lambda g: (g, 0)),
                whole_spec(basis.shape),
                whole_spec(self.lists.shape),
                pl.BlockSpec(memory_space=pl.ANY),
            ],
            out_specs=[pl.BlockSpec((z.rows, z.step_lanes), lambda g: (0, g))] * 2
            + [
                pl.BlockSpec((z.devices, begun, BAND_CH, LANES), lambda g: (0, base + g, 0, 0)),
                pl.BlockSpec((z.devices, z.step_quads, BAND_CH, LANES), lambda g: (0, g, 0, 0)),
            ],
            out_shape=[self.spec_shape] * 2
            + [self.message(held.shape[1]), self.message(z.quads)],
            input_output_aliases={4: 2},
            name="spectra_next",
            **self.common(z.steps, chunks),
        )(*operands)


def receive_kernel(z, parities, step_pairs, runs, arrays, even_steps, *refs):
    arr_refs, key_ref = refs[:arrays], refs[arrays]
    vis_ref, buf_ref, rows_ref, sems = refs[-4:]
    g = pl.program_id(0)
    lf = z.lane_frames
    few = BAND_CH // 2
    steps = few // step_pairs
    depth = buf_ref.shape[2] * BAND_CH
    slots = buf_ref.shape[0]
    at = g % steps

    def copies(c):
        return [
            pltpu.make_async_copy(
                arr_refs[array].at[:, first : first + count],
                buf_ref.at[c % slots, :, place : place + count],
                sems.at[c % slots, i],
            )
            for i, (array, first, count, place) in enumerate(runs[c])
        ]

    for c in range(len(runs)):

        @pl.when(g == c * steps)
        def _():
            if c == 0:
                for copy in copies(c):
                    copy.start()
            for copy in copies(c):
                copy.wait()
            if c + 1 < len(runs):
                for copy in copies(c + 1):
                    copy.start()

    @pl.when(at == 0)
    def _():
        c = g // steps
        slot = lax.broadcasted_iota(jnp.int32, (z.groups * LANES, FSUB), 0)
        lane_group = lax.broadcasted_iota(jnp.int32, (BAND_CH, LANES), 1) // z.cap
        masks = [jnp.where(lane_group == i, 1.0, 0.0).astype(jnp.bfloat16) for i in range(lf)]
        for tau in range(lf):
            tiles = []
            for big in range(z.groups):
                tile = buf_ref[c % slots, big * lf + tau] * masks[0]
                for lane in range(1, lf):
                    tile = tile + buf_ref[c % slots, big * lf + (lane ^ tau)] * masks[lane]
                tiles.append(tile.reshape(depth, LANES))
            key = key_ref[c, tau : tau + 1, :]
            pick = jnp.where(slot == key, 1.0, 0.0).astype(jnp.bfloat16)
            rows = jnp.dot(
                jnp.concatenate(tiles, axis=1), pick, preferred_element_type=jnp.float32
            )
            for side in range(FSUB // LANES):
                rows_ref[side, tau * depth : (tau + 1) * depth, :] = rows[
                    :, side * LANES : (side + 1) * LANES
                ]

    def correlate(todo):
        operands = []
        for i, p in todo:
            halves = []
            for part in range(2):
                first = p * BAND_CH + part * few + at * step_pairs + i
                halves.append(
                    jnp.concatenate(
                        [
                            rows_ref[side, pl.ds(first, FR, stride=parities * BAND_CH), :]
                            for side in range(FSUB // LANES)
                        ],
                        axis=1,
                    )
                )
            real, imag = halves
            both = jnp.concatenate([real, imag], axis=0)
            turned = jnp.concatenate([-imag, real], axis=0)
            right = jnp.concatenate([both, turned], axis=1).astype(jnp.bfloat16)
            operands.append((both.astype(jnp.bfloat16).T, right))
        outs = [
            jnp.dot(left, right, preferred_element_type=jnp.float32)
            for left, right in operands
        ]
        for (i, p), out in zip(todo, outs):
            out = out * (1.0 / FR)
            vis_ref[i, p, 0] = out[:, :FSUB]
            vis_ref[i, p, 1] = out[:, FSUB:]

    every = [(i, p) for i in range(step_pairs) for p in range(parities)]
    if even_steps:
        begin = len(runs) * steps - even_steps

        @pl.when(g < begin)
        def _():
            correlate(every)

        @pl.when(g >= begin)
        def _():
            correlate([(i, p) for i, p in every if p == 0])

    else:
        correlate(every)


def receive_call(z, chunk, parity, arrived, keys, vis, even_last=False):
    parities = 2 if parity is None else 1
    step_pairs = 4 // parities
    steps = BAND_CH // 2 // step_pairs
    at = 0 if parity is None else parity
    out_shape = jax.ShapeDtypeStruct((z.chan_dev // 2, 2, 2, FSUB, FSUB), jnp.float32)
    arrays = []
    runs = []
    for one in arrived:
        runs.append([])
        for got, first, count, place in one:
            if not any(got is x for x in arrays):
                arrays.append(got)
            index = [got is x for x in arrays].index(True)
            runs[-1].append((index, first, count, place))
    units = parities * z.quads
    slots = min(2, len(runs))
    operands = arrays + [keys]
    in_specs = [pl.BlockSpec(memory_space=pl.ANY)] * len(arrays) + [whole_spec(keys.shape)]
    aliases = {}
    if vis is not None:
        in_specs.append(pl.BlockSpec(memory_space=pl.ANY))
        aliases = {len(operands): 0}
        operands.append(vis)
    share = parities * len(runs)
    return pl.pallas_call(
        functools.partial(
            receive_kernel, z, parities, step_pairs, runs, len(arrays), steps if even_last else 0
        ),
        grid=(len(runs) * steps,),
        in_specs=in_specs,
        out_specs=pl.BlockSpec(
            (step_pairs, parities, 2, FSUB, FSUB),
            lambda g: (chunk * steps + g, at, 0, 0, 0),
        ),
        out_shape=out_shape,
        input_output_aliases=aliases,
        scratch_shapes=[
            pltpu.VMEM((slots, z.devices, units, BAND_CH, LANES), jnp.bfloat16),
            pltpu.VMEM((FSUB // LANES, z.lane_frames * units * BAND_CH, LANES), jnp.float32),
            pltpu.SemaphoreType.DMA((slots, max(len(x) for x in runs))),
        ],
        compiler_params=pltpu.CompilerParams(vmem_limit_bytes=VMEM // 2),
        cost_estimate=pl.CostEstimate(
            flops=2_000_000_000 * share, bytes_accessed=5_000_000 * share, transcendentals=0
        ),
        name="correlate",
    )(*operands)


def beam_kernel(z, me_ref, *refs):
    spec_refs = refs[: z.chunks]
    cos_base, sin_base, cos_step, sin_step, sum_ref, out_ref, prod_ref, row_ref = refs[z.chunks :]
    count = z.chan_dev
    weights = []
    for g in range(BEAMS):
        c0, s0 = cos_base[0, g : g + 1, :], sin_base[0, g : g + 1, :]
        c1, s1 = cos_step[g], sin_step[g]
        weights.append(
            ((c0 * c1 - s0 * s1).astype(jnp.bfloat16), (s0 * c1 + c0 * s1).astype(jnp.bfloat16))
        )
    for q in range(z.quads):
        lanes = slice(q * z.width, (q + 1) * z.width)
        x = [ref[:, lanes] for ref in spec_refs]
        real = jnp.concatenate([v[:BAND_CH] for v in x], axis=0)
        imag = jnp.concatenate([v[BAND_CH:] for v in x], axis=0)
        for g in range(BEAMS):
            c, s = weights[g]
            pair = (c * real + s * imag, c * imag - s * real)
            for part in range(2):
                row = (part * BEAMS + g) * count
                both = pair[part][:, :LANES] + pair[part][:, LANES:]
                prod_ref[row : row + count, q * LANES : (q + 1) * LANES] = both
    sums = jnp.dot(prod_ref[...], sum_ref[...], preferred_element_type=jnp.float32)
    sums = sums * (1.0 / np.sqrt(F))
    few = BAND_CH // 2
    for j in range(2 * BEAMS):
        for i in range(count // few):
            first = i // 2 * BAND_CH + i % 2
            top = j * count + i * few
            row_ref[j, pl.ds(first, few, stride=2), :] = sums[top : top + few]
        out_ref[0, :, j * FR : (j + 1) * FR] = row_ref[j][:, :FR]


def beam_call(z, me, spectra, delays):
    bits = z.devices.bit_length() - 1
    lanes = FR * z.feed_dev
    halves = delays.reshape(BEAMS, 2, 1, z.cap)
    spread = jnp.broadcast_to(halves, (BEAMS, 2, z.lane_frames, z.cap)).reshape(BEAMS, z.width)
    unit = 2.0 * jnp.pi / NFFT
    owners = jnp.arange(z.devices, dtype=jnp.int32).astype(jnp.float32) * z.chan_dev
    inner = np.arange(z.chunks)[:, None] * BAND_CH + ORDER[None, :]
    inner = jnp.asarray(inner.reshape(-1).astype(np.float32))
    base = unit * (spread[None, :, :] * owners[:, None, None])
    step = unit * (spread[:, None, :] * inner[None, :, None])
    frame = (np.arange(FR * z.cap) // LANES) * z.lane_frames
    frame = frame + (np.arange(FR * z.cap) % LANES) // z.cap
    sums = (frame[:, None] == np.arange(LANES)[None, :]).astype(ml_dtypes.bfloat16)

    def owner(j, me_ref):
        k = 0
        for b in range(bits):
            k = k | (((j >> b) & 1) << (bits - 1 - b))
        return me_ref[0] ^ k

    base_spec = pl.BlockSpec(
        (1, BEAMS, z.width), lambda j, me_ref: (owner(j, me_ref), 0, 0)
    )
    grid_spec = pltpu.PrefetchScalarGridSpec(
        num_scalar_prefetch=1,
        grid=(z.devices,),
        in_specs=[
            pl.BlockSpec((z.rows_dev, lanes), lambda j, me_ref: (owner(j, me_ref), 0))
            for _ in range(z.chunks)
        ]
        + [base_spec, base_spec, whole_spec(step.shape), whole_spec(step.shape)]
        + [whole_spec(sums.shape)],
        out_specs=pl.BlockSpec(
            (1, z.chan_dev, 2 * BEAMS * FR), lambda j, me_ref: (j, 0, 0)
        ),
        scratch_shapes=[
            pltpu.VMEM((2 * BEAMS * z.chan_dev, FR * z.cap), jnp.bfloat16),
            pltpu.VMEM((2 * BEAMS, z.chan_dev, LANES), jnp.float32),
        ],
    )
    return pl.pallas_call(
        functools.partial(beam_kernel, z),
        grid_spec=grid_spec,
        out_shape=jax.ShapeDtypeStruct((z.devices, z.chan_dev, 2 * BEAMS * FR), jnp.float32),
        compiler_params=pltpu.CompilerParams(vmem_limit_bytes=VMEM),
        cost_estimate=pl.CostEstimate(
            flops=20_000_000_000, bytes_accessed=20_000_000, transcendentals=0
        ),
        name="beam_sums",
    )(
        me, *spectra, jnp.cos(base), jnp.sin(base), jnp.cos(step), jnp.sin(step),
        jnp.asarray(sums),
    )


def swap(z, x, offset):
    return lax.ppermute(x, "chan", [(i, i ^ offset) for i in range(z.devices)])


def exchange(x):
    return lax.all_to_all(x, "chan", split_axis=0, concat_axis=0, tiled=True)


def on_device(voltages, delays, band_feeds):
    z = Sizes(lax.axis_size("chan"), voltages.shape[0])
    me = lax.axis_index("chan")
    me_array = me.astype(jnp.int32).reshape(1)

    own = lax.dynamic_slice_in_dim(band_feeds, me * z.bands_here, z.bands_here, 0)
    source = own // z.feed_dev
    before = jnp.sum(
        (own[:, None, :] < (source * z.feed_dev)[:, :, None]).astype(jnp.int32), axis=2
    )
    place = jnp.arange(FSUB, dtype=jnp.int32)[None, :] - before
    tau = jnp.arange(z.lane_frames, dtype=jnp.int32)
    big = (source // z.lane_frames) * LANES + place
    group = (source % z.lane_frames)[:, None, :] ^ tau[None, :, None]
    take_key = big[:, None, :] + z.cap * group

    calls = Spectra(z, me_array, voltages, band_feeds)
    early = list(range(z.early))
    basis = calls.basis(early)
    share = 2 * z.step_quads
    step = z.early * share
    arrived = [[] for _ in range(z.chunks)]
    steps = z.parts[0]
    filt, *spectra, send = calls.first(0, steps, early, basis, steps * step, [])
    got = exchange(send)
    for c in early:
        arrived[c] += [(got, g * step + c * share, share, g * share) for g in range(steps)]
    if len(z.parts) > 1:
        begin, steps = steps, z.parts[1]
        base = steps * step
        begun = 3 * z.step_quads
        filt, *spectra, send = calls.first(
            begin, steps, early, basis, base + z.steps * begun, [filt, *spectra]
        )
        *more, send, last = calls.next([z.chunks - 2, z.chunks - 1], filt, send)
        spectra = spectra + more
        got = exchange(send)
        for c in early:
            arrived[c] += [
                (got, g * step + c * share, share, (begin + g) * share) for g in range(steps)
            ]
        for g in range(z.steps):
            first = base + g * begun
            arrived[-2].append((got, first, share, g * share))
            arrived[-1] += [
                (got, first + share + q, 1, g * share + 2 * q) for q in range(z.step_quads)
            ]

    beams, bit = beam_call(z, me_array, spectra, delays), 1
    while beams.shape[0] > 1:
        half = beams.shape[0] // 2
        away = beams[half:].astype(jnp.bfloat16) if half == 1 else beams[half:]
        beams, bit = beams[:half] + swap(z, away, bit).astype(jnp.float32), 2 * bit
    if len(z.parts) > 1:
        last, beams = lax.optimization_barrier((last, beams))
        got = exchange(last)
        k = z.chunks - 1
        vis = receive_call(z, 0, None, arrived, take_key, None, even_last=True)
        vis = receive_call(z, k, 1, [[(got, 0, z.quads, 0)]], take_key[k:], vis)
    else:
        vis = receive_call(z, 0, None, arrived, take_key, None)
    beams = beams.reshape(z.chan_dev, 2 * BEAMS * FR)
    return (vis.reshape(z.chan_dev, 2, FSUB, FSUB), beams)


def solution(mesh):
    in_specs = (P(("grp", "chan"), None), P(None, ("grp", "chan")), P())
    out_specs = (P(("grp", "chan"), None, None, None), P(("grp", "chan"), None))
    return jax.shard_map(
        on_device, mesh=mesh, in_specs=in_specs, out_specs=out_specs, check_vma=False
    )
```

```python
import functools

import jax
import jax.numpy as jnp
import ml_dtypes
import numpy as np
from jax import lax
from jax.experimental import pallas as pl
from jax.experimental.pallas import tpu as pltpu
from jax.sharding import PartitionSpec as P

F = 1024
CHANNELS = 1024
TAPS = 4
BAND_CH = 16
BEAMS = 4
FR = 48
NFFT = 2048
BANDS = 64
FSUB = 256
LANES = 128
VMEM = 56 * 1024 * 1024

NT = (((1,), (1,)), ((), ()))


def fir_window():
    ids = np.arange(TAPS * NFFT, dtype=np.float64)
    centered = (ids - 0.5 * TAPS * NFFT + 0.5) / NFFT
    hann_part = 0.5 - 0.5 * np.cos(2.0 * np.pi * (ids + 0.5) / (TAPS * NFFT))
    return (np.sinc(centered) * hann_part).reshape(TAPS, NFFT)


ORDER = np.concatenate([np.arange(0, BAND_CH, 2), np.arange(1, BAND_CH, 2)])


def dft_rows(chan_ids):
    m = np.arange(NFFT // 2, dtype=np.int64)
    turns = (chan_ids[..., None].astype(np.int64) * m) % NFFT
    table = 2.0 * np.pi * np.arange(NFFT) / NFFT
    cosine = np.cos(table).astype(np.float32).astype(ml_dtypes.bfloat16)
    sine = (-np.sin(table)).astype(np.float32).astype(ml_dtypes.bfloat16)
    return np.stack([cosine[turns], sine[turns]], axis=1)


class Sizes:
    def __init__(self, devices, feed_dev):
        self.devices = devices
        self.feed_dev = feed_dev
        self.cap = feed_dev // 2
        self.lane_frames = LANES // self.cap
        self.quads = FR // self.lane_frames
        self.width = self.lane_frames * feed_dev
        self.steps = 6 if self.quads % 6 == 0 else self.quads
        self.step_frames = FR // self.steps
        self.step_quads = self.quads // self.steps
        self.step_lanes = self.step_frames * feed_dev
        self.chan_dev = CHANNELS // devices
        self.bands_here = BANDS // devices
        self.chunks = self.chan_dev // BAND_CH
        self.rows_dev = 2 * BAND_CH
        self.rows = devices * self.rows_dev
        self.groups = devices // self.lane_frames
        self.early = min(2, self.chunks)
        if self.chunks == 4:
            self.parts = (self.steps // 2, self.steps - self.steps // 2)
        else:
            self.early, self.parts = self.chunks, (self.steps,)


def find_places(z, me, lists):
    base = me * z.feed_dev
    first = jnp.sum((lists < base).astype(jnp.int32), axis=1, keepdims=True)
    lane = lax.broadcasted_iota(jnp.int32, (lists.shape[0], LANES), 1)
    at = first + lane % z.cap
    parts = []
    for side in range(FSUB // LANES):
        index = jnp.clip(at - side * LANES, 0, LANES - 1)
        half = lists[:, side * LANES : (side + 1) * LANES]
        parts.append(jnp.take_along_axis(half, index, axis=1, mode="promise_in_bounds"))
    loc = jnp.where(at < LANES, parts[0], parts[1]) - base
    return jnp.clip(loc, 0, z.feed_dev - 1)


def emit_spectra(z, scale, chunk, me_ref, spectra, loc_ref, spec_ref, sends):
    lane = lax.broadcasted_iota(jnp.int32, (z.rows_dev, LANES), 1)
    frame = (lane // z.cap) ^ (me_ref[0] % z.lane_frames)
    start = frame * z.cap
    few = BAND_CH // 2
    for owner in range(z.devices):
        top = owner * BAND_CH
        rows = [x[top + p : top + p + few] for p in (0, few) for x in spectra]
        rows = jnp.concatenate(rows, axis=0) * scale
        spec_ref[owner * z.rows_dev : (owner + 1) * z.rows_dev, :] = rows.astype(jnp.bfloat16)
        band = owner * z.bands_here + chunk
        loc = loc_ref[band : band + 1, :]
        index = start + loc % z.cap
        lower = jnp.broadcast_to(loc, index.shape) < z.cap
        for q in range(z.step_quads):
            parts = []
            for side in range(2):
                left = q * z.width + side * LANES
                parts.append(
                    jnp.take_along_axis(
                        rows[:, left : left + LANES], index, axis=1, mode="promise_in_bounds"
                    )
                )
            picked = jnp.where(lower, parts[0], parts[1])
            for parity, (send_ref, unit, stride) in enumerate(sends):
                half = [
                    picked[p * BAND_CH + parity * few : p * BAND_CH + parity * few + few]
                    for p in range(2)
                ]
                half = jnp.concatenate(half, axis=0).astype(jnp.bfloat16)
                send_ref[owner, unit + q * stride] = half


def product(z, basis_ref, parity, c, begin, end, samples):
    rows = slice(c * z.rows // 2, (c + 1) * z.rows // 2)
    return lax.dot_general(
        basis_ref[parity, rows, begin:end], samples, NT, preferred_element_type=jnp.float32
    )


def filter_tile(z, main_ref, halo, win_ref, off, f0):
    lanes = slice(off, off + LANES)
    taps = [win_ref[k : k + 1, lanes] for k in range(TAPS)]
    frames = []
    for t in range(z.step_frames + TAPS - 1):
        if t < z.step_frames:
            x = main_ref[f0 : f0 + 16, t * NFFT + off : t * NFFT + off + LANES]
        else:
            x = halo[t - z.step_frames][f0 : f0 + 16, lanes]
        frames.append(x.astype(jnp.float32))
    totals = []
    for t in range(z.step_frames):
        total = taps[0] * frames[t]
        for k in range(1, TAPS):
            total = total + taps[k] * frames[t + k]
        totals.append(total)
    if z.cap < 16:
        totals = [
            jnp.concatenate([totals[t][h : h + 8], totals[t + 1][h : h + 8]], axis=0)
            for t in range(0, z.step_frames, 2)
            for h in (0, 8)
        ]
    out = []
    for i, total in enumerate(totals):
        if z.cap < 16:
            t, half, feed = 2 * (i // 2), i % 2, 0
        else:
            t, half, feed = i, f0 // z.cap, f0 % z.cap
        row = (t // z.lane_frames) * z.width + half * LANES
        row += (t % z.lane_frames) * z.cap + feed
        out.append((row, total.astype(jnp.bfloat16)))
    return out


def filter_fold(z, main_ref, halo, win_ref, filt_ref, off):
    far = off + NFFT // 2
    folded = {}
    for f0 in range(0, z.feed_dev, 16):
        low = filter_tile(z, main_ref, halo, win_ref, off, f0)
        high = filter_tile(z, main_ref, halo, win_ref, far, f0)
        for (row, a), (_, b) in zip(low, high):
            folded[row] = (a + b, a - b)
            filt_ref[row : row + 16, off : off + LANES] = folded[row][0]
            filt_ref[row : row + 16, far : far + LANES] = folded[row][1]
    return [
        jnp.concatenate([folded[row][parity] for row in sorted(folded)], axis=0)
        for parity in range(2)
    ]


def first_kernel(
    z, scale, chunks, held, me_ref, main_ref, h0_ref, h1_ref, h2_ref, win_ref, basis_ref,
    lists_ref, *refs,
):
    filt_ref, spec_refs, send_ref, loc_ref = refs[held], refs[held + 1 : -2], refs[-2], refs[-1]
    halo = (h0_ref, h1_ref, h2_ref)
    loc_ref[...] = find_places(z, me_ref[0], lists_ref[...])
    piece = 512
    count = len(chunks)
    spectra = [[None, None] for _ in chunks]
    for off in range(0, NFFT // 2, piece):
        tiles = [
            filter_fold(z, main_ref, halo, win_ref, filt_ref, tile)
            for tile in range(off, off + piece, LANES)
        ]
        for parity in range(2):
            samples = jnp.concatenate([tile[parity] for tile in tiles], axis=1)
            for c in range(count):
                part = product(z, basis_ref, parity, c, off, off + piece, samples)
                old = spectra[c][parity]
                spectra[c][parity] = part if old is None else old + part
    for c, chunk in enumerate(chunks):
        unit = c * 2 * z.step_quads
        sends = [(send_ref, unit, 2), (send_ref, unit + 1, 2)]
        emit_spectra(z, scale, chunk, me_ref, spectra[c], loc_ref, spec_refs[c], sends)


def next_kernel(z, scale, chunks, me_ref, filt_ref, basis_ref, lists_ref, held_ref, *refs):
    begun_ref, last_ref, loc_ref = refs[2], refs[3], refs[-1]
    loc_ref[...] = find_places(z, me_ref[0], lists_ref[...])
    half = NFFT // 2
    spectra = [
        [
            product(z, basis_ref, p, c, 0, half, filt_ref[:, p * half : (p + 1) * half])
            for p in range(2)
        ]
        for c in range(2)
    ]
    sends = [
        [(begun_ref, 0, 2), (begun_ref, 1, 2)],
        [(begun_ref, 2 * z.step_quads, 1), (last_ref, 0, 1)],
    ]
    for c, chunk in enumerate(chunks):
        emit_spectra(z, scale, chunk, me_ref, spectra[c], loc_ref, refs[c], sends[c])


def whole_spec(shape):
    return pl.BlockSpec(shape, lambda *g: (0,) * len(shape))


class Spectra:

    def __init__(self, z, me, voltages, band_feeds):
        window = fir_window()
        self.z = z
        self.me = me
        self.scale = float(np.sqrt(2.0 / np.sum(window * window)))
        self.window = jnp.asarray(window.astype(np.float32))
        self.voltages = voltages
        self.lists = band_feeds
        self.ids = np.arange(CHANNELS).reshape(z.devices, z.chunks, BAND_CH)
        self.me_spec = pl.BlockSpec(memory_space=pltpu.SMEM)
        self.spec_shape = jax.ShapeDtypeStruct((z.rows, FR * z.feed_dev), jnp.bfloat16)
        self.filt_shape = jax.ShapeDtypeStruct((FR * z.feed_dev, NFFT), jnp.bfloat16)

    def basis(self, chunks):
        sides = []
        for parity in range(2):
            rows = [dft_rows(self.ids[:, k, parity::2].reshape(-1)) for k in chunks]
            rows = np.stack(rows).reshape(len(chunks), self.z.devices, BAND_CH // 2, 2, -1)
            rows = np.transpose(rows, (0, 1, 3, 2, 4))
            sides.append(rows.reshape(len(chunks) * self.z.rows // 2, NFFT // 2))
        return jnp.asarray(np.stack(sides))

    def message(self, units):
        return jax.ShapeDtypeStruct((self.z.devices, units, BAND_CH, LANES), jnp.bfloat16)

    def common(self, steps, chunks):
        z = self.z
        flops = len(chunks) * z.rows * NFFT * z.step_lanes * steps
        return dict(
            grid=(steps,),
            scratch_shapes=[pltpu.VMEM((BANDS, LANES), jnp.int32)],
            compiler_params=pltpu.CompilerParams(vmem_limit_bytes=VMEM),
            cost_estimate=pl.CostEstimate(
                flops=flops, bytes_accessed=3_000_000 * steps, transcendentals=0
            ),
        )

    def first(self, begin, steps, chunks, basis, units, held):
        z = self.z
        count = len(chunks)

        def halo_spec(h):
            return pl.BlockSpec(
                (z.feed_dev, NFFT), lambda g: (0, z.step_frames * (begin + g + 1) + h)
            )

        send_block = (z.devices, count * 2 * z.step_quads, BAND_CH, LANES)
        operands = [self.me] + [self.voltages] * 4 + [self.window, basis, self.lists]
        aliases = {len(operands) + i: i for i in range(len(held))}
        return pl.pallas_call(
            functools.partial(first_kernel, z, self.scale, chunks, len(held)),
            in_specs=[
                self.me_spec,
                pl.BlockSpec((z.feed_dev, z.step_frames * NFFT), lambda g: (0, begin + g)),
                halo_spec(0),
                halo_spec(1),
                halo_spec(2),
                whole_spec((TAPS, NFFT)),
                whole_spec(basis.shape),
                whole_spec(self.lists.shape),
            ]
            + [pl.BlockSpec(memory_space=pl.ANY)] * len(held),
            out_specs=[
                pl.BlockSpec((z.step_lanes, NFFT), lambda g: (begin + g, 0)),
            ]
            + [pl.BlockSpec((z.rows, z.step_lanes), lambda g: (0, begin + g))] * count
            + [pl.BlockSpec(send_block, lambda g: (0, g, 0, 0))],
            out_shape=[self.filt_shape] + [self.spec_shape] * count + [self.message(units)],
            input_output_aliases=aliases,
            name="filter_spectra",
            **self.common(steps, chunks),
        )(*operands, *held)

    def next(self, chunks, filt, held):
        z = self.z
        basis = self.basis(chunks)
        begun = 3 * z.step_quads
        base = held.shape[1] // begun - z.steps
        operands = [self.me, filt, basis, self.lists, held]
        return pl.pallas_call(
            functools.partial(next_kernel, z, self.scale, chunks),
            in_specs=[
                self.me_spec,
                pl.BlockSpec((z.step_lanes, NFFT), lambda g: (g, 0)),
                whole_spec(basis.shape),
                whole_spec(self.lists.shape),
                pl.BlockSpec(memory_space=pl.ANY),
            ],
            out_specs=[pl.BlockSpec((z.rows, z.step_lanes), lambda g: (0, g))] * 2
            + [
                pl.BlockSpec((z.devices, begun, BAND_CH, LANES), lambda g: (0, base + g, 0, 0)),
                pl.BlockSpec((z.devices, z.step_quads, BAND_CH, LANES), lambda g: (0, g, 0, 0)),
            ],
            out_shape=[self.spec_shape] * 2
            + [self.message(held.shape[1]), self.message(z.quads)],
            input_output_aliases={4: 2},
            name="spectra_next",
            **self.common(z.steps, chunks),
        )(*operands)


def receive_kernel(z, parities, step_pairs, runs, arrays, even_steps, *refs):
    arr_refs, key_ref = refs[:arrays], refs[arrays]
    vis_ref, buf_ref, rows_ref, pick_ref, sems = refs[-5:]
    g = pl.program_id(0)
    lf = z.lane_frames
    few = BAND_CH // 2
    steps = few // step_pairs
    depth = buf_ref.shape[2] * BAND_CH
    slots = buf_ref.shape[0]
    at = g % steps

    def copies(c):
        return [
            pltpu.make_async_copy(
                arr_refs[array].at[:, first : first + count],
                buf_ref.at[c % slots, :, place : place + count],
                sems.at[c % slots, i],
            )
            for i, (array, first, count, place) in enumerate(runs[c])
        ]

    @pl.when(g == 0)
    def _():
        for copy in copies(0):
            copy.start()

    @pl.when(at == 0)
    def _():
        slot = lax.broadcasted_iota(jnp.int32, (z.groups * LANES, FSUB), 0)
        for tau in range(lf):
            key = key_ref[g // steps, tau : tau + 1, :]
            pick_ref[tau] = jnp.where(slot == key, 1.0, 0.0).astype(jnp.bfloat16)

    for c in range(len(runs)):

        @pl.when(g == c * steps)
        def _():
            for copy in copies(c):
                copy.wait()
            if c + 1 < len(runs):
                for copy in copies(c + 1):
                    copy.start()

    @pl.when(at == 0)
    def _():
        c = g // steps
        lane_group = lax.broadcasted_iota(jnp.int32, (depth, LANES), 1) // z.cap
        for tau in range(lf):
            tiles = []
            for big in range(z.groups):
                tile = buf_ref[c % slots, big * lf + tau].reshape(depth, LANES)
                for lane in range(1, lf):
                    block = buf_ref[c % slots, big * lf + (lane ^ tau)].reshape(depth, LANES)
                    tile = jnp.where(lane_group == lane, block, tile)
                tiles.append(tile)
            rows = jnp.dot(
                jnp.concatenate(tiles, axis=1), pick_ref[tau], preferred_element_type=jnp.float32
            )
            for side in range(FSUB // LANES):
                rows_ref[side, tau * depth : (tau + 1) * depth, :] = rows[
                    :, side * LANES : (side + 1) * LANES
                ]

    def correlate(todo):
        operands = []
        for i, p in todo:
            halves = []
            for part in range(2):
                first = p * BAND_CH + part * few + at * step_pairs + i
                halves.append(
                    jnp.concatenate(
                        [
                            rows_ref[side, pl.ds(first, FR, stride=parities * BAND_CH), :]
                            for side in range(FSUB // LANES)
                        ],
                        axis=1,
                    )
                )
            real, imag = halves
            both = jnp.concatenate([real, imag], axis=0)
            turned = jnp.concatenate([-imag, real], axis=0)
            right = jnp.concatenate([both, turned], axis=1).astype(jnp.bfloat16)
            operands.append((both.astype(jnp.bfloat16).T, right))
        outs = [
            jnp.dot(left, right, preferred_element_type=jnp.float32)
            for left, right in operands
        ]
        for (i, p), out in zip(todo, outs):
            out = out * (1.0 / FR)
            vis_ref[i, p, 0] = out[:, :FSUB]
            vis_ref[i, p, 1] = out[:, FSUB:]

    every = [(i, p) for i in range(step_pairs) for p in range(parities)]
    if even_steps:
        begin = len(runs) * steps - even_steps

        @pl.when(g < begin)
        def _():
            correlate(every)

        @pl.when(g >= begin)
        def _():
            correlate([(i, p) for i, p in every if p == 0])

    else:
        correlate(every)


def receive_call(z, chunk, parity, arrived, keys, vis, even_last=False):
    parities = 2 if parity is None else 1
    step_pairs = 4
    steps = BAND_CH // 2 // step_pairs
    at = 0 if parity is None else parity
    out_shape = jax.ShapeDtypeStruct((z.chan_dev // 2, 2, 2, FSUB, FSUB), jnp.float32)
    arrays = []
    runs = []
    for one in arrived:
        runs.append([])
        for got, first, count, place in one:
            if not any(got is x for x in arrays):
                arrays.append(got)
            index = [got is x for x in arrays].index(True)
            runs[-1].append((index, first, count, place))
    units = parities * z.quads
    slots = min(2, len(runs))
    operands = arrays + [keys]
    in_specs = [pl.BlockSpec(memory_space=pl.ANY)] * len(arrays) + [whole_spec(keys.shape)]
    aliases = {}
    if vis is not None:
        in_specs.append(pl.BlockSpec(memory_space=pl.ANY))
        aliases = {len(operands): 0}
        operands.append(vis)
    share = parities * len(runs)
    return pl.pallas_call(
        functools.partial(
            receive_kernel, z, parities, step_pairs, runs, len(arrays), steps if even_last else 0
        ),
        grid=(len(runs) * steps,),
        in_specs=in_specs,
        out_specs=pl.BlockSpec(
            (step_pairs, parities, 2, FSUB, FSUB),
            lambda g: (chunk * steps + g, at, 0, 0, 0),
        ),
        out_shape=out_shape,
        input_output_aliases=aliases,
        scratch_shapes=[
            pltpu.VMEM((slots, z.devices, units, BAND_CH, LANES), jnp.bfloat16),
            pltpu.VMEM((FSUB // LANES, z.lane_frames * units * BAND_CH, LANES), jnp.float32),
            pltpu.VMEM((z.lane_frames, z.groups * LANES, FSUB), jnp.bfloat16),
            pltpu.SemaphoreType.DMA((slots, max(len(x) for x in runs))),
        ],
        compiler_params=pltpu.CompilerParams(vmem_limit_bytes=VMEM // 2),
        cost_estimate=pl.CostEstimate(
            flops=2_000_000_000 * share, bytes_accessed=5_000_000 * share, transcendentals=0
        ),
        name="correlate",
    )(*operands)


def beam_kernel(z, me_ref, *refs):
    spec_refs = refs[: z.chunks]
    cos_base, sin_base, cos_step, sin_step, sum_ref, out_ref, prod_ref, row_ref = refs[z.chunks :]
    count = z.chan_dev
    weights = []
    for g in range(BEAMS):
        c0, s0 = cos_base[0, g : g + 1, :], sin_base[0, g : g + 1, :]
        c1, s1 = cos_step[g], sin_step[g]
        weights.append(
            ((c0 * c1 - s0 * s1).astype(jnp.bfloat16), (s0 * c1 + c0 * s1).astype(jnp.bfloat16))
        )
    for q in range(z.quads):
        lanes = slice(q * z.width, (q + 1) * z.width)
        x = [ref[:, lanes] for ref in spec_refs]
        real = jnp.concatenate([v[:BAND_CH] for v in x], axis=0)
        imag = jnp.concatenate([v[BAND_CH:] for v in x], axis=0)
        for g in range(BEAMS):
            c, s = weights[g]
            pair = (c * real + s * imag, c * imag - s * real)
            for part in range(2):
                row = (part * BEAMS + g) * count
                both = pair[part][:, :LANES] + pair[part][:, LANES:]
                prod_ref[row : row + count, q * LANES : (q + 1) * LANES] = both
    sums = jnp.dot(prod_ref[...], sum_ref[...], preferred_element_type=jnp.float32)
    sums = sums * (1.0 / np.sqrt(F))
    few = BAND_CH // 2
    for j in range(2 * BEAMS):
        for i in range(count // few):
            first = i // 2 * BAND_CH + i % 2
            top = j * count + i * few
            row_ref[j, pl.ds(first, few, stride=2), :] = sums[top : top + few]
        out_ref[0, :, j * FR : (j + 1) * FR] = row_ref[j][:, :FR]


def beam_call(z, me, spectra, delays):
    bits = z.devices.bit_length() - 1
    lanes = FR * z.feed_dev
    halves = delays.reshape(BEAMS, 2, 1, z.cap)
    spread = jnp.broadcast_to(halves, (BEAMS, 2, z.lane_frames, z.cap)).reshape(BEAMS, z.width)
    unit = 2.0 * jnp.pi / NFFT
    owners = jnp.arange(z.devices, dtype=jnp.int32).astype(jnp.float32) * z.chan_dev
    inner = np.arange(z.chunks)[:, None] * BAND_CH + ORDER[None, :]
    inner = jnp.asarray(inner.reshape(-1).astype(np.float32))
    base = unit * (spread[None, :, :] * owners[:, None, None])
    step = unit * (spread[:, None, :] * inner[None, :, None])
    frame = (np.arange(FR * z.cap) // LANES) * z.lane_frames
    frame = frame + (np.arange(FR * z.cap) % LANES) // z.cap
    sums = (frame[:, None] == np.arange(LANES)[None, :]).astype(ml_dtypes.bfloat16)

    def owner(j, me_ref):
        k = 0
        for b in range(bits):
            k = k | (((j >> b) & 1) << (bits - 1 - b))
        return me_ref[0] ^ k

    base_spec = pl.BlockSpec(
        (1, BEAMS, z.width), lambda j, me_ref: (owner(j, me_ref), 0, 0)
    )
    grid_spec = pltpu.PrefetchScalarGridSpec(
        num_scalar_prefetch=1,
        grid=(z.devices,),
        in_specs=[
            pl.BlockSpec((z.rows_dev, lanes), lambda j, me_ref: (owner(j, me_ref), 0))
            for _ in range(z.chunks)
        ]
        + [base_spec, base_spec, whole_spec(step.shape), whole_spec(step.shape)]
        + [whole_spec(sums.shape)],
        out_specs=pl.BlockSpec(
            (1, z.chan_dev, 2 * BEAMS * FR), lambda j, me_ref: (j, 0, 0)
        ),
        scratch_shapes=[
            pltpu.VMEM((2 * BEAMS * z.chan_dev, FR * z.cap), jnp.bfloat16),
            pltpu.VMEM((2 * BEAMS, z.chan_dev, LANES), jnp.float32),
        ],
    )
    return pl.pallas_call(
        functools.partial(beam_kernel, z),
        grid_spec=grid_spec,
        out_shape=jax.ShapeDtypeStruct((z.devices, z.chan_dev, 2 * BEAMS * FR), jnp.float32),
        compiler_params=pltpu.CompilerParams(vmem_limit_bytes=VMEM),
        cost_estimate=pl.CostEstimate(
            flops=20_000_000_000, bytes_accessed=20_000_000, transcendentals=0
        ),
        name="beam_sums",
    )(
        me, *spectra, jnp.cos(base), jnp.sin(base), jnp.cos(step), jnp.sin(step),
        jnp.asarray(sums),
    )


def swap(z, x, offset):
    return lax.ppermute(x, "chan", [(i, i ^ offset) for i in range(z.devices)])


def exchange(x):
    return lax.all_to_all(x, "chan", split_axis=0, concat_axis=0, tiled=True)


def on_device(voltages, delays, band_feeds):
    z = Sizes(lax.axis_size("chan"), voltages.shape[0])
    me = lax.axis_index("chan")
    me_array = me.astype(jnp.int32).reshape(1)

    own = lax.dynamic_slice_in_dim(band_feeds, me * z.bands_here, z.bands_here, 0)
    source = own // z.feed_dev
    before = jnp.sum(
        (own[:, None, :] < (source * z.feed_dev)[:, :, None]).astype(jnp.int32), axis=2
    )
    place = jnp.arange(FSUB, dtype=jnp.int32)[None, :] - before
    tau = jnp.arange(z.lane_frames, dtype=jnp.int32)
    big = (source // z.lane_frames) * LANES + place
    group = (source % z.lane_frames)[:, None, :] ^ tau[None, :, None]
    take_key = big[:, None, :] + z.cap * group

    calls = Spectra(z, me_array, voltages, band_feeds)
    early = list(range(z.early))
    basis = calls.basis(early)
    share = 2 * z.step_quads
    step = z.early * share
    arrived = [[] for _ in range(z.chunks)]
    steps = z.parts[0]
    filt, *spectra, send = calls.first(0, steps, early, basis, steps * step, [])
    got = exchange(send)
    for c in early:
        arrived[c] += [(got, g * step + c * share, share, g * share) for g in range(steps)]
    if len(z.parts) > 1:
        begin, steps = steps, z.parts[1]
        base = steps * step
        begun = 3 * z.step_quads
        filt, *spectra, send = calls.first(
            begin, steps, early, basis, base + z.steps * begun, [filt, *spectra]
        )
        *more, send, last = calls.next([z.chunks - 2, z.chunks - 1], filt, send)
        spectra = spectra + more
        got = exchange(send)
        for c in early:
            arrived[c] += [
                (got, g * step + c * share, share, (begin + g) * share) for g in range(steps)
            ]
        for g in range(z.steps):
            first = base + g * begun
            arrived[-2].append((got, first, share, g * share))
            arrived[-1] += [
                (got, first + share + q, 1, g * share + 2 * q) for q in range(z.step_quads)
            ]

    beams, bit = beam_call(z, me_array, spectra, delays), 1
    while beams.shape[0] > 1:
        half = beams.shape[0] // 2
        kept, away = beams[:half], beams[half:]
        if half > 1:
            beams, bit = kept + swap(z, away, bit), 2 * bit
        else:
            beams = away = swap(z, away.astype(jnp.bfloat16), bit)
    if len(z.parts) > 1:
        last, kept, away = lax.optimization_barrier((last, kept, away))
        got = exchange(last)
        k = z.chunks - 1
        vis = receive_call(z, 0, None, arrived, take_key, None, even_last=True)
        vis = receive_call(z, k, 1, [[(got, 0, z.quads, 0)]], take_key[k:], vis)
    else:
        vis = receive_call(z, 0, None, arrived, take_key, None)
    beams = (kept + away.astype(jnp.float32)).reshape(z.chan_dev, 2 * BEAMS * FR)
    return (vis.reshape(z.chan_dev, 2, FSUB, FSUB), beams)


def solution(mesh):
    in_specs = (P(("grp", "chan"), None), P(None, ("grp", "chan")), P())
    out_specs = (P(("grp", "chan"), None, None, None), P(("grp", "chan"), None))
    return jax.shard_map(
        on_device, mesh=mesh, in_specs=in_specs, out_specs=out_specs, check_vma=False
    )
```

```python
import functools

import jax
import jax.numpy as jnp
import ml_dtypes
import numpy as np
from jax import lax
from jax.experimental import pallas as pl
from jax.experimental.pallas import tpu as pltpu
from jax.sharding import PartitionSpec as P

F = 1024
CHANNELS = 1024
TAPS = 4
BAND_CH = 16
BEAMS = 4
FR = 48
NFFT = 2048
BANDS = 64
FSUB = 256
LANES = 128
VMEM = 56 * 1024 * 1024

NT = (((1,), (1,)), ((), ()))


def fir_window():
    ids = np.arange(TAPS * NFFT, dtype=np.float64)
    centered = (ids - 0.5 * TAPS * NFFT + 0.5) / NFFT
    hann_part = 0.5 - 0.5 * np.cos(2.0 * np.pi * (ids + 0.5) / (TAPS * NFFT))
    return (np.sinc(centered) * hann_part).reshape(TAPS, NFFT)


ORDER = np.concatenate([np.arange(0, BAND_CH, 2), np.arange(1, BAND_CH, 2)])


def dft_rows(chan_ids):
    m = np.arange(NFFT // 2, dtype=np.int64)
    turns = (chan_ids[..., None].astype(np.int64) * m) % NFFT
    table = 2.0 * np.pi * np.arange(NFFT) / NFFT
    cosine = np.cos(table).astype(np.float32).astype(ml_dtypes.bfloat16)
    sine = (-np.sin(table)).astype(np.float32).astype(ml_dtypes.bfloat16)
    return np.stack([cosine[turns], sine[turns]], axis=1)


class Sizes:
    def __init__(self, devices, feed_dev):
        self.devices = devices
        self.feed_dev = feed_dev
        self.cap = feed_dev // 2
        self.lane_frames = LANES // self.cap
        self.quads = FR // self.lane_frames
        self.width = self.lane_frames * feed_dev
        self.steps = 6 if self.quads % 6 == 0 else self.quads
        self.step_frames = FR // self.steps
        self.step_quads = self.quads // self.steps
        self.step_lanes = self.step_frames * feed_dev
        self.chan_dev = CHANNELS // devices
        self.bands_here = BANDS // devices
        self.chunks = self.chan_dev // BAND_CH
        self.rows_dev = 2 * BAND_CH
        self.rows = devices * self.rows_dev
        self.groups = devices // self.lane_frames
        self.early = min(2, self.chunks)
        if self.chunks == 4:
            self.parts = (self.steps // 2, self.steps - self.steps // 2)
        else:
            self.early, self.parts = self.chunks, (self.steps,)


def find_places(z, me, lists):
    base = me * z.feed_dev
    first = jnp.sum((lists < base).astype(jnp.int32), axis=1, keepdims=True)
    lane = lax.broadcasted_iota(jnp.int32, (lists.shape[0], LANES), 1)
    at = first + lane % z.cap
    parts = []
    for side in range(FSUB // LANES):
        index = jnp.clip(at - side * LANES, 0, LANES - 1)
        half = lists[:, side * LANES : (side + 1) * LANES]
        parts.append(jnp.take_along_axis(half, index, axis=1, mode="promise_in_bounds"))
    loc = jnp.where(at < LANES, parts[0], parts[1]) - base
    return jnp.clip(loc, 0, z.feed_dev - 1)


def emit_spectra(z, scale, chunk, me_ref, spectra, loc_ref, spec_ref, sends, quads, base=0):
    lane = lax.broadcasted_iota(jnp.int32, (z.rows_dev, LANES), 1)
    frame = (lane // z.cap) ^ (me_ref[0] % z.lane_frames)
    start = frame * z.cap
    few = BAND_CH // 2
    for owner in range(z.devices):
        top = owner * BAND_CH
        rows = [x[top + p : top + p + few] for p in (0, few) for x in spectra]
        rows = jnp.concatenate(rows, axis=0) * scale
        columns = slice(base * z.width, (base + quads) * z.width)
        spec_ref[owner * z.rows_dev : (owner + 1) * z.rows_dev, columns] = rows.astype(
            jnp.bfloat16
        )
        band = owner * z.bands_here + chunk
        loc = loc_ref[band : band + 1, :]
        index = start + loc % z.cap
        lower = jnp.broadcast_to(loc, index.shape) < z.cap
        for q in range(quads):
            parts = []
            for side in range(2):
                left = q * z.width + side * LANES
                parts.append(
                    jnp.take_along_axis(
                        rows[:, left : left + LANES], index, axis=1, mode="promise_in_bounds"
                    )
                )
            picked = jnp.where(lower, parts[0], parts[1])
            for parity, (send_ref, unit, stride) in enumerate(sends):
                half = [
                    picked[p * BAND_CH + parity * few : p * BAND_CH + parity * few + few]
                    for p in range(2)
                ]
                half = jnp.concatenate(half, axis=0).astype(jnp.bfloat16)
                send_ref[owner, unit + (base + q) * stride] = half


def filter_tile(z, main_ref, halo, win_ref, off, f0, begin):
    lanes = slice(off, off + LANES)
    taps = [win_ref[k : k + 1, lanes] for k in range(TAPS)]
    frames = []
    for t in range(begin, begin + z.lane_frames + TAPS - 1):
        if t < z.step_frames:
            x = main_ref[f0 : f0 + 16, t * NFFT + off : t * NFFT + off + LANES]
        else:
            x = halo[t - z.step_frames][f0 : f0 + 16, lanes]
        frames.append(x.astype(jnp.float32))
    totals = []
    for t in range(z.lane_frames):
        total = taps[0] * frames[t]
        for k in range(1, TAPS):
            total = total + taps[k] * frames[t + k]
        totals.append(total)
    if z.cap < 16:
        totals = [
            jnp.concatenate([totals[t][h : h + 8], totals[t + 1][h : h + 8]], axis=0)
            for t in range(0, z.lane_frames, 2)
            for h in (0, 8)
        ]
    out = []
    for i, total in enumerate(totals):
        if z.cap < 16:
            t, half, feed = 2 * (i // 2), i % 2, 0
        else:
            t, half, feed = i, f0 // z.cap, f0 % z.cap
        out.append((half * LANES + t * z.cap + feed, total.astype(jnp.bfloat16)))
    return out


def filter_fold(z, main_ref, halo, win_ref, filt_ref, off, quad):
    far = off + NFFT // 2
    begin = quad * z.lane_frames
    folded = {}
    for f0 in range(0, z.feed_dev, 16):
        low = filter_tile(z, main_ref, halo, win_ref, off, f0, begin)
        high = filter_tile(z, main_ref, halo, win_ref, far, f0, begin)
        for (row, a), (_, b) in zip(low, high):
            folded[row] = (a + b, a - b)
            top = quad * z.width + row
            filt_ref[top : top + 16, off : off + LANES] = folded[row][0]
            filt_ref[top : top + 16, far : far + LANES] = folded[row][1]
    return [
        jnp.concatenate([folded[row][parity] for row in sorted(folded)], axis=0)
        for parity in range(2)
    ]


def product(z, basis_ref, parity, c, samples):
    rows = slice(c * z.rows // 2, (c + 1) * z.rows // 2)
    return lax.dot_general(
        basis_ref[parity, rows, :], samples, NT, preferred_element_type=jnp.float32
    )


def first_kernel(
    z, scale, chunks, held, me_ref, main_ref, h0_ref, h1_ref, h2_ref, win_ref, basis_ref,
    lists_ref, *refs,
):
    filt_ref, spec_refs, send_ref, loc_ref = refs[held], refs[held + 1 : -2], refs[-2], refs[-1]
    halo = (h0_ref, h1_ref, h2_ref)
    loc_ref[...] = find_places(z, me_ref[0], lists_ref[...])

    def emit(quad, spectra):
        for c, chunk in enumerate(chunks):
            unit = c * 2 * z.step_quads
            sends = [(send_ref, unit, 2), (send_ref, unit + 1, 2)]
            emit_spectra(
                z, scale, chunk, me_ref, spectra[c], loc_ref, spec_refs[c], sends, 1, quad
            )

    before = None
    for quad in range(z.step_quads):
        tiles = [
            filter_fold(z, main_ref, halo, win_ref, filt_ref, off, quad)
            for off in range(0, NFFT // 2, LANES)
        ]
        samples = [jnp.concatenate([tile[p] for tile in tiles], axis=1) for p in range(2)]
        if before is not None:
            emit(quad - 1, before)
        before = [
            [product(z, basis_ref, p, c, samples[p]) for p in range(2)]
            for c in range(len(chunks))
        ]
    emit(z.step_quads - 1, before)


def next_kernel(z, scale, chunks, me_ref, filt_ref, basis_ref, lists_ref, held_ref, *refs):
    begun_ref, last_ref, loc_ref = refs[2], refs[3], refs[-1]
    loc_ref[...] = find_places(z, me_ref[0], lists_ref[...])
    half = NFFT // 2
    spectra = [
        [
            product(z, basis_ref, p, c, filt_ref[:, p * half : (p + 1) * half])
            for p in range(2)
        ]
        for c in range(2)
    ]
    sends = [
        [(begun_ref, 0, 2), (begun_ref, 1, 2)],
        [(begun_ref, 2 * z.step_quads, 1), (last_ref, 0, 1)],
    ]
    for c, chunk in enumerate(chunks):
        emit_spectra(
            z, scale, chunk, me_ref, spectra[c], loc_ref, refs[c], sends[c], z.step_quads
        )


def whole_spec(shape):
    return pl.BlockSpec(shape, lambda *g: (0,) * len(shape))


class Spectra:

    def __init__(self, z, me, voltages, band_feeds):
        window = fir_window()
        self.z = z
        self.me = me
        self.scale = float(np.sqrt(2.0 / np.sum(window * window)))
        self.window = jnp.asarray(window.astype(np.float32))
        self.voltages = voltages
        self.lists = band_feeds
        self.ids = np.arange(CHANNELS).reshape(z.devices, z.chunks, BAND_CH)
        self.me_spec = pl.BlockSpec(memory_space=pltpu.SMEM)
        self.spec_shape = jax.ShapeDtypeStruct((z.rows, FR * z.feed_dev), jnp.bfloat16)
        self.filt_shape = jax.ShapeDtypeStruct((FR * z.feed_dev, NFFT), jnp.bfloat16)

    def basis(self, chunks):
        sides = []
        for parity in range(2):
            rows = [dft_rows(self.ids[:, k, parity::2].reshape(-1)) for k in chunks]
            rows = np.stack(rows).reshape(len(chunks), self.z.devices, BAND_CH // 2, 2, -1)
            rows = np.transpose(rows, (0, 1, 3, 2, 4))
            sides.append(rows.reshape(len(chunks) * self.z.rows // 2, NFFT // 2))
        return jnp.asarray(np.stack(sides))

    def message(self, units):
        return jax.ShapeDtypeStruct((self.z.devices, units, BAND_CH, LANES), jnp.bfloat16)

    def common(self, steps, chunks):
        z = self.z
        flops = len(chunks) * z.rows * NFFT * z.step_lanes * steps
        return dict(
            grid=(steps,),
            scratch_shapes=[pltpu.VMEM((BANDS, LANES), jnp.int32)],
            compiler_params=pltpu.CompilerParams(vmem_limit_bytes=VMEM),
            cost_estimate=pl.CostEstimate(
                flops=flops, bytes_accessed=3_000_000 * steps, transcendentals=0
            ),
        )

    def first(self, begin, steps, chunks, basis, units, held):
        z = self.z
        count = len(chunks)

        def halo_spec(h):
            return pl.BlockSpec(
                (z.feed_dev, NFFT), lambda g: (0, z.step_frames * (begin + g + 1) + h)
            )

        send_block = (z.devices, count * 2 * z.step_quads, BAND_CH, LANES)
        operands = [self.me] + [self.voltages] * 4 + [self.window, basis, self.lists]
        aliases = {len(operands) + i: i for i in range(len(held))}
        return pl.pallas_call(
            functools.partial(first_kernel, z, self.scale, chunks, len(held)),
            in_specs=[
                self.me_spec,
                pl.BlockSpec((z.feed_dev, z.step_frames * NFFT), lambda g: (0, begin + g)),
                halo_spec(0),
                halo_spec(1),
                halo_spec(2),
                whole_spec((TAPS, NFFT)),
                whole_spec(basis.shape),
                whole_spec(self.lists.shape),
            ]
            + [pl.BlockSpec(memory_space=pl.ANY)] * len(held),
            out_specs=[
                pl.BlockSpec((z.step_lanes, NFFT), lambda g: (begin + g, 0)),
            ]
            + [pl.BlockSpec((z.rows, z.step_lanes), lambda g: (0, begin + g))] * count
            + [pl.BlockSpec(send_block, lambda g: (0, g, 0, 0))],
            out_shape=[self.filt_shape] + [self.spec_shape] * count + [self.message(units)],
            input_output_aliases=aliases,
            name="filter_spectra",
            **self.common(steps, chunks),
        )(*operands, *held)

    def next(self, chunks, filt, held):
        z = self.z
        basis = self.basis(chunks)
        begun = 3 * z.step_quads
        base = held.shape[1] // begun - z.steps
        operands = [self.me, filt, basis, self.lists, held]
        return pl.pallas_call(
            functools.partial(next_kernel, z, self.scale, chunks),
            in_specs=[
                self.me_spec,
                pl.BlockSpec((z.step_lanes, NFFT), lambda g: (g, 0)),
                whole_spec(basis.shape),
                whole_spec(self.lists.shape),
                pl.BlockSpec(memory_space=pl.ANY),
            ],
            out_specs=[pl.BlockSpec((z.rows, z.step_lanes), lambda g: (0, g))] * 2
            + [
                pl.BlockSpec((z.devices, begun, BAND_CH, LANES), lambda g: (0, base + g, 0, 0)),
                pl.BlockSpec((z.devices, z.step_quads, BAND_CH, LANES), lambda g: (0, g, 0, 0)),
            ],
            out_shape=[self.spec_shape] * 2
            + [self.message(held.shape[1]), self.message(z.quads)],
            input_output_aliases={4: 2},
            name="spectra_next",
            **self.common(z.steps, chunks),
        )(*operands)


def receive_kernel(z, parities, step_pairs, runs, arrays, even_steps, *refs):
    arr_refs, key_ref = refs[:arrays], refs[arrays]
    vis_ref, buf_ref, rows_ref, pick_ref, sems = refs[-5:]
    g = pl.program_id(0)
    lf = z.lane_frames
    few = BAND_CH // 2
    steps = few // step_pairs
    depth = buf_ref.shape[2] * BAND_CH
    slots = buf_ref.shape[0]
    at = g % steps

    def copies(c):
        return [
            pltpu.make_async_copy(
                arr_refs[array].at[:, first : first + count],
                buf_ref.at[c % slots, :, place : place + count],
                sems.at[c % slots, i],
            )
            for i, (array, first, count, place) in enumerate(runs[c])
        ]

    @pl.when(g == 0)
    def _():
        for copy in copies(0):
            copy.start()

    @pl.when(at == 0)
    def _():
        slot = lax.broadcasted_iota(jnp.int32, (z.groups * LANES, FSUB), 0)
        for tau in range(lf):
            key = key_ref[g // steps, tau : tau + 1, :]
            pick_ref[tau] = jnp.where(slot == key, 1.0, 0.0).astype(jnp.bfloat16)

    for c in range(len(runs)):

        @pl.when(g == c * steps)
        def _():
            for copy in copies(c):
                copy.wait()
            if c + 1 < len(runs):
                for copy in copies(c + 1):
                    copy.start()

    @pl.when(at == 0)
    def _():
        c = g // steps
        lane_group = lax.broadcasted_iota(jnp.int32, (depth, LANES), 1) // z.cap
        for tau in range(lf):
            tiles = []
            for big in range(z.groups):
                tile = buf_ref[c % slots, big * lf + tau].reshape(depth, LANES)
                for lane in range(1, lf):
                    block = buf_ref[c % slots, big * lf + (lane ^ tau)].reshape(depth, LANES)
                    tile = jnp.where(lane_group == lane, block, tile)
                tiles.append(tile)
            rows = jnp.dot(
                jnp.concatenate(tiles, axis=1), pick_ref[tau], preferred_element_type=jnp.float32
            )
            for side in range(FSUB // LANES):
                rows_ref[side, tau * depth : (tau + 1) * depth, :] = rows[
                    :, side * LANES : (side + 1) * LANES
                ]

    def correlate(todo):
        operands = []
        for i, p in todo:
            halves = []
            for part in range(2):
                first = p * BAND_CH + part * few + at * step_pairs + i
                halves.append(
                    jnp.concatenate(
                        [
                            rows_ref[side, pl.ds(first, FR, stride=parities * BAND_CH), :]
                            for side in range(FSUB // LANES)
                        ],
                        axis=1,
                    )
                )
            real, imag = halves
            both = jnp.concatenate([real, imag], axis=0)
            turned = jnp.concatenate([-imag, real], axis=0)
            right = jnp.concatenate([both, turned], axis=1).astype(jnp.bfloat16)
            operands.append((both.astype(jnp.bfloat16).T, right))
        outs = [
            jnp.dot(left, right, preferred_element_type=jnp.float32)
            for left, right in operands
        ]
        for (i, p), out in zip(todo, outs):
            out = out * (1.0 / FR)
            vis_ref[i, p, 0] = out[:, :FSUB]
            vis_ref[i, p, 1] = out[:, FSUB:]

    every = [(i, p) for i in range(step_pairs) for p in range(parities)]
    if even_steps:
        begin = len(runs) * steps - even_steps

        @pl.when(g < begin)
        def _():
            correlate(every)

        @pl.when(g >= begin)
        def _():
            correlate([(i, p) for i, p in every if p == 0])

    else:
        correlate(every)


def receive_call(z, chunk, parity, arrived, keys, vis, even_last=False):
    parities = 2 if parity is None else 1
    step_pairs = 4
    steps = BAND_CH // 2 // step_pairs
    at = 0 if parity is None else parity
    out_shape = jax.ShapeDtypeStruct((z.chan_dev // 2, 2, 2, FSUB, FSUB), jnp.float32)
    arrays = []
    runs = []
    for one in arrived:
        runs.append([])
        for got, first, count, place in one:
            if not any(got is x for x in arrays):
                arrays.append(got)
            index = [got is x for x in arrays].index(True)
            runs[-1].append((index, first, count, place))
    units = parities * z.quads
    slots = min(2, len(runs))
    operands = arrays + [keys]
    in_specs = [pl.BlockSpec(memory_space=pl.ANY)] * len(arrays) + [whole_spec(keys.shape)]
    aliases = {}
    if vis is not None:
        in_specs.append(pl.BlockSpec(memory_space=pl.ANY))
        aliases = {len(operands): 0}
        operands.append(vis)
    share = parities * len(runs)
    return pl.pallas_call(
        functools.partial(
            receive_kernel, z, parities, step_pairs, runs, len(arrays), steps if even_last else 0
        ),
        grid=(len(runs) * steps,),
        in_specs=in_specs,
        out_specs=pl.BlockSpec(
            (step_pairs, parities, 2, FSUB, FSUB),
            lambda g: (chunk * steps + g, at, 0, 0, 0),
        ),
        out_shape=out_shape,
        input_output_aliases=aliases,
        scratch_shapes=[
            pltpu.VMEM((slots, z.devices, units, BAND_CH, LANES), jnp.bfloat16),
            pltpu.VMEM((FSUB // LANES, z.lane_frames * units * BAND_CH, LANES), jnp.float32),
            pltpu.VMEM((z.lane_frames, z.groups * LANES, FSUB), jnp.bfloat16),
            pltpu.SemaphoreType.DMA((slots, max(len(x) for x in runs))),
        ],
        compiler_params=pltpu.CompilerParams(vmem_limit_bytes=VMEM // 2),
        cost_estimate=pl.CostEstimate(
            flops=2_000_000_000 * share, bytes_accessed=5_000_000 * share, transcendentals=0
        ),
        name="correlate",
    )(*operands)


def beam_kernel(z, me_ref, *refs):
    spec_refs = refs[: z.chunks]
    cos_base, sin_base, cos_step, sin_step, sum_ref, out_ref, prod_ref, row_ref = refs[z.chunks :]
    count = z.chan_dev
    weights = []
    for g in range(BEAMS):
        c0, s0 = cos_base[0, g : g + 1, :], sin_base[0, g : g + 1, :]
        c1, s1 = cos_step[g], sin_step[g]
        weights.append(
            ((c0 * c1 - s0 * s1).astype(jnp.bfloat16), (s0 * c1 + c0 * s1).astype(jnp.bfloat16))
        )
    for q in range(z.quads):
        lanes = slice(q * z.width, (q + 1) * z.width)
        x = [ref[:, lanes] for ref in spec_refs]
        real = jnp.concatenate([v[:BAND_CH] for v in x], axis=0)
        imag = jnp.concatenate([v[BAND_CH:] for v in x], axis=0)
        for g in range(BEAMS):
            c, s = weights[g]
            pair = (c * real + s * imag, c * imag - s * real)
            for part in range(2):
                row = (part * BEAMS + g) * count
                both = pair[part][:, :LANES] + pair[part][:, LANES:]
                prod_ref[row : row + count, q * LANES : (q + 1) * LANES] = both
    sums = jnp.dot(prod_ref[...], sum_ref[...], preferred_element_type=jnp.float32)
    sums = sums * (1.0 / np.sqrt(F))
    few = BAND_CH // 2
    for j in range(2 * BEAMS):
        for i in range(count // few):
            first = i // 2 * BAND_CH + i % 2
            top = j * count + i * few
            row_ref[j, pl.ds(first, few, stride=2), :] = sums[top : top + few]
        out_ref[0, :, j * FR : (j + 1) * FR] = row_ref[j][:, :FR]


def beam_call(z, me, spectra, delays):
    bits = z.devices.bit_length() - 1
    lanes = FR * z.feed_dev
    halves = delays.reshape(BEAMS, 2, 1, z.cap)
    spread = jnp.broadcast_to(halves, (BEAMS, 2, z.lane_frames, z.cap)).reshape(BEAMS, z.width)
    unit = 2.0 * jnp.pi / NFFT
    owners = jnp.arange(z.devices, dtype=jnp.int32).astype(jnp.float32) * z.chan_dev
    inner = np.arange(z.chunks)[:, None] * BAND_CH + ORDER[None, :]
    inner = jnp.asarray(inner.reshape(-1).astype(np.float32))
    base = unit * (spread[None, :, :] * owners[:, None, None])
    step = unit * (spread[:, None, :] * inner[None, :, None])
    frame = (np.arange(FR * z.cap) // LANES) * z.lane_frames
    frame = frame + (np.arange(FR * z.cap) % LANES) // z.cap
    sums = (frame[:, None] == np.arange(LANES)[None, :]).astype(ml_dtypes.bfloat16)

    def owner(j, me_ref):
        k = 0
        for b in range(bits):
            k = k | (((j >> b) & 1) << (bits - 1 - b))
        return me_ref[0] ^ k

    base_spec = pl.BlockSpec(
        (1, BEAMS, z.width), lambda j, me_ref: (owner(j, me_ref), 0, 0)
    )
    grid_spec = pltpu.PrefetchScalarGridSpec(
        num_scalar_prefetch=1,
        grid=(z.devices,),
        in_specs=[
            pl.BlockSpec((z.rows_dev, lanes), lambda j, me_ref: (owner(j, me_ref), 0))
            for _ in range(z.chunks)
        ]
        + [base_spec, base_spec, whole_spec(step.shape), whole_spec(step.shape)]
        + [whole_spec(sums.shape)],
        out_specs=pl.BlockSpec(
            (1, z.chan_dev, 2 * BEAMS * FR), lambda j, me_ref: (j, 0, 0)
        ),
        scratch_shapes=[
            pltpu.VMEM((2 * BEAMS * z.chan_dev, FR * z.cap), jnp.bfloat16),
            pltpu.VMEM((2 * BEAMS, z.chan_dev, LANES), jnp.float32),
        ],
    )
    return pl.pallas_call(
        functools.partial(beam_kernel, z),
        grid_spec=grid_spec,
        out_shape=jax.ShapeDtypeStruct((z.devices, z.chan_dev, 2 * BEAMS * FR), jnp.float32),
        compiler_params=pltpu.CompilerParams(vmem_limit_bytes=VMEM),
        cost_estimate=pl.CostEstimate(
            flops=20_000_000_000, bytes_accessed=20_000_000, transcendentals=0
        ),
        name="beam_sums",
    )(
        me, *spectra, jnp.cos(base), jnp.sin(base), jnp.cos(step), jnp.sin(step),
        jnp.asarray(sums),
    )


def swap(z, x, offset):
    return lax.ppermute(x, "chan", [(i, i ^ offset) for i in range(z.devices)])


def exchange(x):
    return lax.all_to_all(x, "chan", split_axis=0, concat_axis=0, tiled=True)


def on_device(voltages, delays, band_feeds):
    z = Sizes(lax.axis_size("chan"), voltages.shape[0])
    me = lax.axis_index("chan")
    me_array = me.astype(jnp.int32).reshape(1)

    own = lax.dynamic_slice_in_dim(band_feeds, me * z.bands_here, z.bands_here, 0)
    source = own // z.feed_dev
    before = jnp.sum(
        (own[:, None, :] < (source * z.feed_dev)[:, :, None]).astype(jnp.int32), axis=2
    )
    place = jnp.arange(FSUB, dtype=jnp.int32)[None, :] - before
    tau = jnp.arange(z.lane_frames, dtype=jnp.int32)
    big = (source // z.lane_frames) * LANES + place
    group = (source % z.lane_frames)[:, None, :] ^ tau[None, :, None]
    take_key = big[:, None, :] + z.cap * group

    calls = Spectra(z, me_array, voltages, band_feeds)
    early = list(range(z.early))
    basis = calls.basis(early)
    share = 2 * z.step_quads
    step = z.early * share
    arrived = [[] for _ in range(z.chunks)]
    steps = z.parts[0]
    filt, *spectra, send = calls.first(0, steps, early, basis, steps * step, [])
    got = exchange(send)
    for c in early:
        arrived[c] += [(got, g * step + c * share, share, g * share) for g in range(steps)]
    if len(z.parts) > 1:
        begin, steps = steps, z.parts[1]
        base = steps * step
        begun = 3 * z.step_quads
        filt, *spectra, send = calls.first(
            begin, steps, early, basis, base + z.steps * begun, [filt, *spectra]
        )
        *more, send, last = calls.next([z.chunks - 2, z.chunks - 1], filt, send)
        spectra = spectra + more
        got = exchange(send)
        for c in early:
            arrived[c] += [
                (got, g * step + c * share, share, (begin + g) * share) for g in range(steps)
            ]
        for g in range(z.steps):
            first = base + g * begun
            arrived[-2].append((got, first, share, g * share))
            arrived[-1] += [
                (got, first + share + q, 1, g * share + 2 * q) for q in range(z.step_quads)
            ]

    beams, bit = beam_call(z, me_array, spectra, delays), 1
    while beams.shape[0] > 1:
        half = beams.shape[0] // 2
        kept, away = beams[:half], beams[half:]
        if half > 1:
            beams, bit = kept + swap(z, away, bit), 2 * bit
        else:
            beams = away = swap(z, away.astype(jnp.bfloat16), bit)
    if len(z.parts) > 1:
        last, kept, away = lax.optimization_barrier((last, kept, away))
        got = exchange(last)
        k = z.chunks - 1
        vis = receive_call(z, 0, None, arrived, take_key, None, even_last=True)
        vis = receive_call(z, k, 1, [[(got, 0, z.quads, 0)]], take_key[k:], vis)
    else:
        vis = receive_call(z, 0, None, arrived, take_key, None)
    beams = (kept + away.astype(jnp.float32)).reshape(z.chan_dev, 2 * BEAMS * FR)
    return (vis.reshape(z.chan_dev, 2, FSUB, FSUB), beams)


def solution(mesh):
    in_specs = (P(("grp", "chan"), None), P(None, ("grp", "chan")), P())
    out_specs = (P(("grp", "chan"), None, None, None), P(("grp", "chan"), None))
    return jax.shard_map(
        on_device, mesh=mesh, in_specs=in_specs, out_specs=out_specs, check_vma=False
    )
```

```python
import copy
import functools

import jax
import jax.numpy as jnp
import ml_dtypes
import numpy as np
from jax import lax
from jax.experimental import pallas as pl
from jax.experimental.pallas import tpu as pltpu
from jax.sharding import PartitionSpec as P

F = 1024
CHANNELS = 1024
TAPS = 4
BAND_CH = 16
BEAMS = 4
FR = 48
NFFT = 2048
BANDS = 64
FSUB = 256
LANES = 128
VMEM = 56 * 1024 * 1024

NT = (((1,), (1,)), ((), ()))


def fir_window():
    ids = np.arange(TAPS * NFFT, dtype=np.float64)
    centered = (ids - 0.5 * TAPS * NFFT + 0.5) / NFFT
    hann_part = 0.5 - 0.5 * np.cos(2.0 * np.pi * (ids + 0.5) / (TAPS * NFFT))
    return (np.sinc(centered) * hann_part).reshape(TAPS, NFFT)


ORDER = np.concatenate([np.arange(0, BAND_CH, 2), np.arange(1, BAND_CH, 2)])


def dft_rows(chan_ids):
    m = np.arange(NFFT // 2, dtype=np.int64)
    turns = (chan_ids[..., None].astype(np.int64) * m) % NFFT
    table = 2.0 * np.pi * np.arange(NFFT) / NFFT
    cosine = np.cos(table).astype(np.float32).astype(ml_dtypes.bfloat16)
    sine = (-np.sin(table)).astype(np.float32).astype(ml_dtypes.bfloat16)
    return np.stack([cosine[turns], sine[turns]], axis=1)


class Sizes:
    def __init__(self, devices, feed_dev):
        self.devices = devices
        self.feed_dev = feed_dev
        self.cap = feed_dev // 2
        self.lane_frames = LANES // self.cap
        self.quads = FR // self.lane_frames
        self.width = self.lane_frames * feed_dev
        self.set_steps(6 if self.quads % 6 == 0 else self.quads)
        self.chan_dev = CHANNELS // devices
        self.bands_here = BANDS // devices
        self.chunks = self.chan_dev // BAND_CH
        self.rows_dev = 2 * BAND_CH
        self.rows = devices * self.rows_dev
        self.groups = devices // self.lane_frames
        self.early = min(2, self.chunks)
        if self.chunks == 4:
            self.parts = (self.quads * 5 // 12, self.quads - self.quads * 5 // 12)
        else:
            self.early, self.parts = self.chunks, (self.quads,)

    def set_steps(self, steps):
        self.steps = steps
        self.step_frames = FR // steps
        self.step_quads = self.quads // steps
        self.step_lanes = self.step_frames * self.feed_dev


def find_places(z, me, lists):
    base = me * z.feed_dev
    first = jnp.sum((lists < base).astype(jnp.int32), axis=1, keepdims=True)
    lane = lax.broadcasted_iota(jnp.int32, (lists.shape[0], LANES), 1)
    at = first + lane % z.cap
    parts = []
    for side in range(FSUB // LANES):
        index = jnp.clip(at - side * LANES, 0, LANES - 1)
        half = lists[:, side * LANES : (side + 1) * LANES]
        parts.append(jnp.take_along_axis(half, index, axis=1, mode="promise_in_bounds"))
    loc = jnp.where(at < LANES, parts[0], parts[1]) - base
    return jnp.clip(loc, 0, z.feed_dev - 1)


def emit_spectra(z, scale, chunk, me_ref, spectra, loc_ref, spec_ref, sends, quads, base=0):
    lane = lax.broadcasted_iota(jnp.int32, (z.rows_dev, LANES), 1)
    frame = (lane // z.cap) ^ (me_ref[0] % z.lane_frames)
    start = frame * z.cap
    few = BAND_CH // 2
    for owner in range(z.devices):
        top = owner * BAND_CH
        rows = [x[top + p : top + p + few] for p in (0, few) for x in spectra]
        rows = jnp.concatenate(rows, axis=0) * scale
        columns = slice(base * z.width, (base + quads) * z.width)
        spec_ref[owner * z.rows_dev : (owner + 1) * z.rows_dev, columns] = rows.astype(
            jnp.bfloat16
        )
        band = owner * z.bands_here + chunk
        loc = loc_ref[band : band + 1, :]
        index = start + loc % z.cap
        lower = jnp.broadcast_to(loc, index.shape) < z.cap
        for q in range(quads):
            parts = []
            for side in range(2):
                left = q * z.width + side * LANES
                parts.append(
                    jnp.take_along_axis(
                        rows[:, left : left + LANES], index, axis=1, mode="promise_in_bounds"
                    )
                )
            picked = jnp.where(lower, parts[0], parts[1])
            for parity, (send_ref, unit, stride) in enumerate(sends):
                half = [
                    picked[p * BAND_CH + parity * few : p * BAND_CH + parity * few + few]
                    for p in range(2)
                ]
                half = jnp.concatenate(half, axis=0).astype(jnp.bfloat16)
                send_ref[owner, unit + (base + q) * stride] = half


def filter_tile(z, main_ref, halo, win_ref, off, f0, begin):
    lanes = slice(off, off + LANES)
    taps = [win_ref[k : k + 1, lanes] for k in range(TAPS)]
    frames = []
    for t in range(begin, begin + z.lane_frames + TAPS - 1):
        if t < z.step_frames:
            x = main_ref[f0 : f0 + 16, t * NFFT + off : t * NFFT + off + LANES]
        else:
            x = halo[t - z.step_frames][f0 : f0 + 16, lanes]
        frames.append(x.astype(jnp.float32))
    totals = []
    for t in range(z.lane_frames):
        total = taps[0] * frames[t]
        for k in range(1, TAPS):
            total = total + taps[k] * frames[t + k]
        totals.append(total)
    if z.cap < 16:
        totals = [
            jnp.concatenate([totals[t][h : h + 8], totals[t + 1][h : h + 8]], axis=0)
            for t in range(0, z.lane_frames, 2)
            for h in (0, 8)
        ]
    out = []
    for i, total in enumerate(totals):
        if z.cap < 16:
            t, half, feed = 2 * (i // 2), i % 2, 0
        else:
            t, half, feed = i, f0 // z.cap, f0 % z.cap
        out.append((half * LANES + t * z.cap + feed, total.astype(jnp.bfloat16)))
    return out


def filter_fold(z, main_ref, halo, win_ref, filt_ref, off, quad):
    far = off + NFFT // 2
    begin = quad * z.lane_frames
    folded = {}
    for f0 in range(0, z.feed_dev, 16):
        low = filter_tile(z, main_ref, halo, win_ref, off, f0, begin)
        high = filter_tile(z, main_ref, halo, win_ref, far, f0, begin)
        for (row, a), (_, b) in zip(low, high):
            folded[row] = (a + b, a - b)
            top = quad * z.width + row
            filt_ref[top : top + 16, off : off + LANES] = folded[row][0]
            filt_ref[top : top + 16, far : far + LANES] = folded[row][1]
    return [
        jnp.concatenate([folded[row][parity] for row in sorted(folded)], axis=0)
        for parity in range(2)
    ]


def product(z, basis_ref, parity, c, samples):
    rows = slice(c * z.rows // 2, (c + 1) * z.rows // 2)
    return lax.dot_general(
        basis_ref[parity, rows, :], samples, NT, preferred_element_type=jnp.float32
    )


def first_kernel(
    z, scale, chunks, held, me_ref, main_ref, h0_ref, h1_ref, h2_ref, win_ref, basis_ref,
    lists_ref, *refs,
):
    filt_ref, spec_refs, send_ref, loc_ref = refs[held], refs[held + 1 : -2], refs[-2], refs[-1]
    halo = (h0_ref, h1_ref, h2_ref)
    loc_ref[...] = find_places(z, me_ref[0], lists_ref[...])

    def emit(quad, spectra):
        for c, chunk in enumerate(chunks):
            unit = c * 2 * z.step_quads
            sends = [(send_ref, unit, 2), (send_ref, unit + 1, 2)]
            emit_spectra(
                z, scale, chunk, me_ref, spectra[c], loc_ref, spec_refs[c], sends, 1, quad
            )

    before = None
    for quad in range(z.step_quads):
        tiles = [
            filter_fold(z, main_ref, halo, win_ref, filt_ref, off, quad)
            for off in range(0, NFFT // 2, LANES)
        ]
        samples = [jnp.concatenate([tile[p] for tile in tiles], axis=1) for p in range(2)]
        if before is not None:
            emit(quad - 1, before)
        before = [
            [product(z, basis_ref, p, c, samples[p]) for p in range(2)]
            for c in range(len(chunks))
        ]
    emit(z.step_quads - 1, before)


def next_kernel(z, scale, chunks, me_ref, filt_ref, basis_ref, lists_ref, held_ref, *refs):
    begun_ref, last_ref, loc_ref = refs[2], refs[3], refs[-1]
    loc_ref[...] = find_places(z, me_ref[0], lists_ref[...])
    half = NFFT // 2
    spectra = [
        [
            product(z, basis_ref, p, c, filt_ref[:, p * half : (p + 1) * half])
            for p in range(2)
        ]
        for c in range(2)
    ]
    sends = [
        [(begun_ref, 0, 2), (begun_ref, 1, 2)],
        [(begun_ref, 2 * z.step_quads, 1), (last_ref, 0, 1)],
    ]
    for c, chunk in enumerate(chunks):
        emit_spectra(
            z, scale, chunk, me_ref, spectra[c], loc_ref, refs[c], sends[c], z.step_quads
        )


def whole_spec(shape):
    return pl.BlockSpec(shape, lambda *g: (0,) * len(shape))


class Spectra:

    def __init__(self, z, me, voltages, band_feeds):
        window = fir_window()
        self.z = z
        self.fine = copy.copy(z)
        self.fine.set_steps(z.quads)
        self.me = me
        self.scale = float(np.sqrt(2.0 / np.sum(window * window)))
        self.window = jnp.asarray(window.astype(np.float32))
        self.voltages = voltages
        self.lists = band_feeds
        self.ids = np.arange(CHANNELS).reshape(z.devices, z.chunks, BAND_CH)
        self.me_spec = pl.BlockSpec(memory_space=pltpu.SMEM)
        self.spec_shape = jax.ShapeDtypeStruct((z.rows, FR * z.feed_dev), jnp.bfloat16)
        self.filt_shape = jax.ShapeDtypeStruct((FR * z.feed_dev, NFFT), jnp.bfloat16)

    def basis(self, chunks):
        sides = []
        for parity in range(2):
            rows = [dft_rows(self.ids[:, k, parity::2].reshape(-1)) for k in chunks]
            rows = np.stack(rows).reshape(len(chunks), self.z.devices, BAND_CH // 2, 2, -1)
            rows = np.transpose(rows, (0, 1, 3, 2, 4))
            sides.append(rows.reshape(len(chunks) * self.z.rows // 2, NFFT // 2))
        return jnp.asarray(np.stack(sides))

    def message(self, units):
        return jax.ShapeDtypeStruct((self.z.devices, units, BAND_CH, LANES), jnp.bfloat16)

    def common(self, steps, chunks):
        z = self.z
        flops = len(chunks) * z.rows * NFFT * z.step_lanes * steps
        return dict(
            grid=(steps,),
            scratch_shapes=[pltpu.VMEM((BANDS, LANES), jnp.int32)],
            compiler_params=pltpu.CompilerParams(vmem_limit_bytes=VMEM),
            cost_estimate=pl.CostEstimate(
                flops=flops, bytes_accessed=3_000_000 * steps, transcendentals=0
            ),
        )

    def first(self, begin, steps, chunks, basis, units, base, held):
        z = self.fine
        count = len(chunks)
        base = base // (count * 2 * z.step_quads)

        def halo_spec(h):
            return pl.BlockSpec(
                (z.feed_dev, NFFT), lambda g: (0, z.step_frames * (begin + g + 1) + h)
            )

        send_block = (z.devices, count * 2 * z.step_quads, BAND_CH, LANES)
        operands = [self.me] + [self.voltages] * 4 + [self.window, basis, self.lists]
        aliases = {len(operands) + i: i for i in range(len(held))}
        return pl.pallas_call(
            functools.partial(first_kernel, z, self.scale, chunks, len(held)),
            in_specs=[
                self.me_spec,
                pl.BlockSpec((z.feed_dev, z.step_frames * NFFT), lambda g: (0, begin + g)),
                halo_spec(0),
                halo_spec(1),
                halo_spec(2),
                whole_spec((TAPS, NFFT)),
                whole_spec(basis.shape),
                whole_spec(self.lists.shape),
            ]
            + [pl.BlockSpec(memory_space=pl.ANY)] * len(held),
            out_specs=[
                pl.BlockSpec((z.step_lanes, NFFT), lambda g: (begin + g, 0)),
            ]
            + [pl.BlockSpec((z.rows, z.step_lanes), lambda g: (0, begin + g))] * count
            + [pl.BlockSpec(send_block, lambda g: (0, base + g, 0, 0))],
            out_shape=[self.filt_shape] + [self.spec_shape] * count + [self.message(units)],
            input_output_aliases=aliases,
            name="filter_spectra",
            **self.common(steps, chunks),
        )(*operands, *held)

    def next(self, chunks, filt, held):
        z = self.z
        basis = self.basis(chunks)
        begun = 3 * z.step_quads
        operands = [self.me, filt, basis, self.lists, held]
        return pl.pallas_call(
            functools.partial(next_kernel, z, self.scale, chunks),
            in_specs=[
                self.me_spec,
                pl.BlockSpec((z.step_lanes, NFFT), lambda g: (g, 0)),
                whole_spec(basis.shape),
                whole_spec(self.lists.shape),
                pl.BlockSpec(memory_space=pl.ANY),
            ],
            out_specs=[pl.BlockSpec((z.rows, z.step_lanes), lambda g: (0, g))] * 2
            + [
                pl.BlockSpec((z.devices, begun, BAND_CH, LANES), lambda g: (0, g, 0, 0)),
                pl.BlockSpec((z.devices, z.step_quads, BAND_CH, LANES), lambda g: (0, g, 0, 0)),
            ],
            out_shape=[self.spec_shape] * 2
            + [self.message(held.shape[1]), self.message(z.quads)],
            input_output_aliases={4: 2},
            name="spectra_next",
            **self.common(z.steps, chunks),
        )(*operands)


def receive_kernel(z, parities, step_pairs, runs, arrays, even_steps, *refs):
    arr_refs, key_ref = refs[:arrays], refs[arrays]
    vis_ref, buf_ref, rows_ref, pick_ref, sems = refs[-5:]
    g = pl.program_id(0)
    lf = z.lane_frames
    few = BAND_CH // 2
    steps = few // step_pairs
    depth = buf_ref.shape[2] * BAND_CH
    slots = buf_ref.shape[0]
    at = g % steps

    def copies(c):
        return [
            pltpu.make_async_copy(
                arr_refs[array].at[:, first : first + count],
                buf_ref.at[c % slots, :, place : place + count],
                sems.at[c % slots, i],
            )
            for i, (array, first, count, place) in enumerate(runs[c])
        ]

    @pl.when(g == 0)
    def _():
        for one in copies(0):
            one.start()

    @pl.when(at == 0)
    def _():
        slot = lax.broadcasted_iota(jnp.int32, (z.groups * LANES, FSUB), 0)
        for tau in range(lf):
            key = key_ref[g // steps, tau : tau + 1, :]
            pick_ref[tau] = jnp.where(slot == key, 1.0, 0.0).astype(jnp.bfloat16)

    for c in range(len(runs)):

        @pl.when(g == c * steps)
        def _():
            for one in copies(c):
                one.wait()
            if c + 1 < len(runs):
                for one in copies(c + 1):
                    one.start()

    @pl.when(at == 0)
    def _():
        c = g // steps
        lane_group = lax.broadcasted_iota(jnp.int32, (depth, LANES), 1) // z.cap
        for tau in range(lf):
            tiles = []
            for big in range(z.groups):
                tile = buf_ref[c % slots, big * lf + tau].reshape(depth, LANES)
                for lane in range(1, lf):
                    block = buf_ref[c % slots, big * lf + (lane ^ tau)].reshape(depth, LANES)
                    tile = jnp.where(lane_group == lane, block, tile)
                tiles.append(tile)
            rows = jnp.dot(
                jnp.concatenate(tiles, axis=1), pick_ref[tau], preferred_element_type=jnp.float32
            )
            for side in range(FSUB // LANES):
                rows_ref[side, tau * depth : (tau + 1) * depth, :] = rows[
                    :, side * LANES : (side + 1) * LANES
                ]

    def correlate(todo):
        operands = []
        for i, p in todo:
            halves = []
            for part in range(2):
                first = p * BAND_CH + part * few + at * step_pairs + i
                halves.append(
                    jnp.concatenate(
                        [
                            rows_ref[side, pl.ds(first, FR, stride=parities * BAND_CH), :]
                            for side in range(FSUB // LANES)
                        ],
                        axis=1,
                    )
                )
            real, imag = halves
            both = jnp.concatenate([real, imag], axis=0)
            turned = jnp.concatenate([-imag, real], axis=0)
            right = jnp.concatenate([both, turned], axis=1).astype(jnp.bfloat16)
            operands.append((both.astype(jnp.bfloat16).T, right))
        outs = [
            jnp.dot(left, right, preferred_element_type=jnp.float32)
            for left, right in operands
        ]
        for (i, p), out in zip(todo, outs):
            out = out * (1.0 / FR)
            vis_ref[i, p, 0] = out[:, :FSUB]
            vis_ref[i, p, 1] = out[:, FSUB:]

    every = [(i, p) for i in range(step_pairs) for p in range(parities)]
    if even_steps:
        begin = len(runs) * steps - even_steps

        @pl.when(g < begin)
        def _():
            correlate(every)

        @pl.when(g >= begin)
        def _():
            correlate([(i, p) for i, p in every if p == 0])

    else:
        correlate(every)


def receive_call(z, chunk, parity, arrived, keys, vis, even_last=False):
    parities = 2 if parity is None else 1
    step_pairs = 4
    steps = BAND_CH // 2 // step_pairs
    at = 0 if parity is None else parity
    out_shape = jax.ShapeDtypeStruct((z.chan_dev // 2, 2, 2, FSUB, FSUB), jnp.float32)
    arrays = []
    runs = []
    for one in arrived:
        runs.append([])
        for got, first, count, place in one:
            if not any(got is x for x in arrays):
                arrays.append(got)
            index = [got is x for x in arrays].index(True)
            runs[-1].append((index, first, count, place))
    units = parities * z.quads
    slots = min(2, len(runs))
    operands = arrays + [keys]
    in_specs = [pl.BlockSpec(memory_space=pl.ANY)] * len(arrays) + [whole_spec(keys.shape)]
    aliases = {}
    if vis is not None:
        in_specs.append(pl.BlockSpec(memory_space=pl.ANY))
        aliases = {len(operands): 0}
        operands.append(vis)
    share = parities * len(runs)
    return pl.pallas_call(
        functools.partial(
            receive_kernel, z, parities, step_pairs, runs, len(arrays), steps if even_last else 0
        ),
        grid=(len(runs) * steps,),
        in_specs=in_specs,
        out_specs=pl.BlockSpec(
            (step_pairs, parities, 2, FSUB, FSUB),
            lambda g: (chunk * steps + g, at, 0, 0, 0),
        ),
        out_shape=out_shape,
        input_output_aliases=aliases,
        scratch_shapes=[
            pltpu.VMEM((slots, z.devices, units, BAND_CH, LANES), jnp.bfloat16),
            pltpu.VMEM((FSUB // LANES, z.lane_frames * units * BAND_CH, LANES), jnp.float32),
            pltpu.VMEM((z.lane_frames, z.groups * LANES, FSUB), jnp.bfloat16),
            pltpu.SemaphoreType.DMA((slots, max(len(x) for x in runs))),
        ],
        compiler_params=pltpu.CompilerParams(vmem_limit_bytes=VMEM // 2),
        cost_estimate=pl.CostEstimate(
            flops=2_000_000_000 * share, bytes_accessed=5_000_000 * share, transcendentals=0
        ),
        name="correlate",
    )(*operands)


def beam_kernel(z, me_ref, *refs):
    spec_refs = refs[: z.chunks]
    cos_base, sin_base, cos_step, sin_step, sum_ref, out_ref, prod_ref, row_ref = refs[z.chunks :]
    count = z.chan_dev
    weights = []
    for g in range(BEAMS):
        c0, s0 = cos_base[0, g : g + 1, :], sin_base[0, g : g + 1, :]
        c1, s1 = cos_step[g], sin_step[g]
        weights.append(
            ((c0 * c1 - s0 * s1).astype(jnp.bfloat16), (s0 * c1 + c0 * s1).astype(jnp.bfloat16))
        )
    for q in range(z.quads):
        lanes = slice(q * z.width, (q + 1) * z.width)
        x = [ref[:, lanes] for ref in spec_refs]
        real = jnp.concatenate([v[:BAND_CH] for v in x], axis=0)
        imag = jnp.concatenate([v[BAND_CH:] for v in x], axis=0)
        for g in range(BEAMS):
            c, s = weights[g]
            pair = (c * real + s * imag, c * imag - s * real)
            for part in range(2):
                row = (part * BEAMS + g) * count
                both = pair[part][:, :LANES] + pair[part][:, LANES:]
                prod_ref[row : row + count, q * LANES : (q + 1) * LANES] = both
    sums = jnp.dot(prod_ref[...], sum_ref[...], preferred_element_type=jnp.float32)
    sums = sums * (1.0 / np.sqrt(F))
    few = BAND_CH // 2
    for j in range(2 * BEAMS):
        for i in range(count // few):
            first = i // 2 * BAND_CH + i % 2
            top = j * count + i * few
            row_ref[j, pl.ds(first, few, stride=2), :] = sums[top : top + few]
        out_ref[0, :, j * FR : (j + 1) * FR] = row_ref[j][:, :FR]


def beam_call(z, me, spectra, delays):
    bits = z.devices.bit_length() - 1
    lanes = FR * z.feed_dev
    halves = delays.reshape(BEAMS, 2, 1, z.cap)
    spread = jnp.broadcast_to(halves, (BEAMS, 2, z.lane_frames, z.cap)).reshape(BEAMS, z.width)
    unit = 2.0 * jnp.pi / NFFT
    owners = jnp.arange(z.devices, dtype=jnp.int32).astype(jnp.float32) * z.chan_dev
    inner = np.arange(z.chunks)[:, None] * BAND_CH + ORDER[None, :]
    inner = jnp.asarray(inner.reshape(-1).astype(np.float32))
    base = unit * (spread[None, :, :] * owners[:, None, None])
    step = unit * (spread[:, None, :] * inner[None, :, None])
    frame = (np.arange(FR * z.cap) // LANES) * z.lane_frames
    frame = frame + (np.arange(FR * z.cap) % LANES) // z.cap
    sums = (frame[:, None] == np.arange(LANES)[None, :]).astype(ml_dtypes.bfloat16)

    def owner(j, me_ref):
        k = 0
        for b in range(bits):
            k = k | (((j >> b) & 1) << (bits - 1 - b))
        return me_ref[0] ^ k

    base_spec = pl.BlockSpec(
        (1, BEAMS, z.width), lambda j, me_ref: (owner(j, me_ref), 0, 0)
    )
    grid_spec = pltpu.PrefetchScalarGridSpec(
        num_scalar_prefetch=1,
        grid=(z.devices,),
        in_specs=[
            pl.BlockSpec((z.rows_dev, lanes), lambda j, me_ref: (owner(j, me_ref), 0))
            for _ in range(z.chunks)
        ]
        + [base_spec, base_spec, whole_spec(step.shape), whole_spec(step.shape)]
        + [whole_spec(sums.shape)],
        out_specs=pl.BlockSpec(
            (1, z.chan_dev, 2 * BEAMS * FR), lambda j, me_ref: (j, 0, 0)
        ),
        scratch_shapes=[
            pltpu.VMEM((2 * BEAMS * z.chan_dev, FR * z.cap), jnp.bfloat16),
            pltpu.VMEM((2 * BEAMS, z.chan_dev, LANES), jnp.float32),
        ],
    )
    return pl.pallas_call(
        functools.partial(beam_kernel, z),
        grid_spec=grid_spec,
        out_shape=jax.ShapeDtypeStruct((z.devices, z.chan_dev, 2 * BEAMS * FR), jnp.float32),
        compiler_params=pltpu.CompilerParams(vmem_limit_bytes=VMEM),
        cost_estimate=pl.CostEstimate(
            flops=20_000_000_000, bytes_accessed=20_000_000, transcendentals=0
        ),
        name="beam_sums",
    )(
        me, *spectra, jnp.cos(base), jnp.sin(base), jnp.cos(step), jnp.sin(step),
        jnp.asarray(sums),
    )


def swap(z, x, offset):
    return lax.ppermute(x, "chan", [(i, i ^ offset) for i in range(z.devices)])


def exchange(x):
    return lax.all_to_all(x, "chan", split_axis=0, concat_axis=0, tiled=True)


def on_device(voltages, delays, band_feeds):
    z = Sizes(lax.axis_size("chan"), voltages.shape[0])
    me = lax.axis_index("chan")
    me_array = me.astype(jnp.int32).reshape(1)

    own = lax.dynamic_slice_in_dim(band_feeds, me * z.bands_here, z.bands_here, 0)
    source = own // z.feed_dev
    before = jnp.sum(
        (own[:, None, :] < (source * z.feed_dev)[:, :, None]).astype(jnp.int32), axis=2
    )
    place = jnp.arange(FSUB, dtype=jnp.int32)[None, :] - before
    tau = jnp.arange(z.lane_frames, dtype=jnp.int32)
    big = (source // z.lane_frames) * LANES + place
    group = (source % z.lane_frames)[:, None, :] ^ tau[None, :, None]
    take_key = big[:, None, :] + z.cap * group

    calls = Spectra(z, me_array, voltages, band_feeds)
    early = list(range(z.early))
    basis = calls.basis(early)
    share = 2 * calls.fine.step_quads
    step = z.early * share
    arrived = [[] for _ in range(z.chunks)]
    steps = z.parts[0]
    filt, *spectra, send = calls.first(0, steps, early, basis, steps * step, 0, [])
    got = exchange(send)
    for c in early:
        arrived[c] += [(got, g * step + c * share, share, g * share) for g in range(steps)]
    if len(z.parts) > 1:
        begin, steps = steps, z.parts[1]
        late, begun = 2 * z.step_quads, 3 * z.step_quads
        base = z.steps * begun
        filt, *spectra, send = calls.first(
            begin, steps, early, basis, base + steps * step, base, [filt, *spectra]
        )
        *more, send, last = calls.next([z.chunks - 2, z.chunks - 1], filt, send)
        spectra = spectra + more
        got = exchange(send)
        for c in early:
            arrived[c] += [
                (got, base + g * step + c * share, share, (begin + g) * share)
                for g in range(steps)
            ]
        for g in range(z.steps):
            first = g * begun
            arrived[-2].append((got, first, late, g * late))
            arrived[-1] += [
                (got, first + late + q, 1, g * late + 2 * q) for q in range(z.step_quads)
            ]

    beams, bit = beam_call(z, me_array, spectra, delays), 1
    while beams.shape[0] > 1:
        half = beams.shape[0] // 2
        kept, away = beams[:half], beams[half:]
        if half > 1:
            beams, bit = kept + swap(z, away, bit), 2 * bit
        else:
            beams = away = swap(z, away.astype(jnp.bfloat16), bit)
    if len(z.parts) > 1:
        last, kept, away = lax.optimization_barrier((last, kept, away))
        got = exchange(last)
        k = z.chunks - 1
        vis = receive_call(z, 0, None, arrived, take_key, None, even_last=True)
        vis = receive_call(z, k, 1, [[(got, 0, z.quads, 0)]], take_key[k:], vis)
    else:
        vis = receive_call(z, 0, None, arrived, take_key, None)
    beams = (kept + away.astype(jnp.float32)).reshape(z.chan_dev, 2 * BEAMS * FR)
    return (vis.reshape(z.chan_dev, 2, FSUB, FSUB), beams)


def solution(mesh):
    in_specs = (P(("grp", "chan"), None), P(None, ("grp", "chan")), P())
    out_specs = (P(("grp", "chan"), None, None, None), P(("grp", "chan"), None))
    return jax.shard_map(
        on_device, mesh=mesh, in_specs=in_specs, out_specs=out_specs, check_vma=False
    )
```

```python
import copy
import functools

import jax
import jax.numpy as jnp
import ml_dtypes
import numpy as np
from jax import lax
from jax.experimental import pallas as pl
from jax.experimental.pallas import tpu as pltpu
from jax.sharding import PartitionSpec as P

F = 1024
CHANNELS = 1024
TAPS = 4
BAND_CH = 16
BEAMS = 4
FR = 48
NFFT = 2048
BANDS = 64
FSUB = 256
LANES = 128
VMEM = 56 * 1024 * 1024

NT = (((1,), (1,)), ((), ()))


def fir_window():
    ids = np.arange(TAPS * NFFT, dtype=np.float64)
    centered = (ids - 0.5 * TAPS * NFFT + 0.5) / NFFT
    hann_part = 0.5 - 0.5 * np.cos(2.0 * np.pi * (ids + 0.5) / (TAPS * NFFT))
    return (np.sinc(centered) * hann_part).reshape(TAPS, NFFT)


ORDER = np.concatenate([np.arange(0, BAND_CH, 2), np.arange(1, BAND_CH, 2)])


def dft_rows(chan_ids):
    m = np.arange(NFFT // 2, dtype=np.int64)
    turns = (chan_ids[..., None].astype(np.int64) * m) % NFFT
    table = 2.0 * np.pi * np.arange(NFFT) / NFFT
    cosine = np.cos(table).astype(np.float32).astype(ml_dtypes.bfloat16)
    sine = (-np.sin(table)).astype(np.float32).astype(ml_dtypes.bfloat16)
    return np.stack([cosine[turns], sine[turns]], axis=1)


class Sizes:
    def __init__(self, devices, feed_dev):
        self.devices = devices
        self.feed_dev = feed_dev
        self.cap = feed_dev // 2
        self.lane_frames = LANES // self.cap
        self.quads = FR // self.lane_frames
        self.width = self.lane_frames * feed_dev
        self.set_steps(6 if self.quads % 6 == 0 else self.quads)
        self.chan_dev = CHANNELS // devices
        self.bands_here = BANDS // devices
        self.chunks = self.chan_dev // BAND_CH
        self.rows_dev = 2 * BAND_CH
        self.rows = devices * self.rows_dev
        self.groups = devices // self.lane_frames
        self.early = min(2, self.chunks)
        if self.chunks == 4:
            self.parts = (self.quads * 5 // 12, self.quads - self.quads * 5 // 12)
        else:
            self.early, self.parts = self.chunks, (self.quads,)

    def set_steps(self, steps):
        self.steps = steps
        self.step_frames = FR // steps
        self.step_quads = self.quads // steps
        self.step_lanes = self.step_frames * self.feed_dev


def find_places(z, me, lists):
    base = me * z.feed_dev
    first = jnp.sum((lists < base).astype(jnp.int32), axis=1, keepdims=True)
    lane = lax.broadcasted_iota(jnp.int32, (lists.shape[0], LANES), 1)
    at = first + lane % z.cap
    parts = []
    for side in range(FSUB // LANES):
        index = jnp.clip(at - side * LANES, 0, LANES - 1)
        half = lists[:, side * LANES : (side + 1) * LANES]
        parts.append(jnp.take_along_axis(half, index, axis=1, mode="promise_in_bounds"))
    loc = jnp.where(at < LANES, parts[0], parts[1]) - base
    return jnp.clip(loc, 0, z.feed_dev - 1)


def emit_spectra(z, scale, chunk, me_ref, spectra, loc_ref, spec_ref, sends, quads, base=0):
    lane = lax.broadcasted_iota(jnp.int32, (z.rows_dev, LANES), 1)
    frame = (lane // z.cap) ^ (me_ref[0] % z.lane_frames)
    start = frame * z.cap
    few = BAND_CH // 2
    for owner in range(z.devices):
        top = owner * BAND_CH
        rows = [x[top + p : top + p + few] for p in (0, few) for x in spectra]
        rows = jnp.concatenate(rows, axis=0) * scale
        columns = slice(base * z.width, (base + quads) * z.width)
        spec_ref[owner * z.rows_dev : (owner + 1) * z.rows_dev, columns] = rows.astype(
            jnp.bfloat16
        )
        band = owner * z.bands_here + chunk
        loc = loc_ref[band : band + 1, :]
        index = start + loc % z.cap
        lower = jnp.broadcast_to(loc, index.shape) < z.cap
        for q in range(quads):
            parts = []
            for side in range(2):
                left = q * z.width + side * LANES
                parts.append(
                    jnp.take_along_axis(
                        rows[:, left : left + LANES], index, axis=1, mode="promise_in_bounds"
                    )
                )
            picked = jnp.where(lower, parts[0], parts[1])
            for parity, (send_ref, unit, stride) in enumerate(sends):
                half = [
                    picked[p * BAND_CH + parity * few : p * BAND_CH + parity * few + few]
                    for p in range(2)
                ]
                half = jnp.concatenate(half, axis=0).astype(jnp.bfloat16)
                send_ref[owner, unit + (base + q) * stride] = half


def filter_tile(z, main_ref, halo, win_ref, off, f0, begin):
    lanes = slice(off, off + LANES)
    taps = [win_ref[k : k + 1, lanes] for k in range(TAPS)]
    frames = []
    for t in range(begin, begin + z.lane_frames + TAPS - 1):
        if t < z.step_frames:
            x = main_ref[f0 : f0 + 16, t * NFFT + off : t * NFFT + off + LANES]
        else:
            x = halo[t - z.step_frames][f0 : f0 + 16, lanes]
        frames.append(x.astype(jnp.float32))
    totals = []
    for t in range(z.lane_frames):
        total = taps[0] * frames[t]
        for k in range(1, TAPS):
            total = total + taps[k] * frames[t + k]
        totals.append(total)
    if z.cap < 16:
        totals = [
            jnp.concatenate([totals[t][h : h + 8], totals[t + 1][h : h + 8]], axis=0)
            for t in range(0, z.lane_frames, 2)
            for h in (0, 8)
        ]
    out = []
    for i, total in enumerate(totals):
        if z.cap < 16:
            t, half, feed = 2 * (i // 2), i % 2, 0
        else:
            t, half, feed = i, f0 // z.cap, f0 % z.cap
        out.append((half * LANES + t * z.cap + feed, total.astype(jnp.bfloat16)))
    return out


def filter_fold(z, main_ref, halo, win_ref, filt_ref, off, quad):
    far = off + NFFT // 2
    begin = quad * z.lane_frames
    folded = {}
    for f0 in range(0, z.feed_dev, 16):
        low = filter_tile(z, main_ref, halo, win_ref, off, f0, begin)
        high = filter_tile(z, main_ref, halo, win_ref, far, f0, begin)
        for (row, a), (_, b) in zip(low, high):
            folded[row] = (a + b, a - b)
            top = quad * z.width + row
            filt_ref[top : top + 16, off : off + LANES] = folded[row][0]
            filt_ref[top : top + 16, far : far + LANES] = folded[row][1]
    return [
        jnp.concatenate([folded[row][parity] for row in sorted(folded)], axis=0)
        for parity in range(2)
    ]


def product(z, basis_ref, parity, c, samples):
    rows = slice(c * z.rows // 2, (c + 1) * z.rows // 2)
    return lax.dot_general(
        basis_ref[parity, rows, :], samples, NT, preferred_element_type=jnp.float32
    )


def first_kernel(
    z, scale, chunks, held, me_ref, main_ref, h0_ref, h1_ref, h2_ref, win_ref, basis_ref,
    lists_ref, *refs,
):
    filt_ref, spec_refs, send_ref, loc_ref = refs[held], refs[held + 1 : -2], refs[-2], refs[-1]
    halo = (h0_ref, h1_ref, h2_ref)
    loc_ref[...] = find_places(z, me_ref[0], lists_ref[...])

    def emit(quad, spectra):
        for c, chunk in enumerate(chunks):
            unit = c * 2 * z.step_quads
            sends = [(send_ref, unit, 2), (send_ref, unit + 1, 2)]
            emit_spectra(
                z, scale, chunk, me_ref, spectra[c], loc_ref, spec_refs[c], sends, 1, quad
            )

    before = None
    for quad in range(z.step_quads):
        tiles = [
            filter_fold(z, main_ref, halo, win_ref, filt_ref, off, quad)
            for off in range(0, NFFT // 2, LANES)
        ]
        samples = [jnp.concatenate([tile[p] for tile in tiles], axis=1) for p in range(2)]
        if before is not None:
            emit(quad - 1, before)
        before = [
            [product(z, basis_ref, p, c, samples[p]) for p in range(2)]
            for c in range(len(chunks))
        ]
    emit(z.step_quads - 1, before)


def next_kernel(z, scale, chunks, me_ref, filt_ref, basis_ref, lists_ref, held_ref, *refs):
    begun_ref, last_ref, loc_ref = refs[2], refs[3], refs[-1]
    loc_ref[...] = find_places(z, me_ref[0], lists_ref[...])
    half = NFFT // 2
    spectra = [
        [
            product(z, basis_ref, p, c, filt_ref[:, p * half : (p + 1) * half])
            for p in range(2)
        ]
        for c in range(2)
    ]
    sends = [
        [(begun_ref, 0, 2), (begun_ref, 1, 2)],
        [(begun_ref, 2 * z.step_quads, 1), (last_ref, 0, 1)],
    ]
    for c, chunk in enumerate(chunks):
        emit_spectra(
            z, scale, chunk, me_ref, spectra[c], loc_ref, refs[c], sends[c], z.step_quads
        )


def whole_spec(shape):
    return pl.BlockSpec(shape, lambda *g: (0,) * len(shape))


class Spectra:

    def __init__(self, z, me, voltages, band_feeds):
        window = fir_window()
        self.z = z
        self.fine = copy.copy(z)
        self.fine.set_steps(z.quads)
        self.me = me
        self.scale = float(np.sqrt(2.0 / np.sum(window * window)))
        self.window = jnp.asarray(window.astype(np.float32))
        self.voltages = voltages
        self.lists = band_feeds
        self.ids = np.arange(CHANNELS).reshape(z.devices, z.chunks, BAND_CH)
        self.me_spec = pl.BlockSpec(memory_space=pltpu.SMEM)
        self.spec_shape = jax.ShapeDtypeStruct((z.rows, FR * z.feed_dev), jnp.bfloat16)
        self.filt_shape = jax.ShapeDtypeStruct((FR * z.feed_dev, NFFT), jnp.bfloat16)

    def basis(self, chunks):
        sides = []
        for parity in range(2):
            rows = [dft_rows(self.ids[:, k, parity::2].reshape(-1)) for k in chunks]
            rows = np.stack(rows).reshape(len(chunks), self.z.devices, BAND_CH // 2, 2, -1)
            rows = np.transpose(rows, (0, 1, 3, 2, 4))
            sides.append(rows.reshape(len(chunks) * self.z.rows // 2, NFFT // 2))
        return jnp.asarray(np.stack(sides))

    def message(self, units):
        return jax.ShapeDtypeStruct((self.z.devices, units, BAND_CH, LANES), jnp.bfloat16)

    def common(self, steps, chunks):
        z = self.z
        flops = len(chunks) * z.rows * NFFT * z.step_lanes * steps
        return dict(
            grid=(steps,),
            scratch_shapes=[pltpu.VMEM((BANDS, LANES), jnp.int32)],
            compiler_params=pltpu.CompilerParams(vmem_limit_bytes=VMEM),
            cost_estimate=pl.CostEstimate(
                flops=flops, bytes_accessed=3_000_000 * steps, transcendentals=0
            ),
        )

    def first(self, begin, steps, chunks, basis, units, base, held):
        z = self.fine
        count = len(chunks)
        base = base // (count * 2 * z.step_quads)

        def halo_spec(h):
            return pl.BlockSpec(
                (z.feed_dev, NFFT), lambda g: (0, z.step_frames * (begin + g + 1) + h)
            )

        send_block = (z.devices, count * 2 * z.step_quads, BAND_CH, LANES)
        operands = [self.me] + [self.voltages] * 4 + [self.window, basis, self.lists]
        aliases = {len(operands) + i: i for i in range(len(held))}
        return pl.pallas_call(
            functools.partial(first_kernel, z, self.scale, chunks, len(held)),
            in_specs=[
                self.me_spec,
                pl.BlockSpec((z.feed_dev, z.step_frames * NFFT), lambda g: (0, begin + g)),
                halo_spec(0),
                halo_spec(1),
                halo_spec(2),
                whole_spec((TAPS, NFFT)),
                whole_spec(basis.shape),
                whole_spec(self.lists.shape),
            ]
            + [pl.BlockSpec(memory_space=pl.ANY)] * len(held),
            out_specs=[
                pl.BlockSpec((z.step_lanes, NFFT), lambda g: (begin + g, 0)),
            ]
            + [pl.BlockSpec((z.rows, z.step_lanes), lambda g: (0, begin + g))] * count
            + [pl.BlockSpec(send_block, lambda g: (0, base + g, 0, 0))],
            out_shape=[self.filt_shape] + [self.spec_shape] * count + [self.message(units)],
            input_output_aliases=aliases,
            name="filter_spectra",
            **self.common(steps, chunks),
        )(*operands, *held)

    def next(self, chunks, filt, held):
        z = self.z
        basis = self.basis(chunks)
        begun = 3 * z.step_quads
        operands = [self.me, filt, basis, self.lists, held]
        return pl.pallas_call(
            functools.partial(next_kernel, z, self.scale, chunks),
            in_specs=[
                self.me_spec,
                pl.BlockSpec((z.step_lanes, NFFT), lambda g: (g, 0)),
                whole_spec(basis.shape),
                whole_spec(self.lists.shape),
                pl.BlockSpec(memory_space=pl.ANY),
            ],
            out_specs=[pl.BlockSpec((z.rows, z.step_lanes), lambda g: (0, g))] * 2
            + [
                pl.BlockSpec((z.devices, begun, BAND_CH, LANES), lambda g: (0, g, 0, 0)),
                pl.BlockSpec((z.devices, z.step_quads, BAND_CH, LANES), lambda g: (0, g, 0, 0)),
            ],
            out_shape=[self.spec_shape] * 2
            + [self.message(held.shape[1]), self.message(z.quads)],
            input_output_aliases={4: 2},
            name="spectra_next",
            **self.common(z.steps, chunks),
        )(*operands)


def receive_kernel(z, parities, step_pairs, runs, arrays, even_steps, beams, *refs):
    arr_refs, key_ref = refs[:arrays], refs[arrays]
    buf_ref, rows_ref, pick_ref, sems = refs[-4:]
    vis_ref = refs[-6] if beams else refs[-5]
    g = pl.program_id(0)
    if beams:
        kept_ref, away_ref, beams_ref = refs[arrays + 1], refs[arrays + 2], refs[-5]

        @pl.when(g == 0)
        def _():
            beams_ref[...] = kept_ref[0] + away_ref[0].astype(jnp.float32)

    lf = z.lane_frames
    few = BAND_CH // 2
    steps = few // step_pairs
    depth = buf_ref.shape[2] * BAND_CH
    slots = buf_ref.shape[0]
    at = g % steps

    def copies(c):
        return [
            pltpu.make_async_copy(
                arr_refs[array].at[:, first : first + count],
                buf_ref.at[c % slots, :, place : place + count],
                sems.at[c % slots, i],
            )
            for i, (array, first, count, place) in enumerate(runs[c])
        ]

    @pl.when(g == 0)
    def _():
        for one in copies(0):
            one.start()

    @pl.when(at == 0)
    def _():
        slot = lax.broadcasted_iota(jnp.int32, (z.groups * LANES, FSUB), 0)
        for tau in range(lf):
            key = key_ref[g // steps, tau : tau + 1, :]
            pick_ref[tau] = jnp.where(slot == key, 1.0, 0.0).astype(jnp.bfloat16)

    for c in range(len(runs)):

        @pl.when(g == c * steps)
        def _():
            for one in copies(c):
                one.wait()
            if c + 1 < len(runs):
                for one in copies(c + 1):
                    one.start()

    @pl.when(at == 0)
    def _():
        c = g // steps
        lane_group = lax.broadcasted_iota(jnp.int32, (depth, LANES), 1) // z.cap
        for tau in range(lf):
            tiles = []
            for big in range(z.groups):
                tile = buf_ref[c % slots, big * lf + tau].reshape(depth, LANES)
                for lane in range(1, lf):
                    block = buf_ref[c % slots, big * lf + (lane ^ tau)].reshape(depth, LANES)
                    tile = jnp.where(lane_group == lane, block, tile)
                tiles.append(tile)
            rows = jnp.dot(
                jnp.concatenate(tiles, axis=1), pick_ref[tau], preferred_element_type=jnp.float32
            )
            for side in range(FSUB // LANES):
                rows_ref[side, tau * depth : (tau + 1) * depth, :] = rows[
                    :, side * LANES : (side + 1) * LANES
                ]

    def correlate(todo):
        operands = []
        for i, p in todo:
            halves = []
            for part in range(2):
                first = p * BAND_CH + part * few + at * step_pairs + i
                halves.append(
                    jnp.concatenate(
                        [
                            rows_ref[side, pl.ds(first, FR, stride=parities * BAND_CH), :]
                            for side in range(FSUB // LANES)
                        ],
                        axis=1,
                    )
                )
            real, imag = halves
            both = jnp.concatenate([real, imag], axis=0)
            turned = jnp.concatenate([-imag, real], axis=0)
            right = jnp.concatenate([both, turned], axis=1).astype(jnp.bfloat16)
            operands.append((both.astype(jnp.bfloat16).T, right))
        outs = [
            jnp.dot(left, right, preferred_element_type=jnp.float32)
            for left, right in operands
        ]
        for (i, p), out in zip(todo, outs):
            out = out * (1.0 / FR)
            vis_ref[i, p, 0] = out[:, :FSUB]
            vis_ref[i, p, 1] = out[:, FSUB:]

    every = [(i, p) for i in range(step_pairs) for p in range(parities)]
    if even_steps:
        begin = len(runs) * steps - even_steps

        @pl.when(g < begin)
        def _():
            correlate(every)

        @pl.when(g >= begin)
        def _():
            correlate([(i, p) for i, p in every if p == 0])

    else:
        correlate(every)


def receive_call(z, chunk, parity, arrived, keys, vis, even_last=False, beams=()):
    parities = 2 if parity is None else 1
    step_pairs = 4
    steps = BAND_CH // 2 // step_pairs
    at = 0 if parity is None else parity
    out_shape = jax.ShapeDtypeStruct((z.chan_dev // 2, 2, 2, FSUB, FSUB), jnp.float32)
    arrays = []
    runs = []
    for one in arrived:
        runs.append([])
        for got, first, count, place in one:
            if not any(got is x for x in arrays):
                arrays.append(got)
            index = [got is x for x in arrays].index(True)
            runs[-1].append((index, first, count, place))
    units = parities * z.quads
    slots = min(2, len(runs))
    operands = arrays + [keys]
    in_specs = [pl.BlockSpec(memory_space=pl.ANY)] * len(arrays) + [whole_spec(keys.shape)]
    aliases = {}
    out_specs = [
        pl.BlockSpec(
            (step_pairs, parities, 2, FSUB, FSUB),
            lambda g: (chunk * steps + g, at, 0, 0, 0),
        )
    ]
    out_shape = [out_shape]
    if beams:
        in_specs += [whole_spec(x.shape) for x in beams]
        operands += beams
        out_specs.append(whole_spec(beams[0].shape[1:]))
        out_shape.append(jax.ShapeDtypeStruct(beams[0].shape[1:], jnp.float32))
    if vis is not None:
        in_specs.append(pl.BlockSpec(memory_space=pl.ANY))
        aliases = {len(operands): 0}
        operands.append(vis)
    share = parities * len(runs)
    return pl.pallas_call(
        functools.partial(
            receive_kernel, z, parities, step_pairs, runs, len(arrays),
            steps if even_last else 0, bool(beams),
        ),
        grid=(len(runs) * steps,),
        in_specs=in_specs,
        out_specs=out_specs,
        out_shape=out_shape,
        input_output_aliases=aliases,
        scratch_shapes=[
            pltpu.VMEM((slots, z.devices, units, BAND_CH, LANES), jnp.bfloat16),
            pltpu.VMEM((FSUB // LANES, z.lane_frames * units * BAND_CH, LANES), jnp.float32),
            pltpu.VMEM((z.lane_frames, z.groups * LANES, FSUB), jnp.bfloat16),
            pltpu.SemaphoreType.DMA((slots, max(len(x) for x in runs))),
        ],
        compiler_params=pltpu.CompilerParams(vmem_limit_bytes=VMEM // 2),
        cost_estimate=pl.CostEstimate(
            flops=2_000_000_000 * share, bytes_accessed=5_000_000 * share, transcendentals=0
        ),
        name="correlate",
    )(*operands)


def beam_kernel(z, me_ref, *refs):
    spec_refs = refs[: z.chunks]
    cos_base, sin_base, cos_step, sin_step, sum_ref, out_ref, prod_ref, row_ref = refs[z.chunks :]
    count = z.chan_dev
    weights = []
    for g in range(BEAMS):
        c0, s0 = cos_base[0, g : g + 1, :], sin_base[0, g : g + 1, :]
        c1, s1 = cos_step[g], sin_step[g]
        weights.append(
            ((c0 * c1 - s0 * s1).astype(jnp.bfloat16), (s0 * c1 + c0 * s1).astype(jnp.bfloat16))
        )
    for q in range(z.quads):
        lanes = slice(q * z.width, (q + 1) * z.width)
        x = [ref[:, lanes] for ref in spec_refs]
        real = jnp.concatenate([v[:BAND_CH] for v in x], axis=0)
        imag = jnp.concatenate([v[BAND_CH:] for v in x], axis=0)
        for g in range(BEAMS):
            c, s = weights[g]
            pair = (c * real + s * imag, c * imag - s * real)
            for part in range(2):
                row = (part * BEAMS + g) * count
                both = pair[part][:, :LANES] + pair[part][:, LANES:]
                prod_ref[row : row + count, q * LANES : (q + 1) * LANES] = both
    sums = jnp.dot(prod_ref[...], sum_ref[...], preferred_element_type=jnp.float32)
    sums = sums * (1.0 / np.sqrt(F))
    few = BAND_CH // 2
    for j in range(2 * BEAMS):
        for i in range(count // few):
            first = i // 2 * BAND_CH + i % 2
            top = j * count + i * few
            row_ref[j, pl.ds(first, few, stride=2), :] = sums[top : top + few]
        out_ref[0, :, j * FR : (j + 1) * FR] = row_ref[j][:, :FR]


def beam_call(z, me, spectra, delays):
    bits = z.devices.bit_length() - 1
    lanes = FR * z.feed_dev
    halves = delays.reshape(BEAMS, 2, 1, z.cap)
    spread = jnp.broadcast_to(halves, (BEAMS, 2, z.lane_frames, z.cap)).reshape(BEAMS, z.width)
    unit = 2.0 * jnp.pi / NFFT
    owners = jnp.arange(z.devices, dtype=jnp.int32).astype(jnp.float32) * z.chan_dev
    inner = np.arange(z.chunks)[:, None] * BAND_CH + ORDER[None, :]
    inner = jnp.asarray(inner.reshape(-1).astype(np.float32))
    base = unit * (spread[None, :, :] * owners[:, None, None])
    step = unit * (spread[:, None, :] * inner[None, :, None])
    frame = (np.arange(FR * z.cap) // LANES) * z.lane_frames
    frame = frame + (np.arange(FR * z.cap) % LANES) // z.cap
    sums = (frame[:, None] == np.arange(LANES)[None, :]).astype(ml_dtypes.bfloat16)

    def owner(j, me_ref):
        k = 0
        for b in range(bits):
            k = k | (((j >> b) & 1) << (bits - 1 - b))
        return me_ref[0] ^ k

    base_spec = pl.BlockSpec(
        (1, BEAMS, z.width), lambda j, me_ref: (owner(j, me_ref), 0, 0)
    )
    grid_spec = pltpu.PrefetchScalarGridSpec(
        num_scalar_prefetch=1,
        grid=(z.devices,),
        in_specs=[
            pl.BlockSpec((z.rows_dev, lanes), lambda j, me_ref: (owner(j, me_ref), 0))
            for _ in range(z.chunks)
        ]
        + [base_spec, base_spec, whole_spec(step.shape), whole_spec(step.shape)]
        + [whole_spec(sums.shape)],
        out_specs=pl.BlockSpec(
            (1, z.chan_dev, 2 * BEAMS * FR), lambda j, me_ref: (j, 0, 0)
        ),
        scratch_shapes=[
            pltpu.VMEM((2 * BEAMS * z.chan_dev, FR * z.cap), jnp.bfloat16),
            pltpu.VMEM((2 * BEAMS, z.chan_dev, LANES), jnp.float32),
        ],
    )
    return pl.pallas_call(
        functools.partial(beam_kernel, z),
        grid_spec=grid_spec,
        out_shape=jax.ShapeDtypeStruct((z.devices, z.chan_dev, 2 * BEAMS * FR), jnp.float32),
        compiler_params=pltpu.CompilerParams(vmem_limit_bytes=VMEM),
        cost_estimate=pl.CostEstimate(
            flops=20_000_000_000, bytes_accessed=20_000_000, transcendentals=0
        ),
        name="beam_sums",
    )(
        me, *spectra, jnp.cos(base), jnp.sin(base), jnp.cos(step), jnp.sin(step),
        jnp.asarray(sums),
    )


def swap(z, x, offset):
    return lax.ppermute(x, "chan", [(i, i ^ offset) for i in range(z.devices)])


def exchange(x):
    return lax.all_to_all(x, "chan", split_axis=0, concat_axis=0, tiled=True)


def on_device(voltages, delays, band_feeds):
    z = Sizes(lax.axis_size("chan"), voltages.shape[0])
    me = lax.axis_index("chan")
    me_array = me.astype(jnp.int32).reshape(1)

    own = lax.dynamic_slice_in_dim(band_feeds, me * z.bands_here, z.bands_here, 0)
    source = own // z.feed_dev
    before = jnp.sum(
        (own[:, None, :] < (source * z.feed_dev)[:, :, None]).astype(jnp.int32), axis=2
    )
    place = jnp.arange(FSUB, dtype=jnp.int32)[None, :] - before
    tau = jnp.arange(z.lane_frames, dtype=jnp.int32)
    big = (source // z.lane_frames) * LANES + place
    group = (source % z.lane_frames)[:, None, :] ^ tau[None, :, None]
    take_key = big[:, None, :] + z.cap * group

    calls = Spectra(z, me_array, voltages, band_feeds)
    early = list(range(z.early))
    basis = calls.basis(early)
    share = 2 * calls.fine.step_quads
    step = z.early * share
    arrived = [[] for _ in range(z.chunks)]
    steps = z.parts[0]
    filt, *spectra, send = calls.first(0, steps, early, basis, steps * step, 0, [])
    got = exchange(send)
    for c in early:
        arrived[c] += [(got, g * step + c * share, share, g * share) for g in range(steps)]
    if len(z.parts) > 1:
        begin, steps = steps, z.parts[1]
        late, begun = 2 * z.step_quads, 3 * z.step_quads
        base = z.steps * begun
        filt, *spectra, send = calls.first(
            begin, steps, early, basis, base + steps * step, base, [filt, *spectra]
        )
        *more, send, last = calls.next([z.chunks - 2, z.chunks - 1], filt, send)
        spectra = spectra + more
        got = exchange(send)
        for c in early:
            arrived[c] += [
                (got, base + g * step + c * share, share, (begin + g) * share)
                for g in range(steps)
            ]
        for g in range(z.steps):
            first = g * begun
            arrived[-2].append((got, first, late, g * late))
            arrived[-1] += [
                (got, first + late + q, 1, g * late + 2 * q) for q in range(z.step_quads)
            ]

    beams, bit = beam_call(z, me_array, spectra, delays), 1
    while beams.shape[0] > 2:
        half = beams.shape[0] // 2
        beams, bit = beams[:half] + swap(z, beams[half:], bit), 2 * bit
    kept, away = beams[:1], beams[1:].astype(jnp.bfloat16)
    if len(z.parts) > 1:
        last, kept, away = lax.optimization_barrier((last, kept, away))
        got = exchange(last)
        away = swap(z, away, bit)
        k = z.chunks - 1
        (vis,) = receive_call(z, 0, None, arrived, take_key, None, even_last=True)
        odd = [[(got, 0, z.quads, 0)]]
        vis, beams = receive_call(z, k, 1, odd, take_key[k:], vis, beams=[kept, away])
    else:
        (vis,) = receive_call(z, 0, None, arrived, take_key, None)
        beams = (kept + swap(z, away, bit).astype(jnp.float32)).reshape(z.chan_dev, -1)
    return (vis.reshape(z.chan_dev, 2, FSUB, FSUB), beams)


def solution(mesh):
    in_specs = (P(("grp", "chan"), None), P(None, ("grp", "chan")), P())
    out_specs = (P(("grp", "chan"), None, None, None), P(("grp", "chan"), None))
    return jax.shard_map(
        on_device, mesh=mesh, in_specs=in_specs, out_specs=out_specs, check_vma=False
    )
```

```python
import copy
import functools

import jax
import jax.numpy as jnp
import ml_dtypes
import numpy as np
from jax import lax
from jax.experimental import pallas as pl
from jax.experimental.pallas import tpu as pltpu
from jax.sharding import PartitionSpec as P

F = 1024
CHANNELS = 1024
TAPS = 4
BAND_CH = 16
BEAMS = 4
FR = 48
NFFT = 2048
BANDS = 64
FSUB = 256
LANES = 128
VMEM = 56 * 1024 * 1024

NT = (((1,), (1,)), ((), ()))


def fir_window():
    ids = np.arange(TAPS * NFFT, dtype=np.float64)
    centered = (ids - 0.5 * TAPS * NFFT + 0.5) / NFFT
    hann_part = 0.5 - 0.5 * np.cos(2.0 * np.pi * (ids + 0.5) / (TAPS * NFFT))
    return (np.sinc(centered) * hann_part).reshape(TAPS, NFFT)


ORDER = np.concatenate([np.arange(0, BAND_CH, 2), np.arange(1, BAND_CH, 2)])


def dft_rows(chan_ids):
    m = np.arange(NFFT // 2, dtype=np.int64)
    turns = (chan_ids[..., None].astype(np.int64) * m) % NFFT
    table = 2.0 * np.pi * np.arange(NFFT) / NFFT
    cosine = np.cos(table).astype(np.float32).astype(ml_dtypes.bfloat16)
    sine = (-np.sin(table)).astype(np.float32).astype(ml_dtypes.bfloat16)
    return np.stack([cosine[turns], sine[turns]], axis=1)


class Sizes:
    def __init__(self, devices, feed_dev):
        self.devices = devices
        self.feed_dev = feed_dev
        self.cap = feed_dev // 2
        self.lane_frames = LANES // self.cap
        self.quads = FR // self.lane_frames
        self.width = self.lane_frames * feed_dev
        self.set_steps(6 if self.quads % 6 == 0 else self.quads)
        self.chan_dev = CHANNELS // devices
        self.bands_here = BANDS // devices
        self.chunks = self.chan_dev // BAND_CH
        self.rows_dev = 2 * BAND_CH
        self.rows = devices * self.rows_dev
        self.groups = devices // self.lane_frames
        self.early = min(2, self.chunks)
        if self.chunks == 4:
            self.parts = (self.quads * 5 // 12, self.quads - self.quads * 5 // 12)
        else:
            self.early, self.parts = self.chunks, (self.quads,)

    def set_steps(self, steps):
        self.steps = steps
        self.step_frames = FR // steps
        self.step_quads = self.quads // steps
        self.step_lanes = self.step_frames * self.feed_dev


def find_places(z, me, lists):
    base = me * z.feed_dev
    first = jnp.sum((lists < base).astype(jnp.int32), axis=1, keepdims=True)
    lane = lax.broadcasted_iota(jnp.int32, (lists.shape[0], LANES), 1)
    at = first + lane % z.cap
    parts = []
    for side in range(FSUB // LANES):
        index = jnp.clip(at - side * LANES, 0, LANES - 1)
        half = lists[:, side * LANES : (side + 1) * LANES]
        parts.append(jnp.take_along_axis(half, index, axis=1, mode="promise_in_bounds"))
    loc = jnp.where(at < LANES, parts[0], parts[1]) - base
    return jnp.clip(loc, 0, z.feed_dev - 1)


def emit_spectra(z, scale, chunk, me_ref, spectra, loc_ref, spec_ref, sends, quads, base=0):
    lane = lax.broadcasted_iota(jnp.int32, (z.rows_dev, LANES), 1)
    frame = (lane // z.cap) ^ (me_ref[0] % z.lane_frames)
    start = frame * z.cap
    few = BAND_CH // 2
    for owner in range(z.devices):
        top = owner * BAND_CH
        rows = [x[top + p : top + p + few] for p in (0, few) for x in spectra]
        rows = jnp.concatenate(rows, axis=0) * scale
        columns = slice(base * z.width, (base + quads) * z.width)
        spec_ref[owner * z.rows_dev : (owner + 1) * z.rows_dev, columns] = rows.astype(
            jnp.bfloat16
        )
        band = owner * z.bands_here + chunk
        loc = loc_ref[band : band + 1, :]
        index = start + loc % z.cap
        lower = jnp.broadcast_to(loc, index.shape) < z.cap
        for q in range(quads):
            parts = []
            for side in range(2):
                left = q * z.width + side * LANES
                parts.append(
                    jnp.take_along_axis(
                        rows[:, left : left + LANES], index, axis=1, mode="promise_in_bounds"
                    )
                )
            picked = jnp.where(lower, parts[0], parts[1])
            for parity, (send_ref, unit, stride) in enumerate(sends):
                half = [
                    picked[p * BAND_CH + parity * few : p * BAND_CH + parity * few + few]
                    for p in range(2)
                ]
                half = jnp.concatenate(half, axis=0).astype(jnp.bfloat16)
                send_ref[owner, unit + (base + q) * stride] = half


def filter_tile(z, main_ref, halo, win_ref, off, f0, begin):
    lanes = slice(off, off + LANES)
    taps = [win_ref[k : k + 1, lanes] for k in range(TAPS)]
    frames = []
    for t in range(begin, begin + z.lane_frames + TAPS - 1):
        if t < z.step_frames:
            x = main_ref[f0 : f0 + 16, t * NFFT + off : t * NFFT + off + LANES]
        else:
            x = halo[t - z.step_frames][f0 : f0 + 16, lanes]
        frames.append(x.astype(jnp.float32))
    totals = []
    for t in range(z.lane_frames):
        total = taps[0] * frames[t]
        for k in range(1, TAPS):
            total = total + taps[k] * frames[t + k]
        totals.append(total)
    if z.cap < 16:
        totals = [
            jnp.concatenate([totals[t][h : h + 8], totals[t + 1][h : h + 8]], axis=0)
            for t in range(0, z.lane_frames, 2)
            for h in (0, 8)
        ]
    out = []
    for i, total in enumerate(totals):
        if z.cap < 16:
            t, half, feed = 2 * (i // 2), i % 2, 0
        else:
            t, half, feed = i, f0 // z.cap, f0 % z.cap
        out.append((half * LANES + t * z.cap + feed, total.astype(jnp.bfloat16)))
    return out


def filter_fold(z, main_ref, halo, win_ref, filt_ref, off, quad):
    far = off + NFFT // 2
    begin = quad * z.lane_frames
    folded = {}
    for f0 in range(0, z.feed_dev, 16):
        low = filter_tile(z, main_ref, halo, win_ref, off, f0, begin)
        high = filter_tile(z, main_ref, halo, win_ref, far, f0, begin)
        for (row, a), (_, b) in zip(low, high):
            folded[row] = (a + b, a - b)
            top = quad * z.width + row
            filt_ref[top : top + 16, off : off + LANES] = folded[row][0]
            filt_ref[top : top + 16, far : far + LANES] = folded[row][1]
    return [
        jnp.concatenate([folded[row][parity] for row in sorted(folded)], axis=0)
        for parity in range(2)
    ]


def product(z, basis_ref, parity, c, samples):
    rows = slice(c * z.rows // 2, (c + 1) * z.rows // 2)
    return lax.dot_general(
        basis_ref[parity, rows, :], samples, NT, preferred_element_type=jnp.float32
    )


def first_kernel(
    z, scale, chunks, held, me_ref, main_ref, h0_ref, h1_ref, h2_ref, win_ref, basis_ref,
    lists_ref, *refs,
):
    filt_ref, spec_refs, send_ref = refs[held], refs[held + 1 : -4], refs[-4]
    loc_ref, table_ref, sem = refs[-3:]
    halo = (h0_ref, h1_ref, h2_ref)
    fetch = pltpu.make_async_copy(basis_ref, table_ref, sem)
    begin = pl.program_id(0) == 0

    @pl.when(begin)
    def _():
        fetch.start()

    loc_ref[...] = find_places(z, me_ref[0], lists_ref[...])

    def emit(quad, spectra):
        for c, chunk in enumerate(chunks):
            unit = c * 2 * z.step_quads
            sends = [(send_ref, unit, 2), (send_ref, unit + 1, 2)]
            emit_spectra(
                z, scale, chunk, me_ref, spectra[c], loc_ref, spec_refs[c], sends, 1, quad
            )

    before = None
    for quad in range(z.step_quads):
        tiles = [
            filter_fold(z, main_ref, halo, win_ref, filt_ref, off, quad)
            for off in range(0, NFFT // 2, LANES)
        ]
        samples = [jnp.concatenate([tile[p] for tile in tiles], axis=1) for p in range(2)]
        if before is not None:
            emit(quad - 1, before)
        else:

            @pl.when(begin)
            def _():
                fetch.wait()

        before = [
            [product(z, table_ref, p, c, samples[p]) for p in range(2)]
            for c in range(len(chunks))
        ]
    emit(z.step_quads - 1, before)


def next_kernel(z, scale, chunks, me_ref, filt_ref, basis_ref, lists_ref, held_ref, *refs):
    begun_ref, last_ref, loc_ref = refs[2], refs[3], refs[-1]
    loc_ref[...] = find_places(z, me_ref[0], lists_ref[...])
    half = NFFT // 2
    spectra = [
        [
            product(z, basis_ref, p, c, filt_ref[:, p * half : (p + 1) * half])
            for p in range(2)
        ]
        for c in range(2)
    ]
    sends = [
        [(begun_ref, 0, 2), (begun_ref, 1, 2)],
        [(begun_ref, 2 * z.step_quads, 1), (last_ref, 0, 1)],
    ]
    for c, chunk in enumerate(chunks):
        emit_spectra(
            z, scale, chunk, me_ref, spectra[c], loc_ref, refs[c], sends[c], z.step_quads
        )


def whole_spec(shape):
    return pl.BlockSpec(shape, lambda *g: (0,) * len(shape))


class Spectra:

    def __init__(self, z, me, voltages, band_feeds):
        window = fir_window()
        self.z = z
        self.fine = copy.copy(z)
        self.fine.set_steps(z.quads)
        self.me = me
        self.scale = float(np.sqrt(2.0 / np.sum(window * window)))
        self.window = jnp.asarray(window.astype(np.float32))
        self.voltages = voltages
        self.lists = band_feeds
        self.ids = np.arange(CHANNELS).reshape(z.devices, z.chunks, BAND_CH)
        self.me_spec = pl.BlockSpec(memory_space=pltpu.SMEM)
        self.spec_shape = jax.ShapeDtypeStruct((z.rows, FR * z.feed_dev), jnp.bfloat16)
        self.filt_shape = jax.ShapeDtypeStruct((FR * z.feed_dev, NFFT), jnp.bfloat16)

    def basis(self, chunks):
        sides = []
        for parity in range(2):
            rows = [dft_rows(self.ids[:, k, parity::2].reshape(-1)) for k in chunks]
            rows = np.stack(rows).reshape(len(chunks), self.z.devices, BAND_CH // 2, 2, -1)
            rows = np.transpose(rows, (0, 1, 3, 2, 4))
            sides.append(rows.reshape(len(chunks) * self.z.rows // 2, NFFT // 2))
        return jnp.asarray(np.stack(sides))

    def message(self, units):
        return jax.ShapeDtypeStruct((self.z.devices, units, BAND_CH, LANES), jnp.bfloat16)

    def common(self, steps, chunks, scratch=()):
        z = self.z
        flops = len(chunks) * z.rows * NFFT * z.step_lanes * steps
        return dict(
            grid=(steps,),
            scratch_shapes=[pltpu.VMEM((BANDS, LANES), jnp.int32), *scratch],
            compiler_params=pltpu.CompilerParams(vmem_limit_bytes=VMEM),
            cost_estimate=pl.CostEstimate(
                flops=flops, bytes_accessed=3_000_000 * steps, transcendentals=0
            ),
        )

    def first(self, begin, steps, chunks, basis, units, base, held):
        z = self.fine
        count = len(chunks)
        base = base // (count * 2 * z.step_quads)

        def halo_spec(h):
            return pl.BlockSpec(
                (z.feed_dev, NFFT), lambda g: (0, z.step_frames * (begin + g + 1) + h)
            )

        send_block = (z.devices, count * 2 * z.step_quads, BAND_CH, LANES)
        operands = [self.me] + [self.voltages] * 4 + [self.window, basis, self.lists]
        aliases = {len(operands) + i: i for i in range(len(held))}
        return pl.pallas_call(
            functools.partial(first_kernel, z, self.scale, chunks, len(held)),
            in_specs=[
                self.me_spec,
                pl.BlockSpec((z.feed_dev, z.step_frames * NFFT), lambda g: (0, begin + g)),
                halo_spec(0),
                halo_spec(1),
                halo_spec(2),
                whole_spec((TAPS, NFFT)),
                pl.BlockSpec(memory_space=pltpu.HBM),
                whole_spec(self.lists.shape),
            ]
            + [pl.BlockSpec(memory_space=pl.ANY)] * len(held),
            out_specs=[
                pl.BlockSpec((z.step_lanes, NFFT), lambda g: (begin + g, 0)),
            ]
            + [pl.BlockSpec((z.rows, z.step_lanes), lambda g: (0, begin + g))] * count
            + [pl.BlockSpec(send_block, lambda g: (0, base + g, 0, 0))],
            out_shape=[self.filt_shape] + [self.spec_shape] * count + [self.message(units)],
            input_output_aliases=aliases,
            name="filter_spectra",
            **self.common(
                steps, chunks, [pltpu.VMEM(basis.shape, basis.dtype), pltpu.SemaphoreType.DMA]
            ),
        )(*operands, *held)

    def next(self, chunks, filt, held):
        z = self.z
        basis = self.basis(chunks)
        begun = 3 * z.step_quads
        operands = [self.me, filt, basis, self.lists, held]
        return pl.pallas_call(
            functools.partial(next_kernel, z, self.scale, chunks),
            in_specs=[
                self.me_spec,
                pl.BlockSpec((z.step_lanes, NFFT), lambda g: (g, 0)),
                whole_spec(basis.shape),
                whole_spec(self.lists.shape),
                pl.BlockSpec(memory_space=pl.ANY),
            ],
            out_specs=[pl.BlockSpec((z.rows, z.step_lanes), lambda g: (0, g))] * 2
            + [
                pl.BlockSpec((z.devices, begun, BAND_CH, LANES), lambda g: (0, g, 0, 0)),
                pl.BlockSpec((z.devices, z.step_quads, BAND_CH, LANES), lambda g: (0, g, 0, 0)),
            ],
            out_shape=[self.spec_shape] * 2
            + [self.message(held.shape[1]), self.message(z.quads)],
            input_output_aliases={4: 2},
            name="spectra_next",
            **self.common(z.steps, chunks),
        )(*operands)


def receive_kernel(z, parities, step_pairs, runs, arrays, even_steps, beams, *refs):
    arr_refs, key_ref = refs[:arrays], refs[arrays]
    buf_ref, rows_ref, pick_ref, sems = refs[-4:]
    vis_ref = refs[-6] if beams else refs[-5]
    g = pl.program_id(0)
    if beams:
        kept_ref, away_ref, beams_ref = refs[arrays + 1], refs[arrays + 2], refs[-5]

        @pl.when(g == 0)
        def _():
            beams_ref[...] = kept_ref[0] + away_ref[0].astype(jnp.float32)

    lf = z.lane_frames
    few = BAND_CH // 2
    steps = few // step_pairs
    depth = buf_ref.shape[2] * BAND_CH
    slots = buf_ref.shape[0]
    at = g % steps

    def copies(c):
        return [
            pltpu.make_async_copy(
                arr_refs[array].at[:, first : first + count],
                buf_ref.at[c % slots, :, place : place + count],
                sems.at[c % slots, i],
            )
            for i, (array, first, count, place) in enumerate(runs[c])
        ]

    @pl.when(g == 0)
    def _():
        for one in copies(0):
            one.start()

    @pl.when(at == 0)
    def _():
        slot = lax.broadcasted_iota(jnp.int32, (z.groups * LANES, FSUB), 0)
        for tau in range(lf):
            key = key_ref[g // steps, tau : tau + 1, :]
            pick_ref[tau] = jnp.where(slot == key, 1.0, 0.0).astype(jnp.bfloat16)

    for c in range(len(runs)):

        @pl.when(g == c * steps)
        def _():
            for one in copies(c):
                one.wait()
            if c + 1 < len(runs):
                for one in copies(c + 1):
                    one.start()

    @pl.when(at == 0)
    def _():
        c = g // steps
        lane_group = lax.broadcasted_iota(jnp.int32, (depth, LANES), 1) // z.cap
        for tau in range(lf):
            tiles = []
            for big in range(z.groups):
                tile = buf_ref[c % slots, big * lf + tau].reshape(depth, LANES)
                for lane in range(1, lf):
                    block = buf_ref[c % slots, big * lf + (lane ^ tau)].reshape(depth, LANES)
                    tile = jnp.where(lane_group == lane, block, tile)
                tiles.append(tile)
            rows = jnp.dot(
                jnp.concatenate(tiles, axis=1), pick_ref[tau], preferred_element_type=jnp.float32
            )
            for side in range(FSUB // LANES):
                rows_ref[side, tau * depth : (tau + 1) * depth, :] = rows[
                    :, side * LANES : (side + 1) * LANES
                ]

    def correlate(todo):
        operands = []
        for i, p in todo:
            halves = []
            for part in range(2):
                first = p * BAND_CH + part * few + at * step_pairs + i
                halves.append(
                    jnp.concatenate(
                        [
                            rows_ref[side, pl.ds(first, FR, stride=parities * BAND_CH), :]
                            for side in range(FSUB // LANES)
                        ],
                        axis=1,
                    )
                )
            real, imag = halves
            both = jnp.concatenate([real, imag], axis=0)
            turned = jnp.concatenate([-imag, real], axis=0)
            right = jnp.concatenate([both, turned], axis=1).astype(jnp.bfloat16)
            operands.append((both.astype(jnp.bfloat16).T, right))
        outs = [
            jnp.dot(left, right, preferred_element_type=jnp.float32)
            for left, right in operands
        ]
        for (i, p), out in zip(todo, outs):
            out = out * (1.0 / FR)
            vis_ref[i, p, 0] = out[:, :FSUB]
            vis_ref[i, p, 1] = out[:, FSUB:]

    every = [(i, p) for i in range(step_pairs) for p in range(parities)]
    if even_steps:
        begin = len(runs) * steps - even_steps

        @pl.when(g < begin)
        def _():
            correlate(every)

        @pl.when(g >= begin)
        def _():
            correlate([(i, p) for i, p in every if p == 0])

    else:
        correlate(every)


def receive_call(z, chunk, parity, arrived, keys, vis, even_last=False, beams=()):
    parities = 2 if parity is None else 1
    step_pairs = 4
    steps = BAND_CH // 2 // step_pairs
    at = 0 if parity is None else parity
    out_shape = jax.ShapeDtypeStruct((z.chan_dev // 2, 2, 2, FSUB, FSUB), jnp.float32)
    arrays = []
    runs = []
    for one in arrived:
        runs.append([])
        for got, first, count, place in one:
            if not any(got is x for x in arrays):
                arrays.append(got)
            index = [got is x for x in arrays].index(True)
            runs[-1].append((index, first, count, place))
    units = parities * z.quads
    slots = min(2, len(runs))
    operands = arrays + [keys]
    in_specs = [pl.BlockSpec(memory_space=pl.ANY)] * len(arrays) + [whole_spec(keys.shape)]
    aliases = {}
    out_specs = [
        pl.BlockSpec(
            (step_pairs, parities, 2, FSUB, FSUB),
            lambda g: (chunk * steps + g, at, 0, 0, 0),
        )
    ]
    out_shape = [out_shape]
    if beams:
        in_specs += [whole_spec(x.shape) for x in beams]
        operands += beams
        out_specs.append(whole_spec(beams[0].shape[1:]))
        out_shape.append(jax.ShapeDtypeStruct(beams[0].shape[1:], jnp.float32))
    if vis is not None:
        in_specs.append(pl.BlockSpec(memory_space=pl.ANY))
        aliases = {len(operands): 0}
        operands.append(vis)
    share = parities * len(runs)
    return pl.pallas_call(
        functools.partial(
            receive_kernel, z, parities, step_pairs, runs, len(arrays),
            steps if even_last else 0, bool(beams),
        ),
        grid=(len(runs) * steps,),
        in_specs=in_specs,
        out_specs=out_specs,
        out_shape=out_shape,
        input_output_aliases=aliases,
        scratch_shapes=[
            pltpu.VMEM((slots, z.devices, units, BAND_CH, LANES), jnp.bfloat16),
            pltpu.VMEM(
                (FSUB // LANES, z.lane_frames * units * BAND_CH + z.rows_dev, LANES), jnp.float32
            ),
            pltpu.VMEM((z.lane_frames, z.groups * LANES, FSUB), jnp.bfloat16),
            pltpu.SemaphoreType.DMA((slots, max(len(x) for x in runs))),
        ],
        compiler_params=pltpu.CompilerParams(vmem_limit_bytes=VMEM // 2),
        cost_estimate=pl.CostEstimate(
            flops=2_000_000_000 * share, bytes_accessed=5_000_000 * share, transcendentals=0
        ),
        name="correlate",
    )(*operands)


def beam_kernel(z, me_ref, *refs):
    spec_refs = refs[: z.chunks]
    cos_base, sin_base, cos_step, sin_step, sum_ref, out_ref, prod_ref, row_ref = refs[z.chunks :]
    count = z.chan_dev
    weights = []
    for g in range(BEAMS):
        c0, s0 = cos_base[0, g : g + 1, :], sin_base[0, g : g + 1, :]
        c1, s1 = cos_step[g], sin_step[g]
        weights.append(
            ((c0 * c1 - s0 * s1).astype(jnp.bfloat16), (s0 * c1 + c0 * s1).astype(jnp.bfloat16))
        )
    for q in range(z.quads):
        lanes = slice(q * z.width, (q + 1) * z.width)
        x = [ref[:, lanes] for ref in spec_refs]
        real = jnp.concatenate([v[:BAND_CH] for v in x], axis=0)
        imag = jnp.concatenate([v[BAND_CH:] for v in x], axis=0)
        for g in range(BEAMS):
            c, s = weights[g]
            pair = (c * real + s * imag, c * imag - s * real)
            for part in range(2):
                row = (part * BEAMS + g) * count
                both = pair[part][:, :LANES] + pair[part][:, LANES:]
                prod_ref[row : row + count, q * LANES : (q + 1) * LANES] = both
    sums = jnp.dot(prod_ref[...], sum_ref[...], preferred_element_type=jnp.float32)
    sums = sums * (1.0 / np.sqrt(F))
    few = BAND_CH // 2
    for j in range(2 * BEAMS):
        for i in range(count // few):
            first = i // 2 * BAND_CH + i % 2
            top = j * count + i * few
            row_ref[j, pl.ds(first, few, stride=2), :] = sums[top : top + few]
        out_ref[0, :, j * FR : (j + 1) * FR] = row_ref[j, :count, :FR]


def beam_call(z, me, spectra, delays):
    bits = z.devices.bit_length() - 1
    lanes = FR * z.feed_dev
    halves = delays.reshape(BEAMS, 2, 1, z.cap)
    spread = jnp.broadcast_to(halves, (BEAMS, 2, z.lane_frames, z.cap)).reshape(BEAMS, z.width)
    unit = 2.0 * jnp.pi / NFFT
    owners = jnp.arange(z.devices, dtype=jnp.int32).astype(jnp.float32) * z.chan_dev
    inner = np.arange(z.chunks)[:, None] * BAND_CH + ORDER[None, :]
    inner = jnp.asarray(inner.reshape(-1).astype(np.float32))
    base = unit * (spread[None, :, :] * owners[:, None, None])
    step = unit * (spread[:, None, :] * inner[None, :, None])
    frame = (np.arange(FR * z.cap) // LANES) * z.lane_frames
    frame = frame + (np.arange(FR * z.cap) % LANES) // z.cap
    sums = (frame[:, None] == np.arange(LANES)[None, :]).astype(ml_dtypes.bfloat16)

    def owner(j, me_ref):
        k = 0
        for b in range(bits):
            k = k | (((j >> b) & 1) << (bits - 1 - b))
        return me_ref[0] ^ k

    base_spec = pl.BlockSpec(
        (1, BEAMS, z.width), lambda j, me_ref: (owner(j, me_ref), 0, 0)
    )
    grid_spec = pltpu.PrefetchScalarGridSpec(
        num_scalar_prefetch=1,
        grid=(z.devices,),
        in_specs=[
            pl.BlockSpec((z.rows_dev, lanes), lambda j, me_ref: (owner(j, me_ref), 0))
            for _ in range(z.chunks)
        ]
        + [base_spec, base_spec, whole_spec(step.shape), whole_spec(step.shape)]
        + [whole_spec(sums.shape)],
        out_specs=pl.BlockSpec(
            (1, z.chan_dev, 2 * BEAMS * FR), lambda j, me_ref: (j, 0, 0)
        ),
        scratch_shapes=[
            pltpu.VMEM((2 * BEAMS * z.chan_dev, FR * z.cap), jnp.bfloat16),
            pltpu.VMEM((2 * BEAMS, z.chan_dev + BAND_CH, LANES), jnp.float32),
        ],
    )
    return pl.pallas_call(
        functools.partial(beam_kernel, z),
        grid_spec=grid_spec,
        out_shape=jax.ShapeDtypeStruct((z.devices, z.chan_dev, 2 * BEAMS * FR), jnp.float32),
        compiler_params=pltpu.CompilerParams(vmem_limit_bytes=VMEM),
        cost_estimate=pl.CostEstimate(
            flops=20_000_000_000, bytes_accessed=20_000_000, transcendentals=0
        ),
        name="beam_sums",
    )(
        me, *spectra, jnp.cos(base), jnp.sin(base), jnp.cos(step), jnp.sin(step),
        jnp.asarray(sums),
    )


def swap(z, x, offset):
    return lax.ppermute(x, "chan", [(i, i ^ offset) for i in range(z.devices)])


def exchange(x):
    return lax.all_to_all(x, "chan", split_axis=0, concat_axis=0, tiled=True)


def on_device(voltages, delays, band_feeds):
    z = Sizes(lax.axis_size("chan"), voltages.shape[0])
    me = lax.axis_index("chan")
    me_array = me.astype(jnp.int32).reshape(1)

    own = lax.dynamic_slice_in_dim(band_feeds, me * z.bands_here, z.bands_here, 0)
    source = own // z.feed_dev
    before = jnp.sum(
        (own[:, None, :] < (source * z.feed_dev)[:, :, None]).astype(jnp.int32), axis=2
    )
    place = jnp.arange(FSUB, dtype=jnp.int32)[None, :] - before
    tau = jnp.arange(z.lane_frames, dtype=jnp.int32)
    big = (source // z.lane_frames) * LANES + place
    group = (source % z.lane_frames)[:, None, :] ^ tau[None, :, None]
    take_key = big[:, None, :] + z.cap * group

    calls = Spectra(z, me_array, voltages, band_feeds)
    early = list(range(z.early))
    basis = calls.basis(early)
    share = 2 * calls.fine.step_quads
    step = z.early * share
    arrived = [[] for _ in range(z.chunks)]
    steps = z.parts[0]
    filt, *spectra, send = calls.first(0, steps, early, basis, steps * step, 0, [])
    got = exchange(send)
    for c in early:
        arrived[c] += [(got, g * step + c * share, share, g * share) for g in range(steps)]
    if len(z.parts) > 1:
        begin, steps = steps, z.parts[1]
        late, begun = 2 * z.step_quads, 3 * z.step_quads
        base = z.steps * begun
        filt, *spectra, send = calls.first(
            begin, steps, early, basis, base + steps * step, base, [filt, *spectra]
        )
        *more, send, last = calls.next([z.chunks - 2, z.chunks - 1], filt, send)
        spectra = spectra + more
        got = exchange(send)
        for c in early:
            arrived[c] += [
                (got, base + g * step + c * share, share, (begin + g) * share)
                for g in range(steps)
            ]
        for g in range(z.steps):
            first = g * begun
            arrived[-2].append((got, first, late, g * late))
            arrived[-1] += [
                (got, first + late + q, 1, g * late + 2 * q) for q in range(z.step_quads)
            ]

    beams, bit = beam_call(z, me_array, spectra, delays), 1
    while beams.shape[0] > 2:
        half = beams.shape[0] // 2
        beams, bit = beams[:half] + swap(z, beams[half:], bit), 2 * bit
    kept, away = beams[:1], beams[1:].astype(jnp.bfloat16)
    if len(z.parts) > 1:
        last, kept, away = lax.optimization_barrier((last, kept, away))
        got = exchange(last)
        away = swap(z, away, bit)
        k = z.chunks - 1
        (vis,) = receive_call(z, 0, None, arrived, take_key, None, even_last=True)
        odd = [[(got, 0, z.quads, 0)]]
        vis, beams = receive_call(z, k, 1, odd, take_key[k:], vis, beams=[kept, away])
    else:
        (vis,) = receive_call(z, 0, None, arrived, take_key, None)
        beams = (kept + swap(z, away, bit).astype(jnp.float32)).reshape(z.chan_dev, -1)
    return (vis.reshape(z.chan_dev, 2, FSUB, FSUB), beams)


def solution(mesh):
    in_specs = (P(("grp", "chan"), None), P(None, ("grp", "chan")), P())
    out_specs = (P(("grp", "chan"), None, None, None), P(("grp", "chan"), None))
    return jax.shard_map(
        on_device, mesh=mesh, in_specs=in_specs, out_specs=out_specs, check_vma=False
    )
```

```python
import copy
import functools

import jax
import jax.numpy as jnp
import ml_dtypes
import numpy as np
from jax import lax
from jax.experimental import pallas as pl
from jax.experimental.pallas import tpu as pltpu
from jax.sharding import PartitionSpec as P

F = 1024
CHANNELS = 1024
TAPS = 4
BAND_CH = 16
BEAMS = 4
FR = 48
NFFT = 2048
BANDS = 64
FSUB = 256
LANES = 128
VMEM = 56 * 1024 * 1024

NT = (((1,), (1,)), ((), ()))


def fir_window():
    ids = np.arange(TAPS * NFFT, dtype=np.float64)
    centered = (ids - 0.5 * TAPS * NFFT + 0.5) / NFFT
    hann_part = 0.5 - 0.5 * np.cos(2.0 * np.pi * (ids + 0.5) / (TAPS * NFFT))
    return (np.sinc(centered) * hann_part).reshape(TAPS, NFFT)


ORDER = np.concatenate([np.arange(0, BAND_CH, 2), np.arange(1, BAND_CH, 2)])


def dft_rows(chan_ids):
    m = np.arange(NFFT // 2, dtype=np.int64)
    turns = (chan_ids[..., None].astype(np.int64) * m) % NFFT
    table = 2.0 * np.pi * np.arange(NFFT) / NFFT
    cosine = np.cos(table).astype(np.float32).astype(ml_dtypes.bfloat16)
    sine = (-np.sin(table)).astype(np.float32).astype(ml_dtypes.bfloat16)
    return np.stack([cosine[turns], sine[turns]], axis=1)


class Sizes:
    def __init__(self, devices, feed_dev):
        self.devices = devices
        self.feed_dev = feed_dev
        self.cap = feed_dev // 2
        self.lane_frames = LANES // self.cap
        self.quads = FR // self.lane_frames
        self.width = self.lane_frames * feed_dev
        self.set_steps(6 if self.quads % 6 == 0 else self.quads)
        self.chan_dev = CHANNELS // devices
        self.bands_here = BANDS // devices
        self.chunks = self.chan_dev // BAND_CH
        self.rows_dev = 2 * BAND_CH
        self.rows = devices * self.rows_dev
        self.groups = devices // self.lane_frames
        self.early = min(2, self.chunks)
        if self.chunks == 4:
            self.parts = (self.quads * 5 // 12, self.quads - self.quads * 5 // 12)
        else:
            self.early, self.parts = self.chunks, (self.quads,)

    def set_steps(self, steps):
        self.steps = steps
        self.step_frames = FR // steps
        self.step_quads = self.quads // steps
        self.step_lanes = self.step_frames * self.feed_dev


def find_places(z, me, lists):
    base = me * z.feed_dev
    first = jnp.sum((lists < base).astype(jnp.int32), axis=1, keepdims=True)
    lane = lax.broadcasted_iota(jnp.int32, (lists.shape[0], LANES), 1)
    at = first + lane % z.cap
    parts = []
    for side in range(FSUB // LANES):
        index = jnp.clip(at - side * LANES, 0, LANES - 1)
        half = lists[:, side * LANES : (side + 1) * LANES]
        parts.append(jnp.take_along_axis(half, index, axis=1, mode="promise_in_bounds"))
    loc = jnp.where(at < LANES, parts[0], parts[1]) - base
    return jnp.clip(loc, 0, z.feed_dev - 1)


def emit_spectra(z, scale, chunk, me_ref, spectra, loc_ref, spec_ref, sends, quads, base=0):
    lane = lax.broadcasted_iota(jnp.int32, (z.rows_dev, LANES), 1)
    frame = (lane // z.cap) ^ (me_ref[0] % z.lane_frames)
    start = frame * z.cap
    few = BAND_CH // 2
    for owner in range(z.devices):
        top = owner * BAND_CH
        rows = [x[top + p : top + p + few] for p in (0, few) for x in spectra]
        rows = jnp.concatenate(rows, axis=0) * scale
        columns = slice(base * z.width, (base + quads) * z.width)
        spec_ref[owner * z.rows_dev : (owner + 1) * z.rows_dev, columns] = rows.astype(
            jnp.bfloat16
        )
        band = owner * z.bands_here + chunk
        loc = loc_ref[band : band + 1, :]
        index = start + loc % z.cap
        lower = jnp.broadcast_to(loc, index.shape) < z.cap
        for q in range(quads):
            parts = []
            for side in range(2):
                left = q * z.width + side * LANES
                parts.append(
                    jnp.take_along_axis(
                        rows[:, left : left + LANES], index, axis=1, mode="promise_in_bounds"
                    )
                )
            picked = jnp.where(lower, parts[0], parts[1])
            for parity, (send_ref, unit, stride) in enumerate(sends):
                half = [
                    picked[p * BAND_CH + parity * few : p * BAND_CH + parity * few + few]
                    for p in range(2)
                ]
                half = jnp.concatenate(half, axis=0).astype(jnp.bfloat16)
                send_ref[owner, unit + (base + q) * stride] = half


def filter_tile(z, main_ref, halo, win_ref, off, f0, begin):
    lanes = slice(off, off + LANES)
    taps = [win_ref[k : k + 1, lanes] for k in range(TAPS)]
    frames = []
    for t in range(begin, begin + z.lane_frames + TAPS - 1):
        if t < z.step_frames:
            x = main_ref[f0 : f0 + 16, t * NFFT + off : t * NFFT + off + LANES]
        else:
            x = halo[t - z.step_frames][f0 : f0 + 16, lanes]
        frames.append(x.astype(jnp.float32))
    totals = []
    for t in range(z.lane_frames):
        total = taps[0] * frames[t]
        for k in range(1, TAPS):
            total = total + taps[k] * frames[t + k]
        totals.append(total)
    if z.cap < 16:
        totals = [
            jnp.concatenate([totals[t][h : h + 8], totals[t + 1][h : h + 8]], axis=0)
            for t in range(0, z.lane_frames, 2)
            for h in (0, 8)
        ]
    out = []
    for i, total in enumerate(totals):
        if z.cap < 16:
            t, half, feed = 2 * (i // 2), i % 2, 0
        else:
            t, half, feed = i, f0 // z.cap, f0 % z.cap
        out.append((half * LANES + t * z.cap + feed, total.astype(jnp.bfloat16)))
    return out


def filter_fold(z, main_ref, halo, win_ref, filt_ref, off, quad):
    far = off + NFFT // 2
    begin = quad * z.lane_frames
    folded = {}
    for f0 in range(0, z.feed_dev, 16):
        low = filter_tile(z, main_ref, halo, win_ref, off, f0, begin)
        high = filter_tile(z, main_ref, halo, win_ref, far, f0, begin)
        for (row, a), (_, b) in zip(low, high):
            folded[row] = (a + b, a - b)
            top = quad * z.width + row
            filt_ref[top : top + 16, off : off + LANES] = folded[row][0]
            filt_ref[top : top + 16, far : far + LANES] = folded[row][1]
    return [
        jnp.concatenate([folded[row][parity] for row in sorted(folded)], axis=0)
        for parity in range(2)
    ]


def product(z, basis_ref, parity, c, samples):
    rows = slice(c * z.rows // 2, (c + 1) * z.rows // 2)
    return lax.dot_general(
        basis_ref[parity, rows, :], samples, NT, preferred_element_type=jnp.float32
    )


def first_kernel(
    z, scale, chunks, held, me_ref, main_ref, h0_ref, h1_ref, h2_ref, win_ref, basis_ref,
    lists_ref, *refs,
):
    filt_ref, spec_refs, send_ref, loc_ref = refs[held], refs[held + 1 : -2], refs[-2], refs[-1]
    halo = (h0_ref, h1_ref, h2_ref)
    loc_ref[...] = find_places(z, me_ref[0], lists_ref[...])

    def emit(quad, spectra):
        for c, chunk in enumerate(chunks):
            unit = c * 2 * z.step_quads
            sends = [(send_ref, unit, 2), (send_ref, unit + 1, 2)]
            emit_spectra(
                z, scale, chunk, me_ref, spectra[c], loc_ref, spec_refs[c], sends, 1, quad
            )

    before = None
    for quad in range(z.step_quads):
        tiles = [
            filter_fold(z, main_ref, halo, win_ref, filt_ref, off, quad)
            for off in range(0, NFFT // 2, LANES)
        ]
        samples = [jnp.concatenate([tile[p] for tile in tiles], axis=1) for p in range(2)]
        if before is not None:
            emit(quad - 1, before)
        before = [
            [product(z, basis_ref, p, c, samples[p]) for p in range(2)]
            for c in range(len(chunks))
        ]
    emit(z.step_quads - 1, before)


def next_kernel(z, scale, chunks, me_ref, filt_ref, basis_ref, lists_ref, held_ref, *refs):
    begun_ref, last_ref, loc_ref = refs[2], refs[3], refs[-1]
    loc_ref[...] = find_places(z, me_ref[0], lists_ref[...])
    half = NFFT // 2
    spectra = [
        [
            product(z, basis_ref, p, c, filt_ref[:, p * half : (p + 1) * half])
            for p in range(2)
        ]
        for c in range(2)
    ]
    sends = [
        [(begun_ref, 0, 2), (begun_ref, 1, 2)],
        [(begun_ref, 2 * z.step_quads, 1), (last_ref, 0, 1)],
    ]
    for c, chunk in enumerate(chunks):
        emit_spectra(
            z, scale, chunk, me_ref, spectra[c], loc_ref, refs[c], sends[c], z.step_quads
        )


def whole_spec(shape):
    return pl.BlockSpec(shape, lambda *g: (0,) * len(shape))


class Spectra:

    def __init__(self, z, me, voltages, band_feeds):
        window = fir_window()
        self.z = z
        self.fine = copy.copy(z)
        self.fine.set_steps(z.quads)
        self.me = me
        self.scale = float(np.sqrt(2.0 / np.sum(window * window)))
        self.window = jnp.asarray(window.astype(np.float32))
        self.voltages = voltages
        self.lists = band_feeds
        self.ids = np.arange(CHANNELS).reshape(z.devices, z.chunks, BAND_CH)
        self.me_spec = pl.BlockSpec(memory_space=pltpu.SMEM)
        self.spec_shape = jax.ShapeDtypeStruct((z.rows, FR * z.feed_dev), jnp.bfloat16)
        self.filt_shape = jax.ShapeDtypeStruct((FR * z.feed_dev, NFFT), jnp.bfloat16)

    def basis(self, chunks):
        sides = []
        for parity in range(2):
            rows = [dft_rows(self.ids[:, k, parity::2].reshape(-1)) for k in chunks]
            rows = np.stack(rows).reshape(len(chunks), self.z.devices, BAND_CH // 2, 2, -1)
            rows = np.transpose(rows, (0, 1, 3, 2, 4))
            sides.append(rows.reshape(len(chunks) * self.z.rows // 2, NFFT // 2))
        return jnp.asarray(np.stack(sides))

    def message(self, units):
        return jax.ShapeDtypeStruct((self.z.devices, units, BAND_CH, LANES), jnp.bfloat16)

    def common(self, steps, chunks):
        z = self.z
        flops = len(chunks) * z.rows * NFFT * z.step_lanes * steps
        return dict(
            grid=(steps,),
            scratch_shapes=[pltpu.VMEM((BANDS, LANES), jnp.int32)],
            compiler_params=pltpu.CompilerParams(vmem_limit_bytes=VMEM),
            cost_estimate=pl.CostEstimate(
                flops=flops, bytes_accessed=3_000_000 * steps, transcendentals=0
            ),
        )

    def first(self, begin, steps, chunks, basis, units, base, held):
        z = self.fine
        count = len(chunks)
        base = base // (count * 2 * z.step_quads)

        def halo_spec(h):
            return pl.BlockSpec(
                (z.feed_dev, NFFT), lambda g: (0, z.step_frames * (begin + g + 1) + h)
            )

        send_block = (z.devices, count * 2 * z.step_quads, BAND_CH, LANES)
        operands = [self.me] + [self.voltages] * 4 + [self.window, basis, self.lists]
        aliases = {len(operands) + i: i for i in range(len(held))}
        return pl.pallas_call(
            functools.partial(first_kernel, z, self.scale, chunks, len(held)),
            in_specs=[
                self.me_spec,
                pl.BlockSpec((z.feed_dev, z.step_frames * NFFT), lambda g: (0, begin + g)),
                halo_spec(0),
                halo_spec(1),
                halo_spec(2),
                whole_spec((TAPS, NFFT)),
                whole_spec(basis.shape),
                whole_spec(self.lists.shape),
            ]
            + [pl.BlockSpec(memory_space=pl.ANY)] * len(held),
            out_specs=[
                pl.BlockSpec((z.step_lanes, NFFT), lambda g: (begin + g, 0)),
            ]
            + [pl.BlockSpec((z.rows, z.step_lanes), lambda g: (0, begin + g))] * count
            + [pl.BlockSpec(send_block, lambda g: (0, base + g, 0, 0))],
            out_shape=[self.filt_shape] + [self.spec_shape] * count + [self.message(units)],
            input_output_aliases=aliases,
            name="filter_spectra",
            **self.common(steps, chunks),
        )(*operands, *held)

    def next(self, chunks, filt, held):
        z = self.z
        basis = self.basis(chunks)
        begun = 3 * z.step_quads
        operands = [self.me, filt, basis, self.lists, held]
        return pl.pallas_call(
            functools.partial(next_kernel, z, self.scale, chunks),
            in_specs=[
                self.me_spec,
                pl.BlockSpec((z.step_lanes, NFFT), lambda g: (g, 0)),
                whole_spec(basis.shape),
                whole_spec(self.lists.shape),
                pl.BlockSpec(memory_space=pl.ANY),
            ],
            out_specs=[pl.BlockSpec((z.rows, z.step_lanes), lambda g: (0, g))] * 2
            + [
                pl.BlockSpec((z.devices, begun, BAND_CH, LANES), lambda g: (0, g, 0, 0)),
                pl.BlockSpec((z.devices, z.step_quads, BAND_CH, LANES), lambda g: (0, g, 0, 0)),
            ],
            out_shape=[self.spec_shape] * 2
            + [self.message(held.shape[1]), self.message(z.quads)],
            input_output_aliases={4: 2},
            name="spectra_next",
            **self.common(z.steps, chunks),
        )(*operands)


def receive_kernel(z, parities, step_pairs, runs, arrays, even_steps, beams, *refs):
    arr_refs, key_ref = refs[:arrays], refs[arrays]
    buf_ref, rows_ref, pick_ref, sems = refs[-4:]
    vis_ref = refs[-6] if beams else refs[-5]
    g = pl.program_id(0)
    if beams:
        kept_ref, away_ref, beams_ref = refs[arrays + 1], refs[arrays + 2], refs[-5]

        @pl.when(g == 0)
        def _():
            beams_ref[...] = kept_ref[0] + away_ref[0].astype(jnp.float32)

    lf = z.lane_frames
    few = BAND_CH // 2
    steps = few // step_pairs
    depth = buf_ref.shape[2] * BAND_CH
    slots = buf_ref.shape[0]
    at = g % steps

    def copies(c):
        return [
            pltpu.make_async_copy(
                arr_refs[array].at[:, first : first + count],
                buf_ref.at[c % slots, :, place : place + count],
                sems.at[c % slots, i],
            )
            for i, (array, first, count, place) in enumerate(runs[c])
        ]

    @pl.when(g == 0)
    def _():
        for one in copies(0):
            one.start()

    @pl.when(at == 0)
    def _():
        slot = lax.broadcasted_iota(jnp.int32, (z.groups * LANES, FSUB), 0)
        for tau in range(lf):
            key = key_ref[g // steps, tau : tau + 1, :]
            pick_ref[tau] = jnp.where(slot == key, 1.0, 0.0).astype(jnp.bfloat16)

    for c in range(len(runs)):

        @pl.when(g == c * steps)
        def _():
            for one in copies(c):
                one.wait()
            if c + 1 < len(runs):
                for one in copies(c + 1):
                    one.start()

    @pl.when(at == 0)
    def _():
        c = g // steps
        lane_group = lax.broadcasted_iota(jnp.int32, (depth, LANES), 1) // z.cap
        for tau in range(lf):
            tiles = []
            for big in range(z.groups):
                tile = buf_ref[c % slots, big * lf + tau].reshape(depth, LANES)
                for lane in range(1, lf):
                    block = buf_ref[c % slots, big * lf + (lane ^ tau)].reshape(depth, LANES)
                    tile = jnp.where(lane_group == lane, block, tile)
                tiles.append(tile)
            rows = jnp.dot(
                jnp.concatenate(tiles, axis=1), pick_ref[tau], preferred_element_type=jnp.float32
            )
            for side in range(FSUB // LANES):
                rows_ref[side, tau * depth : (tau + 1) * depth, :] = rows[
                    :, side * LANES : (side + 1) * LANES
                ]

    def correlate(todo):
        operands = []
        for i, p in todo:
            halves = []
            for part in range(2):
                first = p * BAND_CH + part * few + at * step_pairs + i
                halves.append(
                    jnp.concatenate(
                        [
                            rows_ref[side, pl.ds(first, FR, stride=parities * BAND_CH), :]
                            for side in range(FSUB // LANES)
                        ],
                        axis=1,
                    )
                )
            real, imag = halves
            both = jnp.concatenate([real, imag], axis=0)
            turned = jnp.concatenate([-imag, real], axis=0)
            right = jnp.concatenate([both, turned], axis=1).astype(jnp.bfloat16)
            operands.append((both.astype(jnp.bfloat16).T, right))
        outs = [
            jnp.dot(left, right, preferred_element_type=jnp.float32)
            for left, right in operands
        ]
        for (i, p), out in zip(todo, outs):
            out = out * (1.0 / FR)
            vis_ref[i, p, 0] = out[:, :FSUB]
            vis_ref[i, p, 1] = out[:, FSUB:]

    every = [(i, p) for i in range(step_pairs) for p in range(parities)]
    if even_steps:
        begin = len(runs) * steps - even_steps

        @pl.when(g < begin)
        def _():
            correlate(every)

        @pl.when(g >= begin)
        def _():
            correlate([(i, p) for i, p in every if p == 0])

    else:
        correlate(every)


def receive_call(z, chunk, parity, arrived, keys, vis, even_last=False, beams=()):
    parities = 2 if parity is None else 1
    step_pairs = 4
    steps = BAND_CH // 2 // step_pairs
    at = 0 if parity is None else parity
    out_shape = jax.ShapeDtypeStruct((z.chan_dev // 2, 2, 2, FSUB, FSUB), jnp.float32)
    arrays = []
    runs = []
    for one in arrived:
        runs.append([])
        for got, first, count, place in one:
            if not any(got is x for x in arrays):
                arrays.append(got)
            index = [got is x for x in arrays].index(True)
            runs[-1].append((index, first, count, place))
    units = parities * z.quads
    slots = min(2, len(runs))
    operands = arrays + [keys]
    in_specs = [pl.BlockSpec(memory_space=pl.ANY)] * len(arrays) + [whole_spec(keys.shape)]
    aliases = {}
    out_specs = [
        pl.BlockSpec(
            (step_pairs, parities, 2, FSUB, FSUB),
            lambda g: (chunk * steps + g, at, 0, 0, 0),
        )
    ]
    out_shape = [out_shape]
    if beams:
        in_specs += [whole_spec(x.shape) for x in beams]
        operands += beams
        out_specs.append(whole_spec(beams[0].shape[1:]))
        out_shape.append(jax.ShapeDtypeStruct(beams[0].shape[1:], jnp.float32))
    if vis is not None:
        in_specs.append(pl.BlockSpec(memory_space=pl.ANY))
        aliases = {len(operands): 0}
        operands.append(vis)
    share = parities * len(runs)
    return pl.pallas_call(
        functools.partial(
            receive_kernel, z, parities, step_pairs, runs, len(arrays),
            steps if even_last else 0, bool(beams),
        ),
        grid=(len(runs) * steps,),
        in_specs=in_specs,
        out_specs=out_specs,
        out_shape=out_shape,
        input_output_aliases=aliases,
        scratch_shapes=[
            pltpu.VMEM((slots, z.devices, units, BAND_CH, LANES), jnp.bfloat16),
            pltpu.VMEM(
                (FSUB // LANES, z.lane_frames * units * BAND_CH + z.rows_dev, LANES), jnp.float32
            ),
            pltpu.VMEM((z.lane_frames, z.groups * LANES, FSUB), jnp.bfloat16),
            pltpu.SemaphoreType.DMA((slots, max(len(x) for x in runs))),
        ],
        compiler_params=pltpu.CompilerParams(vmem_limit_bytes=VMEM // 2),
        cost_estimate=pl.CostEstimate(
            flops=2_000_000_000 * share, bytes_accessed=5_000_000 * share, transcendentals=0
        ),
        name="correlate",
    )(*operands)


def beam_kernel(z, me_ref, *refs):
    spec_refs = refs[: z.chunks]
    cos_base, sin_base, cos_step, sin_step, sum_ref, out_ref, prod_ref, row_ref = refs[z.chunks :]
    count = z.chan_dev
    weights = []
    for g in range(BEAMS):
        c0, s0 = cos_base[0, g : g + 1, :], sin_base[0, g : g + 1, :]
        c1, s1 = cos_step[g], sin_step[g]
        weights.append(
            ((c0 * c1 - s0 * s1).astype(jnp.bfloat16), (s0 * c1 + c0 * s1).astype(jnp.bfloat16))
        )
    for q in range(z.quads):
        lanes = slice(q * z.width, (q + 1) * z.width)
        x = [ref[:, lanes] for ref in spec_refs]
        real = jnp.concatenate([v[:BAND_CH] for v in x], axis=0)
        imag = jnp.concatenate([v[BAND_CH:] for v in x], axis=0)
        for g in range(BEAMS):
            c, s = weights[g]
            pair = (c * real + s * imag, c * imag - s * real)
            for part in range(2):
                row = (part * BEAMS + g) * count
                both = pair[part][:, :LANES] + pair[part][:, LANES:]
                prod_ref[row : row + count, q * LANES : (q + 1) * LANES] = both
    sums = jnp.dot(prod_ref[...], sum_ref[...], preferred_element_type=jnp.float32)
    sums = sums * (1.0 / np.sqrt(F))
    few = BAND_CH // 2
    for j in range(2 * BEAMS):
        for i in range(count // few):
            first = i // 2 * BAND_CH + i % 2
            top = j * count + i * few
            row_ref[j, pl.ds(first, few, stride=2), :] = sums[top : top + few]
        out_ref[0, :, j * FR : (j + 1) * FR] = row_ref[j, :count, :FR]


def beam_call(z, me, spectra, delays):
    bits = z.devices.bit_length() - 1
    lanes = FR * z.feed_dev
    halves = delays.reshape(BEAMS, 2, 1, z.cap)
    spread = jnp.broadcast_to(halves, (BEAMS, 2, z.lane_frames, z.cap)).reshape(BEAMS, z.width)
    unit = 2.0 * jnp.pi / NFFT
    owners = jnp.arange(z.devices, dtype=jnp.int32).astype(jnp.float32) * z.chan_dev
    inner = np.arange(z.chunks)[:, None] * BAND_CH + ORDER[None, :]
    inner = jnp.asarray(inner.reshape(-1).astype(np.float32))
    base = unit * (spread[None, :, :] * owners[:, None, None])
    step = unit * (spread[:, None, :] * inner[None, :, None])
    frame = (np.arange(FR * z.cap) // LANES) * z.lane_frames
    frame = frame + (np.arange(FR * z.cap) % LANES) // z.cap
    sums = (frame[:, None] == np.arange(LANES)[None, :]).astype(ml_dtypes.bfloat16)

    def owner(j, me_ref):
        k = 0
        for b in range(bits):
            k = k | (((j >> b) & 1) << (bits - 1 - b))
        return me_ref[0] ^ k

    base_spec = pl.BlockSpec(
        (1, BEAMS, z.width), lambda j, me_ref: (owner(j, me_ref), 0, 0)
    )
    grid_spec = pltpu.PrefetchScalarGridSpec(
        num_scalar_prefetch=1,
        grid=(z.devices,),
        in_specs=[
            pl.BlockSpec((z.rows_dev, lanes), lambda j, me_ref: (owner(j, me_ref), 0))
            for _ in range(z.chunks)
        ]
        + [base_spec, base_spec, whole_spec(step.shape), whole_spec(step.shape)]
        + [whole_spec(sums.shape)],
        out_specs=pl.BlockSpec(
            (1, z.chan_dev, 2 * BEAMS * FR), lambda j, me_ref: (j, 0, 0)
        ),
        scratch_shapes=[
            pltpu.VMEM((2 * BEAMS * z.chan_dev, FR * z.cap), jnp.bfloat16),
            pltpu.VMEM((2 * BEAMS, z.chan_dev + BAND_CH, LANES), jnp.float32),
        ],
    )
    return pl.pallas_call(
        functools.partial(beam_kernel, z),
        grid_spec=grid_spec,
        out_shape=jax.ShapeDtypeStruct((z.devices, z.chan_dev, 2 * BEAMS * FR), jnp.float32),
        compiler_params=pltpu.CompilerParams(vmem_limit_bytes=VMEM),
        cost_estimate=pl.CostEstimate(
            flops=20_000_000_000, bytes_accessed=20_000_000, transcendentals=0
        ),
        name="beam_sums",
    )(
        me, *spectra, jnp.cos(base), jnp.sin(base), jnp.cos(step), jnp.sin(step),
        jnp.asarray(sums),
    )


def swap(z, x, offset):
    return lax.ppermute(x, "chan", [(i, i ^ offset) for i in range(z.devices)])


def exchange(x):
    return lax.all_to_all(x, "chan", split_axis=0, concat_axis=0, tiled=True)


def on_device(voltages, delays, band_feeds):
    z = Sizes(lax.axis_size("chan"), voltages.shape[0])
    me = lax.axis_index("chan")
    me_array = me.astype(jnp.int32).reshape(1)

    own = lax.dynamic_slice_in_dim(band_feeds, me * z.bands_here, z.bands_here, 0)
    source = own // z.feed_dev
    before = jnp.sum(
        (own[:, None, :] < (source * z.feed_dev)[:, :, None]).astype(jnp.int32), axis=2
    )
    place = jnp.arange(FSUB, dtype=jnp.int32)[None, :] - before
    tau = jnp.arange(z.lane_frames, dtype=jnp.int32)
    big = (source // z.lane_frames) * LANES + place
    group = (source % z.lane_frames)[:, None, :] ^ tau[None, :, None]
    take_key = big[:, None, :] + z.cap * group

    calls = Spectra(z, me_array, voltages, band_feeds)
    early = list(range(z.early))
    basis = calls.basis(early)
    share = 2 * calls.fine.step_quads
    step = z.early * share
    arrived = [[] for _ in range(z.chunks)]
    steps = z.parts[0]
    filt, *spectra, send = calls.first(0, steps, early, basis, steps * step, 0, [])
    got = exchange(send)
    for c in early:
        arrived[c] += [(got, g * step + c * share, share, g * share) for g in range(steps)]
    if len(z.parts) > 1:
        begin, steps = steps, z.parts[1]
        late, begun = 2 * z.step_quads, 3 * z.step_quads
        base = z.steps * begun
        filt, *spectra, send = calls.first(
            begin, steps, early, basis, base + steps * step, base, [filt, *spectra]
        )
        *more, send, last = calls.next([z.chunks - 2, z.chunks - 1], filt, send)
        spectra = spectra + more
        got = exchange(send)
        for c in early:
            arrived[c] += [
                (got, base + g * step + c * share, share, (begin + g) * share)
                for g in range(steps)
            ]
        for g in range(z.steps):
            first = g * begun
            arrived[-2].append((got, first, late, g * late))
            arrived[-1] += [
                (got, first + late + q, 1, g * late + 2 * q) for q in range(z.step_quads)
            ]

    beams, bit = beam_call(z, me_array, spectra, delays), 1
    while beams.shape[0] > 2:
        half = beams.shape[0] // 2
        beams, bit = beams[:half] + swap(z, beams[half:], bit), 2 * bit
    kept, away = beams[:1], beams[1:].astype(jnp.bfloat16)
    if len(z.parts) > 1:
        last, kept, away = lax.optimization_barrier((last, kept, away))
        got = exchange(last)
        away = swap(z, away, bit)
        k = z.chunks - 1
        (vis,) = receive_call(z, 0, None, arrived, take_key, None, even_last=True)
        odd = [[(got, 0, z.quads, 0)]]
        vis, beams = receive_call(z, k, 1, odd, take_key[k:], vis, beams=[kept, away])
    else:
        (vis,) = receive_call(z, 0, None, arrived, take_key, None)
        beams = (kept + swap(z, away, bit).astype(jnp.float32)).reshape(z.chan_dev, -1)
    return (vis.reshape(z.chan_dev, 2, FSUB, FSUB), beams)


def solution(mesh):
    in_specs = (P(("grp", "chan"), None), P(None, ("grp", "chan")), P())
    out_specs = (P(("grp", "chan"), None, None, None), P(("grp", "chan"), None))
    return jax.shard_map(
        on_device, mesh=mesh, in_specs=in_specs, out_specs=out_specs, check_vma=False
    )
```
